32 devices in a mesh: seq: 8 (over z, y), tp: 4 (over x, core).
Axes of the slice: x: 2, y: 2, z: 4, core: 2. Of those that a mesh axis runs over, the one named last changes fastest.
Arguments:
- lin_query: bfloat16 [2048, 64, 128], P('seq', 'tp'), may hold values from -6 to 6
- lin_key: bfloat16 [2048, 64, 128], P('seq', 'tp'), may hold values from -6 to 6
- lin_value: bfloat16 [2048, 64, 128], P('seq', 'tp'), may hold values from -80 to 80
- lin_gate: bfloat16 [2048, 64, 128], P('seq', 'tp'), may hold values from -6 to 6
- log_decay: float32 [2048, 64], P('seq', 'tp'), may hold values from -1 to 0
- norm_gain: float32 [64, 128], P('tp'), may hold values from 0.1 to 1.9
- doc_ids: int32 [2048], P('seq'), may hold values from 0 to 3, never falling along the last dimension, each value on 1 to 1280 neighbouring positions
- soft_query: bfloat16 [2048, 64, 128], P('seq', 'tp'), may hold values from -200 to 200
- soft_key: bfloat16 [2048, 8, 128], P('seq'), may hold values from -6 to 6
- soft_value: bfloat16 [2048, 8, 128], P('seq'), may hold values from -6 to 6
Outputs:
- lin_out: bfloat16 [2048, 64, 128], P('seq', 'tp')
- soft_out: bfloat16 [2048, 64, 128], P('seq', 'tp')
The draws below stay inside these ranges and needn't reach their ends.
Inputs may be any that keep to these rules, and one draw needn't show every extreme that they name: `doc_ids`: ids never fall along the sequence; each document is one run of 1 to 1280 tokens, and one document has exactly that many.
All inputs are finite; a program needn't handle non-finite values.
Results may differ from the reference program's by a relative error of at most 0.012.
Values may be sent and summed in bfloat16 or wider, within the bound.
No kernel may reach another device: no remote copies, remote signals or barrier semaphores. Data moves between devices by JAX's collectives and lax.ppermute only.
A program may use at most 128 MiB of HBM per device.

```python
import math
import jax
import jax.numpy as jnp
import numpy as np
from jax import lax

HEADS = 64
HEAD_DIM = 128
KV_HEADS = 8
TOK_DEV = 256
DOCS = 4
STREAM_LENGTH = 2048


def draw_lin_value(key, part):
    base_key = jax.random.fold_in(key, 21)
    spread_key = jax.random.fold_in(key, 22)
    shape = (STREAM_LENGTH, HEADS, HEAD_DIM)
    base = jnp.clip(jax.random.normal(base_key, shape, jnp.float32), -6.0, 6.0)
    top_ramp = 3.0
    ramp = jnp.exp(math.log(top_ramp) * jnp.arange(HEADS).astype(jnp.float32) / (HEADS - 1))
    spread = jnp.exp(jax.random.uniform(spread_key, (HEADS,), jnp.float32, math.log(0.7), math.log(1.4)))
    return (base * (ramp * spread)[None, :, None]).astype(jnp.bfloat16)


def draw_log_decay(key, part):
    share_key = jax.random.fold_in(key, 31)
    slow_key = jax.random.fold_in(key, 32)
    fast_key = jax.random.fold_in(key, 33)
    block_key = jax.random.fold_in(key, 34)
    spike_seed = jax.random.fold_in(key, 35)
    keep_key = jax.random.fold_in(key, 36)
    share = 0.5
    slow_heads = jax.random.uniform(share_key, (HEADS,), jnp.float32) < share
    slow_rate = 0.25 * math.log(10.0) / STREAM_LENGTH * jnp.exp(jax.random.uniform(slow_key, (HEADS,), jnp.float32, math.log(0.2), 0.0))
    fast_rate = jnp.exp(jax.random.uniform(fast_key, (HEADS,), jnp.float32, math.log(1.0 / 50.0), math.log(1.0 / 30.0)))
    rate = jnp.where(slow_heads, slow_rate, fast_rate)
    block_count = STREAM_LENGTH // TOK_DEV
    block_factor = jnp.exp(jax.random.uniform(block_key, (block_count, HEADS), jnp.float32, -0.69, 0.69))
    block_factor = jnp.repeat(block_factor, TOK_DEV, axis=0)
    shrink_multiplier = -rate[None, :] * block_factor
    spike_offset = jax.random.randint(spike_seed, (2,), 0, STREAM_LENGTH)
    word_offsets = jnp.arange(STREAM_LENGTH)
    word_spike = jnp.any(word_offsets[:, None] == spike_offset[None, :], axis=1)
    retained_ratio = jax.random.uniform(keep_key, (STREAM_LENGTH, HEADS), jnp.float32, 0.6, 0.8)
    shrink_multiplier = shrink_multiplier + jnp.where(word_spike[:, None], jnp.log(retained_ratio), 0.0)
    return shrink_multiplier.astype(jnp.float32)


def soft_pair(key):
    key_draw = jax.random.fold_in(key, 11)
    query_draw = jax.random.fold_in(key, 12)
    key_rows = jnp.clip(jax.random.normal(key_draw, (STREAM_LENGTH, KV_HEADS, HEAD_DIM), jnp.float32), -6.0, 6.0)
    query_rows = jnp.clip(jax.random.normal(query_draw, (STREAM_LENGTH, HEADS, HEAD_DIM), jnp.float32), -6.0, 6.0)
    return (query_rows, key_rows)


def draw_soft_query(key, part):
    return soft_pair(key)[0].astype(jnp.bfloat16)


def draw_soft_key(key, part):
    return soft_pair(key)[1].astype(jnp.bfloat16)


def shard_levels(own_key, dims, cuts, least, high):
    loudness = 1.0
    for dim, shards_of in cuts:
        heights = jax.random.uniform(jax.random.fold_in(jax.random.fold_in(own_key, 6), dim), (shards_of,), jnp.float32, least / len(cuts), high / len(cuts))
        loudness = loudness * jnp.repeat(jnp.exp(heights), dims[dim] // shards_of).reshape((-1,) + (1,) * (len(dims) - 1 - dim))
    return loudness


def length_profile(number_of, total, limit, skew):
    loads = [(1 << 20) // math.isqrt(standing ** skew) + 1 for standing in range(2, number_of + 1)]
    surplus, given = total - limit - (number_of - 1), [1] * (number_of - 1)
    while surplus > 0:
        movable = [i for i in range(number_of - 1) if given[i] < limit]
        mass, left = sum([loads[i] for i in movable]), surplus
        for i in movable:
            extra = min(limit - given[i], max(1, left * loads[i] // mass), surplus)
            given[i] = given[i] + extra
            surplus = surplus - extra
    return np.array([limit] + given)


def uneven(own_key, number_of, total, most, slope):
    if number_of == 2:
        one = jax.random.randint(own_key, (), max(1, total - most), min(most, total - 1) + 1)
        return jnp.stack([one, total - one])
    lengths = jnp.asarray(length_profile(number_of, total, most, slope), jnp.int32)
    twos = (number_of - 1) // 2
    source_of, taker = lengths[1:1 + 2 * twos:2], lengths[2:2 + 2 * twos:2]
    room = jnp.minimum(source_of - 1, most - taker)
    moved = jax.random.randint(jax.random.fold_in(own_key, 1), (twos,), 0, 1 << 20) % (room + 1)
    lengths = lengths.at[1:1 + 2 * twos:2].set(source_of - moved).at[2:2 + 2 * twos:2].set(taker + moved)
    return lengths[jax.random.permutation(jax.random.fold_in(own_key, 2), number_of)]


def scatter_about(key, shape, scale, limit, cuts=(), held_as=jnp.bfloat16):
    values = scale * jax.random.normal(key, shape, jnp.float32)
    if cuts:
        values = values * shard_levels(key, shape, cuts, -0.22, 0.18)
    return jnp.clip(values, -limit, limit).astype(held_as)


def setup_inputs(seed: int = 0) -> dict:
    keys = jax.random.split(jax.random.key(seed), 11)
    return {
        "lin_query": scatter_about(keys[0], (STREAM_LENGTH, HEADS, HEAD_DIM), 1.0, 6.0, ((0, 8), (1, 4))),
        "lin_key": scatter_about(keys[1], (STREAM_LENGTH, HEADS, HEAD_DIM), 1.0, 6.0, ((0, 8), (1, 4))),
        "lin_value": draw_lin_value(jax.random.fold_in(keys[10], 71), 0),
        "lin_gate": scatter_about(keys[3], (STREAM_LENGTH, HEADS, HEAD_DIM), 1.5, 6.0, ((0, 8), (1, 4))),
        "log_decay": draw_log_decay(jax.random.fold_in(keys[10], 71), 0),
        "norm_gain": jnp.clip(1.0 + 0.18 * jax.random.normal(keys[5], (HEADS, HEAD_DIM), jnp.float32), 0.1, 1.9),
        "doc_ids": jnp.searchsorted(jnp.cumsum(uneven(keys[6], DOCS, STREAM_LENGTH, STREAM_LENGTH * 5 // 8, 0)), jnp.arange(STREAM_LENGTH), side="right").astype(jnp.int32),
        "soft_query": draw_soft_query(jax.random.fold_in(keys[10], 71), 0),
        "soft_key": draw_soft_key(jax.random.fold_in(keys[10], 71), 0),
        "soft_value": scatter_about(keys[9], (STREAM_LENGTH, KV_HEADS, HEAD_DIM), 1.0, 6.0, ((0, 8),)),
    }


def lightning_reference(lin_query, lin_key, lin_value, lin_gate, log_decay, norm_gain, doc_ids):
    block_count = STREAM_LENGTH // TOK_DEV
    query_blocks = lin_query.reshape(block_count, TOK_DEV, HEADS, HEAD_DIM)
    key_blocks = lin_key.reshape(block_count, TOK_DEV, HEADS, HEAD_DIM)
    value_blocks = lin_value.reshape(block_count, TOK_DEV, HEADS, HEAD_DIM)
    decay_blocks = log_decay.reshape(block_count, TOK_DEV, HEADS)
    doc_blocks = doc_ids.reshape(block_count, TOK_DEV)
    token_order = jnp.arange(TOK_DEV).astype(jnp.int32)
    highest = lax.Precision.HIGHEST

    def advance(running, block_data):
        prior_state, prior_doc = running
        query, key_rows, value_rows, shrink_multiplier, block_docs = block_data
        cumul = jnp.cumsum(shrink_multiplier, axis=0)
        visible = (token_order[None, :] <= token_order[:, None]) & (block_docs[None, :] == block_docs[:, None])
        cumul_heads = jnp.transpose(cumul)
        decay_gap = cumul_heads[:, :, None] - cumul_heads[:, None, :]
        factor = jnp.where(visible[None], jnp.exp(jnp.where(visible[None], decay_gap, 0.0)), 0.0)
        scores = jnp.einsum('thd,shd->hts', query.astype(jnp.float32), key_rows.astype(jnp.float32), precision=highest)
        weights = lax.optimization_barrier((scores * factor).astype(jnp.bfloat16))
        inner_part = jnp.einsum('hts,shd->thd', weights.astype(jnp.float32), value_rows.astype(jnp.float32), precision=highest)
        tail_mask = (block_docs == block_docs[-1]).astype(jnp.float32)
        key_scale = jnp.exp(cumul[-1][None, :] - cumul) * tail_mask[:, None]
        scaled_keys = lax.optimization_barrier((key_rows.astype(jnp.float32) * key_scale[:, :, None]).astype(jnp.bfloat16))
        block_state = jnp.einsum('shd,she->hde', scaled_keys.astype(jnp.float32), value_rows.astype(jnp.float32), precision=highest)
        state_rounded = lax.optimization_barrier(prior_state.astype(jnp.bfloat16))
        carried = jnp.einsum('thd,hde->the', query.astype(jnp.float32), state_rounded.astype(jnp.float32), precision=highest)
        open_mask = (block_docs == prior_doc).astype(jnp.float32)
        carried = carried * (jnp.exp(cumul) * open_mask[:, None])[:, :, None]
        linked = (prior_doc == block_docs[0]) & (block_docs[0] == block_docs[-1])
        passed = jnp.where(linked, jnp.exp(cumul[-1]), 0.0)
        next_state = passed[:, None, None] * prior_state + block_state
        return ((next_state, block_docs[-1]), inner_part + carried)
    start_state = jnp.zeros((HEADS, HEAD_DIM, HEAD_DIM), jnp.float32)
    start_doc = jnp.array(-1, dtype=doc_ids.dtype)
    _, mixed_blocks = lax.scan(advance, (start_state, start_doc), (query_blocks, key_blocks, value_blocks, decay_blocks, doc_blocks))
    mixed_heads = mixed_blocks.reshape(STREAM_LENGTH, HEADS, HEAD_DIM)
    square_mean = lax.optimization_barrier(jnp.mean(mixed_heads * mixed_heads, axis=(1, 2)))
    inv_rms = lax.rsqrt(square_mean + 1e-06)
    gated = jax.nn.sigmoid(lin_gate.astype(jnp.float32))
    return (mixed_heads * inv_rms[:, None, None] * norm_gain[None] * gated).astype(jnp.bfloat16)

def softmax_reference(soft_query, soft_key, soft_value, doc_ids):
    group_size = HEADS // KV_HEADS
    block_count = STREAM_LENGTH // TOK_DEV
    word_offsets = jnp.arange(STREAM_LENGTH).astype(jnp.int32)
    keys_by_head = jnp.transpose(soft_key, (1, 0, 2)).astype(jnp.float32)
    values_by_head = jnp.transpose(soft_value, (1, 0, 2)).astype(jnp.float32)
    query_blocks = soft_query.reshape(block_count, TOK_DEV, KV_HEADS, group_size, HEAD_DIM)
    score_scale = HEAD_DIM ** (-0.5)
    highest = lax.Precision.HIGHEST

    def one_block(block_index):
        query = lax.dynamic_index_in_dim(query_blocks, block_index, 0, keepdims=False)
        first_row = (block_index * TOK_DEV).astype(jnp.int32)
        query_pos = first_row + jnp.arange(TOK_DEV).astype(jnp.int32)
        query_docs = lax.dynamic_slice_in_dim(doc_ids, first_row, TOK_DEV)
        visible = (word_offsets[None, :] <= query_pos[:, None]) & (doc_ids[None, :] == query_docs[:, None])

        def one_head(head_index):
            head_query = lax.dynamic_index_in_dim(query, head_index, 1, keepdims=False).astype(jnp.float32)
            head_keys = lax.dynamic_index_in_dim(keys_by_head, head_index, 0, keepdims=False)
            head_values = lax.dynamic_index_in_dim(values_by_head, head_index, 0, keepdims=False)
            score = jnp.einsum('tgd,sd->gts', head_query, head_keys, precision=highest) * score_scale
            score = jnp.where(visible[None], score, -1e+30)
            top_score = lax.optimization_barrier(jnp.max(score, axis=-1, keepdims=True))
            soft_exp = jnp.where(visible[None], jnp.exp(score - top_score), 0.0)
            soft_total = lax.optimization_barrier(jnp.sum(soft_exp, axis=-1))
            soft_weights = lax.optimization_barrier(soft_exp.astype(jnp.bfloat16))
            weighted = jnp.einsum('gts,sd->gtd', soft_weights.astype(jnp.float32), head_values, precision=highest)
            return (weighted / soft_total[..., None]).astype(jnp.bfloat16)
        per_head = lax.map(one_head, jnp.arange(KV_HEADS).astype(jnp.int32))
        return jnp.transpose(per_head, (2, 0, 1, 3)).reshape(TOK_DEV, HEADS, HEAD_DIM)
    result = lax.map(one_block, jnp.arange(block_count).astype(jnp.int32))
    return result.reshape(STREAM_LENGTH, HEADS, HEAD_DIM)

def reference(lin_query, lin_key, lin_value, lin_gate, log_decay, norm_gain, doc_ids, soft_query, soft_key, soft_value):
    lin_out = lightning_reference(lin_query, lin_key, lin_value, lin_gate, log_decay, norm_gain, doc_ids)
    soft_out = softmax_reference(soft_query, soft_key, soft_value, doc_ids)
    return (lin_out, soft_out)
```

```python
import functools

import jax
import jax.numpy as jnp
import numpy as np
from jax import lax
from jax.experimental import pallas as pl
from jax.experimental.pallas import tpu as pltpu
from jax.sharding import PartitionSpec as P

HEADS = 64
HEAD_DIM = 128
KV_HEADS = 8
LANES = 128
GROUP = HEADS // KV_HEADS
F32 = jnp.float32
BF16 = jnp.bfloat16
BIG = float(2**20)
SCORE_TO_EXP2 = HEAD_DIM**-0.5 * float(np.log2(np.e))
INFO = 16
HIGHEST = lax.Precision.HIGHEST

VMEM = pl.BlockSpec(memory_space=pltpu.VMEM)
SMEM = pl.BlockSpec(memory_space=pltpu.SMEM)


def sds(shape, dtype):
    return jax.ShapeDtypeStruct(shape, dtype)


def params(mib):
    return pltpu.CompilerParams(vmem_limit_bytes=mib * 1024 * 1024)


def cost(flops, bytes_accessed, transcendentals=0):
    return pl.CostEstimate(
        flops=int(flops), bytes_accessed=int(bytes_accessed), transcendentals=int(transcendentals)
    )


def doc_columns(doc_rows, tokens):
    parts = []
    for i in range(tokens // LANES):
        row = jnp.broadcast_to(doc_rows[i : i + 1, :], (LANES, LANES))
        parts.append(jnp.transpose(row))
    return jnp.concatenate(parts, axis=0)


def doc_line(doc_rows, tokens):
    return jnp.concatenate([doc_rows[i : i + 1, :] for i in range(tokens // LANES)], axis=1)


def lower_triangle(tokens):
    rows = lax.broadcasted_iota(jnp.int32, (tokens, tokens), 0)
    cols = lax.broadcasted_iota(jnp.int32, (tokens, tokens), 1)
    return rows >= cols


def cumulative(log_decay, tokens):
    return jnp.dot(
        lower_triangle(tokens).astype(F32), log_decay, precision=HIGHEST, preferred_element_type=F32
    )


def pack_kernel(tokens, kv_here, start_ref, key_ref, value_ref, doc_ref, out_ref, scratch):
    start = start_ref[0]
    for which, ref in enumerate((key_ref, value_ref)):
        scratch[...] = ref[...].astype(F32)
        for g in range(kv_here):
            rows = scratch[pl.ds(start + g, tokens, stride=KV_HEADS), :]
            at = (which * kv_here + g) * tokens
            out_ref[at : at + tokens, :] = rows.astype(BF16)
    end = 2 * kv_here * tokens
    out_ref[end : end + INFO, :] = doc_ref[...].astype(BF16)


def pack_kv(start, soft_key, soft_value, doc_rows, tokens, kv_here):
    rows = 2 * kv_here * tokens + INFO
    return pl.pallas_call(
        functools.partial(pack_kernel, tokens, kv_here),
        out_shape=sds((rows, LANES), BF16),
        in_specs=[SMEM, VMEM, VMEM, VMEM],
        out_specs=VMEM,
        scratch_shapes=[pltpu.VMEM((tokens * KV_HEADS, LANES), F32)],
        compiler_params=params(16),
        cost_estimate=cost(0, 4 * tokens * KV_HEADS * LANES * 2),
        name="pack_kv",
    )(start, soft_key, soft_value, doc_rows)


def state_kernel(tokens, heads, y_ref, ld_ref, doc_ref, key_ref, value_ref, keep_ref, send_ref, info_ref, kf, vf, states, ldp):
    half = heads // 2
    y = y_ref[0]
    ldp[...] = jnp.zeros_like(ldp)
    ldp[:, 0:heads] = ld_ref[...]
    cumul = cumulative(ldp[...], tokens)
    total = cumul[tokens - 1 : tokens, :]
    docs = doc_ref[...]
    last_row = tokens // LANES - 1
    first_doc = docs[0:1, 0:1]
    last_doc = docs[last_row : last_row + 1, LANES - 1 : LANES]
    tail = (doc_columns(docs, tokens) == last_doc).astype(F32)
    scale = jnp.exp(total - cumul) * tail
    kf[...] = key_ref[...].astype(F32)
    vf[...] = value_ref[...].astype(F32)
    for h in range(heads):
        keys = (kf[pl.ds(h, tokens, stride=heads), :] * scale[:, h : h + 1]).astype(BF16)
        values = vf[pl.ds(h, tokens, stride=heads), :].astype(BF16)
        states[h * HEAD_DIM : (h + 1) * HEAD_DIM, :] = lax.dot_general(
            keys, values, (((0,), (0,)), ((), ())), preferred_element_type=F32
        )
    size = half * HEAD_DIM
    keep_ref[...] = states[pl.ds(pl.multiple_of(y * size, size), size), :].astype(BF16)
    send_ref[0:size, :] = states[pl.ds(pl.multiple_of((1 - y) * size, size), size), :].astype(BF16)
    upper = pltpu.roll(total, LANES - half, 1)
    rows = lax.broadcasted_iota(jnp.int32, (INFO, LANES), 0)

    def info_of(totals):
        hi = totals.astype(BF16).astype(F32)
        mid = (totals - hi).astype(BF16).astype(F32)
        lo = totals - hi - mid
        return jnp.where(
            rows == 0,
            hi,
            jnp.where(
                rows == 1,
                mid,
                jnp.where(
                    rows == 2, lo, jnp.where(rows == 3, first_doc, jnp.where(rows == 4, last_doc, 0.0))
                ),
            ),
        ).astype(BF16)

    mine = (y == 0).astype(F32)
    info_ref[...] = info_of(total * mine + upper * (1.0 - mine))
    send_ref[size : size + INFO, :] = info_of(total * (1.0 - mine) + upper * mine)


def block_state(y, log_decay, doc_rows, key, value, tokens, heads):
    size = heads // 2 * HEAD_DIM
    return pl.pallas_call(
        functools.partial(state_kernel, tokens, heads),
        out_shape=(sds((size, LANES), BF16), sds((size + INFO, LANES), BF16), sds((INFO, LANES), BF16)),
        in_specs=[SMEM, VMEM, VMEM, VMEM, VMEM],
        out_specs=(VMEM, VMEM, VMEM),
        scratch_shapes=[
            pltpu.VMEM((tokens * heads, LANES), F32),
            pltpu.VMEM((tokens * heads, LANES), F32),
            pltpu.VMEM((heads * HEAD_DIM, LANES), F32),
            pltpu.VMEM((tokens, LANES), F32),
        ],
        compiler_params=params(24),
        cost_estimate=cost(2 * heads * tokens * HEAD_DIM**2, 3 * tokens * heads * LANES * 2),
        name="block_state",
    )(y, log_decay, doc_rows, key, value)


def row_terms(y_ref, own_info, other_info):
    even = y_ref[0] == 0
    own = own_info.astype(F32)
    other = other_info.astype(F32)
    a = jnp.where(even, own, other)
    b = jnp.where(even, other, own)
    decay_a = jnp.exp(a[0:1] + a[1:2] + a[2:3])
    decay_b = jnp.exp(b[0:1] + b[1:2] + b[2:3])
    first_a, last_a = a[3:4], a[4:5]
    first_b, last_b = b[3:4], b[4:5]
    whole_a = (first_a == last_a).astype(F32)
    link_b = ((last_a == first_b) & (first_b == last_b)).astype(F32)
    return even, decay_a, decay_b * link_b, first_a, whole_a, last_a, last_b


def chain_kernel(count, first, arrivals, y_ref, *refs):
    keep_ref, info_ref, other_ref, other_info_ref = refs[:4]
    came, out_ref = refs[4 : 4 + arrivals], refs[4 + arrivals]
    size = count * HEAD_DIM
    even, decay_a, gain_b, first_a, whole_a, _, last_b = row_terms(
        y_ref, info_ref[...], other_info_ref[...]
    )
    if arrivals:
        came_doc = came[0][size : size + 1, :].astype(F32)
        gain_a = decay_a * whole_a * (came_doc == first_a).astype(F32)
    for i in range(count):
        rows = slice(i * HEAD_DIM, (i + 1) * HEAD_DIM)
        lane = slice(first + i, first + i + 1)
        own = keep_ref[rows, :].astype(F32)
        other = other_ref[rows, :].astype(F32)
        total = jnp.where(even, own, other)
        if arrivals:
            total = total + gain_a[:, lane] * came[0][rows, :].astype(F32)
        out_ref[rows, :] = (gain_b[:, lane] * total + jnp.where(even, other, own)).astype(BF16)
    out_ref[size : size + INFO, :] = jnp.broadcast_to(last_b, (INFO, LANES)).astype(BF16)


def chain_step(y, keep, info, other, other_info, came, first, count):
    size = count * HEAD_DIM
    came = [] if came is None else [came]
    return pl.pallas_call(
        functools.partial(chain_kernel, count, first, len(came)),
        out_shape=sds((size + INFO, LANES), BF16),
        in_specs=[SMEM] + [VMEM] * (4 + len(came)),
        out_specs=VMEM,
        compiler_params=params(8),
        cost_estimate=cost(4 * size * LANES, 4 * size * LANES * 2),
        name="chain_step",
    )(y, keep, info, other, other_info, *came)


def prior_kernel(count, first, arrivals, y_ref, *refs):
    keep_ref, info_ref, other_ref, other_info_ref = refs[:4]
    came = refs[4 : 4 + arrivals]
    mine_ref, send_ref, doc_ref = refs[4 + arrivals :]
    size = count * HEAD_DIM
    even, decay_a, _, first_a, whole_a, last_a, _ = row_terms(
        y_ref, info_ref[...], other_info_ref[...]
    )
    came_doc = jnp.zeros((1, LANES), F32)
    for ref in came:
        came_doc = came_doc + ref[size : size + 1, :].astype(F32)
    gain_a = decay_a * whole_a * (came_doc == first_a).astype(F32)
    for i in range(count):
        rows = slice(i * HEAD_DIM, (i + 1) * HEAD_DIM)
        lane = slice(first + i, first + i + 1)
        before_a = jnp.zeros((HEAD_DIM, LANES), F32)
        for ref in came:
            before_a = before_a + ref[rows, :].astype(F32)
        state_a = jnp.where(even, keep_ref[rows, :].astype(F32), other_ref[rows, :].astype(F32))
        before_b = gain_a[:, lane] * before_a + state_a
        mine_ref[rows, :] = jnp.where(even, before_a, before_b).astype(BF16)
        send_ref[rows, :] = jnp.where(even, before_b, before_a).astype(BF16)
    doc_ref[...] = jnp.broadcast_to(jnp.where(even, came_doc, last_a), (8, LANES))


def prior_states(y, keep, info, other, other_info, came, first, count):
    size = count * HEAD_DIM
    return pl.pallas_call(
        functools.partial(prior_kernel, count, first, len(came)),
        out_shape=(sds((size, LANES), BF16), sds((size, LANES), BF16), sds((8, LANES), F32)),
        in_specs=[SMEM] + [VMEM] * (4 + len(came)),
        out_specs=(VMEM, VMEM, VMEM),
        compiler_params=params(8),
        cost_estimate=cost(4 * size * LANES, 6 * size * LANES * 2),
        name="prior_states",
    )(y, keep, info, other, other_info, *came)


def inner_kernel(tokens, heads, ld_ref, ldt_ref, doc_ref, query_ref, key_ref, value_ref, inner_ref, qh_ref, grow_ref, qf, kf, vf, ldp, mask):
    ldp[...] = jnp.zeros_like(ldp)
    ldp[:, 0:heads] = ld_ref[...]
    cumul = cumulative(ldp[...], tokens)
    grow_ref[...] = jnp.exp(cumul)
    cumul_t = lax.dot_general(
        ldt_ref[...],
        lower_triangle(tokens).astype(F32),
        (((1,), (1,)), ((), ())),
        precision=HIGHEST,
        preferred_element_type=F32,
    )
    docs = doc_ref[...]
    column = doc_columns(docs, tokens)
    line = doc_line(docs, tokens)
    same = jnp.concatenate([column] * (tokens // LANES), axis=1) == line
    mask[...] = jnp.where(lower_triangle(tokens) & same, 0.0, -1e9)
    qf[...] = query_ref[...].astype(F32)
    kf[...] = key_ref[...].astype(F32)
    vf[...] = value_ref[...].astype(F32)
    for h in range(heads):
        picked = pl.ds(h, tokens, stride=heads)
        query = qf[picked, :].astype(BF16)
        keys = kf[picked, :].astype(BF16)
        values = vf[picked, :].astype(BF16)
        qh_ref[h * tokens : (h + 1) * tokens, :] = query
        for i in range(tokens // LANES):
            seen = (i + 1) * LANES
            rows = slice(i * LANES, seen)
            scores = lax.dot_general(
                query[rows, :], keys[0:seen, :], (((1,), (1,)), ((), ())), preferred_element_type=F32
            )
            gap = cumul[rows, h : h + 1] - cumul_t[h : h + 1, 0:seen]
            weights = (scores * jnp.exp(gap + mask[rows, 0:seen])).astype(BF16)
            inner_ref[h * tokens + i * LANES : h * tokens + seen, :] = jnp.dot(
                weights, values[0:seen, :], preferred_element_type=F32
            )


def inner_part(log_decay, doc_rows, query, key, value, tokens, heads):
    return pl.pallas_call(
        functools.partial(inner_kernel, tokens, heads),
        out_shape=(
            sds((heads * tokens, LANES), F32),
            sds((heads * tokens, LANES), BF16),
            sds((tokens, LANES), F32),
        ),
        in_specs=[VMEM] * 6,
        out_specs=(VMEM, VMEM, VMEM),
        scratch_shapes=[pltpu.VMEM((tokens * heads, LANES), F32)] * 3
        + [pltpu.VMEM((tokens, LANES), F32), pltpu.VMEM((tokens, tokens), F32)],
        compiler_params=params(32),
        cost_estimate=cost(
            4 * heads * tokens * tokens * HEAD_DIM, tokens * heads * LANES * 12, heads * tokens * tokens
        ),
        name="inner_part",
    )(log_decay, jnp.transpose(log_decay), doc_rows, query, key, value)


def mix_kernel(tokens, heads, pieces, y_ref, doc_ref, prior_doc_ref, grow_ref, inner_ref, qh_ref, *refs):
    mine, other = refs[:pieces], refs[pieces : 2 * pieces]
    mixed_ref, square_ref = refs[2 * pieces :]
    half = heads // 2
    count = half // pieces
    even = y_ref[0] == 0
    is_open = (doc_columns(doc_ref[...], tokens) == prior_doc_ref[0:1, :]).astype(F32)
    gain = grow_ref[...] * is_open
    squares = jnp.zeros((tokens, LANES), F32)
    for h in range(heads):
        piece, i = divmod(h % half, count)
        rows = slice(i * HEAD_DIM, (i + 1) * HEAD_DIM)
        near, far = mine[piece][rows, :], other[piece][rows, :]
        lower = h < half
        state = jnp.where(even, near if lower else far, far if lower else near)
        held = slice(h * tokens, (h + 1) * tokens)
        carried = jnp.dot(qh_ref[held, :], state, preferred_element_type=F32)
        mixed = inner_ref[held, :] + carried * gain[:, h : h + 1]
        squares = squares + mixed * mixed
        mixed_ref[pl.ds(h, tokens, stride=heads), :] = mixed
    square_ref[...] = lax.dot_general(
        jnp.ones((8, LANES), F32),
        squares,
        (((1,), (1,)), ((), ())),
        precision=HIGHEST,
        preferred_element_type=F32,
    )


def mix(y, doc_rows, prior_doc, grow, inner, qh, mine, other, tokens, heads):
    return pl.pallas_call(
        functools.partial(mix_kernel, tokens, heads, len(mine)),
        out_shape=(sds((tokens * heads, LANES), F32), sds((8, tokens), F32)),
        in_specs=[SMEM] + [VMEM] * (5 + 2 * len(mine)),
        out_specs=(VMEM, VMEM),
        compiler_params=params(24),
        cost_estimate=cost(2 * heads * tokens * HEAD_DIM**2, tokens * heads * LANES * 10),
        name="mix",
    )(y, doc_rows, prior_doc, grow, inner, qh, *mine, *other)


def finish_kernel(tokens, heads, sums, gain_ref, gate_ref, mixed_ref, *refs):
    squares, out_ref = refs[:sums], refs[sums]
    total = squares[0][0:1, :]
    for ref in squares[1:]:
        total = total + ref[0:1, :]
    scale = lax.rsqrt(total / (HEADS * HEAD_DIM) + 1e-06)
    rows = jnp.concatenate([scale[:, i * LANES : (i + 1) * LANES] for i in range(tokens // LANES)], axis=0)
    column = doc_columns(rows, tokens)
    step = 32
    for i in range(0, tokens, step):
        at = slice(i * heads, (i + step) * heads)
        gate = jax.nn.sigmoid(gate_ref[at, :].astype(F32)).reshape(step, heads, LANES)
        mixed = mixed_ref[at, :].reshape(step, heads, LANES)
        inv = column[i : i + step, :][:, None, :]
        out = mixed * inv * gain_ref[...][None] * gate
        out_ref[at, :] = out.reshape(step * heads, LANES).astype(BF16)


def finish(gain, gate, mixed, squares, tokens, heads):
    return pl.pallas_call(
        functools.partial(finish_kernel, tokens, heads, len(squares)),
        out_shape=sds((tokens * heads, LANES), BF16),
        in_specs=[VMEM] * (3 + len(squares)),
        out_specs=VMEM,
        compiler_params=params(16),
        cost_estimate=cost(0, tokens * heads * LANES * 8, tokens * heads * LANES),
        name="finish",
    )(gain, gate, mixed, *squares)


def attend_kernel(tokens, step, heads, kv_here, blocks, has_own, has_state, is_last, *refs):
    refs = list(refs)
    doc_ref, query_ref = refs.pop(0), refs.pop(0)
    kv = [refs.pop(0) for _ in range(blocks)]
    state_ref = refs.pop(0) if has_state else None
    out_ref, keys_ext, values_ext, doc_rep, doc_col = refs
    per_group = heads // kv_here
    rows = step * per_group
    span = blocks * tokens
    index = pl.program_id(0)

    @pl.when(index == 0)
    def _():
        lane = lax.broadcasted_iota(jnp.int32, (tokens, LANES), 1).astype(F32)
        column = doc_columns(doc_ref[...], tokens)
        for h in range(per_group):
            doc_rep[pl.ds(h, tokens, stride=per_group), :] = (column == lane).astype(F32)
        for j, ref in enumerate(kv):
            end = 2 * kv_here * tokens
            docs = doc_columns(ref[end : end + INFO, :].astype(F32), tokens)
            bias = jnp.where(docs == lane, 0.0, -BIG).astype(BF16)
            for g in range(kv_here):
                at = slice(j * tokens, (j + 1) * tokens)
                keys_ext[g, at, 0:LANES] = ref[g * tokens : (g + 1) * tokens, :]
                keys_ext[g, at, LANES:] = bias
                begin = (kv_here + g) * tokens
                values_ext[g, at, 0:LANES] = ref[begin : begin + tokens, :]
                values_ext[g, at, LANES:] = jnp.ones((tokens, LANES), BF16)

    one_hot = doc_rep[pl.ds(pl.multiple_of(index * rows, rows), rows), :].astype(BF16)
    query_all = query_ref[...].astype(F32).reshape(step, heads, LANES)
    results = []
    for g in range(kv_here):
        query = query_all[:, g * per_group : (g + 1) * per_group, :].reshape(rows, LANES).astype(BF16)
        query = jnp.concatenate([query, one_hot], axis=1)
        scores = lax.dot_general(
            query, keys_ext[g], (((1,), (1,)), ((), ())), preferred_element_type=F32
        )
        if has_own:
            token = index * step + lax.broadcasted_iota(jnp.int32, (rows, tokens), 0) // per_group
            where_key = lax.broadcasted_iota(jnp.int32, (rows, tokens), 1)
            own = jnp.where(where_key <= token, scores[:, 0:tokens], -BIG)
            scores = own if blocks == 1 else jnp.concatenate([own, scores[:, tokens:]], axis=1)
        top = jnp.max(scores, axis=1, keepdims=True)
        if has_state:
            before = state_ref[g]
            top_before = before[:, 2 * LANES - 1 : 2 * LANES]
            top = jnp.maximum(top, top_before)
        weights = jnp.exp2((scores - top) * SCORE_TO_EXP2).astype(BF16)
        total = jnp.dot(weights, values_ext[g], preferred_element_type=F32)
        if has_state:
            total = total + before * jnp.exp2((top_before - top) * SCORE_TO_EXP2)
        if is_last:
            results.append(total[:, 0:LANES] / total[:, LANES : LANES + 1])
        else:
            lane = lax.broadcasted_iota(jnp.int32, (rows, 2 * LANES), 1)
            out_ref[g] = jnp.where(lane == 2 * LANES - 1, top, total)
    if is_last:
        results = [r.reshape(step, per_group, LANES) for r in results]
        out = results[0] if kv_here == 1 else jnp.concatenate(results, axis=1)
        out_ref[...] = out.reshape(step * heads, LANES).astype(BF16)


def attend(doc_rows, query, kv, state, is_last, has_own, tokens, heads, kv_here):
    step = 64
    per_group = heads // kv_here
    blocks = len(kv)
    span = blocks * tokens
    whole = lambda shape: pl.BlockSpec(shape, lambda i: (0,) * len(shape))
    state_spec = pl.BlockSpec((kv_here, step * per_group, 2 * LANES), lambda i: (0, i, 0))
    row_spec = pl.BlockSpec((step * heads, LANES), lambda i: (i, 0))
    in_specs = [whole((INFO, LANES)), row_spec] + [whole(kv[0].shape)] * blocks
    operands = [doc_rows, query, *kv]
    if state is not None:
        in_specs.append(state_spec)
        operands.append(state)
    if is_last:
        out_shape, out_spec = sds((tokens * heads, LANES), BF16), row_spec
    else:
        out_shape = sds((kv_here, tokens * per_group, 2 * LANES), F32)
        out_spec = state_spec
    moved = 2 * tokens * heads * LANES * 2 + blocks * kv[0].size * 2 + 4 * tokens * heads * LANES * 2
    return pl.pallas_call(
        functools.partial(
            attend_kernel, tokens, step, heads, kv_here, blocks, has_own, state is not None, is_last
        ),
        grid=(tokens // step,),
        out_shape=out_shape,
        in_specs=in_specs,
        out_specs=out_spec,
        scratch_shapes=[
            pltpu.VMEM((kv_here, span, 2 * LANES), BF16),
            pltpu.VMEM((kv_here, span, 2 * LANES), BF16),
            pltpu.VMEM((tokens * per_group, LANES), F32),
            pltpu.VMEM((tokens, LANES), F32),
        ],
        compiler_params=params(40),
        cost_estimate=cost(4 * tokens * heads * span * 2 * LANES, moved, tokens * heads * span),
        name="attend",
    )(*operands)


def body(
    blocks,
    lin_query,
    lin_key,
    lin_value,
    lin_gate,
    log_decay,
    norm_gain,
    doc_ids,
    soft_query,
    soft_key,
    soft_value,
):
    tokens, heads, _ = lin_query.shape
    tensor = HEADS // heads
    kv_here = max(1, heads // GROUP)
    half = heads // 2
    pieces = 2 if half % 2 == 0 else 1
    count = half // pieces
    longest = blocks * tokens * 5 // 8
    window = min(blocks - 1, (longest - 1 + tokens - 1) // tokens)
    flat = lambda x: x.reshape(-1, LANES)
    block = lax.axis_index("seq")
    y = (block % 2).astype(jnp.int32).reshape(1)
    start = (lax.axis_index("tp") * heads // GROUP).astype(jnp.int32).reshape(1)
    doc_rows = (doc_ids + 1).astype(F32).reshape(tokens // LANES, LANES)
    doc_rows = jnp.pad(doc_rows, ((0, INFO - tokens // LANES), (0, 0)))

    def send(x, pairs):
        return lax.ppermute(x, "seq", [p for p in pairs if 0 <= p[0] < blocks and 0 <= p[1] < blocks])

    everyone = range(blocks)
    swap = [(b, b ^ 1) for b in everyone]

    own_kv = pack_kv(start, flat(soft_key), flat(soft_value), doc_rows, tokens, kv_here)
    beside = send(own_kv, [(b, b + 1) for b in everyone if b % 2 == 0])
    lane_kv, cross_kv = [], []
    ahead = own_kv
    for back in range(1, window // 2 + 1):
        ahead = send(ahead, [(b, b + 2) for b in everyone if b >= 2 * (back - 1)])
        lane_kv.append(ahead)
        cross_kv.append(send(ahead, [p for p in swap if p[0] >= 2 * back]))
    extra_kv = []
    if window % 2:
        extra_kv.append(send(own_kv, [(b, b + window) for b in everyone if b % 2 == 1]))

    keep, other, info = block_state(y, log_decay, doc_rows, flat(lin_key), flat(lin_value), tokens, heads)
    size = count * HEAD_DIM
    other_info = None
    came = []
    for piece in range(pieces):
        sent = other[piece * size : (piece + 1) * size]
        if piece == 0:
            sent = jnp.concatenate([sent, other[half * HEAD_DIM :]], axis=0)
        got = send(sent, swap)
        if piece == 0:
            other_info = got[size:]
        came.append([got])
    rows = blocks // 2
    latest = [None] * pieces
    arrived = [[] for _ in range(pieces)]
    held = [keep[p * size : (p + 1) * size] for p in range(pieces)]
    for row in range(rows - 1):
        for p in range(pieces):
            out = chain_step(y, held[p], info, came[p][0], other_info, latest[p], p * count, count)
            latest[p] = send(out, [(2 * row, 2 * row + 2), (2 * row + 1, 2 * row + 3)])
            arrived[p].append(latest[p])
    mine, far = [], []
    prior_doc = None
    for p in range(pieces):
        got, sent, prior_doc = prior_states(
            y, held[p], info, came[p][0], other_info, arrived[p], p * count, count
        )
        mine.append(got)
        far.append(send(sent, swap))

    inner, qh, grow = inner_part(
        log_decay, doc_rows, flat(lin_query), flat(lin_key), flat(lin_value), tokens, heads
    )

    query = flat(soft_query)
    early = [own_kv, beside] + lane_kv[:1]
    late = lane_kv[1:] + cross_kv + extra_kv
    state = attend(doc_rows, query, early, None, False, True, tokens, heads, kv_here)
    soft_out = attend(doc_rows, query, late, state, True, False, tokens, heads, kv_here)

    mixed, squares = mix(y, doc_rows, prior_doc, grow, inner, qh, mine, far, tokens, heads)
    sums = [squares]
    for shift in range(1, tensor):
        sums.append(
            lax.ppermute(squares, "tp", [(t, (t + shift) % tensor) for t in range(tensor)])
        )
    lin_out = finish(norm_gain, flat(lin_gate), mixed, sums, tokens, heads)
    shape = (tokens, heads, HEAD_DIM)
    return lin_out.reshape(shape), soft_out.reshape(shape)


def solution(mesh):
    in_specs = (
        P("seq", "tp", None),
        P("seq", "tp", None),
        P("seq", "tp", None),
        P("seq", "tp", None),
        P("seq", "tp"),
        P("tp", None),
        P("seq"),
        P("seq", "tp", None),
        P("seq", None, None),
        P("seq", None, None),
    )
    out_specs = (P("seq", "tp", None), P("seq", "tp", None))
    return jax.shard_map(
        functools.partial(body, mesh.shape["seq"]),
        mesh=mesh,
        in_specs=in_specs,
        out_specs=out_specs,
        check_vma=False,
    )
```

```python
import functools

import jax
import jax.numpy as jnp
import numpy as np
from jax import lax
from jax.experimental import pallas as pl
from jax.experimental.pallas import tpu as pltpu
from jax.sharding import PartitionSpec as P

HEADS = 64
HEAD_DIM = 128
KV_HEADS = 8
LANES = 128
GROUP = HEADS // KV_HEADS
F32 = jnp.float32
BF16 = jnp.bfloat16
BIG = float(2**20)
SCORE_TO_EXP2 = HEAD_DIM**-0.5 * float(np.log2(np.e))
INFO = 16
HIGHEST = lax.Precision.HIGHEST

VMEM = pl.BlockSpec(memory_space=pltpu.VMEM)
SMEM = pl.BlockSpec(memory_space=pltpu.SMEM)
ANYWHERE = pl.BlockSpec(memory_space=pl.ANY)
STATE_ROWS = HEAD_DIM + 16
CHUNK = 256


def sds(shape, dtype):
    return jax.ShapeDtypeStruct(shape, dtype)


def cost(flops, bytes_accessed, transcendentals=0):
    return pl.CostEstimate(
        flops=int(flops), bytes_accessed=int(bytes_accessed), transcendentals=int(transcendentals)
    )


def call(kernel, name, operands, out_shape, scratch=(), mib=16, estimate=None, scalars=(), after=()):
    outs = out_shape if isinstance(out_shape, tuple) else (out_shape,)
    begin = len(scalars) + len(operands)
    skip = len(after)

    def run(*refs):
        kernel(*refs[:begin], *refs[begin + skip :])

    return pl.pallas_call(
        run,
        out_shape=out_shape,
        in_specs=[SMEM] * len(scalars) + [VMEM] * len(operands) + [ANYWHERE] * skip,
        out_specs=(VMEM,) * len(outs) if isinstance(out_shape, tuple) else VMEM,
        scratch_shapes=list(scratch),
        compiler_params=pltpu.CompilerParams(vmem_limit_bytes=mib * 1024 * 1024),
        cost_estimate=estimate,
        name=name,
    )(*scalars, *operands, *after)


def doc_columns(doc_rows, tokens):
    parts = []
    for i in range(tokens // LANES):
        row = jnp.broadcast_to(doc_rows[i : i + 1, :], (LANES, LANES))
        parts.append(jnp.transpose(row))
    return jnp.concatenate(parts, axis=0)


def doc_line(doc_rows, tokens):
    return jnp.concatenate([doc_rows[i : i + 1, :] for i in range(tokens // LANES)], axis=1)


def doc_numbers(doc_ref):
    return doc_ref[...].astype(F32) + 1.0


def lower_triangle(tokens):
    rows = lax.broadcasted_iota(jnp.int32, (tokens, tokens), 0)
    cols = lax.broadcasted_iota(jnp.int32, (tokens, tokens), 1)
    return rows >= cols


def cumulative(ld_ref, ldp, tokens, heads):
    ldp[...] = jnp.zeros_like(ldp)
    ldp[0:heads, :] = ld_ref[...]
    return lax.dot_general(
        lower_triangle(tokens).astype(F32),
        ldp[...],
        (((1,), (1,)), ((), ())),
        precision=HIGHEST,
        preferred_element_type=F32,
    )


def pack_kernel(tokens, kv_here, start_ref, key_ref, value_ref, doc_ref, out_ref, scratch):
    start = start_ref[0]
    for which, ref in enumerate((key_ref, value_ref)):
        scratch[...] = ref[...].astype(F32)
        for g in range(kv_here):
            rows = scratch[pl.ds(start + g, tokens, stride=KV_HEADS), :]
            at = (which * kv_here + g) * tokens
            if which:
                halves = [jnp.transpose(rows[i : i + LANES, :]) for i in range(0, tokens, LANES)]
                rows = jnp.concatenate(halves, axis=0)
            out_ref[at : at + tokens, :] = rows.astype(BF16)
    end = 2 * kv_here * tokens
    docs = doc_numbers(doc_ref)
    line = lax.broadcasted_iota(jnp.int32, (INFO, LANES), 0)
    info = jnp.zeros((INFO, LANES), F32)
    for i in range(tokens // LANES):
        info = jnp.where(line == i, docs[i : i + 1, :], info)
    out_ref[end : end + INFO, :] = info.astype(BF16)


def pack_kv(start, soft_key, soft_value, docs, tokens, kv_here):
    return call(
        functools.partial(pack_kernel, tokens, kv_here),
        "pack_kv",
        [soft_key, soft_value, docs],
        sds((2 * kv_here * tokens + INFO, LANES), BF16),
        scratch=[pltpu.VMEM((tokens * KV_HEADS, LANES), F32)],
        estimate=cost(0, 4 * tokens * KV_HEADS * LANES * 2),
        scalars=[start],
    )


def state_kernel(tokens, heads, y_ref, ld_ref, doc_ref, key_ref, value_ref, keep_ref, send_ref, info_ref, kf, vf, states, ldp):
    half = heads // 2
    y = y_ref[0]
    cumul = cumulative(ld_ref, ldp, tokens, heads)
    total = cumul[tokens - 1 : tokens, :]
    docs = doc_numbers(doc_ref)
    last_row = tokens // LANES - 1
    first_doc = docs[0:1, 0:1]
    last_doc = docs[last_row : last_row + 1, LANES - 1 : LANES]
    tail = (doc_columns(docs, tokens) == last_doc).astype(F32)
    scale = jnp.exp(total - cumul) * tail
    kf[...] = key_ref[...].astype(F32)
    vf[...] = value_ref[...].astype(F32)
    for h in range(heads):
        keys = (kf[pl.ds(h, tokens, stride=heads), :] * scale[:, h : h + 1]).astype(BF16)
        values = vf[pl.ds(h, tokens, stride=heads), :].astype(BF16)
        states[h * HEAD_DIM : (h + 1) * HEAD_DIM, :] = lax.dot_general(
            keys, values, (((0,), (0,)), ((), ())), preferred_element_type=F32
        )
    size = half * HEAD_DIM
    keep_ref[...] = states[pl.ds(pl.multiple_of(y * size, size), size), :].astype(BF16)
    send_ref[0:size, :] = states[pl.ds(pl.multiple_of((1 - y) * size, size), size), :].astype(BF16)
    upper = pltpu.roll(total, LANES - half, 1)
    rows = lax.broadcasted_iota(jnp.int32, (INFO, LANES), 0)

    def info_of(totals):
        hi = totals.astype(BF16).astype(F32)
        mid = (totals - hi).astype(BF16).astype(F32)
        lo = totals - hi - mid
        info = jnp.zeros((INFO, LANES), F32)
        for i, part in enumerate((hi, mid, lo, first_doc, last_doc)):
            info = jnp.where(rows == i, part, info)
        return info.astype(BF16)

    mine = (y == 0).astype(F32)
    info_ref[...] = info_of(total * mine + upper * (1.0 - mine))
    send_ref[size : size + INFO, :] = info_of(total * (1.0 - mine) + upper * mine)


def block_state(y, log_decay_t, docs, key, value, tokens, heads, after):
    size = heads // 2 * HEAD_DIM
    return call(
        functools.partial(state_kernel, tokens, heads),
        "block_state",
        [log_decay_t, docs, key, value],
        (sds((size, LANES), BF16), sds((size + INFO, LANES), BF16), sds((INFO, LANES), BF16)),
        scratch=[
            pltpu.VMEM((tokens * heads, LANES), F32),
            pltpu.VMEM((tokens * heads, LANES), F32),
            pltpu.VMEM((heads * HEAD_DIM, LANES), F32),
            pltpu.VMEM((LANES, tokens), F32),
        ],
        estimate=cost(2 * heads * tokens * HEAD_DIM**2, 3 * tokens * heads * LANES * 2),
        scalars=[y],
        after=after,
    )


def row_terms(y_ref, own_info, other_info):
    even = y_ref[0] == 0
    own = own_info.astype(F32)
    other = other_info.astype(F32)
    a = jnp.where(even, own, other)
    b = jnp.where(even, other, own)
    decay_a = jnp.exp(a[0:1] + a[1:2] + a[2:3])
    decay_b = jnp.exp(b[0:1] + b[1:2] + b[2:3])
    first_a, last_a = a[3:4], a[4:5]
    first_b, last_b = b[3:4], b[4:5]
    whole_a = (first_a == last_a).astype(F32)
    link_b = ((last_a == first_b) & (first_b == last_b)).astype(F32)
    return even, decay_a, decay_b * link_b, first_a, whole_a, last_a, last_b


def chain_kernel(count, first, arrivals, y_ref, *refs):
    keep_ref, info_ref, other_ref, other_info_ref = refs[:4]
    came, out_ref = refs[4 : 4 + arrivals], refs[4 + arrivals]
    size = count * HEAD_DIM
    even, decay_a, gain_b, first_a, whole_a, _, last_b = row_terms(
        y_ref, info_ref[...], other_info_ref[...]
    )
    if arrivals:
        came_doc = came[0][size : size + 1, :].astype(F32)
        gain_a = decay_a * whole_a * (came_doc == first_a).astype(F32)
    for i in range(count):
        rows = slice(i * HEAD_DIM, (i + 1) * HEAD_DIM)
        lane = slice(first + i, first + i + 1)
        own = keep_ref[rows, :].astype(F32)
        other = other_ref[rows, :].astype(F32)
        total = jnp.where(even, own, other)
        if arrivals:
            total = total + gain_a[:, lane] * came[0][rows, :].astype(F32)
        out_ref[rows, :] = (gain_b[:, lane] * total + jnp.where(even, other, own)).astype(BF16)
    out_ref[size : size + INFO, :] = jnp.broadcast_to(last_b, (INFO, LANES)).astype(BF16)


def chain_step(y, keep, info, other, other_info, came, first, count, after):
    size = count * HEAD_DIM
    came = [] if came is None else [came]
    return call(
        functools.partial(chain_kernel, count, first, len(came)),
        "chain_step",
        [keep, info, other, other_info, *came],
        sds((size + INFO, LANES), BF16),
        estimate=cost(4 * size * LANES, 4 * size * LANES * 2),
        scalars=[y],
        after=after,
    )


def prior_kernel(count, first, arrivals, y_ref, *refs):
    keep_ref, info_ref, other_ref, other_info_ref = refs[:4]
    came = refs[4 : 4 + arrivals]
    mine_ref, send_ref, doc_ref = refs[4 + arrivals :]
    size = count * HEAD_DIM
    even, decay_a, _, first_a, whole_a, last_a, _ = row_terms(
        y_ref, info_ref[...], other_info_ref[...]
    )
    came_doc = jnp.zeros((1, LANES), F32)
    for ref in came:
        came_doc = came_doc + ref[size : size + 1, :].astype(F32)
    gain_a = decay_a * whole_a * (came_doc == first_a).astype(F32)
    for i in range(count):
        rows = slice(i * HEAD_DIM, (i + 1) * HEAD_DIM)
        lane = slice(first + i, first + i + 1)
        before_a = jnp.zeros((HEAD_DIM, LANES), F32)
        for ref in came:
            before_a = before_a + ref[rows, :].astype(F32)
        state_a = jnp.where(even, keep_ref[rows, :].astype(F32), other_ref[rows, :].astype(F32))
        before_b = gain_a[:, lane] * before_a + state_a
        mine_ref[rows, :] = jnp.where(even, before_a, before_b).astype(BF16)
        send_ref[rows, :] = jnp.where(even, before_b, before_a).astype(BF16)
    doc_ref[...] = jnp.broadcast_to(jnp.where(even, came_doc, last_a), (8, LANES))


def prior_states(y, keep, info, other, other_info, came, first, count, after):
    size = count * HEAD_DIM
    return call(
        functools.partial(prior_kernel, count, first, len(came)),
        "prior_states",
        [keep, info, other, other_info, *came],
        (sds((size, LANES), BF16), sds((size, LANES), BF16), sds((8, LANES), F32)),
        estimate=cost(4 * size * LANES, 6 * size * LANES * 2),
        scalars=[y],
        after=after,
    )


def some_heads(ref, tokens, heads, first, count):
    x = ref[...].astype(F32)
    if count == heads:
        return x
    return x.reshape(tokens, heads, LANES)[:, first : first + count, :].reshape(tokens * count, LANES)


def inner_kernel(tokens, heads, first, count, ld_ref, doc_ref, query_ref, key_ref, value_ref, inner_ref, qh_ref, grow_ref, qf, kf, vf, ldp, mask):
    cumul = cumulative(ld_ref, ldp, tokens, heads)
    grow_ref[...] = jnp.exp(cumul)
    cumul_t = lax.dot_general(
        ld_ref[...],
        lower_triangle(tokens).astype(F32),
        (((1,), (1,)), ((), ())),
        precision=HIGHEST,
        preferred_element_type=F32,
    )
    docs = doc_numbers(doc_ref)
    column = doc_columns(docs, tokens)
    same = jnp.concatenate([column] * (tokens // LANES), axis=1) == doc_line(docs, tokens)
    mask[...] = jnp.where(lower_triangle(tokens) & same, 0.0, -1e9)
    qf[...] = some_heads(query_ref, tokens, heads, first, count)
    kf[...] = some_heads(key_ref, tokens, heads, first, count)
    vf[...] = some_heads(value_ref, tokens, heads, first, count)
    for n in range(count):
        h = first + n
        picked = pl.ds(n, tokens, stride=count)
        query = qf[picked, :].astype(BF16)
        keys = kf[picked, :].astype(BF16)
        values = vf[picked, :].astype(BF16)
        qh_ref[n * tokens : (n + 1) * tokens, :] = query
        for i in range(tokens // LANES):
            seen = (i + 1) * LANES
            rows = slice(i * LANES, seen)
            scores = lax.dot_general(
                query[rows, :], keys[0:seen, :], (((1,), (1,)), ((), ())), preferred_element_type=F32
            )
            gap = cumul[rows, h : h + 1] - cumul_t[h : h + 1, 0:seen]
            weights = (scores * jnp.exp(gap + mask[rows, 0:seen])).astype(BF16)
            inner_ref[n * tokens + i * LANES : n * tokens + seen, :] = jnp.dot(
                weights, values[0:seen, :], preferred_element_type=F32
            )


def inner_part(log_decay_t, docs, query, key, value, tokens, heads, first, count, after):
    return call(
        functools.partial(inner_kernel, tokens, heads, first, count),
        "inner_part",
        [log_decay_t, docs, query, key, value],
        (
            sds((count * tokens, LANES), F32),
            sds((count * tokens, LANES), BF16),
            sds((tokens, LANES), F32),
        ),
        scratch=[pltpu.VMEM((tokens * count, LANES), F32)] * 3
        + [pltpu.VMEM((LANES, tokens), F32), pltpu.VMEM((tokens, tokens), F32)],
        mib=24,
        estimate=cost(
            4 * count * tokens * tokens * HEAD_DIM, tokens * heads * LANES * 12, count * tokens * tokens
        ),
        after=after,
    )


def mix_kernel(tokens, heads, parts, pieces, y_ref, doc_ref, prior_doc_ref, grow_ref, *refs):
    refs = list(refs)
    take = lambda n: [refs.pop(0) for _ in range(n)]
    inner, qh, mine, other = take(parts), take(parts), take(pieces), take(pieces)
    mixed_ref, square_ref = refs
    half = heads // 2
    count = half // pieces
    even = y_ref[0] == 0
    is_open = (doc_columns(doc_numbers(doc_ref), tokens) == prior_doc_ref[0:1, :]).astype(F32)
    gain = grow_ref[...] * is_open
    squares = jnp.zeros((tokens, LANES), F32)
    for h in range(heads):
        piece, i = divmod(h % half, count)
        rows = slice(i * HEAD_DIM, (i + 1) * HEAD_DIM)
        near, far = mine[piece][rows, :], other[piece][rows, :]
        lower = h < half
        state = jnp.where(even, near if lower else far, far if lower else near)
        part, n = divmod(h, heads // parts)
        held = slice(n * tokens, (n + 1) * tokens)
        carried = jnp.dot(qh[part][held, :], state, preferred_element_type=F32)
        mixed = inner[part][held, :] + carried * gain[:, h : h + 1]
        squares = squares + mixed * mixed
        mixed_ref[pl.ds(h, tokens, stride=heads), :] = mixed
    square_ref[...] = lax.dot_general(
        jnp.ones((8, LANES), F32),
        squares,
        (((1,), (1,)), ((), ())),
        precision=HIGHEST,
        preferred_element_type=F32,
    )


def mix(y, docs, prior_doc, grow, inner, qh, mine, other, tokens, heads, after):
    return call(
        functools.partial(mix_kernel, tokens, heads, len(inner), len(mine)),
        "mix",
        [docs, prior_doc, grow, *inner, *qh, *mine, *other],
        (sds((tokens * heads, LANES), F32), sds((8, tokens), F32)),
        mib=24,
        estimate=cost(2 * heads * tokens * HEAD_DIM**2, tokens * heads * LANES * 10),
        scalars=[y],
        after=after,
    )


def finish_kernel(tokens, heads, sums, gain_ref, gate_ref, mixed_ref, *refs):
    squares, out_ref = refs[:sums], refs[sums]
    total = squares[0][0:1, :]
    for ref in squares[1:]:
        total = total + ref[0:1, :]
    scale = lax.rsqrt(total / (HEADS * HEAD_DIM) + 1e-06)
    rows = jnp.concatenate([scale[:, i * LANES : (i + 1) * LANES] for i in range(tokens // LANES)], axis=0)
    column = doc_columns(rows, tokens)
    step = 32
    for i in range(0, tokens, step):
        at = slice(i * heads, (i + step) * heads)
        gate = jax.nn.sigmoid(gate_ref[at, :].astype(F32)).reshape(step, heads, LANES)
        mixed = mixed_ref[at, :].reshape(step, heads, LANES)
        inv = column[i : i + step, :][:, None, :]
        out = mixed * inv * gain_ref[...][None] * gate
        out_ref[at, :] = out.reshape(step * heads, LANES).astype(BF16)


def finish(gain, gate, mixed, squares, tokens, heads, after):
    return call(
        functools.partial(finish_kernel, tokens, heads, len(squares)),
        "finish",
        [gain, gate, mixed, *squares],
        sds((tokens * heads, LANES), BF16),
        estimate=cost(0, tokens * heads * LANES * 8, tokens * heads * LANES),
        after=after,
    )


def attend_kernel(tokens, heads, kv_here, blocks, is_first, is_last, *refs):
    refs = list(refs)
    take = lambda n: [refs.pop(0) for _ in range(n)]
    per_group = heads // kv_here
    rows = tokens * per_group
    step = CHUNK // per_group
    if is_first:
        doc_ref, query_ref = take(2)
    else:
        wide_ref, state_ref = take(2)
    kv = take(blocks)
    if is_first:
        wide_ref, out_ref, bias, doc_rep = refs
    else:
        out_ref, bias = refs

    lane = lax.broadcasted_iota(jnp.int32, (tokens, LANES), 1).astype(F32)
    end = 2 * kv_here * tokens
    for j, ref in enumerate(kv):
        docs = doc_columns(ref[end : end + INFO, :].astype(F32), tokens)
        bias[j] = jnp.where(docs == lane, 0.0, -BIG).astype(BF16)
    if is_first:
        column = doc_columns(doc_numbers(doc_ref), tokens)
        for h in range(per_group):
            doc_rep[pl.ds(h, tokens, stride=per_group), :] = (column == lane).astype(F32)
    ones = jnp.ones((STATE_ROWS - HEAD_DIM, tokens), BF16)

    def one(i, carry):
        at = pl.ds(pl.multiple_of(i * CHUNK, CHUNK), CHUNK)
        results = []
        if is_first:
            picked = pl.ds(pl.multiple_of(i * (step * heads), step * heads), step * heads)
            query_all = query_ref[picked, :].astype(F32).reshape(step, heads, LANES)
            one_hot = doc_rep[at, :].astype(BF16)
        for g in range(kv_here):
            if is_first:
                query = query_all[:, g * per_group : (g + 1) * per_group, :].reshape(CHUNK, LANES)
                wide = jnp.concatenate([query.astype(BF16), one_hot], axis=1)
                wide_ref[g, at, :] = wide
            else:
                wide = wide_ref[g, at, :]
            scores = []
            for j, ref in enumerate(kv):
                keys = jnp.concatenate([ref[g * tokens : (g + 1) * tokens, :], bias[j]], axis=1)
                scores.append(
                    lax.dot_general(keys, wide, (((1,), (1,)), ((), ())), preferred_element_type=F32)
                )
            if is_first:
                token = i * step + lax.broadcasted_iota(jnp.int32, (tokens, CHUNK), 1) // per_group
                key_at = lax.broadcasted_iota(jnp.int32, (tokens, CHUNK), 0)
                scores[0] = jnp.where(key_at <= token, scores[0], -BIG)
            top = jnp.max(scores[0], axis=0, keepdims=True)
            for score in scores[1:]:
                top = jnp.maximum(top, jnp.max(score, axis=0, keepdims=True))
            if not is_first:
                before = state_ref[g, :, at]
                top_before = before[STATE_ROWS - 1 : STATE_ROWS, :]
                top = jnp.maximum(top, top_before)
                total = before * jnp.exp2((top_before - top) * SCORE_TO_EXP2)
            else:
                total = None
            for ref, score in zip(kv, scores):
                weights = jnp.exp2((score - top) * SCORE_TO_EXP2).astype(BF16)
                begin = (kv_here + g) * tokens
                parts = [ref[begin + p : begin + p + LANES, :] for p in range(0, tokens, LANES)]
                values = jnp.concatenate([jnp.concatenate(parts, axis=1), ones], axis=0)
                more = jnp.dot(values, weights, preferred_element_type=F32)
                total = more if total is None else total + more
            if is_last:
                results.append(jnp.transpose(total[0:HEAD_DIM] / total[HEAD_DIM : HEAD_DIM + 1]))
            else:
                out_ref[g, 0 : STATE_ROWS - 8, at] = total[0 : STATE_ROWS - 8]
                out_ref[g, STATE_ROWS - 8 : STATE_ROWS, at] = jnp.broadcast_to(top, (8, CHUNK))
        if is_last:
            if kv_here > 1:
                results = [r.reshape(step, per_group, LANES) for r in results]
                results = [jnp.concatenate(results, axis=1).reshape(step * heads, LANES)]
            picked = pl.ds(pl.multiple_of(i * (step * heads), step * heads), step * heads)
            out_ref[picked, :] = results[0].astype(BF16)
        return carry

    lax.fori_loop(0, rows // CHUNK, one, 0)


def attend(first, state, kv, is_last, tokens, heads, kv_here, after):
    is_first = state is None
    blocks = len(kv)
    rows = tokens * heads // kv_here
    wide_shape = sds((kv_here, rows, 2 * LANES), BF16)
    state_shape = sds((kv_here, STATE_ROWS, rows), F32)
    out_shape = sds((tokens * heads, LANES), BF16) if is_last else state_shape
    scratch = [pltpu.VMEM((blocks, tokens, LANES), BF16)]
    if is_first:
        out_shape = (wide_shape, out_shape)
        scratch.append(pltpu.VMEM((rows, LANES), F32))
    span = blocks * tokens
    return call(
        functools.partial(attend_kernel, tokens, heads, kv_here, blocks, is_first, is_last),
        "attend",
        [*first, *([] if is_first else [state]), *kv],
        out_shape,
        scratch=scratch,
        mib=24,
        estimate=cost(
            4 * tokens * heads * span * 2 * LANES, 4 * tokens * heads * LANES * 4, tokens * heads * span
        ),
        after=after,
    )


def body(
    blocks,
    lin_query,
    lin_key,
    lin_value,
    lin_gate,
    log_decay,
    norm_gain,
    doc_ids,
    soft_query,
    soft_key,
    soft_value,
):
    tokens, heads, _ = lin_query.shape
    tensor = HEADS // heads
    kv_here = max(1, heads // GROUP)
    half = heads // 2
    pieces = 2 if half % 2 == 0 else 1
    parts = 2 if half % 8 == 0 else 1
    count = half // pieces
    longest = blocks * tokens * 5 // 8
    window = min(blocks - 1, (longest - 1 + tokens - 1) // tokens)
    flat = lambda x: x.reshape(-1, LANES)
    block = lax.axis_index("seq")
    y = (block % 2).astype(jnp.int32).reshape(1)
    start = (lax.axis_index("tp") * heads // GROUP).astype(jnp.int32).reshape(1)
    docs = doc_ids.reshape(tokens // LANES, LANES)
    decays = jnp.transpose(log_decay)

    def send(x, pairs):
        return lax.ppermute(x, "seq", [p for p in pairs if 0 <= p[0] < blocks and 0 <= p[1] < blocks])

    everyone = range(blocks)
    swap = [(b, b ^ 1) for b in everyone]

    own_kv = pack_kv(start, flat(soft_key), flat(soft_value), docs, tokens, kv_here)
    far_step = window if window % 2 else blocks
    beside = send(own_kv, [(b, b + (far_step if b % 2 else 1)) for b in everyone])
    lane_kv, cross_kv = [], []
    ahead = own_kv
    for back in range(1, window // 2 + 1):
        ahead = send(ahead, [(b, b + 2) for b in everyone if b >= 2 * (back - 1)])
        lane_kv.append(ahead)
        cross_kv.append(send(ahead, [p for p in swap if p[0] >= 2 * back]))

    keep, other, info = block_state(
        y, decays, docs, flat(lin_key), flat(lin_value), tokens, heads, [own_kv]
    )
    size = count * HEAD_DIM
    other_info = None
    came = []
    for piece in range(pieces):
        sent = other[piece * size : (piece + 1) * size]
        if piece == 0:
            sent = jnp.concatenate([sent, other[half * HEAD_DIM :]], axis=0)
        got = send(sent, swap)
        if piece == 0:
            other_info = got[size:]
        came.append(got)
    held = [keep[p * size : (p + 1) * size] for p in range(pieces)]

    state = {}

    def first_attention(after):
        state["wide"], state["sum"] = attend(
            (docs, flat(soft_query)), None, [own_kv], False, tokens, heads, kv_here, after
        )
        return state["sum"]

    def more_attention(kv, is_last, after):
        state["sum"] = attend(
            (state["wide"],), state["sum"], kv, is_last, tokens, heads, kv_here, after
        )
        return state["sum"]

    inner, qh = [], []

    def inner_of(part, after):
        n = heads // parts
        got = inner_part(
            decays, docs, flat(lin_query), flat(lin_key), flat(lin_value), tokens, heads, part * n, n, after
        )
        inner.append(got[0])
        qh.append(got[1])
        state["grow"] = got[2]
        return got[0]

    beside_work = [first_attention]
    beside_work += [functools.partial(inner_of, part) for part in range(parts)]
    beside_work.append(functools.partial(more_attention, [beside] + lane_kv[:1], False))

    latest = [None] * pieces
    arrived = [[] for _ in range(pieces)]
    done = info
    for row in range(blocks // 2 - 1):
        if beside_work:
            done = beside_work.pop(0)([done])
        for p in range(pieces):
            done = chain_step(
                y, held[p], info, came[p], other_info, latest[p], p * count, count, [done]
            )
            latest[p] = send(done, [(2 * row, 2 * row + 2), (2 * row + 1, 2 * row + 3)])
            arrived[p].append(latest[p])
    while beside_work:
        done = beside_work.pop(0)([done])
    mine, far = [], []
    prior_doc = None
    for p in range(pieces):
        done, sent, prior_doc = prior_states(
            y, held[p], info, came[p], other_info, arrived[p], p * count, count, [done]
        )
        mine.append(done)
        far.append(send(sent, swap))
    rest = [kv for pair in zip(cross_kv, lane_kv[1:] + [None]) for kv in pair if kv is not None]
    done = more_attention(rest[:1], False, [done])
    rest = rest[1:]
    mixed, squares = mix(
        y, docs, prior_doc, state["grow"], inner, qh, mine, far, tokens, heads, [done]
    )
    sums = [squares]
    for shift in range(1, tensor):
        sums.append(
            lax.ppermute(squares, "tp", [(t, (t + shift) % tensor) for t in range(tensor)])
        )
    after = [squares]
    while rest:
        soft_out = more_attention(rest[:2], len(rest) <= 2, after)
        rest, after = rest[2:], []
    lin_out = finish(norm_gain, flat(lin_gate), mixed, sums, tokens, heads, [soft_out])
    shape = (tokens, heads, HEAD_DIM)
    return lin_out.reshape(shape), soft_out.reshape(shape)


def solution(mesh):
    in_specs = (
        P("seq", "tp", None),
        P("seq", "tp", None),
        P("seq", "tp", None),
        P("seq", "tp", None),
        P("seq", "tp"),
        P("tp", None),
        P("seq"),
        P("seq", "tp", None),
        P("seq", None, None),
        P("seq", None, None),
    )
    out_specs = (P("seq", "tp", None), P("seq", "tp", None))
    return jax.shard_map(
        functools.partial(body, mesh.shape["seq"]),
        mesh=mesh,
        in_specs=in_specs,
        out_specs=out_specs,
        check_vma=False,
    )
```

```python
import functools

import jax
import jax.numpy as jnp
import numpy as np
from jax import lax
from jax.experimental import pallas as pl
from jax.experimental.pallas import tpu as pltpu
from jax.sharding import PartitionSpec as P

HEADS = 64
HEAD_DIM = 128
KV_HEADS = 8
LANES = 128
GROUP = HEADS // KV_HEADS
F32 = jnp.float32
BF16 = jnp.bfloat16
BIG = float(2**20)
SCORE_TO_EXP2 = HEAD_DIM**-0.5 * float(np.log2(np.e))
INFO = 16
HIGHEST = lax.Precision.HIGHEST

VMEM = pl.BlockSpec(memory_space=pltpu.VMEM)
SMEM = pl.BlockSpec(memory_space=pltpu.SMEM)
HBM = pl.BlockSpec(memory_space=pltpu.HBM)
ANYWHERE = pl.BlockSpec(memory_space=pl.ANY)
STATE_ROWS = HEAD_DIM + 16
CHUNK = 256


def sds(shape, dtype):
    return jax.ShapeDtypeStruct(shape, dtype)


def cost(flops, bytes_accessed, transcendentals=0):
    return pl.CostEstimate(
        flops=int(flops), bytes_accessed=int(bytes_accessed), transcendentals=int(transcendentals)
    )


def call(kernel, name, operands, out_shape, scratch=(), mib=16, estimate=None, scalars=(), after=(), hbm=0, out_hbm=False):
    begin = len(scalars) + len(operands)
    skip = len(after)
    operands = [
        pltpu.with_memory_space_constraint(x, pltpu.HBM) if i < hbm else x for i, x in enumerate(operands)
    ]
    outs = out_shape if isinstance(out_shape, tuple) else (out_shape,)
    out_specs = (VMEM,) * len(outs)
    if out_hbm:
        outs = (pltpu.HBM(outs[0].shape, outs[0].dtype), *outs[1:])
        out_specs = (HBM, *out_specs[1:])

    def run(*refs):
        kernel(*refs[:begin], *refs[begin + skip :])

    out = pl.pallas_call(
        run,
        out_shape=outs,
        in_specs=[SMEM] * len(scalars) + [HBM] * hbm + [VMEM] * (len(operands) - hbm) + [ANYWHERE] * skip,
        out_specs=out_specs,
        scratch_shapes=list(scratch),
        compiler_params=pltpu.CompilerParams(vmem_limit_bytes=mib * 1024 * 1024),
        cost_estimate=estimate,
        name=name,
    )(*scalars, *operands, *after)
    return out if isinstance(out_shape, tuple) else out[0]


def doc_columns(doc_rows, tokens):
    parts = []
    for i in range(tokens // LANES):
        row = jnp.broadcast_to(doc_rows[i : i + 1, :], (LANES, LANES))
        parts.append(jnp.transpose(row))
    return jnp.concatenate(parts, axis=0)


def doc_line(doc_rows, tokens):
    return jnp.concatenate([doc_rows[i : i + 1, :] for i in range(tokens // LANES)], axis=1)


def lower_triangle(tokens):
    rows = lax.broadcasted_iota(jnp.int32, (tokens, tokens), 0)
    cols = lax.broadcasted_iota(jnp.int32, (tokens, tokens), 1)
    return rows >= cols


def front_kernel(tokens, heads, kv_here, pieces, start_ref, y_ref, *refs):
    refs = list(refs)
    take = lambda n: [refs.pop(0) for _ in range(n)]
    sources = take(6)
    kv_ref, doc_out, cumul_ref, info_ref = take(4)
    keep_refs, send_refs = take(pieces), take(pieces)
    held = take(6)
    sems, wide, kf, vf, states, ldp = refs
    docs_in, soft_key, soft_value, decays, lin_key, lin_value = held
    copies = [pltpu.make_async_copy(src, dst, sems.at[i]) for i, (src, dst) in enumerate(zip(sources, held))]
    for copy in copies:
        copy.start()

    copies[0].wait()
    docs = docs_in[...].astype(F32) + 1.0
    line = lax.broadcasted_iota(jnp.int32, (INFO, LANES), 0)
    info = jnp.zeros((INFO, LANES), F32)
    for i in range(tokens // LANES):
        info = jnp.where(line == i, docs[i : i + 1, :], info)
    doc_out[...] = info
    end = 2 * kv_here * tokens
    kv_ref[end : end + INFO, :] = info.astype(BF16)

    start = start_ref[0]
    for which, ref in enumerate((soft_key, soft_value)):
        copies[1 + which].wait()
        wide[...] = ref[...].astype(F32)
        for g in range(kv_here):
            rows = wide[pl.ds(start + g, tokens, stride=KV_HEADS), :]
            at = (which * kv_here + g) * tokens
            if which:
                halves = [jnp.transpose(rows[i : i + LANES, :]) for i in range(0, tokens, LANES)]
                rows = jnp.concatenate(halves, axis=0)
            kv_ref[at : at + tokens, :] = rows.astype(BF16)

    half = heads // 2
    y = y_ref[0]
    copies[3].wait()
    ldp[...] = jnp.zeros_like(ldp)
    ldp[0:heads, :] = decays[...]
    cumul = lax.dot_general(
        lower_triangle(tokens).astype(F32),
        ldp[...],
        (((1,), (1,)), ((), ())),
        precision=HIGHEST,
        preferred_element_type=F32,
    )
    cumul_ref[...] = cumul
    total = cumul[tokens - 1 : tokens, :]
    last_row = tokens // LANES - 1
    first_doc = docs[0:1, 0:1]
    last_doc = docs[last_row : last_row + 1, LANES - 1 : LANES]
    tail = (doc_columns(docs, tokens) == last_doc).astype(F32)
    scale = jnp.exp(total - cumul) * tail
    copies[4].wait()
    kf[...] = lin_key[...].astype(F32)
    copies[5].wait()
    vf[...] = lin_value[...].astype(F32)
    for h in range(heads):
        keys = (kf[pl.ds(h, tokens, stride=heads), :] * scale[:, h : h + 1]).astype(BF16)
        values = vf[pl.ds(h, tokens, stride=heads), :].astype(BF16)
        states[h * HEAD_DIM : (h + 1) * HEAD_DIM, :] = lax.dot_general(
            keys, values, (((0,), (0,)), ((), ())), preferred_element_type=F32
        )
    size = half // pieces * HEAD_DIM
    for p in range(pieces):
        keep_at = pl.multiple_of((y * pieces + p) * size, size)
        send_at = pl.multiple_of(((1 - y) * pieces + p) * size, size)
        keep_refs[p][...] = states[pl.ds(keep_at, size), :].astype(BF16)
        send_refs[p][0:size, :] = states[pl.ds(send_at, size), :].astype(BF16)
    upper = pltpu.roll(total, LANES - half, 1)

    def info_of(totals):
        hi = totals.astype(BF16).astype(F32)
        mid = (totals - hi).astype(BF16).astype(F32)
        lo = totals - hi - mid
        info = jnp.zeros((INFO, LANES), F32)
        for i, part in enumerate((hi, mid, lo, first_doc, last_doc)):
            info = jnp.where(line == i, part, info)
        return info.astype(BF16)

    mine = (y == 0).astype(F32)
    info_ref[...] = info_of(total * mine + upper * (1.0 - mine))
    send_refs[0][size : size + INFO, :] = info_of(total * (1.0 - mine) + upper * mine)


def front(start, y, operands, tokens, heads, kv_here, pieces):
    size = heads // 2 // pieces * HEAD_DIM
    keep = [sds((size, LANES), BF16)] * pieces
    send = [sds((size + (INFO if p == 0 else 0), LANES), BF16) for p in range(pieces)]
    out = call(
        functools.partial(front_kernel, tokens, heads, kv_here, pieces),
        "front",
        operands,
        (
            sds((2 * kv_here * tokens + INFO, LANES), BF16),
            sds((INFO, LANES), F32),
            sds((tokens, LANES), F32),
            sds((INFO, LANES), BF16),
            *keep,
            *send,
        ),
        scratch=[pltpu.VMEM(x.shape, x.dtype) for x in operands]
        + [
            pltpu.SemaphoreType.DMA((len(operands),)),
            pltpu.VMEM((tokens * KV_HEADS, LANES), F32),
            pltpu.VMEM((tokens * heads, LANES), F32),
            pltpu.VMEM((tokens * heads, LANES), F32),
            pltpu.VMEM((heads * HEAD_DIM, LANES), F32),
            pltpu.VMEM((LANES, tokens), F32),
        ],
        mib=24,
        estimate=cost(2 * heads * tokens * HEAD_DIM**2, 5 * tokens * heads * LANES * 2),
        scalars=[start, y],
        hbm=len(operands),
    )
    return (*out[:4], out[4 : 4 + pieces], out[4 + pieces :])


def row_terms(y_ref, own_info, other_info):
    even = y_ref[0] == 0
    own = own_info.astype(F32)
    other = other_info.astype(F32)
    a = jnp.where(even, own, other)
    b = jnp.where(even, other, own)
    decay_a = jnp.exp(a[0:1] + a[1:2] + a[2:3])
    decay_b = jnp.exp(b[0:1] + b[1:2] + b[2:3])
    first_a, last_a = a[3:4], a[4:5]
    first_b, last_b = b[3:4], b[4:5]
    whole_a = (first_a == last_a).astype(F32)
    link_b = ((last_a == first_b) & (first_b == last_b)).astype(F32)
    return even, decay_a, decay_b * link_b, first_a, whole_a, last_a, last_b


def chain_kernel(count, first, arrivals, y_ref, *refs):
    keep_ref, info_ref, other_ref, other_info_ref = refs[:4]
    came, out_ref = refs[4 : 4 + arrivals], refs[4 + arrivals]
    size = count * HEAD_DIM
    even, decay_a, gain_b, first_a, whole_a, _, last_b = row_terms(
        y_ref, info_ref[...], other_info_ref[size : size + INFO, :]
    )
    if arrivals:
        came_doc = came[0][size : size + 1, :].astype(F32)
        gain_a = decay_a * whole_a * (came_doc == first_a).astype(F32)
    for i in range(count):
        rows = slice(i * HEAD_DIM, (i + 1) * HEAD_DIM)
        lane = slice(first + i, first + i + 1)
        own = keep_ref[rows, :].astype(F32)
        other = other_ref[rows, :].astype(F32)
        total = jnp.where(even, own, other)
        if arrivals:
            total = total + gain_a[:, lane] * came[0][rows, :].astype(F32)
        out_ref[rows, :] = (gain_b[:, lane] * total + jnp.where(even, other, own)).astype(BF16)
    out_ref[size : size + INFO, :] = jnp.broadcast_to(last_b, (INFO, LANES)).astype(BF16)


def chain_step(y, keep, info, other, other_info, came, first, count, after):
    size = count * HEAD_DIM
    came = [] if came is None else [came]
    return call(
        functools.partial(chain_kernel, count, first, len(came)),
        "chain_step",
        [keep, info, other, other_info, *came],
        sds((size + INFO, LANES), BF16),
        estimate=cost(4 * size * LANES, 4 * size * LANES * 2),
        scalars=[y],
        after=after,
    )


def prior_kernel(count, first, arrivals, y_ref, *refs):
    keep_ref, info_ref, other_ref, other_info_ref = refs[:4]
    came = refs[4 : 4 + arrivals]
    mine_ref, send_ref, doc_ref = refs[4 + arrivals :]
    size = count * HEAD_DIM
    even, decay_a, _, first_a, whole_a, last_a, _ = row_terms(
        y_ref, info_ref[...], other_info_ref[size : size + INFO, :]
    )
    came_doc = jnp.zeros((1, LANES), F32)
    for ref in came:
        came_doc = came_doc + ref[size : size + 1, :].astype(F32)
    gain_a = decay_a * whole_a * (came_doc == first_a).astype(F32)
    for i in range(count):
        rows = slice(i * HEAD_DIM, (i + 1) * HEAD_DIM)
        lane = slice(first + i, first + i + 1)
        before_a = jnp.zeros((HEAD_DIM, LANES), F32)
        for ref in came:
            before_a = before_a + ref[rows, :].astype(F32)
        state_a = jnp.where(even, keep_ref[rows, :].astype(F32), other_ref[rows, :].astype(F32))
        before_b = gain_a[:, lane] * before_a + state_a
        mine_ref[rows, :] = jnp.where(even, before_a, before_b).astype(BF16)
        send_ref[rows, :] = jnp.where(even, before_b, before_a).astype(BF16)
    doc_ref[...] = jnp.broadcast_to(jnp.where(even, came_doc, last_a), (8, LANES))


def prior_states(y, keep, info, other, other_info, came, first, count, after):
    size = count * HEAD_DIM
    return call(
        functools.partial(prior_kernel, count, first, len(came)),
        "prior_states",
        [keep, info, other, other_info, *came],
        (sds((size, LANES), BF16), sds((size, LANES), BF16), sds((8, LANES), F32)),
        estimate=cost(4 * size * LANES, 6 * size * LANES * 2),
        scalars=[y],
        after=after,
    )


def some_heads(ref, tokens, heads, first, count):
    x = ref[...].astype(F32)
    if count == heads:
        return x
    return x.reshape(tokens, heads, LANES)[:, first : first + count, :].reshape(tokens * count, LANES)


def inner_kernel(tokens, heads, first, count, cumul_ref, doc_ref, query_ref, key_ref, value_ref, inner_ref, qh_ref, qf, kf, vf, mask):
    cumul = cumul_ref[...]
    cumul_t = jnp.transpose(cumul)
    docs = doc_ref[...]
    column = doc_columns(docs, tokens)
    same = jnp.concatenate([column] * (tokens // LANES), axis=1) == doc_line(docs, tokens)
    mask[...] = jnp.where(lower_triangle(tokens) & same, 0.0, -1e9)
    qf[...] = some_heads(query_ref, tokens, heads, first, count)
    kf[...] = some_heads(key_ref, tokens, heads, first, count)
    vf[...] = some_heads(value_ref, tokens, heads, first, count)
    for n in range(count):
        h = first + n
        picked = pl.ds(n, tokens, stride=count)
        query = qf[picked, :].astype(BF16)
        keys = kf[picked, :].astype(BF16)
        values = vf[picked, :].astype(BF16)
        qh_ref[n * tokens : (n + 1) * tokens, :] = query
        for i in range(tokens // LANES):
            seen = (i + 1) * LANES
            rows = slice(i * LANES, seen)
            scores = lax.dot_general(
                query[rows, :], keys[0:seen, :], (((1,), (1,)), ((), ())), preferred_element_type=F32
            )
            gap = cumul[rows, h : h + 1] - cumul_t[h : h + 1, 0:seen]
            weights = (scores * jnp.exp(gap + mask[rows, 0:seen])).astype(BF16)
            inner_ref[n * tokens + i * LANES : n * tokens + seen, :] = jnp.dot(
                weights, values[0:seen, :], preferred_element_type=F32
            )


def inner_part(cumul, docs, query, key, value, tokens, heads, first, count, after):
    return call(
        functools.partial(inner_kernel, tokens, heads, first, count),
        "inner_part",
        [cumul, docs, query, key, value],
        (sds((count * tokens, LANES), F32), sds((count * tokens, LANES), BF16)),
        scratch=[pltpu.VMEM((tokens * count, LANES), F32)] * 3 + [pltpu.VMEM((tokens, tokens), F32)],
        mib=24,
        estimate=cost(
            4 * count * tokens * tokens * HEAD_DIM, tokens * heads * LANES * 12, count * tokens * tokens
        ),
        after=after,
    )


def mix_kernel(tokens, heads, parts, pieces, y_ref, doc_ref, prior_doc_ref, cumul_ref, *refs):
    refs = list(refs)
    take = lambda n: [refs.pop(0) for _ in range(n)]
    inner, qh, mine, other = take(parts), take(parts), take(pieces), take(pieces)
    mixed_ref, square_ref = refs
    half = heads // 2
    count = half // pieces
    even = y_ref[0] == 0
    is_open = (doc_columns(doc_ref[...], tokens) == prior_doc_ref[0:1, :]).astype(F32)
    gain = jnp.exp(cumul_ref[...]) * is_open
    squares = jnp.zeros((tokens, LANES), F32)
    for h in range(heads):
        piece, i = divmod(h % half, count)
        rows = slice(i * HEAD_DIM, (i + 1) * HEAD_DIM)
        near, far = mine[piece][rows, :], other[piece][rows, :]
        lower = h < half
        state = jnp.where(even, near if lower else far, far if lower else near)
        part, n = divmod(h, heads // parts)
        held = slice(n * tokens, (n + 1) * tokens)
        carried = jnp.dot(qh[part][held, :], state, preferred_element_type=F32)
        mixed = inner[part][held, :] + carried * gain[:, h : h + 1]
        squares = squares + mixed * mixed
        mixed_ref[pl.ds(h, tokens, stride=heads), :] = mixed
    square_ref[...] = lax.dot_general(
        jnp.ones((8, LANES), F32),
        squares,
        (((1,), (1,)), ((), ())),
        precision=HIGHEST,
        preferred_element_type=F32,
    )


def mix(y, docs, prior_doc, cumul, inner, qh, mine, other, tokens, heads, after):
    return call(
        functools.partial(mix_kernel, tokens, heads, len(inner), len(mine)),
        "mix",
        [docs, prior_doc, cumul, *inner, *qh, *mine, *other],
        (sds((tokens * heads, LANES), F32), sds((8, tokens), F32)),
        mib=24,
        estimate=cost(2 * heads * tokens * HEAD_DIM**2, tokens * heads * LANES * 10),
        scalars=[y],
        after=after,
    )


def finish_kernel(tokens, heads, sums, step, gain_ref, gate_ref, mixed_ref, *refs):
    squares, (out_ref, done, sems) = refs[:sums], refs[sums:]
    total = squares[0][0:1, :]
    for ref in squares[1:]:
        total = total + ref[0:1, :]
    scale = lax.rsqrt(total / (HEADS * HEAD_DIM) + 1e-06)
    rows = jnp.concatenate([scale[:, i * LANES : (i + 1) * LANES] for i in range(tokens // LANES)], axis=0)
    column = doc_columns(rows, tokens)
    copies = []
    for i in range(0, tokens, step):
        at = pl.ds(i * heads, step * heads)
        gate = jax.nn.sigmoid(gate_ref[at, :].astype(F32)).reshape(step, heads, LANES)
        mixed = mixed_ref[at, :].reshape(step, heads, LANES)
        inv = column[i : i + step, :][:, None, :]
        out = mixed * inv * gain_ref[...][None] * gate
        done[at, :] = out.reshape(step * heads, LANES).astype(BF16)
        copies.append(pltpu.make_async_copy(done.at[at, :], out_ref.at[at, :], sems.at[i // step]))
        copies[-1].start()
    for copy in copies:
        copy.wait()


def finish(gain, gate, mixed, squares, tokens, heads, after):
    step = 64
    return call(
        functools.partial(finish_kernel, tokens, heads, len(squares), step),
        "finish",
        [gain, gate, mixed, *squares],
        sds((tokens * heads, LANES), BF16),
        scratch=[pltpu.VMEM((tokens * heads, LANES), BF16), pltpu.SemaphoreType.DMA((tokens // step,))],
        estimate=cost(0, tokens * heads * LANES * 8, tokens * heads * LANES),
        after=after,
        out_hbm=True,
    )


def attend_kernel(tokens, heads, kv_here, blocks, is_first, is_last, unroll, *refs):
    refs = list(refs)
    take = lambda n: [refs.pop(0) for _ in range(n)]
    per_group = heads // kv_here
    rows = tokens * per_group
    step = CHUNK // per_group
    if is_first:
        doc_ref, query_ref = take(2)
    else:
        wide_ref, state_ref = take(2)
    kv = take(blocks)
    if is_first:
        wide_ref = take(1)[0]
    out_ref = take(1)[0]
    if is_last:
        take(1)[0][...] = jnp.zeros((8, LANES), F32)
    bias = take(1)[0]
    if is_first:
        doc_rep = take(1)[0]
    if is_last:
        done, sems = take(2)

    lane = lax.broadcasted_iota(jnp.int32, (tokens, LANES), 1).astype(F32)
    end = 2 * kv_here * tokens
    for j, ref in enumerate(kv):
        docs = doc_columns(ref[end : end + INFO, :].astype(F32), tokens)
        bias[j] = jnp.where(docs == lane, 0.0, -BIG).astype(BF16)
    if is_first:
        column = doc_columns(doc_ref[...], tokens)
        for h in range(per_group):
            doc_rep[pl.ds(h, tokens, stride=per_group), :] = (column == lane).astype(F32)
    ones = jnp.ones((STATE_ROWS - HEAD_DIM, tokens), BF16)

    def some_chunks(i, carry):
        chains = [(u, g) for u in range(unroll) for g in range(kv_here)]
        chunk = [i * unroll + u for u in range(unroll)]
        at = [pl.ds(pl.multiple_of(c * CHUNK, CHUNK), CHUNK) for c in chunk]
        picked = [pl.ds(pl.multiple_of(c * (step * heads), step * heads), step * heads) for c in chunk]
        scores, results = {}, {}

        def begin(u, g):
            if is_first:
                query = query_ref[picked[u], :].astype(F32).reshape(step, heads, LANES)
                query = query[:, g * per_group : (g + 1) * per_group, :].reshape(CHUNK, LANES)
                wide = jnp.concatenate([query.astype(BF16), doc_rep[at[u], :].astype(BF16)], axis=1)
                wide_ref[g, at[u], :] = wide
            else:
                wide = wide_ref[g, at[u], :]
            out = []
            for j, ref in enumerate(kv):
                keys = jnp.concatenate([ref[g * tokens : (g + 1) * tokens, :], bias[j]], axis=1)
                out.append(
                    lax.dot_general(keys, wide, (((1,), (1,)), ((), ())), preferred_element_type=F32)
                )
            if is_first:
                token = chunk[u] * step + lax.broadcasted_iota(jnp.int32, (tokens, CHUNK), 1) // per_group
                key_at = lax.broadcasted_iota(jnp.int32, (tokens, CHUNK), 0)
                out[0] = jnp.where(key_at <= token, out[0], -BIG)
            scores[u, g] = out

        def end_chain(u, g):
            here = scores.pop((u, g))
            top = jnp.max(here[0], axis=0, keepdims=True)
            for score in here[1:]:
                top = jnp.maximum(top, jnp.max(score, axis=0, keepdims=True))
            total = None
            if not is_first:
                before = state_ref[g, :, at[u]]
                top_before = before[STATE_ROWS - 1 : STATE_ROWS, :]
                top = jnp.maximum(top, top_before)
                total = before * jnp.exp2((top_before - top) * SCORE_TO_EXP2)
            for ref, score in zip(kv, here):
                weights = jnp.exp2((score - top) * SCORE_TO_EXP2).astype(BF16)
                first = (kv_here + g) * tokens
                parts = [ref[first + p : first + p + LANES, :] for p in range(0, tokens, LANES)]
                values = jnp.concatenate([jnp.concatenate(parts, axis=1), ones], axis=0)
                more = jnp.dot(values, weights, preferred_element_type=F32)
                total = more if total is None else total + more
            if is_last:
                results[u, g] = jnp.transpose(total[0:HEAD_DIM] / total[HEAD_DIM : HEAD_DIM + 1])
            else:
                out_ref[g, 0 : STATE_ROWS - 8, at[u]] = total[0 : STATE_ROWS - 8]
                out_ref[g, STATE_ROWS - 8 : STATE_ROWS, at[u]] = jnp.broadcast_to(top, (8, CHUNK))

        ahead = 2
        for n in range(len(chains) + ahead):
            if n < len(chains):
                begin(*chains[n])
            if n >= ahead:
                end_chain(*chains[n - ahead])
        if is_last:
            for u in range(unroll):
                result = [results[u, g] for g in range(kv_here)]
                if kv_here > 1:
                    result = [r.reshape(step, per_group, LANES) for r in result]
                    result = [jnp.concatenate(result, axis=1).reshape(step * heads, LANES)]
                done[picked[u], :] = result[0].astype(BF16)
                pltpu.make_async_copy(
                    done.at[picked[u], :], out_ref.at[picked[u], :], sems.at[chunk[u]]
                ).start()
        return carry

    lax.fori_loop(0, rows // (CHUNK * unroll), some_chunks, 0)
    if is_last:
        for c in range(rows // CHUNK):
            at = pl.ds(c * step * heads, step * heads)
            pltpu.make_async_copy(done.at[at, :], out_ref.at[at, :], sems.at[c]).wait()


def attend(first, state, kv, is_last, tokens, heads, kv_here, after):
    is_first = state is None
    blocks = len(kv)
    rows = tokens * heads // kv_here
    unroll = min(4, rows // CHUNK)
    wide_shape = sds((kv_here, rows, 2 * LANES), BF16)
    state_shape = sds((kv_here, STATE_ROWS, rows), F32)
    out_shape = sds((tokens * heads, LANES), BF16) if is_last else state_shape
    scratch = [pltpu.VMEM((blocks, tokens, LANES), BF16)]
    if is_first:
        out_shape = (wide_shape, out_shape)
        scratch.append(pltpu.VMEM((rows, LANES), F32))
    if is_last:
        out_shape = (out_shape, sds((8, LANES), F32))
        scratch.append(pltpu.VMEM((tokens * heads, LANES), BF16))
        scratch.append(pltpu.SemaphoreType.DMA((rows // CHUNK,)))
    span = blocks * tokens
    return call(
        functools.partial(attend_kernel, tokens, heads, kv_here, blocks, is_first, is_last, unroll),
        "attend",
        [*first, *([] if is_first else [state]), *kv],
        out_shape,
        scratch=scratch,
        mib=24,
        estimate=cost(
            4 * tokens * heads * span * 2 * LANES, 4 * tokens * heads * LANES * 4, tokens * heads * span
        ),
        after=after,
        out_hbm=is_last,
    )


def body(
    blocks,
    lin_query,
    lin_key,
    lin_value,
    lin_gate,
    log_decay,
    norm_gain,
    doc_ids,
    soft_query,
    soft_key,
    soft_value,
):
    tokens, heads, _ = lin_query.shape
    tensor = HEADS // heads
    kv_here = max(1, heads // GROUP)
    half = heads // 2
    pieces = 2 if half % 2 == 0 else 1
    parts = 2 if half % 8 == 0 else 1
    count = half // pieces
    longest = blocks * tokens * 5 // 8
    window = min(blocks - 1, (longest - 1 + tokens - 1) // tokens)
    flat = lambda x: x.reshape(-1, LANES)
    block = lax.axis_index("seq")
    y = (block % 2).astype(jnp.int32).reshape(1)
    start = (lax.axis_index("tp") * heads // GROUP).astype(jnp.int32).reshape(1)
    def send(x, pairs):
        return lax.ppermute(x, "seq", [p for p in pairs if 0 <= p[0] < blocks and 0 <= p[1] < blocks])

    everyone = range(blocks)
    swap = [(b, b ^ 1) for b in everyone]

    own_kv, docs, cumul, info, held, sent = front(
        start,
        y,
        [
            doc_ids.reshape(tokens // LANES, LANES),
            flat(soft_key),
            flat(soft_value),
            jnp.transpose(log_decay),
            flat(lin_key),
            flat(lin_value),
        ],
        tokens,
        heads,
        kv_here,
        pieces,
    )
    came = [send(x, swap) for x in sent]
    far_step = window if window % 2 else blocks
    beside = send(own_kv, [(b, b + (far_step if b % 2 else 1)) for b in everyone])
    lane_kv, cross_kv = [], []
    ahead = own_kv
    for back in range(1, window // 2 + 1):
        ahead = send(ahead, [(b, b + 2) for b in everyone if b >= 2 * (back - 1)])
        lane_kv.append(ahead)
        cross_kv.append(send(ahead, [p for p in swap if p[0] >= 2 * back]))

    state = {}

    def first_attention(after):
        state["wide"], state["sum"] = attend(
            (docs, flat(soft_query)), None, [own_kv], False, tokens, heads, kv_here, after
        )
        return state["sum"]

    def more_attention(kv, is_last, after):
        state["sum"] = attend(
            (state["wide"],), state["sum"], kv, is_last, tokens, heads, kv_here, after
        )
        return state["sum"]

    inner, qh = [], []

    def inner_of(part, after):
        n = heads // parts
        got = inner_part(
            cumul, docs, flat(lin_query), flat(lin_key), flat(lin_value), tokens, heads, part * n, n, after
        )
        inner.append(got[0])
        qh.append(got[1])
        return got[0]

    beside_work = [first_attention]
    beside_work += [functools.partial(inner_of, part) for part in range(parts)]
    beside_work.append(functools.partial(more_attention, [beside] + lane_kv[:1], False))

    latest = [None] * pieces
    arrived = [[] for _ in range(pieces)]
    done = info
    for row in range(blocks // 2 - 1):
        if beside_work:
            done = beside_work.pop(0)([done])
        for p in range(pieces):
            done = chain_step(
                y, held[p], info, came[p], came[0], latest[p], p * count, count, [done]
            )
            latest[p] = send(done, [(2 * row, 2 * row + 2), (2 * row + 1, 2 * row + 3)])
            arrived[p].append(latest[p])
    while beside_work:
        done = beside_work.pop(0)([done])
    mine, far = [], []
    prior_doc = None
    for p in range(pieces):
        done, sent, prior_doc = prior_states(
            y, held[p], info, came[p], came[0], arrived[p], p * count, count, [done]
        )
        mine.append(done)
        far.append(send(sent, swap))
    rest = [kv for pair in zip(cross_kv, lane_kv[1:] + [None]) for kv in pair if kv is not None]
    done = more_attention(rest[:1], False, [done])
    rest = rest[1:]
    mixed, squares = mix(
        y, docs, prior_doc, cumul, inner, qh, mine, far, tokens, heads, [done]
    )
    sums = [squares]
    for shift in range(1, tensor):
        sums.append(
            lax.ppermute(squares, "tp", [(t, (t + shift) % tensor) for t in range(tensor)])
        )
    after = [squares]
    while rest:
        got = more_attention(rest[:2], len(rest) <= 2, after)
        rest, after = rest[2:], []
    soft_out, done = got
    lin_out = finish(norm_gain, flat(lin_gate), mixed, sums, tokens, heads, [done])
    shape = (tokens, heads, HEAD_DIM)
    return lin_out.reshape(shape), soft_out.reshape(shape)


def solution(mesh):
    in_specs = (
        P("seq", "tp", None),
        P("seq", "tp", None),
        P("seq", "tp", None),
        P("seq", "tp", None),
        P("seq", "tp"),
        P("tp", None),
        P("seq"),
        P("seq", "tp", None),
        P("seq", None, None),
        P("seq", None, None),
    )
    out_specs = (P("seq", "tp", None), P("seq", "tp", None))
    return jax.shard_map(
        functools.partial(body, mesh.shape["seq"]),
        mesh=mesh,
        in_specs=in_specs,
        out_specs=out_specs,
        check_vma=False,
    )
```

```python
import functools

import jax
import jax.numpy as jnp
import numpy as np
from jax import lax
from jax.experimental import pallas as pl
from jax.experimental.pallas import tpu as pltpu
from jax.sharding import PartitionSpec as P

HEADS = 64
HEAD_DIM = 128
KV_HEADS = 8
LANES = 128
GROUP = HEADS // KV_HEADS
F32 = jnp.float32
BF16 = jnp.bfloat16
BIG = float(2**20)
SCORE_TO_EXP2 = HEAD_DIM**-0.5 * float(np.log2(np.e))
INFO = 16
HIGHEST = lax.Precision.HIGHEST

VMEM = pl.BlockSpec(memory_space=pltpu.VMEM)
SMEM = pl.BlockSpec(memory_space=pltpu.SMEM)
HBM = pl.BlockSpec(memory_space=pltpu.HBM)
ANYWHERE = pl.BlockSpec(memory_space=pl.ANY)
STATE_ROWS = HEAD_DIM + 16
CHUNK = 256


def sds(shape, dtype):
    return jax.ShapeDtypeStruct(shape, dtype)


def cost(flops, bytes_accessed, transcendentals=0):
    return pl.CostEstimate(
        flops=int(flops), bytes_accessed=int(bytes_accessed), transcendentals=int(transcendentals)
    )


def call(kernel, name, operands, out_shape, scratch=(), mib=16, estimate=None, scalars=(), after=(), hbm=0, out_hbm=False):
    begin = len(scalars) + len(operands)
    skip = len(after)
    operands = [
        pltpu.with_memory_space_constraint(x, pltpu.HBM) if i < hbm else x for i, x in enumerate(operands)
    ]
    outs = out_shape if isinstance(out_shape, tuple) else (out_shape,)
    out_specs = (VMEM,) * len(outs)
    if out_hbm:
        outs = (pltpu.HBM(outs[0].shape, outs[0].dtype), *outs[1:])
        out_specs = (HBM, *out_specs[1:])

    def run(*refs):
        kernel(*refs[:begin], *refs[begin + skip :])

    out = pl.pallas_call(
        run,
        out_shape=outs,
        in_specs=[SMEM] * len(scalars) + [HBM] * hbm + [VMEM] * (len(operands) - hbm) + [ANYWHERE] * skip,
        out_specs=out_specs,
        scratch_shapes=list(scratch),
        compiler_params=pltpu.CompilerParams(vmem_limit_bytes=mib * 1024 * 1024),
        cost_estimate=estimate,
        name=name,
    )(*scalars, *operands, *after)
    return out if isinstance(out_shape, tuple) else out[0]


def doc_columns(doc_rows, tokens):
    parts = []
    for i in range(tokens // LANES):
        row = jnp.broadcast_to(doc_rows[i : i + 1, :], (LANES, LANES))
        parts.append(jnp.transpose(row))
    return jnp.concatenate(parts, axis=0)


def doc_line(doc_rows, tokens):
    return jnp.concatenate([doc_rows[i : i + 1, :] for i in range(tokens // LANES)], axis=1)


def lower_triangle(tokens):
    rows = lax.broadcasted_iota(jnp.int32, (tokens, tokens), 0)
    cols = lax.broadcasted_iota(jnp.int32, (tokens, tokens), 1)
    return rows >= cols


def front_kernel(tokens, heads, kv_here, pieces, start_ref, y_ref, *refs):
    refs = list(refs)
    take = lambda n: [refs.pop(0) for _ in range(n)]
    sources = take(6)
    kv_ref, doc_out, cumul_ref, info_ref = take(4)
    keep_refs, send_refs = take(pieces), take(pieces)
    held = take(6)
    sems, wide, kf, vf, states, ldp = refs
    docs_in, soft_key, soft_value, decays, lin_key, lin_value = held
    copies = [pltpu.make_async_copy(src, dst, sems.at[i]) for i, (src, dst) in enumerate(zip(sources, held))]
    for copy in copies:
        copy.start()

    copies[0].wait()
    docs = docs_in[...].astype(F32) + 1.0
    line = lax.broadcasted_iota(jnp.int32, (INFO, LANES), 0)
    info = jnp.zeros((INFO, LANES), F32)
    for i in range(tokens // LANES):
        info = jnp.where(line == i, docs[i : i + 1, :], info)
    doc_out[...] = info
    end = 2 * kv_here * tokens
    kv_ref[end : end + INFO, :] = info.astype(BF16)

    start = start_ref[0]
    for which, ref in enumerate((soft_key, soft_value)):
        copies[1 + which].wait()
        wide[...] = ref[...].astype(F32)
        for g in range(kv_here):
            rows = wide[pl.ds(start + g, tokens, stride=KV_HEADS), :]
            at = (which * kv_here + g) * tokens
            if which:
                halves = [jnp.transpose(rows[i : i + LANES, :]) for i in range(0, tokens, LANES)]
                rows = jnp.concatenate(halves, axis=0)
            kv_ref[at : at + tokens, :] = rows.astype(BF16)

    half = heads // 2
    y = y_ref[0]
    copies[3].wait()
    ldp[...] = jnp.zeros_like(ldp)
    ldp[0:heads, :] = decays[...]
    cumul = lax.dot_general(
        lower_triangle(tokens).astype(F32),
        ldp[...],
        (((1,), (1,)), ((), ())),
        precision=HIGHEST,
        preferred_element_type=F32,
    )
    cumul_ref[...] = cumul
    total = cumul[tokens - 1 : tokens, :]
    last_row = tokens // LANES - 1
    first_doc = docs[0:1, 0:1]
    last_doc = docs[last_row : last_row + 1, LANES - 1 : LANES]
    tail = (doc_columns(docs, tokens) == last_doc).astype(F32)
    scale = jnp.exp(total - cumul) * tail
    copies[4].wait()
    kf[...] = lin_key[...].astype(F32)
    copies[5].wait()
    vf[...] = lin_value[...].astype(F32)
    for h in range(heads):
        keys = (kf[pl.ds(h, tokens, stride=heads), :] * scale[:, h : h + 1]).astype(BF16)
        values = vf[pl.ds(h, tokens, stride=heads), :].astype(BF16)
        states[h * HEAD_DIM : (h + 1) * HEAD_DIM, :] = lax.dot_general(
            keys, values, (((0,), (0,)), ((), ())), preferred_element_type=F32
        )
    size = half // pieces * HEAD_DIM
    for p in range(pieces):
        keep_at = pl.multiple_of((y * pieces + p) * size, size)
        send_at = pl.multiple_of(((1 - y) * pieces + p) * size, size)
        keep_refs[p][...] = states[pl.ds(keep_at, size), :].astype(BF16)
        send_refs[p][0:size, :] = states[pl.ds(send_at, size), :].astype(BF16)
    upper = pltpu.roll(total, LANES - half, 1)

    def info_of(totals):
        return info_rows((*in_parts(totals), first_doc, last_doc))

    mine = (y == 0).astype(F32)
    info_ref[...] = info_of(total * mine + upper * (1.0 - mine))
    send_refs[0][size : size + INFO, :] = info_of(total * (1.0 - mine) + upper * mine)


def front(start, y, operands, tokens, heads, kv_here, pieces):
    size = heads // 2 // pieces * HEAD_DIM
    keep = [sds((size, LANES), BF16)] * pieces
    send = [sds((size + (INFO if p == 0 else 0), LANES), BF16) for p in range(pieces)]
    out = call(
        functools.partial(front_kernel, tokens, heads, kv_here, pieces),
        "front",
        operands,
        (
            sds((2 * kv_here * tokens + INFO, LANES), BF16),
            sds((INFO, LANES), F32),
            sds((tokens, LANES), F32),
            sds((INFO, LANES), BF16),
            *keep,
            *send,
        ),
        scratch=[pltpu.VMEM(x.shape, x.dtype) for x in operands]
        + [
            pltpu.SemaphoreType.DMA((len(operands),)),
            pltpu.VMEM((tokens * KV_HEADS, LANES), F32),
            pltpu.VMEM((tokens * heads, LANES), F32),
            pltpu.VMEM((tokens * heads, LANES), F32),
            pltpu.VMEM((heads * HEAD_DIM, LANES), F32),
            pltpu.VMEM((LANES, tokens), F32),
        ],
        mib=24,
        estimate=cost(2 * heads * tokens * HEAD_DIM**2, 5 * tokens * heads * LANES * 2),
        scalars=[start, y],
        hbm=len(operands),
    )
    return (*out[:4], out[4 : 4 + pieces], out[4 + pieces :])


def in_parts(x):
    hi = x.astype(BF16).astype(F32)
    mid = (x - hi).astype(BF16).astype(F32)
    return hi, mid, x - hi - mid


def info_rows(parts):
    line = lax.broadcasted_iota(jnp.int32, (INFO, LANES), 0)
    info = jnp.zeros((INFO, LANES), F32)
    for i, part in enumerate(parts):
        info = jnp.where(line == i, part, info)
    return info.astype(BF16)


def read_map(ref, size):
    info = ref[size : size + INFO, :].astype(F32)
    return info[0:1] + info[1:2] + info[2:3], info[3:4], info[4:5]


def row_terms(y_ref, own_info, other_info):
    even = y_ref[0] == 0
    own = own_info.astype(F32)
    other = other_info.astype(F32)
    a = jnp.where(even, own, other)
    b = jnp.where(even, other, own)
    decay_a = jnp.exp(a[0:1] + a[1:2] + a[2:3])
    decay_b = jnp.exp(b[0:1] + b[1:2] + b[2:3])
    first_a, last_a = a[3:4], a[4:5]
    first_b, last_b = b[3:4], b[4:5]
    whole_a = (first_a == last_a).astype(F32)
    link_b = ((last_a == first_b) & (first_b == last_b)).astype(F32)
    return even, decay_a * whole_a, decay_b * link_b, first_a, last_a, last_b


def row_kernel(count, first, y_ref, keep_ref, info_ref, other_ref, other_info_ref, out_ref):
    size = count * HEAD_DIM
    even, gain_a, gain_b, first_a, _, last_b = row_terms(
        y_ref, info_ref[...], other_info_ref[size : size + INFO, :]
    )
    for i in range(count):
        rows = slice(i * HEAD_DIM, (i + 1) * HEAD_DIM)
        lane = slice(first + i, first + i + 1)
        own = keep_ref[rows, :].astype(F32)
        other = other_ref[rows, :].astype(F32)
        state_a, state_b = jnp.where(even, own, other), jnp.where(even, other, own)
        out_ref[rows, :] = (gain_b[:, lane] * state_a + state_b).astype(BF16)
    out_ref[size : size + INFO, :] = info_rows((*in_parts(gain_a * gain_b), first_a, last_b))


def row_map(y, keep, info, other, other_info, first, count, after):
    size = count * HEAD_DIM
    return call(
        functools.partial(row_kernel, count, first),
        "row_map",
        [keep, info, other, other_info],
        sds((size + INFO, LANES), BF16),
        estimate=cost(4 * size * LANES, 4 * size * LANES * 2),
        scalars=[y],
        after=after,
    )


def scan_kernel(count, first, has_before, upper_ref, *refs):
    refs = list(refs)
    mine_ref, came_ref = refs[:2]
    before_ref = refs[2] if has_before else None
    run_ref, out_ref = refs[-2:]
    size = count * HEAD_DIM
    upper = upper_ref[0] == 1
    gain_m, first_m, last_m = read_map(mine_ref, size)
    gain_c, first_c, last_c = read_map(came_ref, size)
    link = jnp.where(upper, (last_c == first_m).astype(F32), (last_m == first_c).astype(F32))
    gain = jnp.where(upper, gain_m, gain_c) * link
    for i in range(count):
        rows = slice(i * HEAD_DIM, (i + 1) * HEAD_DIM)
        lane = slice(first + i, first + i + 1)
        mine, came = mine_ref[rows, :].astype(F32), came_ref[rows, :].astype(F32)
        lower_sum, upper_sum = jnp.where(upper, came, mine), jnp.where(upper, mine, came)
        run_ref[rows, :] = (gain[:, lane] * lower_sum + upper_sum).astype(BF16)
    run_ref[size : size + INFO, :] = info_rows(
        (
            *in_parts(gain * jnp.where(upper, gain_c, gain_m)),
            jnp.where(upper, first_c, first_m),
            jnp.where(upper, last_m, last_c),
        )
    )
    if not has_before:
        out_ref[...] = jnp.where(upper, came_ref[...], jnp.zeros_like(came_ref))
        return
    gain_b, first_b, last_b = read_map(before_ref, size)
    empty = first_b == 0.0
    factor = jnp.where(empty, 1.0, gain_b * (last_c == first_b).astype(F32))
    for i in range(count):
        rows = slice(i * HEAD_DIM, (i + 1) * HEAD_DIM)
        lane = slice(first + i, first + i + 1)
        before = before_ref[rows, :].astype(F32)
        joined = factor[:, lane] * came_ref[rows, :].astype(F32) + before
        out_ref[rows, :] = jnp.where(upper, joined, before).astype(BF16)
    out_ref[size : size + INFO, :] = info_rows(
        (
            *in_parts(jnp.where(upper, factor * gain_c, gain_b)),
            jnp.where(upper, first_c, first_b),
            jnp.where(upper, jnp.where(empty, last_c, last_b), last_b),
        )
    )


def scan_step(upper, mine, came, before, first, count, after):
    size = count * HEAD_DIM
    shape = sds((size + INFO, LANES), BF16)
    before = [] if before is None else [before]
    return call(
        functools.partial(scan_kernel, count, first, len(before)),
        "scan_step",
        [mine, came, *before],
        (shape, shape),
        estimate=cost(6 * size * LANES, 6 * size * LANES * 2),
        scalars=[upper],
        after=after,
    )


def prior_kernel(count, first, has_before, y_ref, upper_ref, *refs):
    keep_ref, info_ref, other_ref, other_info_ref, came_ref = refs[:5]
    before_ref = refs[5] if has_before else None
    mine_ref, send_ref, doc_ref = refs[-3:]
    size = count * HEAD_DIM
    upper = (upper_ref[0] == 1).astype(F32)
    even, gain_a, _, first_a, last_a, _ = row_terms(
        y_ref, info_ref[...], other_info_ref[size : size + INFO, :]
    )
    _, _, last_c = read_map(came_ref, size)
    factor, doc = upper, upper * last_c
    if has_before:
        gain_b, first_b, last_b = read_map(before_ref, size)
        empty = first_b == 0.0
        factor = upper * jnp.where(empty, 1.0, gain_b * (last_c == first_b).astype(F32))
        doc = jnp.where(empty, doc, last_b)
    else:
        factor = jnp.broadcast_to(factor, (1, LANES))
    gain_a = gain_a * (doc == first_a).astype(F32)
    for i in range(count):
        rows = slice(i * HEAD_DIM, (i + 1) * HEAD_DIM)
        lane = slice(first + i, first + i + 1)
        before_a = factor[:, lane] * came_ref[rows, :].astype(F32)
        if has_before:
            before_a = before_a + before_ref[rows, :].astype(F32)
        state_a = jnp.where(even, keep_ref[rows, :].astype(F32), other_ref[rows, :].astype(F32))
        before_b = gain_a[:, lane] * before_a + state_a
        mine_ref[rows, :] = jnp.where(even, before_a, before_b).astype(BF16)
        send_ref[rows, :] = jnp.where(even, before_b, before_a).astype(BF16)
    doc_ref[...] = jnp.broadcast_to(jnp.where(even, doc, last_a), (8, LANES))


def prior_states(y, upper, keep, info, other, other_info, came, before, first, count, after):
    size = count * HEAD_DIM
    before = [] if before is None else [before]
    return call(
        functools.partial(prior_kernel, count, first, len(before)),
        "prior_states",
        [keep, info, other, other_info, came, *before],
        (sds((size, LANES), BF16), sds((size, LANES), BF16), sds((8, LANES), F32)),
        estimate=cost(4 * size * LANES, 6 * size * LANES * 2),
        scalars=[y, upper],
        after=after,
    )


def some_heads(ref, tokens, heads, first, count):
    x = ref[...].astype(F32)
    if count == heads:
        return x
    return x.reshape(tokens, heads, LANES)[:, first : first + count, :].reshape(tokens * count, LANES)


def inner_kernel(tokens, heads, first, count, cumul_ref, doc_ref, query_ref, key_ref, value_ref, inner_ref, qh_ref, qf, kf, vf, mask):
    cumul = cumul_ref[...]
    cumul_t = jnp.transpose(cumul)
    docs = doc_ref[...]
    column = doc_columns(docs, tokens)
    same = jnp.concatenate([column] * (tokens // LANES), axis=1) == doc_line(docs, tokens)
    mask[...] = jnp.where(lower_triangle(tokens) & same, 0.0, -1e9)
    qf[...] = some_heads(query_ref, tokens, heads, first, count)
    kf[...] = some_heads(key_ref, tokens, heads, first, count)
    vf[...] = some_heads(value_ref, tokens, heads, first, count)
    for n in range(count):
        h = first + n
        picked = pl.ds(n, tokens, stride=count)
        query = qf[picked, :].astype(BF16)
        keys = kf[picked, :].astype(BF16)
        values = vf[picked, :].astype(BF16)
        qh_ref[n * tokens : (n + 1) * tokens, :] = query
        for i in range(tokens // LANES):
            seen = (i + 1) * LANES
            rows = slice(i * LANES, seen)
            scores = lax.dot_general(
                query[rows, :], keys[0:seen, :], (((1,), (1,)), ((), ())), preferred_element_type=F32
            )
            gap = cumul[rows, h : h + 1] - cumul_t[h : h + 1, 0:seen]
            weights = (scores * jnp.exp(gap + mask[rows, 0:seen])).astype(BF16)
            inner_ref[n * tokens + i * LANES : n * tokens + seen, :] = jnp.dot(
                weights, values[0:seen, :], preferred_element_type=F32
            )


def inner_part(cumul, docs, query, key, value, tokens, heads, first, count, after):
    return call(
        functools.partial(inner_kernel, tokens, heads, first, count),
        "inner_part",
        [cumul, docs, query, key, value],
        (sds((count * tokens, LANES), F32), sds((count * tokens, LANES), BF16)),
        scratch=[pltpu.VMEM((tokens * count, LANES), F32)] * 3 + [pltpu.VMEM((tokens, tokens), F32)],
        mib=24,
        estimate=cost(
            4 * count * tokens * tokens * HEAD_DIM, tokens * heads * LANES * 12, count * tokens * tokens
        ),
        after=after,
    )


def mix_kernel(tokens, heads, parts, pieces, y_ref, doc_ref, prior_doc_ref, cumul_ref, *refs):
    refs = list(refs)
    take = lambda n: [refs.pop(0) for _ in range(n)]
    inner, qh, mine, other = take(parts), take(parts), take(pieces), take(pieces)
    mixed_ref, square_ref = refs
    half = heads // 2
    count = half // pieces
    even = y_ref[0] == 0
    is_open = (doc_columns(doc_ref[...], tokens) == prior_doc_ref[0:1, :]).astype(F32)
    gain = jnp.exp(cumul_ref[...]) * is_open
    squares = jnp.zeros((tokens, LANES), F32)
    for h in range(heads):
        piece, i = divmod(h % half, count)
        rows = slice(i * HEAD_DIM, (i + 1) * HEAD_DIM)
        near, far = mine[piece][rows, :], other[piece][rows, :]
        lower = h < half
        state = jnp.where(even, near if lower else far, far if lower else near)
        part, n = divmod(h, heads // parts)
        held = slice(n * tokens, (n + 1) * tokens)
        carried = jnp.dot(qh[part][held, :], state, preferred_element_type=F32)
        mixed = inner[part][held, :] + carried * gain[:, h : h + 1]
        squares = squares + mixed * mixed
        mixed_ref[pl.ds(h, tokens, stride=heads), :] = mixed
    square_ref[...] = lax.dot_general(
        jnp.ones((8, LANES), F32),
        squares,
        (((1,), (1,)), ((), ())),
        precision=HIGHEST,
        preferred_element_type=F32,
    )


def mix(y, docs, prior_doc, cumul, inner, qh, mine, other, tokens, heads, after):
    return call(
        functools.partial(mix_kernel, tokens, heads, len(inner), len(mine)),
        "mix",
        [docs, prior_doc, cumul, *inner, *qh, *mine, *other],
        (sds((tokens * heads, LANES), F32), sds((8, tokens), F32)),
        mib=24,
        estimate=cost(2 * heads * tokens * HEAD_DIM**2, tokens * heads * LANES * 10),
        scalars=[y],
        after=after,
    )


def finish_kernel(tokens, heads, sums, step, gain_ref, gate_ref, mixed_ref, *refs):
    squares, (out_ref, done, sems) = refs[:sums], refs[sums:]
    total = squares[0][0:1, :]
    for ref in squares[1:]:
        total = total + ref[0:1, :]
    scale = lax.rsqrt(total / (HEADS * HEAD_DIM) + 1e-06)
    rows = jnp.concatenate([scale[:, i * LANES : (i + 1) * LANES] for i in range(tokens // LANES)], axis=0)
    column = doc_columns(rows, tokens)
    copies = []
    for i in range(0, tokens, step):
        at = pl.ds(i * heads, step * heads)
        gate = jax.nn.sigmoid(gate_ref[at, :].astype(F32)).reshape(step, heads, LANES)
        mixed = mixed_ref[at, :].reshape(step, heads, LANES)
        inv = column[i : i + step, :][:, None, :]
        out = mixed * inv * gain_ref[...][None] * gate
        done[at, :] = out.reshape(step * heads, LANES).astype(BF16)
        copies.append(pltpu.make_async_copy(done.at[at, :], out_ref.at[at, :], sems.at[i // step]))
        copies[-1].start()
    for copy in copies:
        copy.wait()


def finish(gain, gate, mixed, squares, tokens, heads, after):
    step = 64
    return call(
        functools.partial(finish_kernel, tokens, heads, len(squares), step),
        "finish",
        [gain, gate, mixed, *squares],
        sds((tokens * heads, LANES), BF16),
        scratch=[pltpu.VMEM((tokens * heads, LANES), BF16), pltpu.SemaphoreType.DMA((tokens // step,))],
        estimate=cost(0, tokens * heads * LANES * 8, tokens * heads * LANES),
        after=after,
        out_hbm=True,
    )


def attend_kernel(tokens, heads, kv_here, blocks, is_first, is_last, unroll, *refs):
    refs = list(refs)
    take = lambda n: [refs.pop(0) for _ in range(n)]
    per_group = heads // kv_here
    rows = tokens * per_group
    step = CHUNK // per_group
    if is_first:
        doc_ref, query_ref = take(2)
    else:
        wide_ref, state_ref = take(2)
    kv = take(blocks)
    if is_first:
        wide_ref = take(1)[0]
    out_ref = take(1)[0]
    if is_last:
        take(1)[0][...] = jnp.zeros((8, LANES), F32)
    bias = take(1)[0]
    if is_first:
        doc_rep = take(1)[0]
    if is_last:
        done, sems = take(2)

    lane = lax.broadcasted_iota(jnp.int32, (tokens, LANES), 1).astype(F32)
    end = 2 * kv_here * tokens
    for j, ref in enumerate(kv):
        docs = doc_columns(ref[end : end + INFO, :].astype(F32), tokens)
        bias[j] = jnp.where(docs == lane, 0.0, -BIG).astype(BF16)
    if is_first:
        column = doc_columns(doc_ref[...], tokens)
        for h in range(per_group):
            doc_rep[pl.ds(h, tokens, stride=per_group), :] = (column == lane).astype(F32)
    ones = jnp.ones((STATE_ROWS - HEAD_DIM, tokens), BF16)

    def some_chunks(i, carry):
        chains = [(u, g) for u in range(unroll) for g in range(kv_here)]
        chunk = [i * unroll + u for u in range(unroll)]
        at = [pl.ds(pl.multiple_of(c * CHUNK, CHUNK), CHUNK) for c in chunk]
        picked = [pl.ds(pl.multiple_of(c * (step * heads), step * heads), step * heads) for c in chunk]
        scores, results = {}, {}

        def begin(u, g):
            if is_first:
                query = query_ref[picked[u], :].astype(F32).reshape(step, heads, LANES)
                query = query[:, g * per_group : (g + 1) * per_group, :].reshape(CHUNK, LANES)
                wide = jnp.concatenate([query.astype(BF16), doc_rep[at[u], :].astype(BF16)], axis=1)
                wide_ref[g, at[u], :] = wide
            else:
                wide = wide_ref[g, at[u], :]
            out = []
            for j, ref in enumerate(kv):
                keys = jnp.concatenate([ref[g * tokens : (g + 1) * tokens, :], bias[j]], axis=1)
                out.append(
                    lax.dot_general(keys, wide, (((1,), (1,)), ((), ())), preferred_element_type=F32)
                )
            if is_first:
                token = chunk[u] * step + lax.broadcasted_iota(jnp.int32, (tokens, CHUNK), 1) // per_group
                key_at = lax.broadcasted_iota(jnp.int32, (tokens, CHUNK), 0)
                out[0] = jnp.where(key_at <= token, out[0], -BIG)
            scores[u, g] = out

        def end_chain(u, g):
            here = scores.pop((u, g))
            top = jnp.max(here[0], axis=0, keepdims=True)
            for score in here[1:]:
                top = jnp.maximum(top, jnp.max(score, axis=0, keepdims=True))
            total = None
            if not is_first:
                before = state_ref[g, :, at[u]]
                top_before = before[STATE_ROWS - 1 : STATE_ROWS, :]
                top = jnp.maximum(top, top_before)
                total = before * jnp.exp2((top_before - top) * SCORE_TO_EXP2)
            for ref, score in zip(kv, here):
                weights = jnp.exp2((score - top) * SCORE_TO_EXP2).astype(BF16)
                first = (kv_here + g) * tokens
                parts = [ref[first + p : first + p + LANES, :] for p in range(0, tokens, LANES)]
                values = jnp.concatenate([jnp.concatenate(parts, axis=1), ones], axis=0)
                more = jnp.dot(values, weights, preferred_element_type=F32)
                total = more if total is None else total + more
            if is_last:
                results[u, g] = jnp.transpose(total[0:HEAD_DIM] / total[HEAD_DIM : HEAD_DIM + 1])
            else:
                out_ref[g, 0 : STATE_ROWS - 8, at[u]] = total[0 : STATE_ROWS - 8]
                out_ref[g, STATE_ROWS - 8 : STATE_ROWS, at[u]] = jnp.broadcast_to(top, (8, CHUNK))

        ahead = 2
        for n in range(len(chains) + ahead):
            if n < len(chains):
                begin(*chains[n])
            if n >= ahead:
                end_chain(*chains[n - ahead])
        if is_last:
            for u in range(unroll):
                result = [results[u, g] for g in range(kv_here)]
                if kv_here > 1:
                    result = [r.reshape(step, per_group, LANES) for r in result]
                    result = [jnp.concatenate(result, axis=1).reshape(step * heads, LANES)]
                done[picked[u], :] = result[0].astype(BF16)
                pltpu.make_async_copy(
                    done.at[picked[u], :], out_ref.at[picked[u], :], sems.at[chunk[u]]
                ).start()
        return carry

    lax.fori_loop(0, rows // (CHUNK * unroll), some_chunks, 0)
    if is_last:
        for c in range(rows // CHUNK):
            at = pl.ds(c * step * heads, step * heads)
            pltpu.make_async_copy(done.at[at, :], out_ref.at[at, :], sems.at[c]).wait()


def attend(first, state, kv, is_last, tokens, heads, kv_here, after):
    is_first = state is None
    blocks = len(kv)
    rows = tokens * heads // kv_here
    unroll = min(4, rows // CHUNK)
    wide_shape = sds((kv_here, rows, 2 * LANES), BF16)
    state_shape = sds((kv_here, STATE_ROWS, rows), F32)
    out_shape = sds((tokens * heads, LANES), BF16) if is_last else state_shape
    scratch = [pltpu.VMEM((blocks, tokens, LANES), BF16)]
    if is_first:
        out_shape = (wide_shape, out_shape)
        scratch.append(pltpu.VMEM((rows, LANES), F32))
    if is_last:
        out_shape = (out_shape, sds((8, LANES), F32))
        scratch.append(pltpu.VMEM((tokens * heads, LANES), BF16))
        scratch.append(pltpu.SemaphoreType.DMA((rows // CHUNK,)))
    span = blocks * tokens
    return call(
        functools.partial(attend_kernel, tokens, heads, kv_here, blocks, is_first, is_last, unroll),
        "attend",
        [*first, *([] if is_first else [state]), *kv],
        out_shape,
        scratch=scratch,
        mib=24,
        estimate=cost(
            4 * tokens * heads * span * 2 * LANES, 4 * tokens * heads * LANES * 4, tokens * heads * span
        ),
        after=after,
        out_hbm=is_last,
    )


def body(
    blocks,
    lin_query,
    lin_key,
    lin_value,
    lin_gate,
    log_decay,
    norm_gain,
    doc_ids,
    soft_query,
    soft_key,
    soft_value,
):
    tokens, heads, _ = lin_query.shape
    tensor = HEADS // heads
    kv_here = max(1, heads // GROUP)
    half = heads // 2
    pieces = 1
    parts = 2 if half % 8 == 0 else 1
    count = half // pieces
    longest = blocks * tokens * 5 // 8
    window = min(blocks - 1, (longest - 1 + tokens - 1) // tokens)
    flat = lambda x: x.reshape(-1, LANES)
    block = lax.axis_index("seq")
    y = (block % 2).astype(jnp.int32).reshape(1)
    start = (lax.axis_index("tp") * heads // GROUP).astype(jnp.int32).reshape(1)
    def send(x, pairs):
        return lax.ppermute(x, "seq", [p for p in pairs if 0 <= p[0] < blocks and 0 <= p[1] < blocks])

    everyone = range(blocks)
    swap = [(b, b ^ 1) for b in everyone]

    own_kv, docs, cumul, info, held, sent = front(
        start,
        y,
        [
            doc_ids.reshape(tokens // LANES, LANES),
            flat(soft_key),
            flat(soft_value),
            jnp.transpose(log_decay),
            flat(lin_key),
            flat(lin_value),
        ],
        tokens,
        heads,
        kv_here,
        pieces,
    )
    came = [send(x, swap) for x in sent]
    far_step = window if window % 2 else blocks
    beside = send(own_kv, [(b, b + (far_step if b % 2 else 1)) for b in everyone])
    lane_kv, cross_kv = [], []
    ahead = own_kv
    for back in range(1, window // 2 + 1):
        ahead = send(ahead, [(b, b + 2) for b in everyone if b >= 2 * (back - 1)])
        lane_kv.append(ahead)
        cross_kv.append(send(ahead, [p for p in swap if p[0] >= 2 * back]))

    state = {}

    def first_attention(after):
        state["wide"], state["sum"] = attend(
            (docs, flat(soft_query)), None, [own_kv], False, tokens, heads, kv_here, after
        )
        return state["sum"]

    def more_attention(kv, is_last, after):
        state["sum"] = attend(
            (state["wide"],), state["sum"], kv, is_last, tokens, heads, kv_here, after
        )
        return state["sum"]

    inner, qh = [], []

    def inner_of(part, after):
        n = heads // parts
        got = inner_part(
            cumul, docs, flat(lin_query), flat(lin_key), flat(lin_value), tokens, heads, part * n, n, after
        )
        inner.append(got[0])
        qh.append(got[1])
        return got[0]

    beside_work = [first_attention]
    beside_work += [functools.partial(inner_of, part) for part in range(parts)]
    beside_work.append(functools.partial(more_attention, [beside] + lane_kv[:1], False))

    done = info
    mine, far = [], []
    prior_doc = None
    run, before = [None] * pieces, [None] * pieces
    stages = (blocks // 2).bit_length() - 1
    for stage in range(stages + 1):
        if beside_work:
            done = beside_work.pop(0)([done])
        if stage == stages:
            while beside_work:
                done = beside_work.pop(0)([done])
        upper = ((block >> stage) & 1).astype(jnp.int32).reshape(1)
        for p in range(pieces):
            at = (p * count, count, [done])
            if stage == 0:
                done = run[p] = row_map(y, held[p], info, came[p], came[0], *at)
            elif stage < stages:
                run[p], before[p] = scan_step(upper, run[p], got[p], before[p], *at)
                done = run[p]
            else:
                done, sent, prior_doc = prior_states(
                    y, upper, held[p], info, came[p], came[0], got[p], before[p], *at
                )
                mine.append(done)
                far.append(send(sent, swap))
        if stage < stages:
            got = [send(x, [(b, b ^ (2 << stage)) for b in everyone]) for x in run]
    rest = [kv for pair in zip(cross_kv, lane_kv[1:] + [None]) for kv in pair if kv is not None]
    done = more_attention(rest[:1], False, [done])
    rest = rest[1:]
    mixed, squares = mix(
        y, docs, prior_doc, cumul, inner, qh, mine, far, tokens, heads, [done]
    )
    sums = [squares]
    for other in range(1, tensor):
        sums.append(lax.ppermute(squares, "tp", [(t, t ^ other) for t in range(tensor)]))
    after = [squares]
    while rest:
        got = more_attention(rest[:2], len(rest) <= 2, after)
        rest, after = rest[2:], []
    soft_out, done = got
    lin_out = finish(norm_gain, flat(lin_gate), mixed, sums, tokens, heads, [done])
    shape = (tokens, heads, HEAD_DIM)
    return lin_out.reshape(shape), soft_out.reshape(shape)


def solution(mesh):
    in_specs = (
        P("seq", "tp", None),
        P("seq", "tp", None),
        P("seq", "tp", None),
        P("seq", "tp", None),
        P("seq", "tp"),
        P("tp", None),
        P("seq"),
        P("seq", "tp", None),
        P("seq", None, None),
        P("seq", None, None),
    )
    out_specs = (P("seq", "tp", None), P("seq", "tp", None))
    return jax.shard_map(
        functools.partial(body, mesh.shape["seq"]),
        mesh=mesh,
        in_specs=in_specs,
        out_specs=out_specs,
        check_vma=False,
    )
```

```python
import functools

import jax
import jax.numpy as jnp
import numpy as np
from jax import lax
from jax.experimental import pallas as pl
from jax.experimental.pallas import tpu as pltpu
from jax.sharding import PartitionSpec as P

HEADS = 64
HEAD_DIM = 128
KV_HEADS = 8
LANES = 128
GROUP = HEADS // KV_HEADS
F32 = jnp.float32
BF16 = jnp.bfloat16
BIG = float(2**20)
SCORE_TO_EXP2 = HEAD_DIM**-0.5 * float(np.log2(np.e))
INFO = 16
HIGHEST = lax.Precision.HIGHEST

VMEM = pl.BlockSpec(memory_space=pltpu.VMEM)
SMEM = pl.BlockSpec(memory_space=pltpu.SMEM)
HBM = pl.BlockSpec(memory_space=pltpu.HBM)
ANYWHERE = pl.BlockSpec(memory_space=pl.ANY)
STATE_ROWS = HEAD_DIM + 16
CHUNK = 256


def sds(shape, dtype):
    return jax.ShapeDtypeStruct(shape, dtype)


def cost(flops, bytes_accessed, transcendentals=0):
    return pl.CostEstimate(
        flops=int(flops) // 64, bytes_accessed=int(bytes_accessed) // 64, transcendentals=int(transcendentals) // 64
    )


def call(kernel, name, place, operands, out_shape, scratch=(), mib=16, estimate=None, after=(), hbm=0, out_hbm=False):
    begin = 1 + len(operands)
    skip = len(after)
    operands = [
        pltpu.with_memory_space_constraint(x, pltpu.HBM) if i < hbm else x for i, x in enumerate(operands)
    ]
    outs = out_shape if isinstance(out_shape, tuple) else (out_shape,)
    out_specs = (VMEM,) * len(outs)
    outs = tuple(
        (pltpu.HBM if out_hbm and i == 0 else pltpu.VMEM)(x.shape, x.dtype) for i, x in enumerate(outs)
    )
    if out_hbm:
        out_specs = (HBM, *out_specs[1:])

    def run(*refs):
        kernel(*refs[:begin], *refs[begin + skip :])

    out = pl.pallas_call(
        run,
        out_shape=outs,
        in_specs=[SMEM] + [HBM] * hbm + [VMEM] * (len(operands) - hbm) + [ANYWHERE] * skip,
        out_specs=out_specs,
        scratch_shapes=list(scratch),
        compiler_params=pltpu.CompilerParams(vmem_limit_bytes=mib * 1024 * 1024),
        cost_estimate=estimate,
        name=name,
    )(place, *operands, *after)
    return out if isinstance(out_shape, tuple) else out[0]


def doc_columns(doc_rows, tokens):
    parts = []
    for i in range(tokens // LANES):
        row = jnp.broadcast_to(doc_rows[i : i + 1, :], (LANES, LANES))
        parts.append(jnp.transpose(row))
    return jnp.concatenate(parts, axis=0)


def doc_line(doc_rows, tokens):
    return jnp.concatenate([doc_rows[i : i + 1, :] for i in range(tokens // LANES)], axis=1)


def lower_triangle(tokens):
    rows = lax.broadcasted_iota(jnp.int32, (tokens, tokens), 0)
    cols = lax.broadcasted_iota(jnp.int32, (tokens, tokens), 1)
    return rows >= cols


def front_kernel(tokens, heads, kv_here, pieces, place_ref, *refs):
    refs = list(refs)
    take = lambda n: [refs.pop(0) for _ in range(n)]
    sources = take(6)
    kv_ref, doc_out, cumul_ref, info_ref = take(4)
    keep_refs, send_refs = take(pieces), take(pieces)
    held = take(6)
    sems, wide, kf, vf, states, ldp = refs
    docs_in, soft_key, soft_value, decays, lin_key, lin_value = held
    copies = [pltpu.make_async_copy(src, dst, sems.at[i]) for i, (src, dst) in enumerate(zip(sources, held))]
    for copy in copies:
        copy.start()

    copies[0].wait()
    docs = docs_in[...].astype(F32) + 1.0
    line = lax.broadcasted_iota(jnp.int32, (INFO, LANES), 0)
    info = jnp.zeros((INFO, LANES), F32)
    for i in range(tokens // LANES):
        info = jnp.where(line == i, docs[i : i + 1, :], info)
    doc_out[...] = info
    end = 2 * kv_here * tokens
    kv_ref[end : end + INFO, :] = info.astype(BF16)

    start = place_ref[1]
    for which, ref in enumerate((soft_key, soft_value)):
        copies[1 + which].wait()
        wide[...] = ref[...].astype(F32)
        for g in range(kv_here):
            rows = wide[pl.ds(start + g, tokens, stride=KV_HEADS), :]
            at = (which * kv_here + g) * tokens
            if which:
                halves = [jnp.transpose(rows[i : i + LANES, :]) for i in range(0, tokens, LANES)]
                rows = jnp.concatenate(halves, axis=0)
            kv_ref[at : at + tokens, :] = rows.astype(BF16)

    half = heads // 2
    y = place_ref[0] % 2
    copies[3].wait()
    ldp[...] = jnp.zeros_like(ldp)
    ldp[0:heads, :] = decays[...]
    cumul = lax.dot_general(
        lower_triangle(tokens).astype(F32),
        ldp[...],
        (((1,), (1,)), ((), ())),
        precision=HIGHEST,
        preferred_element_type=F32,
    )
    cumul_ref[...] = cumul
    total = cumul[tokens - 1 : tokens, :]
    last_row = tokens // LANES - 1
    first_doc = docs[0:1, 0:1]
    last_doc = docs[last_row : last_row + 1, LANES - 1 : LANES]
    tail = (doc_columns(docs, tokens) == last_doc).astype(F32)
    scale = jnp.exp(total - cumul) * tail
    copies[4].wait()
    kf[...] = lin_key[...].astype(F32)
    copies[5].wait()
    vf[...] = lin_value[...].astype(F32)
    for h in range(heads):
        keys = (kf[pl.ds(h, tokens, stride=heads), :] * scale[:, h : h + 1]).astype(BF16)
        values = vf[pl.ds(h, tokens, stride=heads), :].astype(BF16)
        states[h * HEAD_DIM : (h + 1) * HEAD_DIM, :] = lax.dot_general(
            keys, values, (((0,), (0,)), ((), ())), preferred_element_type=F32
        )
    size = half // pieces * HEAD_DIM
    for p in range(pieces):
        keep_at = pl.multiple_of((y * pieces + p) * size, size)
        send_at = pl.multiple_of(((1 - y) * pieces + p) * size, size)
        keep_refs[p][...] = states[pl.ds(keep_at, size), :].astype(BF16)
        send_refs[p][0:size, :] = states[pl.ds(send_at, size), :].astype(BF16)
    upper = pltpu.roll(total, LANES - half, 1)

    def info_of(totals):
        return info_rows((*in_parts(totals), first_doc, last_doc))

    mine = (y == 0).astype(F32)
    info_ref[...] = info_of(total * mine + upper * (1.0 - mine))
    send_refs[0][size : size + INFO, :] = info_of(total * (1.0 - mine) + upper * mine)


def front(place, operands, tokens, heads, kv_here, pieces):
    size = heads // 2 // pieces * HEAD_DIM
    keep = [sds((size, LANES), BF16)] * pieces
    send = [sds((size + (INFO if p == 0 else 0), LANES), BF16) for p in range(pieces)]
    out = call(
        functools.partial(front_kernel, tokens, heads, kv_here, pieces),
        "front",
        place,
        operands,
        (
            sds((2 * kv_here * tokens + INFO, LANES), BF16),
            sds((INFO, LANES), F32),
            sds((tokens, LANES), F32),
            sds((INFO, LANES), BF16),
            *keep,
            *send,
        ),
        scratch=[pltpu.VMEM(x.shape, x.dtype) for x in operands]
        + [
            pltpu.SemaphoreType.DMA((len(operands),)),
            pltpu.VMEM((tokens * KV_HEADS, LANES), F32),
            pltpu.VMEM((tokens * heads, LANES), F32),
            pltpu.VMEM((tokens * heads, LANES), F32),
            pltpu.VMEM((heads * HEAD_DIM, LANES), F32),
            pltpu.VMEM((LANES, tokens), F32),
        ],
        mib=24,
        estimate=cost(2 * heads * tokens * HEAD_DIM**2, 5 * tokens * heads * LANES * 2),
        hbm=len(operands),
    )
    return (*out[:4], out[4 : 4 + pieces], out[4 + pieces :])


def in_parts(x):
    hi = x.astype(BF16).astype(F32)
    mid = (x - hi).astype(BF16).astype(F32)
    return hi, mid, x - hi - mid


def info_rows(parts):
    line = lax.broadcasted_iota(jnp.int32, (INFO, LANES), 0)
    info = jnp.zeros((INFO, LANES), F32)
    for i, part in enumerate(parts):
        info = jnp.where(line == i, part, info)
    return info.astype(BF16)


def read_map(ref, size):
    info = ref[size : size + INFO, :].astype(F32)
    return info[0:1] + info[1:2] + info[2:3], info[3:4], info[4:5]


def row_terms(place_ref, own_info, other_info):
    even = place_ref[0] % 2 == 0
    own = own_info.astype(F32)
    other = other_info.astype(F32)
    a = jnp.where(even, own, other)
    b = jnp.where(even, other, own)
    decay_a = jnp.exp(a[0:1] + a[1:2] + a[2:3])
    decay_b = jnp.exp(b[0:1] + b[1:2] + b[2:3])
    first_a, last_a = a[3:4], a[4:5]
    first_b, last_b = b[3:4], b[4:5]
    whole_a = (first_a == last_a).astype(F32)
    link_b = ((last_a == first_b) & (first_b == last_b)).astype(F32)
    return even, decay_a * whole_a, decay_b * link_b, first_a, last_a, last_b


def row_kernel(count, first, place_ref, keep_ref, info_ref, other_ref, other_info_ref, out_ref):
    size = count * HEAD_DIM
    even, gain_a, gain_b, first_a, _, last_b = row_terms(
        place_ref, info_ref[...], other_info_ref[size : size + INFO, :]
    )
    for i in range(count):
        rows = slice(i * HEAD_DIM, (i + 1) * HEAD_DIM)
        lane = slice(first + i, first + i + 1)
        own = keep_ref[rows, :].astype(F32)
        other = other_ref[rows, :].astype(F32)
        state_a, state_b = jnp.where(even, own, other), jnp.where(even, other, own)
        out_ref[rows, :] = (gain_b[:, lane] * state_a + state_b).astype(BF16)
    out_ref[size : size + INFO, :] = info_rows((*in_parts(gain_a * gain_b), first_a, last_b))


def row_map(place, keep, info, other, other_info, first, count, after):
    size = count * HEAD_DIM
    return call(
        functools.partial(row_kernel, count, first),
        "row_map",
        place,
        [keep, info, other, other_info],
        sds((size + INFO, LANES), BF16),
        estimate=cost(4 * size * LANES, 4 * size * LANES * 2),
        after=after,
    )


def scan_kernel(count, first, has_before, stage, place_ref, *refs):
    refs = list(refs)
    mine_ref, came_ref = refs[:2]
    before_ref = refs[2] if has_before else None
    run_ref, out_ref = refs[-2:]
    size = count * HEAD_DIM
    upper = (place_ref[0] >> stage) & 1 == 1
    gain_m, first_m, last_m = read_map(mine_ref, size)
    gain_c, first_c, last_c = read_map(came_ref, size)
    link = jnp.where(upper, (last_c == first_m).astype(F32), (last_m == first_c).astype(F32))
    gain = jnp.where(upper, gain_m, gain_c) * link
    for i in range(count):
        rows = slice(i * HEAD_DIM, (i + 1) * HEAD_DIM)
        lane = slice(first + i, first + i + 1)
        mine, came = mine_ref[rows, :].astype(F32), came_ref[rows, :].astype(F32)
        lower_sum, upper_sum = jnp.where(upper, came, mine), jnp.where(upper, mine, came)
        run_ref[rows, :] = (gain[:, lane] * lower_sum + upper_sum).astype(BF16)
    run_ref[size : size + INFO, :] = info_rows(
        (
            *in_parts(gain * jnp.where(upper, gain_c, gain_m)),
            jnp.where(upper, first_c, first_m),
            jnp.where(upper, last_m, last_c),
        )
    )
    if not has_before:
        out_ref[...] = jnp.where(upper, came_ref[...], jnp.zeros_like(came_ref))
        return
    gain_b, first_b, last_b = read_map(before_ref, size)
    empty = first_b == 0.0
    factor = jnp.where(empty, 1.0, gain_b * (last_c == first_b).astype(F32))
    for i in range(count):
        rows = slice(i * HEAD_DIM, (i + 1) * HEAD_DIM)
        lane = slice(first + i, first + i + 1)
        before = before_ref[rows, :].astype(F32)
        joined = factor[:, lane] * came_ref[rows, :].astype(F32) + before
        out_ref[rows, :] = jnp.where(upper, joined, before).astype(BF16)
    out_ref[size : size + INFO, :] = info_rows(
        (
            *in_parts(jnp.where(upper, factor * gain_c, gain_b)),
            jnp.where(upper, first_c, first_b),
            jnp.where(upper, jnp.where(empty, last_c, last_b), last_b),
        )
    )


def scan_step(place, stage, mine, came, before, first, count, after):
    size = count * HEAD_DIM
    shape = sds((size + INFO, LANES), BF16)
    before = [] if before is None else [before]
    return call(
        functools.partial(scan_kernel, count, first, len(before), stage),
        "scan_step",
        place,
        [mine, came, *before],
        (shape, shape),
        estimate=cost(6 * size * LANES, 6 * size * LANES * 2),
        after=after,
    )


def prior_kernel(count, first, has_before, stage, place_ref, *refs):
    keep_ref, info_ref, other_ref, other_info_ref, came_ref = refs[:5]
    before_ref = refs[5] if has_before else None
    mine_ref, send_ref, doc_ref = refs[-3:]
    size = count * HEAD_DIM
    upper = ((place_ref[0] >> stage) & 1).astype(F32)
    even, gain_a, _, first_a, last_a, _ = row_terms(
        place_ref, info_ref[...], other_info_ref[size : size + INFO, :]
    )
    _, _, last_c = read_map(came_ref, size)
    factor, doc = upper, upper * last_c
    if has_before:
        gain_b, first_b, last_b = read_map(before_ref, size)
        empty = first_b == 0.0
        factor = upper * jnp.where(empty, 1.0, gain_b * (last_c == first_b).astype(F32))
        doc = jnp.where(empty, doc, last_b)
    else:
        factor = jnp.broadcast_to(factor, (1, LANES))
    gain_a = gain_a * (doc == first_a).astype(F32)
    for i in range(count):
        rows = slice(i * HEAD_DIM, (i + 1) * HEAD_DIM)
        lane = slice(first + i, first + i + 1)
        before_a = factor[:, lane] * came_ref[rows, :].astype(F32)
        if has_before:
            before_a = before_a + before_ref[rows, :].astype(F32)
        state_a = jnp.where(even, keep_ref[rows, :].astype(F32), other_ref[rows, :].astype(F32))
        before_b = gain_a[:, lane] * before_a + state_a
        mine_ref[rows, :] = jnp.where(even, before_a, before_b).astype(BF16)
        send_ref[rows, :] = jnp.where(even, before_b, before_a).astype(BF16)
    doc_ref[...] = jnp.broadcast_to(jnp.where(even, doc, last_a), (8, LANES))


def prior_states(place, stage, keep, info, other, other_info, came, before, first, count, after):
    size = count * HEAD_DIM
    before = [] if before is None else [before]
    return call(
        functools.partial(prior_kernel, count, first, len(before), stage),
        "prior_states",
        place,
        [keep, info, other, other_info, came, *before],
        (sds((size, LANES), BF16), sds((size, LANES), BF16), sds((8, LANES), F32)),
        estimate=cost(4 * size * LANES, 6 * size * LANES * 2),
        after=after,
    )


def some_heads(ref, tokens, heads, first, count):
    x = ref[...].astype(F32)
    if count == heads:
        return x
    return x.reshape(tokens, heads, LANES)[:, first : first + count, :].reshape(tokens * count, LANES)


def inner_kernel(tokens, heads, first, count, place_ref, cumul_ref, doc_ref, query_ref, key_ref, value_ref, inner_ref, qh_ref, qf, kf, vf, mask):
    cumul = cumul_ref[...]
    cumul_t = jnp.transpose(cumul)
    docs = doc_ref[...]
    column = doc_columns(docs, tokens)
    same = jnp.concatenate([column] * (tokens // LANES), axis=1) == doc_line(docs, tokens)
    mask[...] = jnp.where(lower_triangle(tokens) & same, 0.0, -1e9)
    qf[...] = some_heads(query_ref, tokens, heads, first, count)
    kf[...] = some_heads(key_ref, tokens, heads, first, count)
    vf[...] = some_heads(value_ref, tokens, heads, first, count)
    for n in range(count):
        h = first + n
        picked = pl.ds(n, tokens, stride=count)
        query = qf[picked, :].astype(BF16)
        keys = kf[picked, :].astype(BF16)
        values = vf[picked, :].astype(BF16)
        qh_ref[n * tokens : (n + 1) * tokens, :] = query
        for i in range(tokens // LANES):
            seen = (i + 1) * LANES
            rows = slice(i * LANES, seen)
            scores = lax.dot_general(
                query[rows, :], keys[0:seen, :], (((1,), (1,)), ((), ())), preferred_element_type=F32
            )
            gap = cumul[rows, h : h + 1] - cumul_t[h : h + 1, 0:seen]
            weights = (scores * jnp.exp(gap + mask[rows, 0:seen])).astype(BF16)
            inner_ref[n * tokens + i * LANES : n * tokens + seen, :] = jnp.dot(
                weights, values[0:seen, :], preferred_element_type=F32
            )


def inner_part(place, cumul, docs, query, key, value, tokens, heads, first, count, after):
    return call(
        functools.partial(inner_kernel, tokens, heads, first, count),
        "inner_part",
        place,
        [cumul, docs, query, key, value],
        (sds((count * tokens, LANES), F32), sds((count * tokens, LANES), BF16)),
        scratch=[pltpu.VMEM((tokens * count, LANES), F32)] * 3 + [pltpu.VMEM((tokens, tokens), F32)],
        mib=24,
        estimate=cost(
            4 * count * tokens * tokens * HEAD_DIM, tokens * heads * LANES * 12, count * tokens * tokens
        ),
        after=after,
    )


def mix_kernel(tokens, heads, parts, pieces, place_ref, doc_ref, prior_doc_ref, cumul_ref, *refs):
    refs = list(refs)
    take = lambda n: [refs.pop(0) for _ in range(n)]
    inner, qh, mine, other = take(parts), take(parts), take(pieces), take(pieces)
    mixed_ref, square_ref = refs
    half = heads // 2
    count = half // pieces
    even = place_ref[0] % 2 == 0
    is_open = (doc_columns(doc_ref[...], tokens) == prior_doc_ref[0:1, :]).astype(F32)
    gain = jnp.exp(cumul_ref[...]) * is_open
    squares = jnp.zeros((tokens, LANES), F32)
    for h in range(heads):
        piece, i = divmod(h % half, count)
        rows = slice(i * HEAD_DIM, (i + 1) * HEAD_DIM)
        near, far = mine[piece][rows, :], other[piece][rows, :]
        lower = h < half
        state = jnp.where(even, near if lower else far, far if lower else near)
        part, n = divmod(h, heads // parts)
        held = slice(n * tokens, (n + 1) * tokens)
        carried = jnp.dot(qh[part][held, :], state, preferred_element_type=F32)
        mixed = inner[part][held, :] + carried * gain[:, h : h + 1]
        squares = squares + mixed * mixed
        mixed_ref[pl.ds(h, tokens, stride=heads), :] = mixed
    square_ref[...] = lax.dot_general(
        jnp.ones((8, LANES), F32),
        squares,
        (((1,), (1,)), ((), ())),
        precision=HIGHEST,
        preferred_element_type=F32,
    )


def mix(place, docs, prior_doc, cumul, inner, qh, mine, other, tokens, heads, after):
    return call(
        functools.partial(mix_kernel, tokens, heads, len(inner), len(mine)),
        "mix",
        place,
        [docs, prior_doc, cumul, *inner, *qh, *mine, *other],
        (sds((tokens * heads, LANES), F32), sds((8, tokens), F32)),
        mib=24,
        estimate=cost(2 * heads * tokens * HEAD_DIM**2, tokens * heads * LANES * 10),
        after=after,
    )


def finish_kernel(tokens, heads, sums, step, place_ref, gain_ref, gate_ref, mixed_ref, *refs):
    squares, (out_ref, done, sems) = refs[:sums], refs[sums:]
    total = squares[0][0:1, :]
    for ref in squares[1:]:
        total = total + ref[0:1, :]
    scale = lax.rsqrt(total / (HEADS * HEAD_DIM) + 1e-06)
    rows = jnp.concatenate([scale[:, i * LANES : (i + 1) * LANES] for i in range(tokens // LANES)], axis=0)
    column = doc_columns(rows, tokens)
    copies = []
    for i in range(0, tokens, step):
        at = pl.ds(i * heads, step * heads)
        gate = jax.nn.sigmoid(gate_ref[at, :].astype(F32)).reshape(step, heads, LANES)
        mixed = mixed_ref[at, :].reshape(step, heads, LANES)
        inv = column[i : i + step, :][:, None, :]
        out = mixed * inv * gain_ref[...][None] * gate
        done[at, :] = out.reshape(step * heads, LANES).astype(BF16)
        copies.append(pltpu.make_async_copy(done.at[at, :], out_ref.at[at, :], sems.at[i // step]))
        copies[-1].start()
    for copy in copies:
        copy.wait()


def finish(place, gain, gate, mixed, squares, tokens, heads, after):
    step = 64
    return call(
        functools.partial(finish_kernel, tokens, heads, len(squares), step),
        "finish",
        place,
        [gain, gate, mixed, *squares],
        sds((tokens * heads, LANES), BF16),
        scratch=[pltpu.VMEM((tokens * heads, LANES), BF16), pltpu.SemaphoreType.DMA((tokens // step,))],
        estimate=cost(0, tokens * heads * LANES * 8, tokens * heads * LANES),
        after=after,
        out_hbm=True,
    )


def attend_kernel(tokens, heads, kv_here, least, is_first, is_last, unroll, place_ref, *refs):
    refs = list(refs)
    take = lambda n: [refs.pop(0) for _ in range(n)]
    per_group = heads // kv_here
    rows = tokens * per_group
    step = CHUNK // per_group
    if is_first:
        doc_ref, query_ref = take(2)
    else:
        wide_ref, state_ref = take(2)
    kv = take(len(least))
    if is_first:
        wide_ref = take(1)[0]
    out_ref = take(1)[0]
    if is_last:
        take(1)[0][...] = jnp.zeros((8, LANES), F32)
    bias = take(1)[0]
    if is_first:
        doc_rep = take(1)[0]
    if is_last:
        done, sems = take(2)

    lane = lax.broadcasted_iota(jnp.int32, (tokens, LANES), 1).astype(F32)
    end = 2 * kv_here * tokens
    block = place_ref[0]
    for j, ref in enumerate(kv):
        valid = (block >= jnp.where(block % 2 == 0, *least[j])).astype(F32)
        docs = doc_columns(ref[end : end + INFO, :].astype(F32) * valid, tokens)
        bias[j] = jnp.where(docs == lane, 0.0, -BIG).astype(BF16)
    if is_first:
        column = doc_columns(doc_ref[...], tokens)
        for h in range(per_group):
            doc_rep[pl.ds(h, tokens, stride=per_group), :] = (column == lane).astype(F32)
    ones = jnp.ones((STATE_ROWS - HEAD_DIM, tokens), BF16)

    def some_chunks(i, carry):
        chains = [(u, g) for u in range(unroll) for g in range(kv_here)]
        chunk = [i * unroll + u for u in range(unroll)]
        at = [pl.ds(pl.multiple_of(c * CHUNK, CHUNK), CHUNK) for c in chunk]
        picked = [pl.ds(pl.multiple_of(c * (step * heads), step * heads), step * heads) for c in chunk]
        scores, results = {}, {}

        def begin(u, g):
            if is_first:
                query = query_ref[picked[u], :].astype(F32).reshape(step, heads, LANES)
                query = query[:, g * per_group : (g + 1) * per_group, :].reshape(CHUNK, LANES)
                wide = jnp.concatenate([query.astype(BF16), doc_rep[at[u], :].astype(BF16)], axis=1)
                wide_ref[g, at[u], :] = wide
            else:
                wide = wide_ref[g, at[u], :]
            out = []
            for j, ref in enumerate(kv):
                keys = jnp.concatenate([ref[g * tokens : (g + 1) * tokens, :], bias[j]], axis=1)
                out.append(
                    lax.dot_general(keys, wide, (((1,), (1,)), ((), ())), preferred_element_type=F32)
                )
            if is_first:
                token = chunk[u] * step + lax.broadcasted_iota(jnp.int32, (tokens, CHUNK), 1) // per_group
                key_at = lax.broadcasted_iota(jnp.int32, (tokens, CHUNK), 0)
                out[0] = jnp.where(key_at <= token, out[0], -BIG)
            scores[u, g] = out

        def end_chain(u, g):
            here = scores.pop((u, g))
            top = jnp.max(here[0], axis=0, keepdims=True)
            for score in here[1:]:
                top = jnp.maximum(top, jnp.max(score, axis=0, keepdims=True))
            total = None
            if not is_first:
                before = state_ref[g, :, at[u]]
                top_before = before[STATE_ROWS - 1 : STATE_ROWS, :]
                top = jnp.maximum(top, top_before)
                total = before * jnp.exp2((top_before - top) * SCORE_TO_EXP2)
            for ref, score in zip(kv, here):
                weights = jnp.exp2((score - top) * SCORE_TO_EXP2).astype(BF16)
                first = (kv_here + g) * tokens
                parts = [ref[first + p : first + p + LANES, :] for p in range(0, tokens, LANES)]
                values = jnp.concatenate([jnp.concatenate(parts, axis=1), ones], axis=0)
                more = jnp.dot(values, weights, preferred_element_type=F32)
                total = more if total is None else total + more
            if is_last:
                results[u, g] = jnp.transpose(total[0:HEAD_DIM] / total[HEAD_DIM : HEAD_DIM + 1])
            else:
                out_ref[g, 0 : STATE_ROWS - 8, at[u]] = total[0 : STATE_ROWS - 8]
                out_ref[g, STATE_ROWS - 8 : STATE_ROWS, at[u]] = jnp.broadcast_to(top, (8, CHUNK))

        ahead = 2
        for n in range(len(chains) + ahead):
            if n < len(chains):
                begin(*chains[n])
            if n >= ahead:
                end_chain(*chains[n - ahead])
        if is_last:
            for u in range(unroll):
                result = [results[u, g] for g in range(kv_here)]
                if kv_here > 1:
                    result = [r.reshape(step, per_group, LANES) for r in result]
                    result = [jnp.concatenate(result, axis=1).reshape(step * heads, LANES)]
                done[picked[u], :] = result[0].astype(BF16)
                pltpu.make_async_copy(
                    done.at[picked[u], :], out_ref.at[picked[u], :], sems.at[chunk[u]]
                ).start()
        return carry

    lax.fori_loop(0, rows // (CHUNK * unroll), some_chunks, 0)
    if is_last:
        for c in range(rows // CHUNK):
            at = pl.ds(c * step * heads, step * heads)
            pltpu.make_async_copy(done.at[at, :], out_ref.at[at, :], sems.at[c]).wait()


def attend(place, first, state, kv, is_last, tokens, heads, kv_here, after):
    is_first = state is None
    least = tuple(pair for _, pair in kv)
    kv = [block for block, _ in kv]
    blocks = len(kv)
    rows = tokens * heads // kv_here
    unroll = min(4, rows // CHUNK)
    wide_shape = sds((kv_here, rows, 2 * LANES), BF16)
    state_shape = sds((kv_here, STATE_ROWS, rows), F32)
    out_shape = sds((tokens * heads, LANES), BF16) if is_last else state_shape
    scratch = [pltpu.VMEM((blocks, tokens, LANES), BF16)]
    if is_first:
        out_shape = (wide_shape, out_shape)
        scratch.append(pltpu.VMEM((rows, LANES), F32))
    if is_last:
        out_shape = (out_shape, sds((8, LANES), F32))
        scratch.append(pltpu.VMEM((tokens * heads, LANES), BF16))
        scratch.append(pltpu.SemaphoreType.DMA((rows // CHUNK,)))
    span = blocks * tokens
    return call(
        functools.partial(attend_kernel, tokens, heads, kv_here, least, is_first, is_last, unroll),
        "attend",
        place,
        [*first, *([] if is_first else [state]), *kv],
        out_shape,
        scratch=scratch,
        mib=24,
        estimate=cost(
            4 * tokens * heads * span * 2 * LANES, 4 * tokens * heads * LANES * 4, tokens * heads * span
        ),
        after=after,
        out_hbm=is_last,
    )


def body(
    blocks,
    lin_query,
    lin_key,
    lin_value,
    lin_gate,
    log_decay,
    norm_gain,
    doc_ids,
    soft_query,
    soft_key,
    soft_value,
):
    tokens, heads, _ = lin_query.shape
    tensor = HEADS // heads
    kv_here = max(1, heads // GROUP)
    half = heads // 2
    pieces = 2 if half % 2 == 0 else 1
    parts = 2 if half % 8 == 0 else 1
    count = half // pieces
    longest = blocks * tokens * 5 // 8
    window = min(blocks - 1, (longest - 1 + tokens - 1) // tokens)
    flat = lambda x: x.reshape(-1, LANES)
    block = lax.axis_index("seq")
    place = jnp.stack([block, lax.axis_index("tp") * heads // GROUP]).astype(jnp.int32)

    def send(x, pairs):
        return lax.ppermute(x, "seq", [(a, b % blocks) for a, b in pairs])

    everyone = range(blocks)
    swap = [(b, b ^ 1) for b in everyone]

    own_kv, docs, cumul, info, held, sent = front(
        place,
        [
            doc_ids.reshape(tokens // LANES, LANES),
            flat(soft_key),
            flat(soft_value),
            jnp.transpose(log_decay),
            flat(lin_key),
            flat(lin_value),
        ],
        tokens,
        heads,
        kv_here,
        pieces,
    )
    came = [send(x, swap) for x in sent]
    odd_window = window % 2 == 1
    beside = send(own_kv, [(b, b + (1 if b % 2 == 0 else window if odd_window else -1)) for b in everyone])
    beside = (beside, (window if odd_window else blocks, 1))
    lane_kv, cross_kv = [], []
    ahead = own_kv
    for back in range(1, window // 2 + 1):
        ahead = send(ahead, [(b, b + 2) for b in everyone])
        lane_kv.append((ahead, (2 * back, 2 * back)))
        cross_kv.append((send(ahead, swap), (2 * back, 2 * back + 1)))
    held = list(held)

    state = {}

    def first_attention(after):
        state["wide"], state["sum"] = attend(
            place, (docs, flat(soft_query)), None, [(own_kv, (0, 0))], False, tokens, heads, kv_here, after
        )
        return state["sum"]

    def more_attention(kv, is_last, after):
        state["sum"] = attend(
            place, (state["wide"],), state["sum"], kv, is_last, tokens, heads, kv_here, after
        )
        return state["sum"]

    inner, qh = [], []

    def inner_of(part, after):
        n = heads // parts
        got = inner_part(
            place, cumul, docs, flat(lin_query), flat(lin_key), flat(lin_value), tokens, heads, part * n, n, after
        )
        inner.append(got[0])
        qh.append(got[1])
        return got[0]

    beside_work = [first_attention]
    beside_work += [functools.partial(inner_of, part) for part in range(parts)]
    beside_work.append(functools.partial(more_attention, [beside] + lane_kv[:1], False))

    done = info
    mine, far = [], []
    prior_doc = None
    run, before = [None] * pieces, [None] * pieces
    stages = (blocks // 2).bit_length() - 1
    for stage in range(stages + 1):
        if beside_work:
            done = beside_work.pop(0)([done])
        if stage == stages:
            while beside_work:
                done = beside_work.pop(0)([done])
        for p in range(pieces):
            at = (p * count, count, [done])
            if stage == 0:
                done = run[p] = row_map(place, held[p], info, came[p], came[0], *at)
            elif stage < stages:
                run[p], before[p] = scan_step(place, stage, run[p], got[p], before[p], *at)
                done = run[p]
            else:
                done, sent, prior_doc = prior_states(
                    place, stage, held[p], info, came[p], came[0], got[p], before[p], *at
                )
                mine.append(done)
                far.append(send(sent, swap))
        if stage < stages:
            got = [send(x, [(b, b ^ (2 << stage)) for b in everyone]) for x in run]
    rest = [kv for pair in zip(cross_kv, lane_kv[1:] + [None]) for kv in pair if kv is not None]
    done = more_attention(rest[:1], False, [done])
    rest = rest[1:]
    mixed, squares = mix(
        place, docs, prior_doc, cumul, inner, qh, mine, far, tokens, heads, [done]
    )
    sums = [squares]
    for other in range(1, tensor):
        sums.append(lax.ppermute(squares, "tp", [(t, t ^ other) for t in range(tensor)]))
    after = [squares]
    while rest:
        got = more_attention(rest[:2], len(rest) <= 2, after)
        rest, after = rest[2:], []
    soft_out, done = got
    lin_out = finish(place, norm_gain, flat(lin_gate), mixed, sums, tokens, heads, [done])
    shape = (tokens, heads, HEAD_DIM)
    return lin_out.reshape(shape), soft_out.reshape(shape)


def solution(mesh):
    in_specs = (
        P("seq", "tp", None),
        P("seq", "tp", None),
        P("seq", "tp", None),
        P("seq", "tp", None),
        P("seq", "tp"),
        P("tp", None),
        P("seq"),
        P("seq", "tp", None),
        P("seq", None, None),
        P("seq", None, None),
    )
    out_specs = (P("seq", "tp", None), P("seq", "tp", None))
    return jax.shard_map(
        functools.partial(body, mesh.shape["seq"]),
        mesh=mesh,
        in_specs=in_specs,
        out_specs=out_specs,
        check_vma=False,
    )
```

```python
import functools

import jax
import jax.numpy as jnp
import numpy as np
from jax import lax
from jax.experimental import pallas as pl
from jax.experimental.pallas import tpu as pltpu
from jax.sharding import PartitionSpec as P

HEADS = 64
HEAD_DIM = 128
KV_HEADS = 8
LANES = 128
GROUP = HEADS // KV_HEADS
F32 = jnp.float32
BF16 = jnp.bfloat16
BIG = float(2**20)
SCORE_TO_EXP2 = HEAD_DIM**-0.5 * float(np.log2(np.e))
INFO = 16
HIGHEST = lax.Precision.HIGHEST

VMEM = pl.BlockSpec(memory_space=pltpu.VMEM)
SMEM = pl.BlockSpec(memory_space=pltpu.SMEM)
HBM = pl.BlockSpec(memory_space=pltpu.HBM)
ANYWHERE = pl.BlockSpec(memory_space=pl.ANY)
STATE_ROWS = HEAD_DIM + 16
CHUNK = 256


def sds(shape, dtype):
    return jax.ShapeDtypeStruct(shape, dtype)


def cost(flops, bytes_accessed, transcendentals=0):
    return pl.CostEstimate(
        flops=int(flops), bytes_accessed=int(bytes_accessed), transcendentals=int(transcendentals)
    )


def call(kernel, name, scalars, operands, out_shape, scratch=(), mib=16, estimate=None, after=(), hbm=0, out_hbm=False):
    begin = len(scalars) + len(operands)
    skip = len(after)
    operands = [
        pltpu.with_memory_space_constraint(x, pltpu.HBM) if i < hbm else x for i, x in enumerate(operands)
    ]
    outs = out_shape if isinstance(out_shape, tuple) else (out_shape,)
    out_specs = (VMEM,) * len(outs)
    outs = tuple(
        (pltpu.HBM if out_hbm and i == 0 else pltpu.VMEM)(x.shape, x.dtype) for i, x in enumerate(outs)
    )
    if out_hbm:
        out_specs = (HBM, *out_specs[1:])

    def run(*refs):
        kernel(*refs[:begin], *refs[begin + skip :])

    out = pl.pallas_call(
        run,
        out_shape=outs,
        in_specs=[SMEM] * len(scalars) + [HBM] * hbm + [VMEM] * (len(operands) - hbm) + [ANYWHERE] * skip,
        out_specs=out_specs,
        scratch_shapes=list(scratch),
        compiler_params=pltpu.CompilerParams(vmem_limit_bytes=mib * 1024 * 1024),
        cost_estimate=estimate,
        name=name,
    )(*scalars, *operands, *after)
    return out if isinstance(out_shape, tuple) else out[0]


def doc_columns(doc_rows, tokens):
    parts = []
    for i in range(tokens // LANES):
        row = jnp.broadcast_to(doc_rows[i : i + 1, :], (LANES, LANES))
        parts.append(jnp.transpose(row))
    return jnp.concatenate(parts, axis=0)


def doc_line(doc_rows, tokens):
    return jnp.concatenate([doc_rows[i : i + 1, :] for i in range(tokens // LANES)], axis=1)


def lower_triangle(tokens):
    rows = lax.broadcasted_iota(jnp.int32, (tokens, tokens), 0)
    cols = lax.broadcasted_iota(jnp.int32, (tokens, tokens), 1)
    return rows >= cols


def fetch_kernel(tokens, heads, kv_here, start_ref, *refs):
    refs = list(refs)
    take = lambda n: [refs.pop(0) for _ in range(n)]
    sources = take(6)
    kv_ref, doc_out, cumul_ref, key_out, value_out = take(5)
    held = take(4)
    sems, wide, ldp = refs
    docs_in, decays, soft_key, soft_value = held
    targets = [*held, key_out, value_out]
    copies = [
        pltpu.make_async_copy(source, target, sems.at[i])
        for i, (source, target) in enumerate(zip(sources, targets))
    ]
    for copy in copies:
        copy.start()

    copies[0].wait()
    docs = docs_in[...].astype(F32) + 1.0
    line = lax.broadcasted_iota(jnp.int32, (INFO, LANES), 0)
    info = jnp.zeros((INFO, LANES), F32)
    for i in range(tokens // LANES):
        info = jnp.where(line == i, docs[i : i + 1, :], info)
    doc_out[...] = info
    end = 2 * kv_here * tokens
    kv_ref[end : end + INFO, :] = info.astype(BF16)

    copies[1].wait()
    ldp[...] = jnp.zeros_like(ldp)
    ldp[0:heads, :] = decays[...]
    cumul_ref[...] = lax.dot_general(
        lower_triangle(tokens).astype(F32),
        ldp[...],
        (((1,), (1,)), ((), ())),
        precision=HIGHEST,
        preferred_element_type=F32,
    )

    start = start_ref[0]
    for which, ref in enumerate((soft_key, soft_value)):
        copies[2 + which].wait()
        wide[...] = ref[...].astype(F32)
        for g in range(kv_here):
            rows = wide[pl.ds(start + g, tokens, stride=KV_HEADS), :]
            at = (which * kv_here + g) * tokens
            if which:
                halves = [jnp.transpose(rows[i : i + LANES, :]) for i in range(0, tokens, LANES)]
                rows = jnp.concatenate(halves, axis=0)
            kv_ref[at : at + tokens, :] = rows.astype(BF16)
    copies[4].wait()
    copies[5].wait()


def fetch(start, operands, tokens, heads, kv_here):
    return call(
        functools.partial(fetch_kernel, tokens, heads, kv_here),
        "fetch",
        [start],
        operands,
        (
            sds((2 * kv_here * tokens + INFO, LANES), BF16),
            sds((INFO, LANES), F32),
            sds((tokens, LANES), F32),
            sds(operands[4].shape, BF16),
            sds(operands[5].shape, BF16),
        ),
        scratch=[pltpu.VMEM(x.shape, x.dtype) for x in operands[:4]]
        + [
            pltpu.SemaphoreType.DMA((len(operands),)),
            pltpu.VMEM((tokens * KV_HEADS, LANES), F32),
            pltpu.VMEM((LANES, tokens), F32),
        ],
        estimate=cost(0, 3 * tokens * heads * LANES * 2),
        hbm=len(operands),
    )


def state_kernel(tokens, heads, pieces, place_ref, *refs):
    refs = list(refs)
    take = lambda n: [refs.pop(0) for _ in range(n)]
    cumul_ref, doc_ref, key_ref, value_ref, info_ref = take(5)
    keep_refs, send_refs = take(pieces), take(pieces)
    kf, vf, states = refs
    half = heads // 2
    y = place_ref[0] % 2
    cumul, docs = cumul_ref[...], doc_ref[...]
    total = cumul[tokens - 1 : tokens, :]
    last_row = tokens // LANES - 1
    first_doc = docs[0:1, 0:1]
    last_doc = docs[last_row : last_row + 1, LANES - 1 : LANES]
    tail = (doc_columns(docs, tokens) == last_doc).astype(F32)
    scale = jnp.exp(total - cumul) * tail
    kf[...] = key_ref[...].astype(F32)
    vf[...] = value_ref[...].astype(F32)
    for h in range(heads):
        keys = (kf[pl.ds(h, tokens, stride=heads), :] * scale[:, h : h + 1]).astype(BF16)
        values = vf[pl.ds(h, tokens, stride=heads), :].astype(BF16)
        states[h * HEAD_DIM : (h + 1) * HEAD_DIM, :] = lax.dot_general(
            keys, values, (((0,), (0,)), ((), ())), preferred_element_type=F32
        )
    size = half // pieces * HEAD_DIM
    for p in range(pieces):
        keep_at = pl.multiple_of((y * pieces + p) * size, size)
        send_at = pl.multiple_of(((1 - y) * pieces + p) * size, size)
        keep_refs[p][...] = states[pl.ds(keep_at, size), :].astype(BF16)
        send_refs[p][0:size, :] = states[pl.ds(send_at, size), :].astype(BF16)
    upper = pltpu.roll(total, LANES - half, 1)

    def info_of(totals):
        return info_rows((*in_parts(totals), first_doc, last_doc))

    mine = (y == 0).astype(F32)
    info_ref[...] = info_of(total * mine + upper * (1.0 - mine))
    send_refs[0][size : size + INFO, :] = info_of(total * (1.0 - mine) + upper * mine)


def block_state(place, cumul, docs, key, value, tokens, heads, pieces):
    size = heads // 2 // pieces * HEAD_DIM
    keep = [sds((size, LANES), BF16)] * pieces
    send = [sds((size + (INFO if p == 0 else 0), LANES), BF16) for p in range(pieces)]
    out = call(
        functools.partial(state_kernel, tokens, heads, pieces),
        "block_state",
        [place],
        [cumul, docs, key, value],
        (sds((INFO, LANES), BF16), *keep, *send),
        scratch=[
            pltpu.VMEM((tokens * heads, LANES), F32),
            pltpu.VMEM((tokens * heads, LANES), F32),
            pltpu.VMEM((heads * HEAD_DIM, LANES), F32),
        ],
        estimate=cost(2 * heads * tokens * HEAD_DIM**2, 5 * tokens * heads * LANES * 2),
    )
    return out[0], out[1 : 1 + pieces], out[1 + pieces :]


def in_parts(x):
    hi = x.astype(BF16).astype(F32)
    mid = (x - hi).astype(BF16).astype(F32)
    return hi, mid, x - hi - mid


def info_rows(parts):
    line = lax.broadcasted_iota(jnp.int32, (INFO, LANES), 0)
    info = jnp.zeros((INFO, LANES), F32)
    for i, part in enumerate(parts):
        info = jnp.where(line == i, part, info)
    return info.astype(BF16)


def read_map(ref, size):
    info = ref[size : size + INFO, :].astype(F32)
    return info[0:1] + info[1:2] + info[2:3], info[3:4], info[4:5]


def row_terms(place_ref, own_info, other_info):
    even = place_ref[0] % 2 == 0
    own = own_info.astype(F32)
    other = other_info.astype(F32)
    a = jnp.where(even, own, other)
    b = jnp.where(even, other, own)
    decay_a = jnp.exp(a[0:1] + a[1:2] + a[2:3])
    decay_b = jnp.exp(b[0:1] + b[1:2] + b[2:3])
    first_a, last_a = a[3:4], a[4:5]
    first_b, last_b = b[3:4], b[4:5]
    whole_a = (first_a == last_a).astype(F32)
    link_b = ((last_a == first_b) & (first_b == last_b)).astype(F32)
    return even, decay_a * whole_a, decay_b * link_b, first_a, last_a, last_b


def row_kernel(count, first, place_ref, keep_ref, info_ref, other_ref, other_info_ref, *refs):
    out_ref = refs[len(refs) // 2]
    if len(refs) > 1:
        refs[2][...] = refs[0][...]
    size = count * HEAD_DIM
    even, gain_a, gain_b, first_a, _, last_b = row_terms(
        place_ref, info_ref[...], other_info_ref[size : size + INFO, :]
    )
    for i in range(count):
        rows = slice(i * HEAD_DIM, (i + 1) * HEAD_DIM)
        lane = slice(first + i, first + i + 1)
        own = keep_ref[rows, :].astype(F32)
        other = other_ref[rows, :].astype(F32)
        state_a, state_b = jnp.where(even, own, other), jnp.where(even, other, own)
        out_ref[rows, :] = (gain_b[:, lane] * state_a + state_b).astype(BF16)
    out_ref[size : size + INFO, :] = info_rows((*in_parts(gain_a * gain_b), first_a, last_b))


def row_map(place, keep, info, other, other_info, first, count, after, relay=None):
    size = count * HEAD_DIM
    relay = [] if relay is None else [relay]
    out = call(
        functools.partial(row_kernel, count, first),
        "row_map",
        [place],
        [keep, info, other, other_info, *relay],
        (sds((size + INFO, LANES), BF16), *[sds(x.shape, BF16) for x in relay]),
        estimate=cost(4 * size * LANES, 4 * size * LANES * 2),
        after=after,
    )
    return out if relay else out[0]


def scan_kernel(count, first, has_before, stage, place_ref, *refs):
    refs = list(refs)
    mine_ref, came_ref = refs[:2]
    before_ref = refs[2] if has_before else None
    run_ref, out_ref = refs[-2:]
    size = count * HEAD_DIM
    upper = (place_ref[0] >> stage) & 1 == 1
    gain_m, first_m, last_m = read_map(mine_ref, size)
    gain_c, first_c, last_c = read_map(came_ref, size)
    link = jnp.where(upper, (last_c == first_m).astype(F32), (last_m == first_c).astype(F32))
    gain = jnp.where(upper, gain_m, gain_c) * link
    for i in range(count):
        rows = slice(i * HEAD_DIM, (i + 1) * HEAD_DIM)
        lane = slice(first + i, first + i + 1)
        mine, came = mine_ref[rows, :].astype(F32), came_ref[rows, :].astype(F32)
        lower_sum, upper_sum = jnp.where(upper, came, mine), jnp.where(upper, mine, came)
        run_ref[rows, :] = (gain[:, lane] * lower_sum + upper_sum).astype(BF16)
    run_ref[size : size + INFO, :] = info_rows(
        (
            *in_parts(gain * jnp.where(upper, gain_c, gain_m)),
            jnp.where(upper, first_c, first_m),
            jnp.where(upper, last_m, last_c),
        )
    )
    if not has_before:
        out_ref[...] = jnp.where(upper, came_ref[...], jnp.zeros_like(came_ref))
        return
    gain_b, first_b, last_b = read_map(before_ref, size)
    empty = first_b == 0.0
    factor = jnp.where(empty, 1.0, gain_b * (last_c == first_b).astype(F32))
    for i in range(count):
        rows = slice(i * HEAD_DIM, (i + 1) * HEAD_DIM)
        lane = slice(first + i, first + i + 1)
        before = before_ref[rows, :].astype(F32)
        joined = factor[:, lane] * came_ref[rows, :].astype(F32) + before
        out_ref[rows, :] = jnp.where(upper, joined, before).astype(BF16)
    out_ref[size : size + INFO, :] = info_rows(
        (
            *in_parts(jnp.where(upper, factor * gain_c, gain_b)),
            jnp.where(upper, first_c, first_b),
            jnp.where(upper, jnp.where(empty, last_c, last_b), last_b),
        )
    )


def scan_step(place, stage, mine, came, before, first, count, after):
    size = count * HEAD_DIM
    shape = sds((size + INFO, LANES), BF16)
    before = [] if before is None else [before]
    return call(
        functools.partial(scan_kernel, count, first, len(before), stage),
        "scan_step",
        [place],
        [mine, came, *before],
        (shape, shape),
        estimate=cost(6 * size * LANES, 6 * size * LANES * 2),
        after=after,
    )


def prior_kernel(count, first, has_before, stage, wants_doc, place_ref, *refs):
    keep_ref, info_ref, other_ref, other_info_ref, came_ref = refs[:5]
    before_ref = refs[5] if has_before else None
    mine_ref, send_ref = refs[-3:-1] if wants_doc else refs[-2:]
    size = count * HEAD_DIM
    upper = ((place_ref[0] >> stage) & 1).astype(F32)
    even, gain_a, _, first_a, last_a, _ = row_terms(
        place_ref, info_ref[...], other_info_ref[size : size + INFO, :]
    )
    _, _, last_c = read_map(came_ref, size)
    factor, doc = upper, upper * last_c
    if has_before:
        gain_b, first_b, last_b = read_map(before_ref, size)
        empty = first_b == 0.0
        factor = upper * jnp.where(empty, 1.0, gain_b * (last_c == first_b).astype(F32))
        doc = jnp.where(empty, doc, last_b)
    else:
        factor = jnp.broadcast_to(factor, (1, LANES))
    gain_a = gain_a * (doc == first_a).astype(F32)
    for i in range(count):
        rows = slice(i * HEAD_DIM, (i + 1) * HEAD_DIM)
        lane = slice(first + i, first + i + 1)
        before_a = factor[:, lane] * came_ref[rows, :].astype(F32)
        if has_before:
            before_a = before_a + before_ref[rows, :].astype(F32)
        state_a = jnp.where(even, keep_ref[rows, :].astype(F32), other_ref[rows, :].astype(F32))
        before_b = gain_a[:, lane] * before_a + state_a
        mine_ref[rows, :] = jnp.where(even, before_a, before_b).astype(BF16)
        send_ref[rows, :] = jnp.where(even, before_b, before_a).astype(BF16)
    if wants_doc:
        refs[-1][...] = jnp.broadcast_to(jnp.where(even, doc, last_a), (8, LANES))


def prior_states(place, stage, keep, info, other, other_info, came, before, first, count, after, wants_doc):
    size = count * HEAD_DIM
    docs = (sds((8, LANES), F32),) if wants_doc else ()
    before = [] if before is None else [before]
    return call(
        functools.partial(prior_kernel, count, first, len(before), stage, wants_doc),
        "prior_states",
        [place],
        [keep, info, other, other_info, came, *before],
        (sds((size, LANES), BF16), sds((size, LANES), BF16), *docs),
        estimate=cost(4 * size * LANES, 6 * size * LANES * 2),
        after=after,
    )


def some_heads(ref, tokens, heads, first, count):
    x = ref[...].astype(F32)
    if count == heads:
        return x
    return x.reshape(tokens, heads, LANES)[:, first : first + count, :].reshape(tokens * count, LANES)


def inner_kernel(tokens, heads, first, count, cumul_ref, doc_ref, query_ref, key_ref, value_ref, inner_ref, qh_ref, qf, kf, vf, mask):
    cumul = cumul_ref[...]
    cumul_t = jnp.transpose(cumul)
    docs = doc_ref[...]
    column = doc_columns(docs, tokens)
    same = jnp.concatenate([column] * (tokens // LANES), axis=1) == doc_line(docs, tokens)
    mask[...] = jnp.where(lower_triangle(tokens) & same, 0.0, -1e9)
    qf[...] = some_heads(query_ref, tokens, heads, first, count)
    kf[...] = some_heads(key_ref, tokens, heads, first, count)
    vf[...] = some_heads(value_ref, tokens, heads, first, count)
    for n in range(count):
        h = first + n
        picked = pl.ds(n, tokens, stride=count)
        query = qf[picked, :].astype(BF16)
        keys = kf[picked, :].astype(BF16)
        values = vf[picked, :].astype(BF16)
        qh_ref[n * tokens : (n + 1) * tokens, :] = query
        for i in range(tokens // LANES):
            seen = (i + 1) * LANES
            rows = slice(i * LANES, seen)
            scores = lax.dot_general(
                query[rows, :], keys[0:seen, :], (((1,), (1,)), ((), ())), preferred_element_type=F32
            )
            gap = cumul[rows, h : h + 1] - cumul_t[h : h + 1, 0:seen]
            weights = (scores * jnp.exp(gap + mask[rows, 0:seen])).astype(BF16)
            inner_ref[n * tokens + i * LANES : n * tokens + seen, :] = jnp.dot(
                weights, values[0:seen, :], preferred_element_type=F32
            )


def inner_part(cumul, docs, query, key, value, tokens, heads, first, count, after):
    return call(
        functools.partial(inner_kernel, tokens, heads, first, count),
        "inner_part",
        [],
        [cumul, docs, query, key, value],
        (sds((count * tokens, LANES), F32), sds((count * tokens, LANES), BF16)),
        scratch=[pltpu.VMEM((tokens * count, LANES), F32)] * 3 + [pltpu.VMEM((tokens, tokens), F32)],
        mib=24,
        estimate=cost(
            4 * count * tokens * tokens * HEAD_DIM, tokens * heads * LANES * 12, count * tokens * tokens
        ),
        after=after,
    )


def mix_kernel(tokens, heads, parts, pieces, place_ref, doc_ref, prior_doc_ref, cumul_ref, *refs):
    refs = list(refs)
    take = lambda n: [refs.pop(0) for _ in range(n)]
    inner, qh, mine, other = take(parts), take(parts), take(pieces), take(pieces)
    mixed_ref, square_ref = refs
    half = heads // 2
    count = half // pieces
    even = place_ref[0] % 2 == 0
    is_open = (doc_columns(doc_ref[...], tokens) == prior_doc_ref[0:1, :]).astype(F32)
    gain = jnp.exp(cumul_ref[...]) * is_open
    squares = jnp.zeros((tokens, LANES), F32)
    for h in range(heads):
        piece, i = divmod(h % half, count)
        rows = slice(i * HEAD_DIM, (i + 1) * HEAD_DIM)
        near, far = mine[piece][rows, :], other[piece][rows, :]
        lower = h < half
        state = jnp.where(even, near if lower else far, far if lower else near)
        part, n = divmod(h, heads // parts)
        held = slice(n * tokens, (n + 1) * tokens)
        carried = jnp.dot(qh[part][held, :], state, preferred_element_type=F32)
        mixed = inner[part][held, :] + carried * gain[:, h : h + 1]
        squares = squares + mixed * mixed
        mixed_ref[pl.ds(h, tokens, stride=heads), :] = mixed
    square_ref[...] = lax.dot_general(
        jnp.ones((8, LANES), F32),
        squares,
        (((1,), (1,)), ((), ())),
        precision=HIGHEST,
        preferred_element_type=F32,
    )


def mix(place, docs, prior_doc, cumul, inner, qh, mine, other, tokens, heads, after):
    return call(
        functools.partial(mix_kernel, tokens, heads, len(inner), len(mine)),
        "mix",
        [place],
        [docs, prior_doc, cumul, *inner, *qh, *mine, *other],
        (sds((tokens * heads, LANES), F32), sds((8, tokens), F32)),
        mib=24,
        estimate=cost(2 * heads * tokens * HEAD_DIM**2, tokens * heads * LANES * 10),
        after=after,
    )


def finish_kernel(tokens, heads, sums, step, gain_ref, gate_ref, mixed_ref, *refs):
    squares, (out_ref, done, sems) = refs[:sums], refs[sums:]
    total = squares[0][0:1, :]
    for ref in squares[1:]:
        total = total + ref[0:1, :]
    scale = lax.rsqrt(total / (HEADS * HEAD_DIM) + 1e-06)
    rows = jnp.concatenate([scale[:, i * LANES : (i + 1) * LANES] for i in range(tokens // LANES)], axis=0)
    column = doc_columns(rows, tokens)
    copies = []
    for i in range(0, tokens, step):
        at = pl.ds(i * heads, step * heads)
        gate = jax.nn.sigmoid(gate_ref[at, :].astype(F32)).reshape(step, heads, LANES)
        mixed = mixed_ref[at, :].reshape(step, heads, LANES)
        inv = column[i : i + step, :][:, None, :]
        out = mixed * inv * gain_ref[...][None] * gate
        done[at, :] = out.reshape(step * heads, LANES).astype(BF16)
        copies.append(pltpu.make_async_copy(done.at[at, :], out_ref.at[at, :], sems.at[i // step]))
        copies[-1].start()
    for copy in copies:
        copy.wait()


def finish(gain, gate, mixed, squares, tokens, heads, after):
    step = 64
    return call(
        functools.partial(finish_kernel, tokens, heads, len(squares), step),
        "finish",
        [],
        [gain, gate, mixed, *squares],
        sds((tokens * heads, LANES), BF16),
        scratch=[pltpu.VMEM((tokens * heads, LANES), BF16), pltpu.SemaphoreType.DMA((tokens // step,))],
        estimate=cost(0, tokens * heads * LANES * 8, tokens * heads * LANES),
        after=after,
        out_hbm=True,
    )


def attend_kernel(tokens, heads, kv_here, least, is_first, is_last, unroll, place_ref, *refs):
    refs = list(refs)
    take = lambda n: [refs.pop(0) for _ in range(n)]
    per_group = heads // kv_here
    rows = tokens * per_group
    step = CHUNK // per_group
    if is_first:
        doc_ref, query_ref = take(2)
    else:
        wide_ref, state_ref = take(2)
    kv = take(len(least))
    if is_first:
        wide_ref = take(1)[0]
    out_ref = take(1)[0]
    if is_last:
        take(1)[0][...] = jnp.zeros((8, LANES), F32)
    bias = take(1)[0]
    if is_first:
        doc_rep = take(1)[0]
    if is_last:
        done, sems = take(2)

    lane = lax.broadcasted_iota(jnp.int32, (tokens, LANES), 1).astype(F32)
    end = 2 * kv_here * tokens
    block = place_ref[0]
    for j, ref in enumerate(kv):
        valid = (block >= jnp.where(block % 2 == 0, *least[j])).astype(F32)
        docs = doc_columns(ref[end : end + INFO, :].astype(F32) * valid, tokens)
        bias[j] = jnp.where(docs == lane, 0.0, -BIG).astype(BF16)
    if is_first:
        column = doc_columns(doc_ref[...], tokens)
        for h in range(per_group):
            doc_rep[pl.ds(h, tokens, stride=per_group), :] = (column == lane).astype(F32)
    ones = jnp.ones((STATE_ROWS - HEAD_DIM, tokens), BF16)

    def some_chunks(i, carry):
        chains = [(u, g) for u in range(unroll) for g in range(kv_here)]
        chunk = [i * unroll + u for u in range(unroll)]
        at = [pl.ds(pl.multiple_of(c * CHUNK, CHUNK), CHUNK) for c in chunk]
        picked = [pl.ds(pl.multiple_of(c * (step * heads), step * heads), step * heads) for c in chunk]
        scores, results = {}, {}

        def begin(u, g):
            if is_first:
                query = query_ref[picked[u], :].astype(F32).reshape(step, heads, LANES)
                query = query[:, g * per_group : (g + 1) * per_group, :].reshape(CHUNK, LANES)
                wide = jnp.concatenate([query.astype(BF16), doc_rep[at[u], :].astype(BF16)], axis=1)
                wide_ref[g, at[u], :] = wide
            else:
                wide = wide_ref[g, at[u], :]
            out = []
            for j, ref in enumerate(kv):
                keys = jnp.concatenate([ref[g * tokens : (g + 1) * tokens, :], bias[j]], axis=1)
                out.append(
                    lax.dot_general(keys, wide, (((1,), (1,)), ((), ())), preferred_element_type=F32)
                )
            if is_first:
                token = chunk[u] * step + lax.broadcasted_iota(jnp.int32, (tokens, CHUNK), 1) // per_group
                key_at = lax.broadcasted_iota(jnp.int32, (tokens, CHUNK), 0)
                out[0] = jnp.where(key_at <= token, out[0], -BIG)
            scores[u, g] = out

        def end_chain(u, g):
            here = scores.pop((u, g))
            top = jnp.max(here[0], axis=0, keepdims=True)
            for score in here[1:]:
                top = jnp.maximum(top, jnp.max(score, axis=0, keepdims=True))
            total = None
            if not is_first:
                before = state_ref[g, :, at[u]]
                top_before = before[STATE_ROWS - 1 : STATE_ROWS, :]
                top = jnp.maximum(top, top_before)
                total = before * jnp.exp2((top_before - top) * SCORE_TO_EXP2)
            for ref, score in zip(kv, here):
                weights = jnp.exp2((score - top) * SCORE_TO_EXP2).astype(BF16)
                first = (kv_here + g) * tokens
                parts = [ref[first + p : first + p + LANES, :] for p in range(0, tokens, LANES)]
                values = jnp.concatenate([jnp.concatenate(parts, axis=1), ones], axis=0)
                more = jnp.dot(values, weights, preferred_element_type=F32)
                total = more if total is None else total + more
            if is_last:
                results[u, g] = jnp.transpose(total[0:HEAD_DIM] / total[HEAD_DIM : HEAD_DIM + 1])
            else:
                out_ref[g, 0 : STATE_ROWS - 8, at[u]] = total[0 : STATE_ROWS - 8]
                out_ref[g, STATE_ROWS - 8 : STATE_ROWS, at[u]] = jnp.broadcast_to(top, (8, CHUNK))

        ahead = 2
        for n in range(len(chains) + ahead):
            if n < len(chains):
                begin(*chains[n])
            if n >= ahead:
                end_chain(*chains[n - ahead])
        if is_last:
            for u in range(unroll):
                result = [results[u, g] for g in range(kv_here)]
                if kv_here > 1:
                    result = [r.reshape(step, per_group, LANES) for r in result]
                    result = [jnp.concatenate(result, axis=1).reshape(step * heads, LANES)]
                done[picked[u], :] = result[0].astype(BF16)
                pltpu.make_async_copy(
                    done.at[picked[u], :], out_ref.at[picked[u], :], sems.at[chunk[u]]
                ).start()
        return carry

    lax.fori_loop(0, rows // (CHUNK * unroll), some_chunks, 0)
    if is_last:
        for c in range(rows // CHUNK):
            at = pl.ds(c * step * heads, step * heads)
            pltpu.make_async_copy(done.at[at, :], out_ref.at[at, :], sems.at[c]).wait()


def attend(place, first, state, kv, is_last, tokens, heads, kv_here, after):
    is_first = state is None
    least = tuple(pair for _, pair in kv)
    kv = [block for block, _ in kv]
    blocks = len(kv)
    rows = tokens * heads // kv_here
    unroll = min(4, rows // CHUNK)
    wide_shape = sds((kv_here, rows, 2 * LANES), BF16)
    state_shape = sds((kv_here, STATE_ROWS, rows), F32)
    out_shape = sds((tokens * heads, LANES), BF16) if is_last else state_shape
    scratch = [pltpu.VMEM((blocks, tokens, LANES), BF16)]
    if is_first:
        out_shape = (wide_shape, out_shape)
        scratch.append(pltpu.VMEM((rows, LANES), F32))
    if is_last:
        out_shape = (out_shape, sds((8, LANES), F32))
        scratch.append(pltpu.VMEM((tokens * heads, LANES), BF16))
        scratch.append(pltpu.SemaphoreType.DMA((rows // CHUNK,)))
    span = blocks * tokens
    return call(
        functools.partial(attend_kernel, tokens, heads, kv_here, least, is_first, is_last, unroll),
        "attend",
        [place],
        [*first, *([] if is_first else [state]), *kv],
        out_shape,
        scratch=scratch,
        mib=24,
        estimate=cost(
            4 * tokens * heads * span * 2 * LANES, 4 * tokens * heads * LANES * 4, tokens * heads * span
        ),
        after=after,
        out_hbm=is_last,
    )


def body(
    blocks,
    lin_query,
    lin_key,
    lin_value,
    lin_gate,
    log_decay,
    norm_gain,
    doc_ids,
    soft_query,
    soft_key,
    soft_value,
):
    tokens, heads, _ = lin_query.shape
    tensor = HEADS // heads
    kv_here = max(1, heads // GROUP)
    half = heads // 2
    pieces = 2 if half % 2 == 0 else 1
    parts = 2 if half % 8 == 0 else 1
    count = half // pieces
    longest = blocks * tokens * 5 // 8
    window = min(blocks - 1, (longest - 1 + tokens - 1) // tokens)
    flat = lambda x: x.reshape(-1, LANES)
    block = lax.axis_index("seq")
    place = block.astype(jnp.int32).reshape(1)
    start = (lax.axis_index("tp") * heads // GROUP).astype(jnp.int32).reshape(1)

    def send(x, pairs):
        return lax.ppermute(x, "seq", [(a, b % blocks) for a, b in pairs])

    everyone = range(blocks)
    swap = [(b, b ^ 1) for b in everyone]

    own_kv, docs, cumul, key, value = fetch(
        start,
        [
            doc_ids.reshape(tokens // LANES, LANES),
            jnp.transpose(log_decay),
            flat(soft_key),
            flat(soft_value),
            flat(lin_key),
            flat(lin_value),
        ],
        tokens,
        heads,
        kv_here,
    )

    odd_window = window % 2 == 1
    forward = [(b, b + 2) for b in everyone]
    ahead = send(own_kv, forward)
    beside = send(own_kv, [(b, b + (1 if b % 2 == 0 else window if odd_window else -1)) for b in everyone])
    beside = (beside, (window if odd_window else blocks, 1))

    info, held, sent = block_state(place, cumul, docs, key, value, tokens, heads, pieces)
    came = [send(x, swap) for x in sent]

    state = {}

    def first_attention(after):
        state["wide"], state["sum"] = attend(
            place, (docs, flat(soft_query)), None, [(own_kv, (0, 0))], False, tokens, heads, kv_here, after
        )
        return state["sum"]

    def more_attention(kv, is_last, after):
        state["sum"] = attend(
            place, (state["wide"],), state["sum"], kv, is_last, tokens, heads, kv_here, after
        )
        return state["sum"]

    inner, qh = [], []

    def inner_of(part, after):
        n = heads // parts
        got = inner_part(
            cumul, docs, flat(lin_query), key, value, tokens, heads, part * n, n, after
        )
        inner.append(got[0])
        qh.append(got[1])
        return got[0]

    beside_work = [first_attention]
    beside_work.append(lambda after: more_attention([beside] + lane_kv[:1], False, after))
    beside_work += [functools.partial(inner_of, part) for part in range(parts)]
    lane_kv, cross_kv = [], []

    done = info
    mine, far = [], []
    run, before = [None] * pieces, [None] * pieces
    stages = (blocks // 2).bit_length() - 1
    for stage in range(stages + 1):
        if beside_work:
            done = beside_work.pop(0)([done])
        if stage == stages:
            while beside_work:
                done = beside_work.pop(0)([done])
        for p in range(pieces):
            at = (p * count, count, [done])
            if stage == 0:
                args = (place, held[p], info, came[p], came[0], *at)
                if p == 0:
                    run[p], ahead = row_map(*args, ahead)
                    for back in range(1, window // 2 + 1):
                        lane_kv.append((ahead, (2 * back, 2 * back)))
                        cross_kv.append((send(ahead, swap), (2 * back, 2 * back + 1)))
                        ahead = send(ahead, forward)
                else:
                    run[p] = row_map(*args)
                done = run[p]
            elif stage < stages:
                run[p], before[p] = scan_step(place, stage, run[p], got[p], before[p], *at)
                done = run[p]
            else:
                wants_doc = p == pieces - 1
                done, sent, *docs_before = prior_states(
                    place, stage, held[p], info, came[p], came[0], got[p], before[p], *at, wants_doc
                )
                mine.append(done)
                far.append(send(sent, swap))
        if stage < stages:
            got = [send(x, [(b, b ^ (2 << stage)) for b in everyone]) for x in run]
    rest = [kv for pair in zip(cross_kv, lane_kv[1:] + [None]) for kv in pair if kv is not None]
    done = more_attention(rest[:1], False, [done])
    rest = rest[1:]
    mixed, squares = mix(
        place, docs, docs_before[0], cumul, inner, qh, mine, far, tokens, heads, [done]
    )
    sums = [squares]
    for other in range(1, tensor):
        sums.append(lax.ppermute(squares, "tp", [(t, t ^ other) for t in range(tensor)]))
    after = [squares]
    while rest:
        got = more_attention(rest[:2], len(rest) <= 2, after)
        rest, after = rest[2:], []
    soft_out, done = got
    lin_out = finish(norm_gain, flat(lin_gate), mixed, sums, tokens, heads, [done])
    shape = (tokens, heads, HEAD_DIM)
    return lin_out.reshape(shape), soft_out.reshape(shape)


def solution(mesh):
    in_specs = (
        P("seq", "tp", None),
        P("seq", "tp", None),
        P("seq", "tp", None),
        P("seq", "tp", None),
        P("seq", "tp"),
        P("tp", None),
        P("seq"),
        P("seq", "tp", None),
        P("seq", None, None),
        P("seq", None, None),
    )
    out_specs = (P("seq", "tp", None), P("seq", "tp", None))
    return jax.shard_map(
        functools.partial(body, mesh.shape["seq"]),
        mesh=mesh,
        in_specs=in_specs,
        out_specs=out_specs,
        check_vma=False,
    )
```

```python
import functools

import jax
import jax.numpy as jnp
import numpy as np
from jax import lax
from jax.experimental import pallas as pl
from jax.experimental.pallas import tpu as pltpu
from jax.sharding import PartitionSpec as P

HEADS = 64
HEAD_DIM = 128
KV_HEADS = 8
LANES = 128
GROUP = HEADS // KV_HEADS
F32 = jnp.float32
BF16 = jnp.bfloat16
BIG = float(2**20)
SCORE_TO_EXP2 = HEAD_DIM**-0.5 * float(np.log2(np.e))
INFO = 16
HIGHEST = lax.Precision.HIGHEST

VMEM = pl.BlockSpec(memory_space=pltpu.VMEM)
SMEM = pl.BlockSpec(memory_space=pltpu.SMEM)
HBM = pl.BlockSpec(memory_space=pltpu.HBM)
ANYWHERE = pl.BlockSpec(memory_space=pl.ANY)
STATE_ROWS = HEAD_DIM + 16
CHUNK = 256
GROUP_BLOCKS = 4


def sds(shape, dtype):
    return jax.ShapeDtypeStruct(shape, dtype)


def cost(flops, bytes_accessed, transcendentals=0):
    return pl.CostEstimate(
        flops=int(flops), bytes_accessed=int(bytes_accessed), transcendentals=int(transcendentals)
    )


def call(kernel, name, scalars, operands, out_shape, scratch=(), mib=16, estimate=None, after=(), hbm=0, out_hbm=False):
    begin = len(scalars) + len(operands)
    skip = len(after)
    operands = [
        pltpu.with_memory_space_constraint(x, pltpu.HBM) if i < hbm else x for i, x in enumerate(operands)
    ]
    outs = out_shape if isinstance(out_shape, tuple) else (out_shape,)
    out_specs = (VMEM,) * len(outs)
    outs = tuple(
        (pltpu.HBM if out_hbm and i == 0 else pltpu.VMEM)(x.shape, x.dtype) for i, x in enumerate(outs)
    )
    if out_hbm:
        out_specs = (HBM, *out_specs[1:])

    def run(*refs):
        kernel(*refs[:begin], *refs[begin + skip :])

    out = pl.pallas_call(
        run,
        out_shape=outs,
        in_specs=[SMEM] * len(scalars) + [HBM] * hbm + [VMEM] * (len(operands) - hbm) + [ANYWHERE] * skip,
        out_specs=out_specs,
        scratch_shapes=list(scratch),
        compiler_params=pltpu.CompilerParams(vmem_limit_bytes=mib * 1024 * 1024),
        cost_estimate=estimate,
        name=name,
    )(*scalars, *operands, *after)
    return out if isinstance(out_shape, tuple) else out[0]


def doc_columns(doc_rows, tokens):
    parts = []
    for i in range(tokens // LANES):
        row = jnp.broadcast_to(doc_rows[i : i + 1, :], (LANES, LANES))
        parts.append(jnp.transpose(row))
    return jnp.concatenate(parts, axis=0)


def doc_line(doc_rows, tokens):
    return jnp.concatenate([doc_rows[i : i + 1, :] for i in range(tokens // LANES)], axis=1)


def lower_triangle(tokens):
    rows = lax.broadcasted_iota(jnp.int32, (tokens, tokens), 0)
    cols = lax.broadcasted_iota(jnp.int32, (tokens, tokens), 1)
    return rows >= cols


def fetch_kernel(tokens, heads, kv_here, start_ref, *refs):
    refs = list(refs)
    take = lambda n: [refs.pop(0) for _ in range(n)]
    sources = take(6)
    kv_ref, doc_out, cumul_ref, key_out, value_out = take(5)
    held = take(4)
    sems, wide, ldp = refs
    docs_in, decays, soft_key, soft_value = held
    targets = [*held, key_out, value_out]
    copies = [
        pltpu.make_async_copy(source, target, sems.at[i])
        for i, (source, target) in enumerate(zip(sources, targets))
    ]
    for copy in copies:
        copy.start()

    copies[0].wait()
    docs = docs_in[...].astype(F32) + 1.0
    line = lax.broadcasted_iota(jnp.int32, (INFO, LANES), 0)
    info = jnp.zeros((INFO, LANES), F32)
    for i in range(tokens // LANES):
        info = jnp.where(line == i, docs[i : i + 1, :], info)
    doc_out[...] = info
    end = 2 * kv_here * tokens
    kv_ref[end : end + INFO, :] = info.astype(BF16)

    copies[1].wait()
    ldp[...] = jnp.zeros_like(ldp)
    ldp[0:heads, :] = decays[...]
    cumul_ref[...] = lax.dot_general(
        lower_triangle(tokens).astype(F32),
        ldp[...],
        (((1,), (1,)), ((), ())),
        precision=HIGHEST,
        preferred_element_type=F32,
    )

    start = start_ref[0]
    for which, ref in enumerate((soft_key, soft_value)):
        copies[2 + which].wait()
        wide[...] = ref[...].astype(F32)
        for g in range(kv_here):
            rows = wide[pl.ds(start + g, tokens, stride=KV_HEADS), :]
            at = (which * kv_here + g) * tokens
            if which:
                halves = [jnp.transpose(rows[i : i + LANES, :]) for i in range(0, tokens, LANES)]
                rows = jnp.concatenate(halves, axis=0)
            kv_ref[at : at + tokens, :] = rows.astype(BF16)
    copies[4].wait()
    copies[5].wait()


def fetch(start, operands, tokens, heads, kv_here):
    return call(
        functools.partial(fetch_kernel, tokens, heads, kv_here),
        "fetch",
        [start],
        operands,
        (
            sds((2 * kv_here * tokens + INFO, LANES), BF16),
            sds((INFO, LANES), F32),
            sds((tokens, LANES), F32),
            sds(operands[4].shape, BF16),
            sds(operands[5].shape, BF16),
        ),
        scratch=[pltpu.VMEM(x.shape, x.dtype) for x in operands[:4]]
        + [
            pltpu.SemaphoreType.DMA((len(operands),)),
            pltpu.VMEM((tokens * KV_HEADS, LANES), F32),
            pltpu.VMEM((LANES, tokens), F32),
        ],
        estimate=cost(0, 3 * tokens * heads * LANES * 2),
        hbm=len(operands),
    )


def quarter_rows(heads):
    return heads * HEAD_DIM // GROUP_BLOCKS


def state_kernel(tokens, heads, place_ref, *refs):
    refs = list(refs)
    take = lambda n: [refs.pop(0) for _ in range(n)]
    cumul_ref, doc_ref, key_ref, value_ref = take(4)
    out_refs = take(GROUP_BLOCKS)
    kf, vf, states = refs
    cumul, docs = cumul_ref[...], doc_ref[...]
    total = cumul[tokens - 1 : tokens, :]
    last_row = tokens // LANES - 1
    first_doc = docs[0:1, 0:1]
    last_doc = docs[last_row : last_row + 1, LANES - 1 : LANES]
    tail = (doc_columns(docs, tokens) == last_doc).astype(F32)
    scale = jnp.exp(total - cumul) * tail
    kf[...] = key_ref[...].astype(F32)
    vf[...] = value_ref[...].astype(F32)
    for h in range(heads):
        keys = (kf[pl.ds(h, tokens, stride=heads), :] * scale[:, h : h + 1]).astype(BF16)
        values = vf[pl.ds(h, tokens, stride=heads), :].astype(BF16)
        states[h * HEAD_DIM : (h + 1) * HEAD_DIM, :] = lax.dot_general(
            keys, values, (((0,), (0,)), ((), ())), preferred_element_type=F32
        )
    size = quarter_rows(heads)
    mine = place_ref[0] % GROUP_BLOCKS
    for j, ref in enumerate(out_refs):
        taker = mine ^ j
        ref[0:size, :] = states[pl.ds(pl.multiple_of(taker * size, size), size), :].astype(BF16)
        totals = jnp.zeros_like(total)
        for c in range(GROUP_BLOCKS):
            skip = c * heads // GROUP_BLOCKS
            moved = pltpu.roll(total, LANES - skip, 1) if skip else total
            totals = jnp.where(taker == c, moved, totals)
        ref[size : size + INFO, :] = info_rows((*in_parts(totals), first_doc, last_doc))


def block_state(place, cumul, docs, key, value, tokens, heads):
    return call(
        functools.partial(state_kernel, tokens, heads),
        "block_state",
        [place],
        [cumul, docs, key, value],
        (sds((quarter_rows(heads) + INFO, LANES), BF16),) * GROUP_BLOCKS,
        scratch=[
            pltpu.VMEM((tokens * heads, LANES), F32),
            pltpu.VMEM((tokens * heads, LANES), F32),
            pltpu.VMEM((heads * HEAD_DIM, LANES), F32),
        ],
        estimate=cost(2 * heads * tokens * HEAD_DIM**2, 5 * tokens * heads * LANES * 2),
    )


def in_parts(x):
    hi = x.astype(BF16).astype(F32)
    mid = (x - hi).astype(BF16).astype(F32)
    return hi, mid, x - hi - mid


def info_rows(parts):
    line = lax.broadcasted_iota(jnp.int32, (INFO, LANES), 0)
    info = jnp.zeros((INFO, LANES), F32)
    for i, part in enumerate(parts):
        info = jnp.where(line == i, part, info)
    return info.astype(BF16)


def read_map(ref, size):
    info = ref[size : size + INFO, :].astype(F32)
    return info[0:1] + info[1:2] + info[2:3], info[3:4], info[4:5]


def row_chunks(size):
    unit = min(HEAD_DIM, size)
    return [(slice(i * unit, (i + 1) * unit), slice(i, i + 1)) for i in range(size // unit)]


def in_block_order(place_ref, refs, blocks):
    mine = place_ref[0] % GROUP_BLOCKS
    for j, ref in enumerate(refs):
        blocks[mine ^ j] = ref[...]


def block_maps(blocks, size):
    maps = []
    for c in range(GROUP_BLOCKS):
        info = blocks[c, size : size + INFO, :].astype(F32)
        first, last = info[3:4], info[4:5]
        gain = jnp.exp(info[0:1] + info[1:2] + info[2:3]) * (first == last).astype(F32)
        maps.append((gain, first, last))
    return maps


def group_kernel(size, place_ref, *refs):
    sources = refs[:GROUP_BLOCKS]
    out_ref, blocks = refs[-2 - (len(refs) > GROUP_BLOCKS + 2)], refs[-1]
    if len(refs) > GROUP_BLOCKS + 2:
        refs[-2][...] = refs[GROUP_BLOCKS][...]
    in_block_order(place_ref, sources, blocks)
    maps = block_maps(blocks, size)
    gains = [None]
    for (gain, first, _), (_, _, last_before) in zip(maps[1:], maps[:-1]):
        gains.append(gain * (last_before == first).astype(F32))
    for rows, lane in row_chunks(size):
        total = blocks[0, rows, :].astype(F32)
        for c in range(1, GROUP_BLOCKS):
            total = gains[c][:, lane] * total + blocks[c, rows, :].astype(F32)
        out_ref[rows, :] = total.astype(BF16)
    gain = maps[0][0] * gains[1] * gains[2] * gains[3]
    out_ref[size : size + INFO, :] = info_rows((*in_parts(gain), maps[0][1], maps[-1][2]))


def group_map(place, quarters, size, after, relay):
    relay = [] if relay is None else [relay]
    out = call(
        functools.partial(group_kernel, size),
        "group_map",
        [place],
        [*quarters, *relay],
        (sds((size + INFO, LANES), BF16), *[sds(x.shape, BF16) for x in relay]),
        scratch=[pltpu.VMEM((GROUP_BLOCKS, size + INFO, LANES), BF16)],
        estimate=cost(8 * size * LANES, 10 * size * LANES * 2),
        after=after,
    )
    return out if relay else (out[0], None)


def scan_kernel(size, has_before, bit, place_ref, *refs):
    mine_ref, came_ref = refs[:2]
    before_ref = refs[2] if has_before else None
    run_ref, out_ref = refs[-2:]
    upper = (place_ref[0] >> bit) & 1 == 1
    gain_m, first_m, last_m = read_map(mine_ref, size)
    gain_c, first_c, last_c = read_map(came_ref, size)
    link = jnp.where(upper, (last_c == first_m).astype(F32), (last_m == first_c).astype(F32))
    gain = jnp.where(upper, gain_m, gain_c) * link
    for rows, lane in row_chunks(size):
        mine, came = mine_ref[rows, :].astype(F32), came_ref[rows, :].astype(F32)
        lower_sum, upper_sum = jnp.where(upper, came, mine), jnp.where(upper, mine, came)
        run_ref[rows, :] = (gain[:, lane] * lower_sum + upper_sum).astype(BF16)
    run_ref[size : size + INFO, :] = info_rows(
        (
            *in_parts(gain * jnp.where(upper, gain_c, gain_m)),
            jnp.where(upper, first_c, first_m),
            jnp.where(upper, last_m, last_c),
        )
    )
    if not has_before:
        out_ref[...] = jnp.where(upper, came_ref[...], jnp.zeros_like(came_ref))
        return
    gain_b, first_b, last_b = read_map(before_ref, size)
    empty = first_b == 0.0
    factor = jnp.where(empty, 1.0, gain_b * (last_c == first_b).astype(F32))
    for rows, lane in row_chunks(size):
        before = before_ref[rows, :].astype(F32)
        joined = factor[:, lane] * came_ref[rows, :].astype(F32) + before
        out_ref[rows, :] = jnp.where(upper, joined, before).astype(BF16)
    out_ref[size : size + INFO, :] = info_rows(
        (
            *in_parts(jnp.where(upper, factor * gain_c, gain_b)),
            jnp.where(upper, first_c, first_b),
            jnp.where(upper, jnp.where(empty, last_c, last_b), last_b),
        )
    )


def scan_step(place, bit, mine, came, before, size, after):
    shape = sds((size + INFO, LANES), BF16)
    before = [] if before is None else [before]
    return call(
        functools.partial(scan_kernel, size, len(before), bit),
        "scan_step",
        [place],
        [mine, came, *before],
        (shape, shape),
        estimate=cost(6 * size * LANES, 6 * size * LANES * 2),
        after=after,
    )


def prior_kernel(size, has_before, bit, place_ref, *refs):
    sources, came_ref = refs[:GROUP_BLOCKS], refs[GROUP_BLOCKS]
    before_ref = refs[GROUP_BLOCKS + 1] if has_before else None
    out_refs, doc_ref = refs[-GROUP_BLOCKS - 3 : -3], refs[-3]
    blocks, priors = refs[-2:]
    mine = place_ref[0] % GROUP_BLOCKS
    in_block_order(place_ref, sources, blocks)
    maps = block_maps(blocks, size)
    upper = ((place_ref[0] >> bit) & 1).astype(F32)
    _, _, last_c = read_map(came_ref, size)
    factor, doc = jnp.broadcast_to(upper, (1, LANES)), upper * last_c
    if has_before:
        gain_b, first_b, last_b = read_map(before_ref, size)
        empty = first_b == 0.0
        factor = upper * jnp.where(empty, 1.0, gain_b * (last_c == first_b).astype(F32))
        doc = jnp.where(empty, doc, last_b)
    docs = [doc] + [last for _, _, last in maps[:-1]]
    gains = [gain * (doc == first).astype(F32) for (gain, first, _), doc in zip(maps, docs)]
    for rows, lane in row_chunks(size):
        state = factor[:, lane] * came_ref[rows, :].astype(F32)
        if has_before:
            state = state + before_ref[rows, :].astype(F32)
        for c in range(GROUP_BLOCKS):
            priors[c, rows, :] = state.astype(BF16)
            if c < GROUP_BLOCKS - 1:
                state = gains[c][:, lane] * state + blocks[c, rows, :].astype(F32)
    for j, ref in enumerate(out_refs):
        ref[...] = priors[mine ^ j]
    own_doc = docs[0]
    for c in range(1, GROUP_BLOCKS):
        own_doc = jnp.where(mine == c, docs[c], own_doc)
    doc_ref[...] = jnp.broadcast_to(own_doc, (8, LANES))


def prior_states(place, bit, quarters, came, before, size, after):
    before = [] if before is None else [before]
    return call(
        functools.partial(prior_kernel, size, len(before), bit),
        "prior_states",
        [place],
        [*quarters, came, *before],
        (*[sds((size, LANES), BF16)] * GROUP_BLOCKS, sds((8, LANES), F32)),
        scratch=[
            pltpu.VMEM((GROUP_BLOCKS, size + INFO, LANES), BF16),
            pltpu.VMEM((GROUP_BLOCKS, size, LANES), BF16),
        ],
        estimate=cost(8 * size * LANES, 10 * size * LANES * 2),
        after=after,
    )


def some_heads(ref, tokens, heads, first, count):
    x = ref[...].astype(F32)
    if count == heads:
        return x
    return x.reshape(tokens, heads, LANES)[:, first : first + count, :].reshape(tokens * count, LANES)


def inner_kernel(tokens, heads, first, count, cumul_ref, doc_ref, query_ref, key_ref, value_ref, inner_ref, qh_ref, qf, kf, vf, mask):
    cumul = cumul_ref[...]
    cumul_t = jnp.transpose(cumul)
    docs = doc_ref[...]
    column = doc_columns(docs, tokens)
    same = jnp.concatenate([column] * (tokens // LANES), axis=1) == doc_line(docs, tokens)
    mask[...] = jnp.where(lower_triangle(tokens) & same, 0.0, -1e9)
    qf[...] = some_heads(query_ref, tokens, heads, first, count)
    kf[...] = some_heads(key_ref, tokens, heads, first, count)
    vf[...] = some_heads(value_ref, tokens, heads, first, count)
    for n in range(count):
        h = first + n
        picked = pl.ds(n, tokens, stride=count)
        query = qf[picked, :].astype(BF16)
        keys = kf[picked, :].astype(BF16)
        values = vf[picked, :].astype(BF16)
        qh_ref[n * tokens : (n + 1) * tokens, :] = query
        for i in range(tokens // LANES):
            seen = (i + 1) * LANES
            rows = slice(i * LANES, seen)
            scores = lax.dot_general(
                query[rows, :], keys[0:seen, :], (((1,), (1,)), ((), ())), preferred_element_type=F32
            )
            gap = cumul[rows, h : h + 1] - cumul_t[h : h + 1, 0:seen]
            weights = (scores * jnp.exp(gap + mask[rows, 0:seen])).astype(BF16)
            inner_ref[n * tokens + i * LANES : n * tokens + seen, :] = jnp.dot(
                weights, values[0:seen, :], preferred_element_type=F32
            )


def inner_part(cumul, docs, query, key, value, tokens, heads, first, count, after):
    return call(
        functools.partial(inner_kernel, tokens, heads, first, count),
        "inner_part",
        [],
        [cumul, docs, query, key, value],
        (sds((count * tokens, LANES), F32), sds((count * tokens, LANES), BF16)),
        scratch=[pltpu.VMEM((tokens * count, LANES), F32)] * 3 + [pltpu.VMEM((tokens, tokens), F32)],
        mib=24,
        estimate=cost(
            4 * count * tokens * tokens * HEAD_DIM, tokens * heads * LANES * 12, count * tokens * tokens
        ),
        after=after,
    )


def mix_kernel(tokens, heads, parts, place_ref, doc_ref, prior_doc_ref, cumul_ref, *refs):
    refs = list(refs)
    take = lambda n: [refs.pop(0) for _ in range(n)]
    inner, qh, quarters = take(parts), take(parts), take(GROUP_BLOCKS)
    mixed_ref, square_ref, states = refs
    size = quarter_rows(heads)
    mine = place_ref[0] % GROUP_BLOCKS
    for j, ref in enumerate(quarters):
        states[pl.ds(pl.multiple_of((mine ^ j) * size, size), size), :] = ref[...]
    is_open = (doc_columns(doc_ref[...], tokens) == prior_doc_ref[0:1, :]).astype(F32)
    gain = jnp.exp(cumul_ref[...]) * is_open
    squares = jnp.zeros((tokens, LANES), F32)
    for h in range(heads):
        part, n = divmod(h, heads // parts)
        held = slice(n * tokens, (n + 1) * tokens)
        state = states[h * HEAD_DIM : (h + 1) * HEAD_DIM, :]
        carried = jnp.dot(qh[part][held, :], state, preferred_element_type=F32)
        mixed = inner[part][held, :] + carried * gain[:, h : h + 1]
        squares = squares + mixed * mixed
        mixed_ref[pl.ds(h, tokens, stride=heads), :] = mixed
    square_ref[...] = lax.dot_general(
        jnp.ones((8, LANES), F32),
        squares,
        (((1,), (1,)), ((), ())),
        precision=HIGHEST,
        preferred_element_type=F32,
    )


def mix(place, docs, prior_doc, cumul, inner, qh, quarters, tokens, heads, after):
    return call(
        functools.partial(mix_kernel, tokens, heads, len(inner)),
        "mix",
        [place],
        [docs, prior_doc, cumul, *inner, *qh, *quarters],
        (sds((tokens * heads, LANES), F32), sds((8, tokens), F32)),
        scratch=[pltpu.VMEM((heads * HEAD_DIM, LANES), BF16)],
        mib=24,
        estimate=cost(2 * heads * tokens * HEAD_DIM**2, tokens * heads * LANES * 10),
        after=after,
    )


def finish_kernel(tokens, heads, sums, step, gain_ref, gate_ref, mixed_ref, *refs):
    squares, (out_ref, done, sems) = refs[:sums], refs[sums:]
    total = squares[0][0:1, :]
    for ref in squares[1:]:
        total = total + ref[0:1, :]
    scale = lax.rsqrt(total / (HEADS * HEAD_DIM) + 1e-06)
    rows = jnp.concatenate([scale[:, i * LANES : (i + 1) * LANES] for i in range(tokens // LANES)], axis=0)
    column = doc_columns(rows, tokens)
    copies = []
    for i in range(0, tokens, step):
        at = pl.ds(i * heads, step * heads)
        gate = jax.nn.sigmoid(gate_ref[at, :].astype(F32)).reshape(step, heads, LANES)
        mixed = mixed_ref[at, :].reshape(step, heads, LANES)
        inv = column[i : i + step, :][:, None, :]
        out = mixed * inv * gain_ref[...][None] * gate
        done[at, :] = out.reshape(step * heads, LANES).astype(BF16)
        copies.append(pltpu.make_async_copy(done.at[at, :], out_ref.at[at, :], sems.at[i // step]))
        copies[-1].start()
    for copy in copies:
        copy.wait()


def finish(gain, gate, mixed, squares, tokens, heads, after):
    step = 64
    return call(
        functools.partial(finish_kernel, tokens, heads, len(squares), step),
        "finish",
        [],
        [gain, gate, mixed, *squares],
        sds((tokens * heads, LANES), BF16),
        scratch=[pltpu.VMEM((tokens * heads, LANES), BF16), pltpu.SemaphoreType.DMA((tokens // step,))],
        estimate=cost(0, tokens * heads * LANES * 8, tokens * heads * LANES),
        after=after,
        out_hbm=True,
    )


def attend_kernel(tokens, heads, kv_here, least, is_first, is_last, unroll, place_ref, *refs):
    refs = list(refs)
    take = lambda n: [refs.pop(0) for _ in range(n)]
    per_group = heads // kv_here
    rows = tokens * per_group
    step = CHUNK // per_group
    if is_first:
        doc_ref, query_ref = take(2)
    else:
        wide_ref, state_ref = take(2)
    kv = take(len(least))
    if is_first:
        wide_ref = take(1)[0]
    out_ref = take(1)[0]
    if is_last:
        take(1)[0][...] = jnp.zeros((8, LANES), F32)
    bias = take(1)[0]
    if is_first:
        doc_rep = take(1)[0]
    if is_last:
        done, sems = take(2)

    lane = lax.broadcasted_iota(jnp.int32, (tokens, LANES), 1).astype(F32)
    end = 2 * kv_here * tokens
    block = place_ref[0]
    for j, ref in enumerate(kv):
        valid = (block >= jnp.where(block % 2 == 0, *least[j])).astype(F32)
        docs = doc_columns(ref[end : end + INFO, :].astype(F32) * valid, tokens)
        bias[j] = jnp.where(docs == lane, 0.0, -BIG).astype(BF16)
    if is_first:
        column = doc_columns(doc_ref[...], tokens)
        for h in range(per_group):
            doc_rep[pl.ds(h, tokens, stride=per_group), :] = (column == lane).astype(F32)
    ones = jnp.ones((STATE_ROWS - HEAD_DIM, tokens), BF16)

    def some_chunks(i, carry):
        chains = [(u, g) for u in range(unroll) for g in range(kv_here)]
        chunk = [i * unroll + u for u in range(unroll)]
        at = [pl.ds(pl.multiple_of(c * CHUNK, CHUNK), CHUNK) for c in chunk]
        picked = [pl.ds(pl.multiple_of(c * (step * heads), step * heads), step * heads) for c in chunk]
        scores, results = {}, {}

        def begin(u, g):
            if is_first:
                query = query_ref[picked[u], :].astype(F32).reshape(step, heads, LANES)
                query = query[:, g * per_group : (g + 1) * per_group, :].reshape(CHUNK, LANES)
                wide = jnp.concatenate([query.astype(BF16), doc_rep[at[u], :].astype(BF16)], axis=1)
                wide_ref[g, at[u], :] = wide
            else:
                wide = wide_ref[g, at[u], :]
            out = []
            for j, ref in enumerate(kv):
                keys = jnp.concatenate([ref[g * tokens : (g + 1) * tokens, :], bias[j]], axis=1)
                out.append(
                    lax.dot_general(keys, wide, (((1,), (1,)), ((), ())), preferred_element_type=F32)
                )
            if is_first:
                token = chunk[u] * step + lax.broadcasted_iota(jnp.int32, (tokens, CHUNK), 1) // per_group
                key_at = lax.broadcasted_iota(jnp.int32, (tokens, CHUNK), 0)
                out[0] = jnp.where(key_at <= token, out[0], -BIG)
            scores[u, g] = out

        def end_chain(u, g):
            here = scores.pop((u, g))
            top = jnp.max(here[0], axis=0, keepdims=True)
            for score in here[1:]:
                top = jnp.maximum(top, jnp.max(score, axis=0, keepdims=True))
            total = None
            if not is_first:
                before = state_ref[g, :, at[u]]
                top_before = before[STATE_ROWS - 1 : STATE_ROWS, :]
                top = jnp.maximum(top, top_before)
                total = before * jnp.exp2((top_before - top) * SCORE_TO_EXP2)
            for ref, score in zip(kv, here):
                weights = jnp.exp2((score - top) * SCORE_TO_EXP2).astype(BF16)
                first = (kv_here + g) * tokens
                parts = [ref[first + p : first + p + LANES, :] for p in range(0, tokens, LANES)]
                values = jnp.concatenate([jnp.concatenate(parts, axis=1), ones], axis=0)
                more = jnp.dot(values, weights, preferred_element_type=F32)
                total = more if total is None else total + more
            if is_last:
                results[u, g] = jnp.transpose(total[0:HEAD_DIM] / total[HEAD_DIM : HEAD_DIM + 1])
            else:
                out_ref[g, 0 : STATE_ROWS - 8, at[u]] = total[0 : STATE_ROWS - 8]
                out_ref[g, STATE_ROWS - 8 : STATE_ROWS, at[u]] = jnp.broadcast_to(top, (8, CHUNK))

        ahead = 2
        for n in range(len(chains) + ahead):
            if n < len(chains):
                begin(*chains[n])
            if n >= ahead:
                end_chain(*chains[n - ahead])
        if is_last:
            for u in range(unroll):
                result = [results[u, g] for g in range(kv_here)]
                if kv_here > 1:
                    result = [r.reshape(step, per_group, LANES) for r in result]
                    result = [jnp.concatenate(result, axis=1).reshape(step * heads, LANES)]
                done[picked[u], :] = result[0].astype(BF16)
                pltpu.make_async_copy(
                    done.at[picked[u], :], out_ref.at[picked[u], :], sems.at[chunk[u]]
                ).start()
        return carry

    lax.fori_loop(0, rows // (CHUNK * unroll), some_chunks, 0)
    if is_last:
        for c in range(rows // CHUNK):
            at = pl.ds(c * step * heads, step * heads)
            pltpu.make_async_copy(done.at[at, :], out_ref.at[at, :], sems.at[c]).wait()


def attend(place, first, state, kv, is_last, tokens, heads, kv_here, after):
    is_first = state is None
    least = tuple(pair for _, pair in kv)
    kv = [block for block, _ in kv]
    blocks = len(kv)
    rows = tokens * heads // kv_here
    unroll = min(4, rows // CHUNK)
    wide_shape = sds((kv_here, rows, 2 * LANES), BF16)
    state_shape = sds((kv_here, STATE_ROWS, rows), F32)
    out_shape = sds((tokens * heads, LANES), BF16) if is_last else state_shape
    scratch = [pltpu.VMEM((blocks, tokens, LANES), BF16)]
    if is_first:
        out_shape = (wide_shape, out_shape)
        scratch.append(pltpu.VMEM((rows, LANES), F32))
    if is_last:
        out_shape = (out_shape, sds((8, LANES), F32))
        scratch.append(pltpu.VMEM((tokens * heads, LANES), BF16))
        scratch.append(pltpu.SemaphoreType.DMA((rows // CHUNK,)))
    span = blocks * tokens
    return call(
        functools.partial(attend_kernel, tokens, heads, kv_here, least, is_first, is_last, unroll),
        "attend",
        [place],
        [*first, *([] if is_first else [state]), *kv],
        out_shape,
        scratch=scratch,
        mib=24,
        estimate=cost(
            4 * tokens * heads * span * 2 * LANES, 4 * tokens * heads * LANES * 4, tokens * heads * span
        ),
        after=after,
        out_hbm=is_last,
    )


def body(
    blocks,
    lin_query,
    lin_key,
    lin_value,
    lin_gate,
    log_decay,
    norm_gain,
    doc_ids,
    soft_query,
    soft_key,
    soft_value,
):
    tokens, heads, _ = lin_query.shape
    tensor = HEADS // heads
    kv_here = max(1, heads // GROUP)
    parts = 2 if heads % 16 == 0 else 1
    longest = blocks * tokens * 5 // 8
    window = min(blocks - 1, (longest - 1 + tokens - 1) // tokens)
    flat = lambda x: x.reshape(-1, LANES)
    block = lax.axis_index("seq")
    place = block.astype(jnp.int32).reshape(1)
    start = (lax.axis_index("tp") * heads // GROUP).astype(jnp.int32).reshape(1)

    def send(x, pairs):
        return lax.ppermute(x, "seq", [(a, b % blocks) for a, b in pairs])

    everyone = range(blocks)
    swap = [(b, b ^ 1) for b in everyone]

    own_kv, docs, cumul, key, value = fetch(
        start,
        [
            doc_ids.reshape(tokens // LANES, LANES),
            jnp.transpose(log_decay),
            flat(soft_key),
            flat(soft_value),
            flat(lin_key),
            flat(lin_value),
        ],
        tokens,
        heads,
        kv_here,
    )

    odd_window = window % 2 == 1
    forward = [(b, b + 2) for b in everyone]
    ahead = send(own_kv, forward)
    beside = send(own_kv, [(b, b + (1 if b % 2 == 0 else window if odd_window else -1)) for b in everyone])
    beside = (beside, (window if odd_window else blocks, 1))

    size = quarter_rows(heads)
    others = range(1, GROUP_BLOCKS)
    sent = block_state(place, cumul, docs, key, value, tokens, heads)
    quarters = [sent[0]] + [send(sent[j], [(b, b ^ j) for b in everyone]) for j in others]

    state = {}

    def first_attention(after):
        state["wide"], state["sum"] = attend(
            place, (docs, flat(soft_query)), None, [(own_kv, (0, 0))], False, tokens, heads, kv_here, after
        )
        return state["sum"]

    def more_attention(kv, is_last, after):
        state["sum"] = attend(
            place, (state["wide"],), state["sum"], kv, is_last, tokens, heads, kv_here, after
        )
        return state["sum"]

    inner, qh = [], []

    def inner_of(part, after):
        n = heads // parts
        got = inner_part(
            cumul, docs, flat(lin_query), key, value, tokens, heads, part * n, n, after
        )
        inner.append(got[0])
        qh.append(got[1])
        return got[0]

    done = first_attention([sent[0]])
    run, ahead = group_map(place, quarters, size, [done], ahead)
    lane_kv, cross_kv = [], []
    for back in range(1, window // 2 + 1):
        lane_kv.append((ahead, (2 * back, 2 * back)))
        cross_kv.append((send(ahead, swap), (2 * back, 2 * back + 1)))
        ahead = send(ahead, forward)
    stages = (blocks // GROUP_BLOCKS).bit_length() - 1
    before, done = None, run
    for stage in range(stages):
        came = send(run, [(b, b ^ (GROUP_BLOCKS << stage)) for b in everyone])
        if stage == stages - 1:
            for part in range(parts):
                done = inner_of(part, [done])
        else:
            run, before = scan_step(place, stage + 2, run, came, before, size, [done])
            done = run
    *priors, prior_doc = prior_states(place, stages + 1, quarters, came, before, size, [done])
    priors = [priors[0]] + [send(priors[j], [(b, b ^ j) for b in everyone]) for j in others]
    done = more_attention([beside] + lane_kv[:1], False, [prior_doc])
    rest = [kv for pair in zip(cross_kv, lane_kv[1:] + [None]) for kv in pair if kv is not None]
    mixed, squares = mix(place, docs, prior_doc, cumul, inner, qh, priors, tokens, heads, [done])
    sums = [squares]
    for other in range(1, tensor):
        sums.append(lax.ppermute(squares, "tp", [(t, t ^ other) for t in range(tensor)]))
    after = [squares]
    while rest:
        got = more_attention(rest[:2], len(rest) <= 2, after)
        rest, after = rest[2:], []
    soft_out, done = got
    lin_out = finish(norm_gain, flat(lin_gate), mixed, sums, tokens, heads, [done])
    shape = (tokens, heads, HEAD_DIM)
    return lin_out.reshape(shape), soft_out.reshape(shape)


def solution(mesh):
    in_specs = (
        P("seq", "tp", None),
        P("seq", "tp", None),
        P("seq", "tp", None),
        P("seq", "tp", None),
        P("seq", "tp"),
        P("tp", None),
        P("seq"),
        P("seq", "tp", None),
        P("seq", None, None),
        P("seq", None, None),
    )
    out_specs = (P("seq", "tp", None), P("seq", "tp", None))
    return jax.shard_map(
        functools.partial(body, mesh.shape["seq"]),
        mesh=mesh,
        in_specs=in_specs,
        out_specs=out_specs,
        check_vma=False,
    )
```

```python
import functools

import jax
import jax.numpy as jnp
import numpy as np
from jax import lax
from jax.experimental import pallas as pl
from jax.experimental.pallas import tpu as pltpu
from jax.sharding import PartitionSpec as P

HEADS = 64
HEAD_DIM = 128
KV_HEADS = 8
LANES = 128
GROUP = HEADS // KV_HEADS
F32 = jnp.float32
BF16 = jnp.bfloat16
BIG = float(2**20)
SCORE_TO_EXP2 = HEAD_DIM**-0.5 * float(np.log2(np.e))
INFO = 16
HIGHEST = lax.Precision.HIGHEST

VMEM = pl.BlockSpec(memory_space=pltpu.VMEM)
SMEM = pl.BlockSpec(memory_space=pltpu.SMEM)
HBM = pl.BlockSpec(memory_space=pltpu.HBM)
ANYWHERE = pl.BlockSpec(memory_space=pl.ANY)
STATE_ROWS = HEAD_DIM + 16
CHUNK = 256
GROUP_BLOCKS = 4


def sds(shape, dtype):
    return jax.ShapeDtypeStruct(shape, dtype)


def cost(flops, bytes_accessed, transcendentals=0):
    return pl.CostEstimate(
        flops=int(flops), bytes_accessed=int(bytes_accessed), transcendentals=int(transcendentals)
    )


def call(kernel, name, scalars, operands, out_shape, scratch=(), mib=16, estimate=None, after=(), hbm=0, out_hbm=False):
    begin = len(scalars) + len(operands)
    skip = len(after)
    operands = [
        pltpu.with_memory_space_constraint(x, pltpu.HBM) if i < hbm else x for i, x in enumerate(operands)
    ]
    outs = out_shape if isinstance(out_shape, tuple) else (out_shape,)
    out_specs = (VMEM,) * len(outs)
    outs = tuple(
        (pltpu.HBM if out_hbm and i == 0 else pltpu.VMEM)(x.shape, x.dtype) for i, x in enumerate(outs)
    )
    if out_hbm:
        out_specs = (HBM, *out_specs[1:])

    def run(*refs):
        kernel(*refs[:begin], *refs[begin + skip :])

    out = pl.pallas_call(
        run,
        out_shape=outs,
        in_specs=[SMEM] * len(scalars) + [HBM] * hbm + [VMEM] * (len(operands) - hbm) + [ANYWHERE] * skip,
        out_specs=out_specs,
        scratch_shapes=list(scratch),
        compiler_params=pltpu.CompilerParams(vmem_limit_bytes=mib * 1024 * 1024),
        cost_estimate=estimate,
        name=name,
    )(*scalars, *operands, *after)
    return out if isinstance(out_shape, tuple) else out[0]


def doc_columns(doc_rows, tokens):
    parts = []
    for i in range(tokens // LANES):
        row = jnp.broadcast_to(doc_rows[i : i + 1, :], (LANES, LANES))
        parts.append(jnp.transpose(row))
    return jnp.concatenate(parts, axis=0)


def doc_line(doc_rows, tokens):
    return jnp.concatenate([doc_rows[i : i + 1, :] for i in range(tokens // LANES)], axis=1)


def lower_triangle(tokens):
    rows = lax.broadcasted_iota(jnp.int32, (tokens, tokens), 0)
    cols = lax.broadcasted_iota(jnp.int32, (tokens, tokens), 1)
    return rows >= cols


def fetch_kernel(tokens, heads, kv_here, start_ref, *refs):
    refs = list(refs)
    take = lambda n: [refs.pop(0) for _ in range(n)]
    sources = take(6)
    kv_ref, doc_out, cumul_ref, key_out, value_out = take(5)
    held = take(4)
    sems, wide, ldp = refs
    docs_in, decays, soft_key, soft_value = held
    targets = [*held, key_out, value_out]
    copies = [
        pltpu.make_async_copy(source, target, sems.at[i])
        for i, (source, target) in enumerate(zip(sources, targets))
    ]
    for copy in copies:
        copy.start()

    copies[0].wait()
    docs = docs_in[...].astype(F32) + 1.0
    line = lax.broadcasted_iota(jnp.int32, (INFO, LANES), 0)
    info = jnp.zeros((INFO, LANES), F32)
    for i in range(tokens // LANES):
        info = jnp.where(line == i, docs[i : i + 1, :], info)
    doc_out[...] = info
    end = 2 * kv_here * tokens
    kv_ref[end : end + INFO, :] = info.astype(BF16)

    copies[1].wait()
    ldp[...] = jnp.zeros_like(ldp)
    ldp[0:heads, :] = decays[...]
    cumul_ref[...] = lax.dot_general(
        lower_triangle(tokens).astype(F32),
        ldp[...],
        (((1,), (1,)), ((), ())),
        precision=HIGHEST,
        preferred_element_type=F32,
    )

    start = start_ref[0]
    for which, ref in enumerate((soft_key, soft_value)):
        copies[2 + which].wait()
        wide[...] = ref[...].astype(F32)
        for g in range(kv_here):
            rows = wide[pl.ds(start + g, tokens, stride=KV_HEADS), :]
            at = (which * kv_here + g) * tokens
            if which:
                halves = [jnp.transpose(rows[i : i + LANES, :]) for i in range(0, tokens, LANES)]
                rows = jnp.concatenate(halves, axis=0)
            kv_ref[at : at + tokens, :] = rows.astype(BF16)
    copies[4].wait()
    copies[5].wait()


def fetch(start, operands, tokens, heads, kv_here):
    return call(
        functools.partial(fetch_kernel, tokens, heads, kv_here),
        "fetch",
        [start],
        operands,
        (
            sds((2 * kv_here * tokens + INFO, LANES), BF16),
            sds((INFO, LANES), F32),
            sds((tokens, LANES), F32),
            sds(operands[4].shape, BF16),
            sds(operands[5].shape, BF16),
        ),
        scratch=[pltpu.VMEM(x.shape, x.dtype) for x in operands[:4]]
        + [
            pltpu.SemaphoreType.DMA((len(operands),)),
            pltpu.VMEM((tokens * KV_HEADS, LANES), F32),
            pltpu.VMEM((LANES, tokens), F32),
        ],
        estimate=cost(0, 3 * tokens * heads * LANES * 2),
        hbm=len(operands),
    )


def quarter_rows(heads):
    return heads * HEAD_DIM // GROUP_BLOCKS


def state_kernel(tokens, heads, place_ref, *refs):
    refs = list(refs)
    take = lambda n: [refs.pop(0) for _ in range(n)]
    cumul_ref, doc_ref, key_ref, value_ref = take(4)
    out_refs = take(GROUP_BLOCKS)
    kf, vf, states = refs
    cumul, docs = cumul_ref[...], doc_ref[...]
    total = cumul[tokens - 1 : tokens, :]
    last_row = tokens // LANES - 1
    first_doc = docs[0:1, 0:1]
    last_doc = docs[last_row : last_row + 1, LANES - 1 : LANES]
    tail = (doc_columns(docs, tokens) == last_doc).astype(F32)
    scale = jnp.exp(total - cumul) * tail
    kf[...] = key_ref[...].astype(F32)
    vf[...] = value_ref[...].astype(F32)
    for h in range(heads):
        keys = (kf[pl.ds(h, tokens, stride=heads), :] * scale[:, h : h + 1]).astype(BF16)
        values = vf[pl.ds(h, tokens, stride=heads), :].astype(BF16)
        states[h * HEAD_DIM : (h + 1) * HEAD_DIM, :] = lax.dot_general(
            keys, values, (((0,), (0,)), ((), ())), preferred_element_type=F32
        )
    size = quarter_rows(heads)
    mine = place_ref[0] % GROUP_BLOCKS
    for j, ref in enumerate(out_refs):
        taker = mine ^ j
        ref[0:size, :] = states[pl.ds(pl.multiple_of(taker * size, size), size), :].astype(BF16)
        totals = jnp.zeros_like(total)
        for c in range(GROUP_BLOCKS):
            skip = c * heads // GROUP_BLOCKS
            moved = pltpu.roll(total, LANES - skip, 1) if skip else total
            totals = jnp.where(taker == c, moved, totals)
        ref[size : size + INFO, :] = info_rows((*in_parts(totals), first_doc, last_doc))


def block_state(place, cumul, docs, key, value, tokens, heads):
    return call(
        functools.partial(state_kernel, tokens, heads),
        "block_state",
        [place],
        [cumul, docs, key, value],
        (sds((quarter_rows(heads) + INFO, LANES), BF16),) * GROUP_BLOCKS,
        scratch=[
            pltpu.VMEM((tokens * heads, LANES), F32),
            pltpu.VMEM((tokens * heads, LANES), F32),
            pltpu.VMEM((heads * HEAD_DIM, LANES), F32),
        ],
        estimate=cost(2 * heads * tokens * HEAD_DIM**2, 5 * tokens * heads * LANES * 2),
    )


def in_parts(x):
    hi = x.astype(BF16).astype(F32)
    mid = (x - hi).astype(BF16).astype(F32)
    return hi, mid, x - hi - mid


def info_rows(parts):
    line = lax.broadcasted_iota(jnp.int32, (INFO, LANES), 0)
    info = jnp.zeros((INFO, LANES), F32)
    for i, part in enumerate(parts):
        info = jnp.where(line == i, part, info)
    return info.astype(BF16)


def read_map(ref, size):
    info = ref[size : size + INFO, :].astype(F32)
    return info[0:1] + info[1:2] + info[2:3], info[3:4], info[4:5]


def row_chunks(size):
    unit = min(HEAD_DIM, size)
    return [(slice(i * unit, (i + 1) * unit), slice(i, i + 1)) for i in range(size // unit)]


def in_block_order(place_ref, refs, blocks):
    mine = place_ref[0] % GROUP_BLOCKS
    for j, ref in enumerate(refs):
        blocks[mine ^ j] = ref[...]


def block_maps(blocks, size):
    maps = []
    for c in range(GROUP_BLOCKS):
        info = blocks[c, size : size + INFO, :].astype(F32)
        first, last = info[3:4], info[4:5]
        gain = jnp.exp(info[0:1] + info[1:2] + info[2:3]) * (first == last).astype(F32)
        maps.append((gain, first, last))
    return maps


def group_kernel(size, place_ref, *refs):
    sources = refs[:GROUP_BLOCKS]
    out_ref, blocks = refs[-2 - (len(refs) > GROUP_BLOCKS + 2)], refs[-1]
    if len(refs) > GROUP_BLOCKS + 2:
        refs[-2][...] = refs[GROUP_BLOCKS][...]
    in_block_order(place_ref, sources, blocks)
    maps = block_maps(blocks, size)
    gains = [None]
    for (gain, first, _), (_, _, last_before) in zip(maps[1:], maps[:-1]):
        gains.append(gain * (last_before == first).astype(F32))
    for rows, lane in row_chunks(size):
        total = blocks[0, rows, :].astype(F32)
        for c in range(1, GROUP_BLOCKS):
            total = gains[c][:, lane] * total + blocks[c, rows, :].astype(F32)
        out_ref[rows, :] = total.astype(BF16)
    gain = maps[0][0] * gains[1] * gains[2] * gains[3]
    out_ref[size : size + INFO, :] = info_rows((*in_parts(gain), maps[0][1], maps[-1][2]))


def group_map(place, quarters, size, after, relay):
    relay = [] if relay is None else [relay]
    out = call(
        functools.partial(group_kernel, size),
        "group_map",
        [place],
        [*quarters, *relay],
        (sds((size + INFO, LANES), BF16), *[sds(x.shape, BF16) for x in relay]),
        scratch=[pltpu.VMEM((GROUP_BLOCKS, size + INFO, LANES), BF16)],
        estimate=cost(8 * size * LANES, 10 * size * LANES * 2),
        after=after,
    )
    return out if relay else (out[0], None)


def scan_kernel(size, has_before, bit, place_ref, *refs):
    mine_ref, came_ref = refs[:2]
    before_ref = refs[2] if has_before else None
    run_ref, out_ref = refs[-2:]
    upper = (place_ref[0] >> bit) & 1 == 1
    gain_m, first_m, last_m = read_map(mine_ref, size)
    gain_c, first_c, last_c = read_map(came_ref, size)
    link = jnp.where(upper, (last_c == first_m).astype(F32), (last_m == first_c).astype(F32))
    gain = jnp.where(upper, gain_m, gain_c) * link
    for rows, lane in row_chunks(size):
        mine, came = mine_ref[rows, :].astype(F32), came_ref[rows, :].astype(F32)
        lower_sum, upper_sum = jnp.where(upper, came, mine), jnp.where(upper, mine, came)
        run_ref[rows, :] = (gain[:, lane] * lower_sum + upper_sum).astype(BF16)
    run_ref[size : size + INFO, :] = info_rows(
        (
            *in_parts(gain * jnp.where(upper, gain_c, gain_m)),
            jnp.where(upper, first_c, first_m),
            jnp.where(upper, last_m, last_c),
        )
    )
    if not has_before:
        out_ref[...] = jnp.where(upper, came_ref[...], jnp.zeros_like(came_ref))
        return
    gain_b, first_b, last_b = read_map(before_ref, size)
    empty = first_b == 0.0
    factor = jnp.where(empty, 1.0, gain_b * (last_c == first_b).astype(F32))
    for rows, lane in row_chunks(size):
        before = before_ref[rows, :].astype(F32)
        joined = factor[:, lane] * came_ref[rows, :].astype(F32) + before
        out_ref[rows, :] = jnp.where(upper, joined, before).astype(BF16)
    out_ref[size : size + INFO, :] = info_rows(
        (
            *in_parts(jnp.where(upper, factor * gain_c, gain_b)),
            jnp.where(upper, first_c, first_b),
            jnp.where(upper, jnp.where(empty, last_c, last_b), last_b),
        )
    )


def scan_step(place, bit, mine, came, before, size, after):
    shape = sds((size + INFO, LANES), BF16)
    before = [] if before is None else [before]
    return call(
        functools.partial(scan_kernel, size, len(before), bit),
        "scan_step",
        [place],
        [mine, came, *before],
        (shape, shape),
        estimate=cost(6 * size * LANES, 6 * size * LANES * 2),
        after=after,
    )


def prior_kernel(size, has_before, relays, bit, place_ref, *refs):
    sources, came_ref = refs[:GROUP_BLOCKS], refs[GROUP_BLOCKS]
    before_ref = refs[GROUP_BLOCKS + 1] if has_before else None
    if relays:
        refs[-3][...] = refs[GROUP_BLOCKS + 1 + has_before][...]
    blocks, priors = refs[-2:]
    *out_refs, doc_ref = refs[-GROUP_BLOCKS - 3 - relays : -2 - relays]
    mine = place_ref[0] % GROUP_BLOCKS
    in_block_order(place_ref, sources, blocks)
    maps = block_maps(blocks, size)
    upper = ((place_ref[0] >> bit) & 1).astype(F32)
    _, _, last_c = read_map(came_ref, size)
    factor, doc = jnp.broadcast_to(upper, (1, LANES)), upper * last_c
    if has_before:
        gain_b, first_b, last_b = read_map(before_ref, size)
        empty = first_b == 0.0
        factor = upper * jnp.where(empty, 1.0, gain_b * (last_c == first_b).astype(F32))
        doc = jnp.where(empty, doc, last_b)
    docs = [doc] + [last for _, _, last in maps[:-1]]
    gains = [gain * (doc == first).astype(F32) for (gain, first, _), doc in zip(maps, docs)]
    for rows, lane in row_chunks(size):
        state = factor[:, lane] * came_ref[rows, :].astype(F32)
        if has_before:
            state = state + before_ref[rows, :].astype(F32)
        for c in range(GROUP_BLOCKS):
            priors[c, rows, :] = state.astype(BF16)
            if c < GROUP_BLOCKS - 1:
                state = gains[c][:, lane] * state + blocks[c, rows, :].astype(F32)
    for j, ref in enumerate(out_refs):
        ref[...] = priors[mine ^ j]
    own_doc = docs[0]
    for c in range(1, GROUP_BLOCKS):
        own_doc = jnp.where(mine == c, docs[c], own_doc)
    doc_ref[...] = jnp.broadcast_to(own_doc, (8, LANES))


def prior_states(place, bit, quarters, came, before, size, after, relay):
    before = [] if before is None else [before]
    relay = [] if relay is None else [relay]
    return call(
        functools.partial(prior_kernel, size, len(before), len(relay), bit),
        "prior_states",
        [place],
        [*quarters, came, *before, *relay],
        (
            *[sds((size, LANES), BF16)] * GROUP_BLOCKS,
            sds((8, LANES), F32),
            *[sds(x.shape, BF16) for x in relay],
        ),
        scratch=[
            pltpu.VMEM((GROUP_BLOCKS, size + INFO, LANES), BF16),
            pltpu.VMEM((GROUP_BLOCKS, size, LANES), BF16),
        ],
        estimate=cost(8 * size * LANES, 10 * size * LANES * 2),
        after=after,
    )


def some_heads(ref, tokens, heads, first, count):
    x = ref[...].astype(F32)
    if count == heads:
        return x
    return x.reshape(tokens, heads, LANES)[:, first : first + count, :].reshape(tokens * count, LANES)


def inner_kernel(tokens, heads, first, count, cumul_ref, doc_ref, query_ref, key_ref, value_ref, inner_ref, qh_ref, qf, kf, vf, mask):
    cumul = cumul_ref[...]
    cumul_t = jnp.transpose(cumul)
    docs = doc_ref[...]
    column = doc_columns(docs, tokens)
    same = jnp.concatenate([column] * (tokens // LANES), axis=1) == doc_line(docs, tokens)
    mask[...] = jnp.where(lower_triangle(tokens) & same, 0.0, -1e9)
    qf[...] = some_heads(query_ref, tokens, heads, first, count)
    kf[...] = some_heads(key_ref, tokens, heads, first, count)
    vf[...] = some_heads(value_ref, tokens, heads, first, count)
    for n in range(count):
        h = first + n
        picked = pl.ds(n, tokens, stride=count)
        query = qf[picked, :].astype(BF16)
        keys = kf[picked, :].astype(BF16)
        values = vf[picked, :].astype(BF16)
        qh_ref[n * tokens : (n + 1) * tokens, :] = query
        for i in range(tokens // LANES):
            seen = (i + 1) * LANES
            rows = slice(i * LANES, seen)
            scores = lax.dot_general(
                query[rows, :], keys[0:seen, :], (((1,), (1,)), ((), ())), preferred_element_type=F32
            )
            gap = cumul[rows, h : h + 1] - cumul_t[h : h + 1, 0:seen]
            weights = (scores * jnp.exp(gap + mask[rows, 0:seen])).astype(BF16)
            inner_ref[n * tokens + i * LANES : n * tokens + seen, :] = jnp.dot(
                weights, values[0:seen, :], preferred_element_type=F32
            )


def inner_part(cumul, docs, query, key, value, tokens, heads, first, count, after):
    return call(
        functools.partial(inner_kernel, tokens, heads, first, count),
        "inner_part",
        [],
        [cumul, docs, query, key, value],
        (sds((count * tokens, LANES), F32), sds((count * tokens, LANES), BF16)),
        scratch=[pltpu.VMEM((tokens * count, LANES), F32)] * 3 + [pltpu.VMEM((tokens, tokens), F32)],
        mib=24,
        estimate=cost(
            4 * count * tokens * tokens * HEAD_DIM, tokens * heads * LANES * 12, count * tokens * tokens
        ),
        after=after,
    )


def mix_kernel(tokens, heads, parts, place_ref, doc_ref, prior_doc_ref, cumul_ref, *refs):
    refs = list(refs)
    take = lambda n: [refs.pop(0) for _ in range(n)]
    inner, qh, quarters = take(parts), take(parts), take(GROUP_BLOCKS)
    mixed_ref, square_ref, states = refs
    size = quarter_rows(heads)
    mine = place_ref[0] % GROUP_BLOCKS
    for j, ref in enumerate(quarters):
        states[pl.ds(pl.multiple_of((mine ^ j) * size, size), size), :] = ref[...]
    is_open = (doc_columns(doc_ref[...], tokens) == prior_doc_ref[0:1, :]).astype(F32)
    gain = jnp.exp(cumul_ref[...]) * is_open
    squares = jnp.zeros((tokens, LANES), F32)
    for h in range(heads):
        part, n = divmod(h, heads // parts)
        held = slice(n * tokens, (n + 1) * tokens)
        state = states[h * HEAD_DIM : (h + 1) * HEAD_DIM, :]
        carried = jnp.dot(qh[part][held, :], state, preferred_element_type=F32)
        mixed = inner[part][held, :] + carried * gain[:, h : h + 1]
        squares = squares + mixed * mixed
        mixed_ref[pl.ds(h, tokens, stride=heads), :] = mixed
    square_ref[...] = lax.dot_general(
        jnp.ones((8, LANES), F32),
        squares,
        (((1,), (1,)), ((), ())),
        precision=HIGHEST,
        preferred_element_type=F32,
    )


def mix(place, docs, prior_doc, cumul, inner, qh, quarters, tokens, heads, after):
    return call(
        functools.partial(mix_kernel, tokens, heads, len(inner)),
        "mix",
        [place],
        [docs, prior_doc, cumul, *inner, *qh, *quarters],
        (sds((tokens * heads, LANES), F32), sds((8, tokens), F32)),
        scratch=[pltpu.VMEM((heads * HEAD_DIM, LANES), BF16)],
        mib=24,
        estimate=cost(2 * heads * tokens * HEAD_DIM**2, tokens * heads * LANES * 10),
        after=after,
    )


def finish_kernel(tokens, heads, sums, step, gain_ref, gate_ref, mixed_ref, *refs):
    squares, (out_ref, done, sems) = refs[:sums], refs[sums:]
    total = squares[0][0:1, :]
    for ref in squares[1:]:
        total = total + ref[0:1, :]
    scale = lax.rsqrt(total / (HEADS * HEAD_DIM) + 1e-06)
    rows = jnp.concatenate([scale[:, i * LANES : (i + 1) * LANES] for i in range(tokens // LANES)], axis=0)
    column = doc_columns(rows, tokens)
    copies = []
    for i in range(0, tokens, step):
        at = pl.ds(i * heads, step * heads)
        gate = jax.nn.sigmoid(gate_ref[at, :].astype(F32)).reshape(step, heads, LANES)
        mixed = mixed_ref[at, :].reshape(step, heads, LANES)
        inv = column[i : i + step, :][:, None, :]
        out = mixed * inv * gain_ref[...][None] * gate
        done[at, :] = out.reshape(step * heads, LANES).astype(BF16)
        copies.append(pltpu.make_async_copy(done.at[at, :], out_ref.at[at, :], sems.at[i // step]))
        copies[-1].start()
    for copy in copies:
        copy.wait()


def finish(gain, gate, mixed, squares, tokens, heads, after):
    step = 64
    return call(
        functools.partial(finish_kernel, tokens, heads, len(squares), step),
        "finish",
        [],
        [gain, gate, mixed, *squares],
        sds((tokens * heads, LANES), BF16),
        scratch=[pltpu.VMEM((tokens * heads, LANES), BF16), pltpu.SemaphoreType.DMA((tokens // step,))],
        estimate=cost(0, tokens * heads * LANES * 8, tokens * heads * LANES),
        after=after,
        out_hbm=True,
    )


def attend_kernel(tokens, heads, kv_here, least, is_first, is_last, unroll, place_ref, *refs):
    refs = list(refs)
    take = lambda n: [refs.pop(0) for _ in range(n)]
    per_group = heads // kv_here
    rows = tokens * per_group
    step = CHUNK // per_group
    if is_first:
        doc_ref, query_ref = take(2)
    else:
        wide_ref, state_ref = take(2)
    kv = take(len(least))
    if is_first:
        wide_ref = take(1)[0]
    out_ref = take(1)[0]
    if is_last:
        take(1)[0][...] = jnp.zeros((8, LANES), F32)
    bias = take(1)[0]
    if is_first:
        doc_rep = take(1)[0]
    if is_last:
        done, sems = take(2)

    lane = lax.broadcasted_iota(jnp.int32, (tokens, LANES), 1).astype(F32)
    end = 2 * kv_here * tokens
    block = place_ref[0]
    for j, ref in enumerate(kv):
        valid = (block >= jnp.where(block % 2 == 0, *least[j])).astype(F32)
        docs = doc_columns(ref[end : end + INFO, :].astype(F32) * valid, tokens)
        bias[j] = jnp.where(docs == lane, 0.0, -BIG).astype(BF16)
    if is_first:
        column = doc_columns(doc_ref[...], tokens)
        for h in range(per_group):
            doc_rep[pl.ds(h, tokens, stride=per_group), :] = (column == lane).astype(F32)
    ones = jnp.ones((STATE_ROWS - HEAD_DIM, tokens), BF16)

    def some_chunks(i, carry):
        chains = [(u, g) for u in range(unroll) for g in range(kv_here)]
        chunk = [i * unroll + u for u in range(unroll)]
        at = [pl.ds(pl.multiple_of(c * CHUNK, CHUNK), CHUNK) for c in chunk]
        picked = [pl.ds(pl.multiple_of(c * (step * heads), step * heads), step * heads) for c in chunk]
        scores, results = {}, {}

        def begin(u, g):
            if is_first:
                query = query_ref[picked[u], :].astype(F32).reshape(step, heads, LANES)
                query = query[:, g * per_group : (g + 1) * per_group, :].reshape(CHUNK, LANES)
                wide = jnp.concatenate([query.astype(BF16), doc_rep[at[u], :].astype(BF16)], axis=1)
                wide_ref[g, at[u], :] = wide
            else:
                wide = wide_ref[g, at[u], :]
            out = []
            for j, ref in enumerate(kv):
                keys = jnp.concatenate([ref[g * tokens : (g + 1) * tokens, :], bias[j]], axis=1)
                out.append(
                    lax.dot_general(keys, wide, (((1,), (1,)), ((), ())), preferred_element_type=F32)
                )
            if is_first:
                token = chunk[u] * step + lax.broadcasted_iota(jnp.int32, (tokens, CHUNK), 1) // per_group
                key_at = lax.broadcasted_iota(jnp.int32, (tokens, CHUNK), 0)
                out[0] = jnp.where(key_at <= token, out[0], -BIG)
            scores[u, g] = out

        def end_chain(u, g):
            here = scores.pop((u, g))
            top = jnp.max(here[0], axis=0, keepdims=True)
            for score in here[1:]:
                top = jnp.maximum(top, jnp.max(score, axis=0, keepdims=True))
            total = None
            if not is_first:
                before = state_ref[g, :, at[u]]
                top_before = before[STATE_ROWS - 1 : STATE_ROWS, :]
                top = jnp.maximum(top, top_before)
                total = before * jnp.exp2((top_before - top) * SCORE_TO_EXP2)
            for ref, score in zip(kv, here):
                weights = jnp.exp2((score - top) * SCORE_TO_EXP2).astype(BF16)
                first = (kv_here + g) * tokens
                parts = [ref[first + p : first + p + LANES, :] for p in range(0, tokens, LANES)]
                values = jnp.concatenate([jnp.concatenate(parts, axis=1), ones], axis=0)
                more = jnp.dot(values, weights, preferred_element_type=F32)
                total = more if total is None else total + more
            if is_last:
                results[u, g] = jnp.transpose(total[0:HEAD_DIM] / total[HEAD_DIM : HEAD_DIM + 1])
            else:
                out_ref[g, 0 : STATE_ROWS - 8, at[u]] = total[0 : STATE_ROWS - 8]
                out_ref[g, STATE_ROWS - 8 : STATE_ROWS, at[u]] = jnp.broadcast_to(top, (8, CHUNK))

        ahead = 2
        for n in range(len(chains) + ahead):
            if n < len(chains):
                begin(*chains[n])
            if n >= ahead:
                end_chain(*chains[n - ahead])
        if is_last:
            for u in range(unroll):
                result = [results[u, g] for g in range(kv_here)]
                if kv_here > 1:
                    result = [r.reshape(step, per_group, LANES) for r in result]
                    result = [jnp.concatenate(result, axis=1).reshape(step * heads, LANES)]
                done[picked[u], :] = result[0].astype(BF16)
                pltpu.make_async_copy(
                    done.at[picked[u], :], out_ref.at[picked[u], :], sems.at[chunk[u]]
                ).start()
        return carry

    lax.fori_loop(0, rows // (CHUNK * unroll), some_chunks, 0)
    if is_last:
        for c in range(rows // CHUNK):
            at = pl.ds(c * step * heads, step * heads)
            pltpu.make_async_copy(done.at[at, :], out_ref.at[at, :], sems.at[c]).wait()


def attend(place, first, state, kv, is_last, tokens, heads, kv_here, after):
    is_first = state is None
    least = tuple(pair for _, pair in kv)
    kv = [block for block, _ in kv]
    blocks = len(kv)
    rows = tokens * heads // kv_here
    unroll = min(4, rows // CHUNK)
    wide_shape = sds((kv_here, rows, 2 * LANES), BF16)
    state_shape = sds((kv_here, STATE_ROWS, rows), F32)
    out_shape = sds((tokens * heads, LANES), BF16) if is_last else state_shape
    scratch = [pltpu.VMEM((blocks, tokens, LANES), BF16)]
    if is_first:
        out_shape = (wide_shape, out_shape)
        scratch.append(pltpu.VMEM((rows, LANES), F32))
    if is_last:
        out_shape = (out_shape, sds((8, LANES), F32))
        scratch.append(pltpu.VMEM((tokens * heads, LANES), BF16))
        scratch.append(pltpu.SemaphoreType.DMA((rows // CHUNK,)))
    span = blocks * tokens
    return call(
        functools.partial(attend_kernel, tokens, heads, kv_here, least, is_first, is_last, unroll),
        "attend",
        [place],
        [*first, *([] if is_first else [state]), *kv],
        out_shape,
        scratch=scratch,
        mib=24,
        estimate=cost(
            4 * tokens * heads * span * 2 * LANES, 4 * tokens * heads * LANES * 4, tokens * heads * span
        ),
        after=after,
        out_hbm=is_last,
    )


def body(
    blocks,
    lin_query,
    lin_key,
    lin_value,
    lin_gate,
    log_decay,
    norm_gain,
    doc_ids,
    soft_query,
    soft_key,
    soft_value,
):
    tokens, heads, _ = lin_query.shape
    tensor = HEADS // heads
    kv_here = max(1, heads // GROUP)
    parts = 2 if heads % 16 == 0 else 1
    longest = blocks * tokens * 5 // 8
    window = min(blocks - 1, (longest - 1 + tokens - 1) // tokens)
    flat = lambda x: x.reshape(-1, LANES)
    block = lax.axis_index("seq")
    place = block.astype(jnp.int32).reshape(1)
    start = (lax.axis_index("tp") * heads // GROUP).astype(jnp.int32).reshape(1)

    def send(x, pairs):
        return lax.ppermute(x, "seq", [(a, b % blocks) for a, b in pairs])

    everyone = range(blocks)
    swap = [(b, b ^ 1) for b in everyone]

    own_kv, docs, cumul, key, value = fetch(
        start,
        [
            doc_ids.reshape(tokens // LANES, LANES),
            jnp.transpose(log_decay),
            flat(soft_key),
            flat(soft_value),
            flat(lin_key),
            flat(lin_value),
        ],
        tokens,
        heads,
        kv_here,
    )

    odd_window = window % 2 == 1
    forward = [(b, b + 2) for b in everyone]
    ahead = send(own_kv, forward)
    beside = send(own_kv, [(b, b + (1 if b % 2 == 0 else window if odd_window else -1)) for b in everyone])
    beside = (beside, (window if odd_window else blocks, 1))

    size = quarter_rows(heads)
    others = range(1, GROUP_BLOCKS)
    sent = block_state(place, cumul, docs, key, value, tokens, heads)
    quarters = [sent[0]] + [send(sent[j], [(b, b ^ j) for b in everyone]) for j in others]

    state = {}

    def first_attention(after):
        state["wide"], state["sum"] = attend(
            place, (docs, flat(soft_query)), None, [(own_kv, (0, 0))], False, tokens, heads, kv_here, after
        )
        return state["sum"]

    def more_attention(kv, is_last, after):
        state["sum"] = attend(
            place, (state["wide"],), state["sum"], kv, is_last, tokens, heads, kv_here, after
        )
        return state["sum"]

    inner, qh = [], []

    def inner_of(part, after):
        n = heads // parts
        got = inner_part(
            cumul, docs, flat(lin_query), key, value, tokens, heads, part * n, n, after
        )
        inner.append(got[0])
        qh.append(got[1])
        return got[0]

    done = inner_of(0, [first_attention([sent[0]])])
    run, ahead = group_map(place, quarters, size, [done, beside[0]], ahead)
    lanes = [ahead]
    for _ in range(1, window // 2):
        lanes.append(send(lanes[-1], forward))
    lane_kv = [(kv, (2 * n + 2, 2 * n + 2)) for n, kv in enumerate(lanes)]
    cross_kv = [(send(ahead, swap), (2, 3))]
    stages = (blocks // GROUP_BLOCKS).bit_length() - 1
    before, done = None, run
    for stage in range(stages):
        came = send(run, [(b, b ^ (GROUP_BLOCKS << stage)) for b in everyone])
        if stage == stages - 1:
            for part in range(1, parts):
                done = inner_of(part, [done])
            done = more_attention([beside] + lane_kv[:1], False, [done])
        else:
            run, before = scan_step(place, stage + 2, run, came, before, size, [done])
            done = run
    *priors, prior_doc, relayed = prior_states(
        place, stages + 1, quarters, came, before, size, [done], lanes[1]
    )
    priors = [priors[0]] + [send(priors[j], [(b, b ^ j) for b in everyone]) for j in others]
    lane_kv[1] = (relayed, lane_kv[1][1])
    for n, kv in enumerate([relayed] + lanes[2:]):
        cross_kv.append((send(kv, swap), (2 * n + 4, 2 * n + 5)))
    rest = [kv for pair in zip(cross_kv, lane_kv[1:] + [None]) for kv in pair if kv is not None]
    done = more_attention(rest[:2], False, [prior_doc])
    rest = rest[2:]
    mixed, squares = mix(place, docs, prior_doc, cumul, inner, qh, priors, tokens, heads, [done])
    sums = [squares]
    for other in range(1, tensor):
        sums.append(lax.ppermute(squares, "tp", [(t, t ^ other) for t in range(tensor)]))
    after = [squares]
    while rest:
        got = more_attention(rest[:2], len(rest) <= 2, after)
        rest, after = rest[2:], []
    soft_out, done = got
    lin_out = finish(norm_gain, flat(lin_gate), mixed, sums, tokens, heads, [done])
    shape = (tokens, heads, HEAD_DIM)
    return lin_out.reshape(shape), soft_out.reshape(shape)


def solution(mesh):
    in_specs = (
        P("seq", "tp", None),
        P("seq", "tp", None),
        P("seq", "tp", None),
        P("seq", "tp", None),
        P("seq", "tp"),
        P("tp", None),
        P("seq"),
        P("seq", "tp", None),
        P("seq", None, None),
        P("seq", None, None),
    )
    out_specs = (P("seq", "tp", None), P("seq", "tp", None))
    return jax.shard_map(
        functools.partial(body, mesh.shape["seq"]),
        mesh=mesh,
        in_specs=in_specs,
        out_specs=out_specs,
        check_vma=False,
    )
```

```python
import functools

import jax
import jax.numpy as jnp
import numpy as np
from jax import lax
from jax.experimental import pallas as pl
from jax.experimental.pallas import tpu as pltpu
from jax.sharding import PartitionSpec as P

HEADS = 64
HEAD_DIM = 128
KV_HEADS = 8
LANES = 128
GROUP = HEADS // KV_HEADS
F32 = jnp.float32
BF16 = jnp.bfloat16
BIG = float(2**20)
SCORE_TO_EXP2 = HEAD_DIM**-0.5 * float(np.log2(np.e))
INFO = 16
HIGHEST = lax.Precision.HIGHEST

VMEM = pl.BlockSpec(memory_space=pltpu.VMEM)
SMEM = pl.BlockSpec(memory_space=pltpu.SMEM)
HBM = pl.BlockSpec(memory_space=pltpu.HBM)
ANYWHERE = pl.BlockSpec(memory_space=pl.ANY)
STATE_ROWS = HEAD_DIM + 16
CHUNK = 256
GROUP_BLOCKS = 4


def sds(shape, dtype):
    return jax.ShapeDtypeStruct(shape, dtype)


def cost(flops, bytes_accessed, transcendentals=0):
    return pl.CostEstimate(
        flops=int(flops) // 8, bytes_accessed=int(bytes_accessed) // 8, transcendentals=int(transcendentals) // 8
    )


def call(kernel, name, scalars, operands, out_shape, scratch=(), mib=16, estimate=None, after=(), hbm=0, out_hbm=False, relay=()):
    begin = len(scalars) + len(operands)
    skip = len(after)
    operands = [
        pltpu.with_memory_space_constraint(x, pltpu.HBM) if i < hbm else x for i, x in enumerate(operands)
    ]
    outs = out_shape if isinstance(out_shape, tuple) else (out_shape,)
    out_specs = (VMEM,) * len(outs)
    outs = tuple(
        (pltpu.HBM if out_hbm and i == 0 else pltpu.VMEM)(x.shape, x.dtype) for i, x in enumerate(outs)
    )
    if out_hbm:
        out_specs = (HBM, *out_specs[1:])

    moved = len(relay)
    many = len(outs)
    single = not isinstance(out_shape, tuple) and not relay
    out_specs += (VMEM,) * moved
    outs += tuple(pltpu.VMEM(x.shape, x.dtype) for x in relay)

    def run(*refs):
        rest = refs[begin + skip + moved :]
        for source, target in zip(refs[begin + skip : begin + skip + moved], rest[many : many + moved]):
            target[...] = source[...]
        kernel(*refs[:begin], *rest[:many], *rest[many + moved :])

    out = pl.pallas_call(
        run,
        out_shape=outs,
        in_specs=[SMEM] * len(scalars) + [HBM] * hbm + [VMEM] * (len(operands) - hbm) + [ANYWHERE] * skip + [VMEM] * moved,
        out_specs=out_specs,
        scratch_shapes=list(scratch),
        compiler_params=pltpu.CompilerParams(vmem_limit_bytes=mib * 1024 * 1024),
        cost_estimate=estimate,
        name=name,
    )(*scalars, *operands, *after, *relay)
    return out[0] if single else out


def doc_columns(doc_rows, tokens):
    parts = []
    for i in range(tokens // LANES):
        row = jnp.broadcast_to(doc_rows[i : i + 1, :], (LANES, LANES))
        parts.append(jnp.transpose(row))
    return jnp.concatenate(parts, axis=0)


def doc_line(doc_rows, tokens):
    return jnp.concatenate([doc_rows[i : i + 1, :] for i in range(tokens // LANES)], axis=1)


def lower_triangle(tokens):
    rows = lax.broadcasted_iota(jnp.int32, (tokens, tokens), 0)
    cols = lax.broadcasted_iota(jnp.int32, (tokens, tokens), 1)
    return rows >= cols


def fetch_kernel(tokens, heads, kv_here, start_ref, *refs):
    refs = list(refs)
    take = lambda n: [refs.pop(0) for _ in range(n)]
    sources = take(7)
    kv_ref, doc_out, cumul_ref, key_out, value_out, query_out = take(6)
    held = take(4)
    sems, wide, ldp = refs
    docs_in, decays, soft_key, soft_value = held
    targets = [*held, key_out, value_out, query_out]
    copies = [
        pltpu.make_async_copy(source, target, sems.at[i])
        for i, (source, target) in enumerate(zip(sources, targets))
    ]
    for copy in copies:
        copy.start()

    copies[0].wait()
    docs = docs_in[...].astype(F32) + 1.0
    line = lax.broadcasted_iota(jnp.int32, (INFO, LANES), 0)
    info = jnp.zeros((INFO, LANES), F32)
    for i in range(tokens // LANES):
        info = jnp.where(line == i, docs[i : i + 1, :], info)
    doc_out[...] = info
    end = 2 * kv_here * tokens
    kv_ref[end : end + INFO, :] = info.astype(BF16)

    copies[1].wait()
    ldp[...] = jnp.zeros_like(ldp)
    ldp[0:heads, :] = decays[...]
    cumul_ref[...] = lax.dot_general(
        lower_triangle(tokens).astype(F32),
        ldp[...],
        (((1,), (1,)), ((), ())),
        precision=HIGHEST,
        preferred_element_type=F32,
    )

    start = start_ref[0]
    for which, ref in enumerate((soft_key, soft_value)):
        copies[2 + which].wait()
        wide[...] = ref[...].astype(F32)
        for g in range(kv_here):
            rows = wide[pl.ds(start + g, tokens, stride=KV_HEADS), :]
            at = (which * kv_here + g) * tokens
            if which:
                halves = [jnp.transpose(rows[i : i + LANES, :]) for i in range(0, tokens, LANES)]
                rows = jnp.concatenate(halves, axis=0)
            kv_ref[at : at + tokens, :] = rows.astype(BF16)
    for copy in copies[4:]:
        copy.wait()


def fetch(start, operands, tokens, heads, kv_here):
    return call(
        functools.partial(fetch_kernel, tokens, heads, kv_here),
        "fetch",
        [start],
        operands,
        (
            sds((2 * kv_here * tokens + INFO, LANES), BF16),
            sds((INFO, LANES), F32),
            sds((tokens, LANES), F32),
            sds(operands[4].shape, BF16),
            sds(operands[5].shape, BF16),
            sds(operands[6].shape, BF16),
        ),
        scratch=[pltpu.VMEM(x.shape, x.dtype) for x in operands[:4]]
        + [
            pltpu.SemaphoreType.DMA((len(operands),)),
            pltpu.VMEM((tokens * KV_HEADS, LANES), F32),
            pltpu.VMEM((LANES, tokens), F32),
        ],
        estimate=cost(0, 3 * tokens * heads * LANES * 2),
        hbm=len(operands),
    )


def quarter_rows(heads):
    return heads * HEAD_DIM // GROUP_BLOCKS


def state_kernel(tokens, heads, place_ref, *refs):
    refs = list(refs)
    take = lambda n: [refs.pop(0) for _ in range(n)]
    cumul_ref, doc_ref, key_ref, value_ref = take(4)
    out_refs = take(GROUP_BLOCKS)
    kf, vf, states = refs
    cumul, docs = cumul_ref[...], doc_ref[...]
    total = cumul[tokens - 1 : tokens, :]
    last_row = tokens // LANES - 1
    first_doc = docs[0:1, 0:1]
    last_doc = docs[last_row : last_row + 1, LANES - 1 : LANES]
    tail = (doc_columns(docs, tokens) == last_doc).astype(F32)
    scale = jnp.exp(total - cumul) * tail
    kf[...] = key_ref[...].astype(F32)
    vf[...] = value_ref[...].astype(F32)
    for h in range(heads):
        keys = (kf[pl.ds(h, tokens, stride=heads), :] * scale[:, h : h + 1]).astype(BF16)
        values = vf[pl.ds(h, tokens, stride=heads), :].astype(BF16)
        states[h * HEAD_DIM : (h + 1) * HEAD_DIM, :] = lax.dot_general(
            keys, values, (((0,), (0,)), ((), ())), preferred_element_type=F32
        )
    size = quarter_rows(heads)
    mine = place_ref[0] % GROUP_BLOCKS
    for j, ref in enumerate(out_refs):
        taker = mine ^ j
        ref[0:size, :] = states[pl.ds(pl.multiple_of(taker * size, size), size), :].astype(BF16)
        totals = jnp.zeros_like(total)
        for c in range(GROUP_BLOCKS):
            skip = c * heads // GROUP_BLOCKS
            moved = pltpu.roll(total, LANES - skip, 1) if skip else total
            totals = jnp.where(taker == c, moved, totals)
        ref[size : size + INFO, :] = info_rows((*in_parts(totals), first_doc, last_doc))


def block_state(place, cumul, docs, key, value, tokens, heads):
    return call(
        functools.partial(state_kernel, tokens, heads),
        "block_state",
        [place],
        [cumul, docs, key, value],
        (sds((quarter_rows(heads) + INFO, LANES), BF16),) * GROUP_BLOCKS,
        scratch=[
            pltpu.VMEM((tokens * heads, LANES), F32),
            pltpu.VMEM((tokens * heads, LANES), F32),
            pltpu.VMEM((heads * HEAD_DIM, LANES), F32),
        ],
        estimate=cost(2 * heads * tokens * HEAD_DIM**2, 5 * tokens * heads * LANES * 2),
    )


def in_parts(x):
    hi = x.astype(BF16).astype(F32)
    mid = (x - hi).astype(BF16).astype(F32)
    return hi, mid, x - hi - mid


def info_rows(parts):
    line = lax.broadcasted_iota(jnp.int32, (INFO, LANES), 0)
    info = jnp.zeros((INFO, LANES), F32)
    for i, part in enumerate(parts):
        info = jnp.where(line == i, part, info)
    return info.astype(BF16)


def read_map(ref, size):
    info = ref[size : size + INFO, :].astype(F32)
    return info[0:1] + info[1:2] + info[2:3], info[3:4], info[4:5]


def row_chunks(size):
    unit = min(HEAD_DIM, size)
    return [(slice(i * unit, (i + 1) * unit), slice(i, i + 1)) for i in range(size // unit)]


def in_block_order(place_ref, refs, blocks):
    mine = place_ref[0] % GROUP_BLOCKS
    for j, ref in enumerate(refs):
        blocks[mine ^ j] = ref[...]


def block_maps(blocks, size):
    maps = []
    for c in range(GROUP_BLOCKS):
        info = blocks[c, size : size + INFO, :].astype(F32)
        first, last = info[3:4], info[4:5]
        gain = jnp.exp(info[0:1] + info[1:2] + info[2:3]) * (first == last).astype(F32)
        maps.append((gain, first, last))
    return maps


def group_kernel(size, place_ref, *refs):
    sources = refs[:GROUP_BLOCKS]
    out_ref, blocks = refs[GROUP_BLOCKS:]
    in_block_order(place_ref, sources, blocks)
    maps = block_maps(blocks, size)
    gains = [None]
    for (gain, first, _), (_, _, last_before) in zip(maps[1:], maps[:-1]):
        gains.append(gain * (last_before == first).astype(F32))
    for rows, lane in row_chunks(size):
        total = blocks[0, rows, :].astype(F32)
        for c in range(1, GROUP_BLOCKS):
            total = gains[c][:, lane] * total + blocks[c, rows, :].astype(F32)
        out_ref[rows, :] = total.astype(BF16)
    gain = maps[0][0] * gains[1] * gains[2] * gains[3]
    out_ref[size : size + INFO, :] = info_rows((*in_parts(gain), maps[0][1], maps[-1][2]))


def group_map(place, quarters, size, after, relay):
    return call(
        functools.partial(group_kernel, size),
        "group_map",
        [place],
        quarters,
        (sds((size + INFO, LANES), BF16),),
        scratch=[pltpu.VMEM((GROUP_BLOCKS, size + INFO, LANES), BF16)],
        estimate=cost(8 * size * LANES, 10 * size * LANES * 2),
        after=after,
        relay=relay,
    )


def scan_kernel(size, has_before, bit, place_ref, *refs):
    mine_ref, came_ref = refs[:2]
    before_ref = refs[2] if has_before else None
    run_ref, out_ref = refs[-2:]
    upper = (place_ref[0] >> bit) & 1 == 1
    gain_m, first_m, last_m = read_map(mine_ref, size)
    gain_c, first_c, last_c = read_map(came_ref, size)
    link = jnp.where(upper, (last_c == first_m).astype(F32), (last_m == first_c).astype(F32))
    gain = jnp.where(upper, gain_m, gain_c) * link
    for rows, lane in row_chunks(size):
        mine, came = mine_ref[rows, :].astype(F32), came_ref[rows, :].astype(F32)
        lower_sum, upper_sum = jnp.where(upper, came, mine), jnp.where(upper, mine, came)
        run_ref[rows, :] = (gain[:, lane] * lower_sum + upper_sum).astype(BF16)
    run_ref[size : size + INFO, :] = info_rows(
        (
            *in_parts(gain * jnp.where(upper, gain_c, gain_m)),
            jnp.where(upper, first_c, first_m),
            jnp.where(upper, last_m, last_c),
        )
    )
    if not has_before:
        out_ref[...] = jnp.where(upper, came_ref[...], jnp.zeros_like(came_ref))
        return
    gain_b, first_b, last_b = read_map(before_ref, size)
    empty = first_b == 0.0
    factor = jnp.where(empty, 1.0, gain_b * (last_c == first_b).astype(F32))
    for rows, lane in row_chunks(size):
        before = before_ref[rows, :].astype(F32)
        joined = factor[:, lane] * came_ref[rows, :].astype(F32) + before
        out_ref[rows, :] = jnp.where(upper, joined, before).astype(BF16)
    out_ref[size : size + INFO, :] = info_rows(
        (
            *in_parts(jnp.where(upper, factor * gain_c, gain_b)),
            jnp.where(upper, first_c, first_b),
            jnp.where(upper, jnp.where(empty, last_c, last_b), last_b),
        )
    )


def scan_step(place, bit, mine, came, before, size, after):
    shape = sds((size + INFO, LANES), BF16)
    before = [] if before is None else [before]
    return call(
        functools.partial(scan_kernel, size, len(before), bit),
        "scan_step",
        [place],
        [mine, came, *before],
        (shape, shape),
        estimate=cost(6 * size * LANES, 6 * size * LANES * 2),
        after=after,
    )


def prior_kernel(size, has_before, bit, place_ref, *refs):
    sources, came_ref = refs[:GROUP_BLOCKS], refs[GROUP_BLOCKS]
    before_ref = refs[GROUP_BLOCKS + 1] if has_before else None
    *out_refs, doc_ref, blocks, priors = refs[GROUP_BLOCKS + 1 + has_before :]
    mine = place_ref[0] % GROUP_BLOCKS
    in_block_order(place_ref, sources, blocks)
    maps = block_maps(blocks, size)
    upper = ((place_ref[0] >> bit) & 1).astype(F32)
    _, _, last_c = read_map(came_ref, size)
    factor, doc = jnp.broadcast_to(upper, (1, LANES)), upper * last_c
    if has_before:
        gain_b, first_b, last_b = read_map(before_ref, size)
        empty = first_b == 0.0
        factor = upper * jnp.where(empty, 1.0, gain_b * (last_c == first_b).astype(F32))
        doc = jnp.where(empty, doc, last_b)
    docs = [doc] + [last for _, _, last in maps[:-1]]
    gains = [gain * (doc == first).astype(F32) for (gain, first, _), doc in zip(maps, docs)]
    for rows, lane in row_chunks(size):
        state = factor[:, lane] * came_ref[rows, :].astype(F32)
        if has_before:
            state = state + before_ref[rows, :].astype(F32)
        for c in range(GROUP_BLOCKS):
            priors[c, rows, :] = state.astype(BF16)
            if c < GROUP_BLOCKS - 1:
                state = gains[c][:, lane] * state + blocks[c, rows, :].astype(F32)
    for j, ref in enumerate(out_refs):
        ref[...] = priors[mine ^ j]
    own_doc = docs[0]
    for c in range(1, GROUP_BLOCKS):
        own_doc = jnp.where(mine == c, docs[c], own_doc)
    doc_ref[...] = jnp.broadcast_to(own_doc, (8, LANES))


def prior_states(place, bit, quarters, came, before, size, after, relay):
    before = [] if before is None else [before]
    return call(
        functools.partial(prior_kernel, size, len(before), bit),
        "prior_states",
        [place],
        [*quarters, came, *before],
        (*[sds((size, LANES), BF16)] * GROUP_BLOCKS, sds((8, LANES), F32)),
        scratch=[
            pltpu.VMEM((GROUP_BLOCKS, size + INFO, LANES), BF16),
            pltpu.VMEM((GROUP_BLOCKS, size, LANES), BF16),
        ],
        estimate=cost(8 * size * LANES, 10 * size * LANES * 2),
        after=after,
        relay=relay,
    )


def some_heads(ref, tokens, heads, first, count):
    x = ref[...].astype(F32)
    if count == heads:
        return x
    return x.reshape(tokens, heads, LANES)[:, first : first + count, :].reshape(tokens * count, LANES)


def inner_kernel(tokens, heads, first, count, cumul_ref, doc_ref, query_ref, key_ref, value_ref, inner_ref, qh_ref, qf, kf, vf, mask):
    cumul = cumul_ref[...]
    cumul_t = jnp.transpose(cumul)
    docs = doc_ref[...]
    column = doc_columns(docs, tokens)
    same = jnp.concatenate([column] * (tokens // LANES), axis=1) == doc_line(docs, tokens)
    mask[...] = jnp.where(lower_triangle(tokens) & same, 0.0, -1e9)
    qf[...] = some_heads(query_ref, tokens, heads, first, count)
    kf[...] = some_heads(key_ref, tokens, heads, first, count)
    vf[...] = some_heads(value_ref, tokens, heads, first, count)
    for n in range(count):
        h = first + n
        picked = pl.ds(n, tokens, stride=count)
        query = qf[picked, :].astype(BF16)
        keys = kf[picked, :].astype(BF16)
        values = vf[picked, :].astype(BF16)
        qh_ref[n * tokens : (n + 1) * tokens, :] = query
        for i in range(tokens // LANES):
            seen = (i + 1) * LANES
            rows = slice(i * LANES, seen)
            scores = lax.dot_general(
                query[rows, :], keys[0:seen, :], (((1,), (1,)), ((), ())), preferred_element_type=F32
            )
            gap = cumul[rows, h : h + 1] - cumul_t[h : h + 1, 0:seen]
            weights = (scores * jnp.exp(gap + mask[rows, 0:seen])).astype(BF16)
            inner_ref[n * tokens + i * LANES : n * tokens + seen, :] = jnp.dot(
                weights, values[0:seen, :], preferred_element_type=F32
            )


def inner_part(cumul, docs, query, key, value, tokens, heads, first, count, after):
    return call(
        functools.partial(inner_kernel, tokens, heads, first, count),
        "inner_part",
        [],
        [cumul, docs, query, key, value],
        (sds((count * tokens, LANES), F32), sds((count * tokens, LANES), BF16)),
        scratch=[pltpu.VMEM((tokens * count, LANES), F32)] * 3 + [pltpu.VMEM((tokens, tokens), F32)],
        mib=24,
        estimate=cost(
            4 * count * tokens * tokens * HEAD_DIM, tokens * heads * LANES * 12, count * tokens * tokens
        ),
        after=after,
    )


def mix_kernel(tokens, heads, parts, place_ref, doc_ref, prior_doc_ref, cumul_ref, *refs):
    refs = list(refs)
    take = lambda n: [refs.pop(0) for _ in range(n)]
    inner, qh, quarters = take(parts), take(parts), take(GROUP_BLOCKS)
    mixed_ref, square_ref, states = refs
    size = quarter_rows(heads)
    mine = place_ref[0] % GROUP_BLOCKS
    for j, ref in enumerate(quarters):
        states[pl.ds(pl.multiple_of((mine ^ j) * size, size), size), :] = ref[...]
    is_open = (doc_columns(doc_ref[...], tokens) == prior_doc_ref[0:1, :]).astype(F32)
    gain = jnp.exp(cumul_ref[...]) * is_open
    squares = jnp.zeros((tokens, LANES), F32)
    for h in range(heads):
        part, n = divmod(h, heads // parts)
        held = slice(n * tokens, (n + 1) * tokens)
        state = states[h * HEAD_DIM : (h + 1) * HEAD_DIM, :]
        carried = jnp.dot(qh[part][held, :], state, preferred_element_type=F32)
        mixed = inner[part][held, :] + carried * gain[:, h : h + 1]
        squares = squares + mixed * mixed
        mixed_ref[pl.ds(h, tokens, stride=heads), :] = mixed
    square_ref[...] = lax.dot_general(
        jnp.ones((8, LANES), F32),
        squares,
        (((1,), (1,)), ((), ())),
        precision=HIGHEST,
        preferred_element_type=F32,
    )


def mix(place, docs, prior_doc, cumul, inner, qh, quarters, tokens, heads, after):
    return call(
        functools.partial(mix_kernel, tokens, heads, len(inner)),
        "mix",
        [place],
        [docs, prior_doc, cumul, *inner, *qh, *quarters],
        (sds((tokens * heads, LANES), F32), sds((8, tokens), F32)),
        scratch=[pltpu.VMEM((heads * HEAD_DIM, LANES), BF16)],
        mib=24,
        estimate=cost(2 * heads * tokens * HEAD_DIM**2, tokens * heads * LANES * 10),
        after=after,
    )


def finish_kernel(tokens, heads, sums, step, gain_ref, gate_ref, mixed_ref, *refs):
    squares, (out_ref, done, sems) = refs[:sums], refs[sums:]
    total = squares[0][0:1, :]
    for ref in squares[1:]:
        total = total + ref[0:1, :]
    scale = lax.rsqrt(total / (HEADS * HEAD_DIM) + 1e-06)
    rows = jnp.concatenate([scale[:, i * LANES : (i + 1) * LANES] for i in range(tokens // LANES)], axis=0)
    column = doc_columns(rows, tokens)
    copies = []
    for i in range(0, tokens, step):
        at = pl.ds(i * heads, step * heads)
        gate = jax.nn.sigmoid(gate_ref[at, :].astype(F32)).reshape(step, heads, LANES)
        mixed = mixed_ref[at, :].reshape(step, heads, LANES)
        inv = column[i : i + step, :][:, None, :]
        out = mixed * inv * gain_ref[...][None] * gate
        done[at, :] = out.reshape(step * heads, LANES).astype(BF16)
        copies.append(pltpu.make_async_copy(done.at[at, :], out_ref.at[at, :], sems.at[i // step]))
        copies[-1].start()
    for copy in copies:
        copy.wait()


def finish(gain, gate, mixed, squares, tokens, heads, after):
    step = 64
    return call(
        functools.partial(finish_kernel, tokens, heads, len(squares), step),
        "finish",
        [],
        [gain, gate, mixed, *squares],
        sds((tokens * heads, LANES), BF16),
        scratch=[pltpu.VMEM((tokens * heads, LANES), BF16), pltpu.SemaphoreType.DMA((tokens // step,))],
        estimate=cost(0, tokens * heads * LANES * 8, tokens * heads * LANES),
        after=after,
        out_hbm=True,
    )


def attend_kernel(tokens, heads, kv_here, least, has_choice, is_first, is_last, unroll, place_ref, *refs):
    refs = list(refs)
    take = lambda n: [refs.pop(0) for _ in range(n)]
    per_group = heads // kv_here
    rows = tokens * per_group
    step = CHUNK // per_group
    if is_first:
        doc_ref, query_ref = take(2)
    else:
        wide_ref, state_ref = take(2)
    kv = take(len(least))
    other = take(1)[0] if has_choice else None
    if is_first:
        wide_ref = take(1)[0]
    out_ref = take(1)[0]
    if is_last:
        take(1)[0][...] = jnp.zeros((8, LANES), F32)
    bias = take(1)[0]
    if is_first:
        doc_rep = take(1)[0]
    if is_last:
        done, sems = take(2)
    block = place_ref[0]
    if has_choice:
        slot = take(1)[0]
        slot[...] = jnp.where(block % 2 == 0, kv[0][...], other[...])
        kv[0] = slot

    lane = lax.broadcasted_iota(jnp.int32, (tokens, LANES), 1).astype(F32)
    end = 2 * kv_here * tokens
    for j, ref in enumerate(kv):
        valid = (block >= jnp.where(block % 2 == 0, *least[j])).astype(F32)
        docs = doc_columns(ref[end : end + INFO, :].astype(F32) * valid, tokens)
        bias[j] = jnp.where(docs == lane, 0.0, -BIG).astype(BF16)
    if is_first:
        column = doc_columns(doc_ref[...], tokens)
        for h in range(per_group):
            doc_rep[pl.ds(h, tokens, stride=per_group), :] = (column == lane).astype(F32)
    ones = jnp.ones((STATE_ROWS - HEAD_DIM, tokens), BF16)

    def some_chunks(i, carry):
        chains = [(u, g) for u in range(unroll) for g in range(kv_here)]
        chunk = [i * unroll + u for u in range(unroll)]
        at = [pl.ds(pl.multiple_of(c * CHUNK, CHUNK), CHUNK) for c in chunk]
        picked = [pl.ds(pl.multiple_of(c * (step * heads), step * heads), step * heads) for c in chunk]
        scores, results = {}, {}

        def begin(u, g):
            if is_first:
                query = query_ref[picked[u], :].astype(F32).reshape(step, heads, LANES)
                query = query[:, g * per_group : (g + 1) * per_group, :].reshape(CHUNK, LANES)
                wide = jnp.concatenate([query.astype(BF16), doc_rep[at[u], :].astype(BF16)], axis=1)
                wide_ref[g, at[u], :] = wide
            else:
                wide = wide_ref[g, at[u], :]
            out = []
            for j, ref in enumerate(kv):
                keys = jnp.concatenate([ref[g * tokens : (g + 1) * tokens, :], bias[j]], axis=1)
                out.append(
                    lax.dot_general(keys, wide, (((1,), (1,)), ((), ())), preferred_element_type=F32)
                )
            if is_first:
                token = chunk[u] * step + lax.broadcasted_iota(jnp.int32, (tokens, CHUNK), 1) // per_group
                key_at = lax.broadcasted_iota(jnp.int32, (tokens, CHUNK), 0)
                out[0] = jnp.where(key_at <= token, out[0], -BIG)
            scores[u, g] = out

        def end_chain(u, g):
            here = scores.pop((u, g))
            top = jnp.max(here[0], axis=0, keepdims=True)
            for score in here[1:]:
                top = jnp.maximum(top, jnp.max(score, axis=0, keepdims=True))
            total = None
            if not is_first:
                before = state_ref[g, :, at[u]]
                top_before = before[STATE_ROWS - 1 : STATE_ROWS, :]
                top = jnp.maximum(top, top_before)
                total = before * jnp.exp2((top_before - top) * SCORE_TO_EXP2)
            for ref, score in zip(kv, here):
                weights = jnp.exp2((score - top) * SCORE_TO_EXP2).astype(BF16)
                first = (kv_here + g) * tokens
                parts = [ref[first + p : first + p + LANES, :] for p in range(0, tokens, LANES)]
                values = jnp.concatenate([jnp.concatenate(parts, axis=1), ones], axis=0)
                more = jnp.dot(values, weights, preferred_element_type=F32)
                total = more if total is None else total + more
            if is_last:
                results[u, g] = jnp.transpose(total[0:HEAD_DIM] / total[HEAD_DIM : HEAD_DIM + 1])
            else:
                out_ref[g, 0 : STATE_ROWS - 8, at[u]] = total[0 : STATE_ROWS - 8]
                out_ref[g, STATE_ROWS - 8 : STATE_ROWS, at[u]] = jnp.broadcast_to(top, (8, CHUNK))

        ahead = 2
        for n in range(len(chains) + ahead):
            if n < len(chains):
                begin(*chains[n])
            if n >= ahead:
                end_chain(*chains[n - ahead])
        if is_last:
            for u in range(unroll):
                result = [results[u, g] for g in range(kv_here)]
                if kv_here > 1:
                    result = [r.reshape(step, per_group, LANES) for r in result]
                    result = [jnp.concatenate(result, axis=1).reshape(step * heads, LANES)]
                done[picked[u], :] = result[0].astype(BF16)
                pltpu.make_async_copy(
                    done.at[picked[u], :], out_ref.at[picked[u], :], sems.at[chunk[u]]
                ).start()
        return carry

    lax.fori_loop(0, rows // (CHUNK * unroll), some_chunks, 0)
    if is_last:
        for c in range(rows // CHUNK):
            at = pl.ds(c * step * heads, step * heads)
            pltpu.make_async_copy(done.at[at, :], out_ref.at[at, :], sems.at[c]).wait()


def attend(place, first, state, kv, is_last, tokens, heads, kv_here, after, odd=None):
    is_first = state is None
    least = tuple(pair for _, pair in kv)
    kv = [block for block, _ in kv]
    blocks = len(kv)
    rows = tokens * heads // kv_here
    unroll = min(4, rows // CHUNK)
    wide_shape = sds((kv_here, rows, 2 * LANES), BF16)
    state_shape = sds((kv_here, STATE_ROWS, rows), F32)
    out_shape = sds((tokens * heads, LANES), BF16) if is_last else state_shape
    scratch = [pltpu.VMEM((blocks, tokens, LANES), BF16)]
    if is_first:
        out_shape = (wide_shape, out_shape)
        scratch.append(pltpu.VMEM((rows, LANES), F32))
    if is_last:
        out_shape = (out_shape, sds((8, LANES), F32))
        scratch.append(pltpu.VMEM((tokens * heads, LANES), BF16))
        scratch.append(pltpu.SemaphoreType.DMA((rows // CHUNK,)))
    if odd is not None:
        scratch.append(pltpu.VMEM(odd.shape, BF16))
    span = blocks * tokens
    return call(
        functools.partial(attend_kernel, tokens, heads, kv_here, least, odd is not None, is_first, is_last, unroll),
        "attend",
        [place],
        [*first, *([] if is_first else [state]), *kv, *([] if odd is None else [odd])],
        out_shape,
        scratch=scratch,
        mib=24,
        estimate=cost(
            4 * tokens * heads * span * 2 * LANES, 4 * tokens * heads * LANES * 4, tokens * heads * span
        ),
        after=after,
        out_hbm=is_last,
    )


def body(
    blocks,
    lin_query,
    lin_key,
    lin_value,
    lin_gate,
    log_decay,
    norm_gain,
    doc_ids,
    soft_query,
    soft_key,
    soft_value,
):
    tokens, heads, _ = lin_query.shape
    tensor = HEADS // heads
    kv_here = max(1, heads // GROUP)
    parts = 2 if heads % 16 == 0 else 1
    longest = blocks * tokens * 5 // 8
    window = min(blocks - 1, (longest - 1 + tokens - 1) // tokens)
    flat = lambda x: x.reshape(-1, LANES)
    block = lax.axis_index("seq")
    place = block.astype(jnp.int32).reshape(1)
    start = (lax.axis_index("tp") * heads // GROUP).astype(jnp.int32).reshape(1)

    def send(x, pairs):
        return lax.ppermute(x, "seq", [(a, b % blocks) for a, b in pairs])

    everyone = range(blocks)
    swap = [(b, b ^ 1) for b in everyone]

    own_kv, docs, cumul, key, value, soft_query = fetch(
        start,
        [
            doc_ids.reshape(tokens // LANES, LANES),
            jnp.transpose(log_decay),
            flat(soft_key),
            flat(soft_value),
            flat(lin_key),
            flat(lin_value),
            flat(soft_query),
        ],
        tokens,
        heads,
        kv_here,
    )

    forward = [(b, b + 2) for b in everyone]
    beside = send(own_kv, swap)
    ahead = send(own_kv, forward)
    second = send(own_kv, [(b, b + 4) for b in everyone])

    size = quarter_rows(heads)
    others = range(1, GROUP_BLOCKS)
    sent = block_state(place, cumul, docs, key, value, tokens, heads)
    quarters = [sent[0]] + [send(sent[j], [(b, b ^ j) for b in everyone]) for j in others]

    state = {}

    def first_attention(after):
        state["wide"], state["sum"] = attend(
            place, (docs, soft_query), None, [(own_kv, (0, 0))], False, tokens, heads, kv_here, after
        )
        return state["sum"]

    def more_attention(kv, is_last, after, odd=None):
        state["sum"] = attend(
            place, (state["wide"],), state["sum"], kv, is_last, tokens, heads, kv_here, after, odd
        )
        return state["sum"]

    inner, qh = [], []

    def inner_of(part, after):
        n = heads // parts
        got = inner_part(
            cumul, docs, flat(lin_query), key, value, tokens, heads, part * n, n, after
        )
        inner.append(got[0])
        qh.append(got[1])
        return got[0]

    done = first_attention([sent[0], beside])
    if parts > 1:
        done = inner_of(0, [done])
    run, lane = group_map(place, quarters, size, [done], [ahead])
    lane_kv, cross_kv = [(lane, (2, 2)), (second, (4, 4))], [(send(lane, swap), (2, 3))]
    stages = (blocks // GROUP_BLOCKS).bit_length() - 1
    before, done = None, run
    for stage in range(stages):
        came = send(run, [(b, b ^ (GROUP_BLOCKS << stage)) for b in everyone])
        if stage == stages - 1:
            done = more_attention(lane_kv, False, [done])
            done = inner_of(parts - 1, [done])
        else:
            run, before = scan_step(place, stage + 2, run, came, before, size, [done])
            done = run
    *priors, prior_doc, own_copy, lane = prior_states(
        place, stages + 1, quarters, came, before, size, [done], [own_kv, second]
    )
    priors = [priors[0]] + [send(priors[j], [(b, b ^ j) for b in everyone]) for j in others]
    done = more_attention(cross_kv, False, [prior_doc])
    far = None
    if window % 2:
        pairs = {b: b for b in everyone}
        for b in range(1, blocks - window, 2):
            pairs[b], pairs[b + window] = b + window, b
        far = send(own_copy, list(pairs.items()))
    rest = [(send(lane, swap), (4, 5))]
    for back in range(3, window // 2 + 1):
        lane = send(lane, forward)
        rest.append((lane, (2 * back, 2 * back)))
        rest.append((send(lane, swap), (2 * back, 2 * back + 1)))
    slot = (beside if far is None else far, (blocks if far is None else window, 1))
    mixed, squares = mix(place, docs, prior_doc, cumul, inner, qh, priors, tokens, heads, [done])
    sums = [squares]
    for other in range(1, tensor):
        sums.append(lax.ppermute(squares, "tp", [(t, t ^ other) for t in range(tensor)]))
    rest, done = [slot] + rest, squares
    while rest:
        got = more_attention(rest[:2], len(rest) <= 2, [done], beside if rest[0] is slot else None)
        rest, done = rest[2:], got
    soft_out, done = got
    lin_out = finish(norm_gain, flat(lin_gate), mixed, sums, tokens, heads, [done])
    shape = (tokens, heads, HEAD_DIM)
    return lin_out.reshape(shape), soft_out.reshape(shape)


def solution(mesh):
    in_specs = (
        P("seq", "tp", None),
        P("seq", "tp", None),
        P("seq", "tp", None),
        P("seq", "tp", None),
        P("seq", "tp"),
        P("tp", None),
        P("seq"),
        P("seq", "tp", None),
        P("seq", None, None),
        P("seq", None, None),
    )
    out_specs = (P("seq", "tp", None), P("seq", "tp", None))
    return jax.shard_map(
        functools.partial(body, mesh.shape["seq"]),
        mesh=mesh,
        in_specs=in_specs,
        out_specs=out_specs,
        check_vma=False,
    )
```

```python
import functools

import jax
import jax.numpy as jnp
import numpy as np
from jax import lax
from jax.experimental import pallas as pl
from jax.experimental.pallas import tpu as pltpu
from jax.sharding import PartitionSpec as P

HEADS = 64
HEAD_DIM = 128
KV_HEADS = 8
LANES = 128
GROUP = HEADS // KV_HEADS
F32 = jnp.float32
BF16 = jnp.bfloat16
BIG = float(2**20)
SCORE_TO_EXP2 = HEAD_DIM**-0.5 * float(np.log2(np.e))
INFO = 16
HIGHEST = lax.Precision.HIGHEST

VMEM = pl.BlockSpec(memory_space=pltpu.VMEM)
SMEM = pl.BlockSpec(memory_space=pltpu.SMEM)
HBM = pl.BlockSpec(memory_space=pltpu.HBM)
ANYWHERE = pl.BlockSpec(memory_space=pl.ANY)
STATE_ROWS = HEAD_DIM + 16
CHUNK = 256
GROUP_BLOCKS = 4


def sds(shape, dtype):
    return jax.ShapeDtypeStruct(shape, dtype)


def cost(flops, bytes_accessed, transcendentals=0):
    return pl.CostEstimate(
        flops=int(flops) , bytes_accessed=int(bytes_accessed) , transcendentals=int(transcendentals)
    )


def call(kernel, name, scalars, operands, out_shape, scratch=(), mib=16, estimate=None, after=(), hbm=0, out_hbm=False, relay=()):
    begin = len(scalars) + len(operands)
    skip = len(after)
    operands = [
        pltpu.with_memory_space_constraint(x, pltpu.HBM) if i < hbm else x for i, x in enumerate(operands)
    ]
    outs = out_shape if isinstance(out_shape, tuple) else (out_shape,)
    out_specs = (VMEM,) * len(outs)
    outs = tuple(
        (pltpu.HBM if out_hbm and i == 0 else pltpu.VMEM)(x.shape, x.dtype) for i, x in enumerate(outs)
    )
    if out_hbm:
        out_specs = (HBM, *out_specs[1:])

    moved = len(relay)
    many = len(outs)
    single = not isinstance(out_shape, tuple) and not relay
    out_specs += (VMEM,) * moved
    outs += tuple(pltpu.VMEM(x.shape, x.dtype) for x in relay)

    def run(*refs):
        rest = refs[begin + skip + moved :]
        for source, target in zip(refs[begin + skip : begin + skip + moved], rest[many : many + moved]):
            target[...] = source[...]
        kernel(*refs[:begin], *rest[:many], *rest[many + moved :])

    out = pl.pallas_call(
        run,
        out_shape=outs,
        in_specs=[SMEM] * len(scalars) + [HBM] * hbm + [VMEM] * (len(operands) - hbm) + [ANYWHERE] * skip + [VMEM] * moved,
        out_specs=out_specs,
        scratch_shapes=list(scratch),
        compiler_params=pltpu.CompilerParams(vmem_limit_bytes=mib * 1024 * 1024),
        cost_estimate=estimate,
        name=name,
    )(*scalars, *operands, *after, *relay)
    return out[0] if single else out


def doc_columns(doc_rows, tokens):
    parts = []
    for i in range(tokens // LANES):
        row = jnp.broadcast_to(doc_rows[i : i + 1, :], (LANES, LANES))
        parts.append(jnp.transpose(row))
    return jnp.concatenate(parts, axis=0)


def doc_line(doc_rows, tokens):
    return jnp.concatenate([doc_rows[i : i + 1, :] for i in range(tokens // LANES)], axis=1)


def lower_triangle(tokens):
    rows = lax.broadcasted_iota(jnp.int32, (tokens, tokens), 0)
    cols = lax.broadcasted_iota(jnp.int32, (tokens, tokens), 1)
    return rows >= cols


def fetch_kernel(tokens, heads, kv_here, start_ref, *refs):
    refs = list(refs)
    take = lambda n: [refs.pop(0) for _ in range(n)]
    sources = take(6)
    kv_ref, doc_out, cumul_ref, key_out, value_out = take(5)
    held = take(4)
    sems, wide, ldp = refs
    docs_in, decays, soft_key, soft_value = held
    targets = [*held, key_out, value_out]
    copies = [
        pltpu.make_async_copy(source, target, sems.at[i])
        for i, (source, target) in enumerate(zip(sources, targets))
    ]
    for copy in copies:
        copy.start()

    copies[0].wait()
    docs = docs_in[...].astype(F32) + 1.0
    line = lax.broadcasted_iota(jnp.int32, (INFO, LANES), 0)
    info = jnp.zeros((INFO, LANES), F32)
    for i in range(tokens // LANES):
        info = jnp.where(line == i, docs[i : i + 1, :], info)
    doc_out[...] = info
    end = 2 * kv_here * tokens
    kv_ref[end : end + INFO, :] = info.astype(BF16)

    copies[1].wait()
    ldp[...] = jnp.zeros_like(ldp)
    ldp[0:heads, :] = decays[...]
    cumul_ref[...] = lax.dot_general(
        lower_triangle(tokens).astype(F32),
        ldp[...],
        (((1,), (1,)), ((), ())),
        precision=HIGHEST,
        preferred_element_type=F32,
    )

    start = start_ref[0]
    for which, ref in enumerate((soft_key, soft_value)):
        copies[2 + which].wait()
        wide[...] = ref[...].astype(F32)
        for g in range(kv_here):
            rows = wide[pl.ds(start + g, tokens, stride=KV_HEADS), :]
            at = (which * kv_here + g) * tokens
            if which:
                halves = [jnp.transpose(rows[i : i + LANES, :]) for i in range(0, tokens, LANES)]
                rows = jnp.concatenate(halves, axis=0)
            kv_ref[at : at + tokens, :] = rows.astype(BF16)
    for copy in copies[4:]:
        copy.wait()


def fetch(start, operands, tokens, heads, kv_here):
    return call(
        functools.partial(fetch_kernel, tokens, heads, kv_here),
        "fetch",
        [start],
        operands,
        (
            sds((2 * kv_here * tokens + INFO, LANES), BF16),
            sds((INFO, LANES), F32),
            sds((tokens, LANES), F32),
            sds(operands[4].shape, BF16),
            sds(operands[5].shape, BF16),
        ),
        scratch=[pltpu.VMEM(x.shape, x.dtype) for x in operands[:4]]
        + [
            pltpu.SemaphoreType.DMA((len(operands),)),
            pltpu.VMEM((tokens * KV_HEADS, LANES), F32),
            pltpu.VMEM((LANES, tokens), F32),
        ],
        estimate=cost(0, 3 * tokens * heads * LANES * 2),
        hbm=len(operands),
    )


def quarter_rows(heads):
    return heads * HEAD_DIM // GROUP_BLOCKS


def state_kernel(tokens, heads, place_ref, *refs):
    refs = list(refs)
    take = lambda n: [refs.pop(0) for _ in range(n)]
    cumul_ref, doc_ref, key_ref, value_ref = take(4)
    out_refs = take(GROUP_BLOCKS)
    kf, vf, states = refs
    cumul, docs = cumul_ref[...], doc_ref[...]
    total = cumul[tokens - 1 : tokens, :]
    last_row = tokens // LANES - 1
    first_doc = docs[0:1, 0:1]
    last_doc = docs[last_row : last_row + 1, LANES - 1 : LANES]
    tail = (doc_columns(docs, tokens) == last_doc).astype(F32)
    scale = jnp.exp(total - cumul) * tail
    kf[...] = key_ref[...].astype(F32)
    vf[...] = value_ref[...].astype(F32)
    for h in range(heads):
        keys = (kf[pl.ds(h, tokens, stride=heads), :] * scale[:, h : h + 1]).astype(BF16)
        values = vf[pl.ds(h, tokens, stride=heads), :].astype(BF16)
        states[h * HEAD_DIM : (h + 1) * HEAD_DIM, :] = lax.dot_general(
            keys, values, (((0,), (0,)), ((), ())), preferred_element_type=F32
        )
    size = quarter_rows(heads)
    mine = place_ref[0] % GROUP_BLOCKS
    for j, ref in enumerate(out_refs):
        taker = mine ^ j
        ref[0:size, :] = states[pl.ds(pl.multiple_of(taker * size, size), size), :].astype(BF16)
        totals = jnp.zeros_like(total)
        for c in range(GROUP_BLOCKS):
            skip = c * heads // GROUP_BLOCKS
            moved = pltpu.roll(total, LANES - skip, 1) if skip else total
            totals = jnp.where(taker == c, moved, totals)
        ref[size : size + INFO, :] = info_rows((*in_parts(totals), first_doc, last_doc))


def block_state(place, cumul, docs, key, value, tokens, heads):
    return call(
        functools.partial(state_kernel, tokens, heads),
        "block_state",
        [place],
        [cumul, docs, key, value],
        (sds((quarter_rows(heads) + INFO, LANES), BF16),) * GROUP_BLOCKS,
        scratch=[
            pltpu.VMEM((tokens * heads, LANES), F32),
            pltpu.VMEM((tokens * heads, LANES), F32),
            pltpu.VMEM((heads * HEAD_DIM, LANES), F32),
        ],
        estimate=cost(2 * heads * tokens * HEAD_DIM**2, 5 * tokens * heads * LANES * 2),
    )


def in_parts(x):
    hi = x.astype(BF16).astype(F32)
    mid = (x - hi).astype(BF16).astype(F32)
    return hi, mid, x - hi - mid


def info_rows(parts):
    line = lax.broadcasted_iota(jnp.int32, (INFO, LANES), 0)
    info = jnp.zeros((INFO, LANES), F32)
    for i, part in enumerate(parts):
        info = jnp.where(line == i, part, info)
    return info.astype(BF16)


def read_map(ref, size):
    info = ref[size : size + INFO, :].astype(F32)
    return info[0:1] + info[1:2] + info[2:3], info[3:4], info[4:5]


def row_chunks(size):
    unit = min(HEAD_DIM, size)
    return [(slice(i * unit, (i + 1) * unit), slice(i, i + 1)) for i in range(size // unit)]


def in_block_order(place_ref, refs, blocks):
    mine = place_ref[0] % GROUP_BLOCKS
    for j, ref in enumerate(refs):
        blocks[mine ^ j] = ref[...]


def block_maps(blocks, size):
    maps = []
    for c in range(GROUP_BLOCKS):
        info = blocks[c, size : size + INFO, :].astype(F32)
        first, last = info[3:4], info[4:5]
        gain = jnp.exp(info[0:1] + info[1:2] + info[2:3]) * (first == last).astype(F32)
        maps.append((gain, first, last))
    return maps


def group_kernel(size, place_ref, *refs):
    sources = refs[:GROUP_BLOCKS]
    out_ref, blocks = refs[GROUP_BLOCKS:]
    in_block_order(place_ref, sources, blocks)
    maps = block_maps(blocks, size)
    gains = [None]
    for (gain, first, _), (_, _, last_before) in zip(maps[1:], maps[:-1]):
        gains.append(gain * (last_before == first).astype(F32))
    for rows, lane in row_chunks(size):
        total = blocks[0, rows, :].astype(F32)
        for c in range(1, GROUP_BLOCKS):
            total = gains[c][:, lane] * total + blocks[c, rows, :].astype(F32)
        out_ref[rows, :] = total.astype(BF16)
    gain = maps[0][0] * gains[1] * gains[2] * gains[3]
    out_ref[size : size + INFO, :] = info_rows((*in_parts(gain), maps[0][1], maps[-1][2]))


def group_map(place, quarters, size, after, relay):
    return call(
        functools.partial(group_kernel, size),
        "group_map",
        [place],
        quarters,
        (sds((size + INFO, LANES), BF16),),
        scratch=[pltpu.VMEM((GROUP_BLOCKS, size + INFO, LANES), BF16)],
        estimate=cost(8 * size * LANES, 10 * size * LANES * 2),
        after=after,
        relay=relay,
    )


def scan_kernel(size, has_before, bit, place_ref, *refs):
    mine_ref, came_ref = refs[:2]
    before_ref = refs[2] if has_before else None
    run_ref, out_ref = refs[-2:]
    upper = (place_ref[0] >> bit) & 1 == 1
    gain_m, first_m, last_m = read_map(mine_ref, size)
    gain_c, first_c, last_c = read_map(came_ref, size)
    link = jnp.where(upper, (last_c == first_m).astype(F32), (last_m == first_c).astype(F32))
    gain = jnp.where(upper, gain_m, gain_c) * link
    for rows, lane in row_chunks(size):
        mine, came = mine_ref[rows, :].astype(F32), came_ref[rows, :].astype(F32)
        lower_sum, upper_sum = jnp.where(upper, came, mine), jnp.where(upper, mine, came)
        run_ref[rows, :] = (gain[:, lane] * lower_sum + upper_sum).astype(BF16)
    run_ref[size : size + INFO, :] = info_rows(
        (
            *in_parts(gain * jnp.where(upper, gain_c, gain_m)),
            jnp.where(upper, first_c, first_m),
            jnp.where(upper, last_m, last_c),
        )
    )
    if not has_before:
        out_ref[...] = jnp.where(upper, came_ref[...], jnp.zeros_like(came_ref))
        return
    gain_b, first_b, last_b = read_map(before_ref, size)
    empty = first_b == 0.0
    factor = jnp.where(empty, 1.0, gain_b * (last_c == first_b).astype(F32))
    for rows, lane in row_chunks(size):
        before = before_ref[rows, :].astype(F32)
        joined = factor[:, lane] * came_ref[rows, :].astype(F32) + before
        out_ref[rows, :] = jnp.where(upper, joined, before).astype(BF16)
    out_ref[size : size + INFO, :] = info_rows(
        (
            *in_parts(jnp.where(upper, factor * gain_c, gain_b)),
            jnp.where(upper, first_c, first_b),
            jnp.where(upper, jnp.where(empty, last_c, last_b), last_b),
        )
    )


def scan_step(place, bit, mine, came, before, size, after):
    shape = sds((size + INFO, LANES), BF16)
    before = [] if before is None else [before]
    return call(
        functools.partial(scan_kernel, size, len(before), bit),
        "scan_step",
        [place],
        [mine, came, *before],
        (shape, shape),
        estimate=cost(6 * size * LANES, 6 * size * LANES * 2),
        after=after,
    )


def prior_kernel(size, has_before, bit, place_ref, *refs):
    sources, came_ref = refs[:GROUP_BLOCKS], refs[GROUP_BLOCKS]
    before_ref = refs[GROUP_BLOCKS + 1] if has_before else None
    *out_refs, doc_ref, blocks, priors = refs[GROUP_BLOCKS + 1 + has_before :]
    mine = place_ref[0] % GROUP_BLOCKS
    in_block_order(place_ref, sources, blocks)
    maps = block_maps(blocks, size)
    upper = ((place_ref[0] >> bit) & 1).astype(F32)
    _, _, last_c = read_map(came_ref, size)
    factor, doc = jnp.broadcast_to(upper, (1, LANES)), upper * last_c
    if has_before:
        gain_b, first_b, last_b = read_map(before_ref, size)
        empty = first_b == 0.0
        factor = upper * jnp.where(empty, 1.0, gain_b * (last_c == first_b).astype(F32))
        doc = jnp.where(empty, doc, last_b)
    docs = [doc] + [last for _, _, last in maps[:-1]]
    gains = [gain * (doc == first).astype(F32) for (gain, first, _), doc in zip(maps, docs)]
    for rows, lane in row_chunks(size):
        state = factor[:, lane] * came_ref[rows, :].astype(F32)
        if has_before:
            state = state + before_ref[rows, :].astype(F32)
        for c in range(GROUP_BLOCKS):
            priors[c, rows, :] = state.astype(BF16)
            if c < GROUP_BLOCKS - 1:
                state = gains[c][:, lane] * state + blocks[c, rows, :].astype(F32)
    for j, ref in enumerate(out_refs):
        ref[...] = priors[mine ^ j]
    own_doc = docs[0]
    for c in range(1, GROUP_BLOCKS):
        own_doc = jnp.where(mine == c, docs[c], own_doc)
    doc_ref[...] = jnp.broadcast_to(own_doc, (8, LANES))


def prior_states(place, bit, quarters, came, before, size, after, relay=()):
    before = [] if before is None else [before]
    return call(
        functools.partial(prior_kernel, size, len(before), bit),
        "prior_states",
        [place],
        [*quarters, came, *before],
        (*[sds((size, LANES), BF16)] * GROUP_BLOCKS, sds((8, LANES), F32)),
        scratch=[
            pltpu.VMEM((GROUP_BLOCKS, size + INFO, LANES), BF16),
            pltpu.VMEM((GROUP_BLOCKS, size, LANES), BF16),
        ],
        estimate=cost(8 * size * LANES, 10 * size * LANES * 2),
        after=after,
        relay=relay,
    )


def some_heads(ref, tokens, heads, first, count):
    x = ref[...].astype(F32)
    if count == heads:
        return x
    return x.reshape(tokens, heads, LANES)[:, first : first + count, :].reshape(tokens * count, LANES)


def inner_kernel(tokens, heads, first, count, cumul_ref, doc_ref, query_ref, key_ref, value_ref, inner_ref, qh_ref, qf, kf, vf, mask):
    cumul = cumul_ref[...]
    cumul_t = jnp.transpose(cumul)
    docs = doc_ref[...]
    column = doc_columns(docs, tokens)
    same = jnp.concatenate([column] * (tokens // LANES), axis=1) == doc_line(docs, tokens)
    mask[...] = jnp.where(lower_triangle(tokens) & same, 0.0, -1e9)
    qf[...] = some_heads(query_ref, tokens, heads, first, count)
    kf[...] = some_heads(key_ref, tokens, heads, first, count)
    vf[...] = some_heads(value_ref, tokens, heads, first, count)
    for n in range(count):
        h = first + n
        picked = pl.ds(n, tokens, stride=count)
        query = qf[picked, :].astype(BF16)
        keys = kf[picked, :].astype(BF16)
        values = vf[picked, :].astype(BF16)
        qh_ref[n * tokens : (n + 1) * tokens, :] = query
        for i in range(tokens // LANES):
            seen = (i + 1) * LANES
            rows = slice(i * LANES, seen)
            scores = lax.dot_general(
                query[rows, :], keys[0:seen, :], (((1,), (1,)), ((), ())), preferred_element_type=F32
            )
            gap = cumul[rows, h : h + 1] - cumul_t[h : h + 1, 0:seen]
            weights = (scores * jnp.exp(gap + mask[rows, 0:seen])).astype(BF16)
            inner_ref[n * tokens + i * LANES : n * tokens + seen, :] = jnp.dot(
                weights, values[0:seen, :], preferred_element_type=F32
            )


def inner_part(cumul, docs, query, key, value, tokens, heads, first, count, after):
    return call(
        functools.partial(inner_kernel, tokens, heads, first, count),
        "inner_part",
        [],
        [cumul, docs, query, key, value],
        (sds((count * tokens, LANES), F32), sds((count * tokens, LANES), BF16)),
        scratch=[pltpu.VMEM((tokens * count, LANES), F32)] * 3 + [pltpu.VMEM((tokens, tokens), F32)],
        mib=24,
        estimate=cost(
            4 * count * tokens * tokens * HEAD_DIM, tokens * heads * LANES * 12, count * tokens * tokens
        ),
        after=after,
    )


def mix_kernel(tokens, heads, parts, place_ref, doc_ref, prior_doc_ref, cumul_ref, *refs):
    refs = list(refs)
    take = lambda n: [refs.pop(0) for _ in range(n)]
    inner, qh, quarters = take(parts), take(parts), take(GROUP_BLOCKS)
    mixed_ref, square_ref, states = refs
    size = quarter_rows(heads)
    mine = place_ref[0] % GROUP_BLOCKS
    for j, ref in enumerate(quarters):
        states[pl.ds(pl.multiple_of((mine ^ j) * size, size), size), :] = ref[...]
    is_open = (doc_columns(doc_ref[...], tokens) == prior_doc_ref[0:1, :]).astype(F32)
    gain = jnp.exp(cumul_ref[...]) * is_open
    squares = jnp.zeros((tokens, LANES), F32)
    for h in range(heads):
        part, n = divmod(h, heads // parts)
        held = slice(n * tokens, (n + 1) * tokens)
        state = states[h * HEAD_DIM : (h + 1) * HEAD_DIM, :]
        carried = jnp.dot(qh[part][held, :], state, preferred_element_type=F32)
        mixed = inner[part][held, :] + carried * gain[:, h : h + 1]
        squares = squares + mixed * mixed
        mixed_ref[pl.ds(h, tokens, stride=heads), :] = mixed
    square_ref[...] = lax.dot_general(
        jnp.ones((8, LANES), F32),
        squares,
        (((1,), (1,)), ((), ())),
        precision=HIGHEST,
        preferred_element_type=F32,
    )


def mix(place, docs, prior_doc, cumul, inner, qh, quarters, tokens, heads, after):
    return call(
        functools.partial(mix_kernel, tokens, heads, len(inner)),
        "mix",
        [place],
        [docs, prior_doc, cumul, *inner, *qh, *quarters],
        (sds((tokens * heads, LANES), F32), sds((8, tokens), F32)),
        scratch=[pltpu.VMEM((heads * HEAD_DIM, LANES), BF16)],
        mib=24,
        estimate=cost(2 * heads * tokens * HEAD_DIM**2, tokens * heads * LANES * 10),
        after=after,
    )


def finish_kernel(tokens, heads, sums, step, gain_ref, gate_ref, mixed_ref, *refs):
    squares, (out_ref, done, sems) = refs[:sums], refs[sums:]
    total = squares[0][0:1, :]
    for ref in squares[1:]:
        total = total + ref[0:1, :]
    scale = lax.rsqrt(total / (HEADS * HEAD_DIM) + 1e-06)
    rows = jnp.concatenate([scale[:, i * LANES : (i + 1) * LANES] for i in range(tokens // LANES)], axis=0)
    column = doc_columns(rows, tokens)
    copies = []
    for i in range(0, tokens, step):
        at = pl.ds(i * heads, step * heads)
        gate = jax.nn.sigmoid(gate_ref[at, :].astype(F32)).reshape(step, heads, LANES)
        mixed = mixed_ref[at, :].reshape(step, heads, LANES)
        inv = column[i : i + step, :][:, None, :]
        out = mixed * inv * gain_ref[...][None] * gate
        done[at, :] = out.reshape(step * heads, LANES).astype(BF16)
        copies.append(pltpu.make_async_copy(done.at[at, :], out_ref.at[at, :], sems.at[i // step]))
        copies[-1].start()
    for copy in copies:
        copy.wait()


def finish(gain, gate, mixed, squares, tokens, heads, after):
    step = 64
    return call(
        functools.partial(finish_kernel, tokens, heads, len(squares), step),
        "finish",
        [],
        [gain, gate, mixed, *squares],
        sds((tokens * heads, LANES), BF16),
        scratch=[pltpu.VMEM((tokens * heads, LANES), BF16), pltpu.SemaphoreType.DMA((tokens // step,))],
        estimate=cost(0, tokens * heads * LANES * 8, tokens * heads * LANES),
        after=after,
        out_hbm=True,
    )


def attend_kernel(tokens, heads, kv_here, least, is_first, is_last, unroll, place_ref, *refs):
    refs = list(refs)
    take = lambda n: [refs.pop(0) for _ in range(n)]
    per_group = heads // kv_here
    rows = tokens * per_group
    step = CHUNK // per_group
    if is_first:
        doc_ref, query_ref = take(2)
    else:
        wide_ref, state_ref = take(2)
    kv = take(len(least))
    if is_first:
        wide_ref = take(1)[0]
    out_ref = take(1)[0]
    if is_last:
        take(1)[0][...] = jnp.zeros((8, LANES), F32)
    bias = take(1)[0]
    if is_first:
        doc_rep = take(1)[0]
    if is_last:
        done, sems = take(2)
    block = place_ref[0]

    lane = lax.broadcasted_iota(jnp.int32, (tokens, LANES), 1).astype(F32)
    end = 2 * kv_here * tokens
    for j, ref in enumerate(kv):
        valid = (block >= jnp.where(block % 2 == 0, *least[j])).astype(F32)
        docs = doc_columns(ref[end : end + INFO, :].astype(F32) * valid, tokens)
        bias[j] = jnp.where(docs == lane, 0.0, -BIG).astype(BF16)
    if is_first:
        column = doc_columns(doc_ref[...], tokens)
        for h in range(per_group):
            doc_rep[pl.ds(h, tokens, stride=per_group), :] = (column == lane).astype(F32)
    ones = jnp.ones((STATE_ROWS - HEAD_DIM, tokens), BF16)

    def some_chunks(i, carry):
        chains = [(u, g) for u in range(unroll) for g in range(kv_here)]
        chunk = [i * unroll + u for u in range(unroll)]
        at = [pl.ds(pl.multiple_of(c * CHUNK, CHUNK), CHUNK) for c in chunk]
        picked = [pl.ds(pl.multiple_of(c * (step * heads), step * heads), step * heads) for c in chunk]
        scores, results = {}, {}

        def begin(u, g):
            if is_first:
                query = query_ref[picked[u], :].astype(F32).reshape(step, heads, LANES)
                query = query[:, g * per_group : (g + 1) * per_group, :].reshape(CHUNK, LANES)
                wide = jnp.concatenate([query.astype(BF16), doc_rep[at[u], :].astype(BF16)], axis=1)
                wide_ref[g, at[u], :] = wide
            else:
                wide = wide_ref[g, at[u], :]
            out = []
            for j, ref in enumerate(kv):
                keys = jnp.concatenate([ref[g * tokens : (g + 1) * tokens, :], bias[j]], axis=1)
                out.append(
                    lax.dot_general(keys, wide, (((1,), (1,)), ((), ())), preferred_element_type=F32)
                )
            if is_first:
                token = chunk[u] * step + lax.broadcasted_iota(jnp.int32, (tokens, CHUNK), 1) // per_group
                key_at = lax.broadcasted_iota(jnp.int32, (tokens, CHUNK), 0)
                out[0] = jnp.where(key_at <= token, out[0], -BIG)
            scores[u, g] = out

        def end_chain(u, g):
            here = scores.pop((u, g))
            top = jnp.max(here[0], axis=0, keepdims=True)
            for score in here[1:]:
                top = jnp.maximum(top, jnp.max(score, axis=0, keepdims=True))
            total = None
            if not is_first:
                before = state_ref[g, :, at[u]]
                top_before = before[STATE_ROWS - 1 : STATE_ROWS, :]
                top = jnp.maximum(top, top_before)
                total = before * jnp.exp2((top_before - top) * SCORE_TO_EXP2)
            for ref, score in zip(kv, here):
                weights = jnp.exp2((score - top) * SCORE_TO_EXP2).astype(BF16)
                first = (kv_here + g) * tokens
                parts = [ref[first + p : first + p + LANES, :] for p in range(0, tokens, LANES)]
                values = jnp.concatenate([jnp.concatenate(parts, axis=1), ones], axis=0)
                more = jnp.dot(values, weights, preferred_element_type=F32)
                total = more if total is None else total + more
            if is_last:
                results[u, g] = jnp.transpose(total[0:HEAD_DIM] / total[HEAD_DIM : HEAD_DIM + 1])
            else:
                out_ref[g, 0 : STATE_ROWS - 8, at[u]] = total[0 : STATE_ROWS - 8]
                out_ref[g, STATE_ROWS - 8 : STATE_ROWS, at[u]] = jnp.broadcast_to(top, (8, CHUNK))

        ahead = 2
        for n in range(len(chains) + ahead):
            if n < len(chains):
                begin(*chains[n])
            if n >= ahead:
                end_chain(*chains[n - ahead])
        if is_last:
            for u in range(unroll):
                result = [results[u, g] for g in range(kv_here)]
                if kv_here > 1:
                    result = [r.reshape(step, per_group, LANES) for r in result]
                    result = [jnp.concatenate(result, axis=1).reshape(step * heads, LANES)]
                done[picked[u], :] = result[0].astype(BF16)
                pltpu.make_async_copy(
                    done.at[picked[u], :], out_ref.at[picked[u], :], sems.at[chunk[u]]
                ).start()
        return carry

    lax.fori_loop(0, rows // (CHUNK * unroll), some_chunks, 0)
    if is_last:
        for c in range(rows // CHUNK):
            at = pl.ds(c * step * heads, step * heads)
            pltpu.make_async_copy(done.at[at, :], out_ref.at[at, :], sems.at[c]).wait()


def attend(place, first, state, kv, is_last, tokens, heads, kv_here, after, relay=()):
    is_first = state is None
    least = tuple(pair for _, pair in kv)
    kv = [block for block, _ in kv]
    blocks = len(kv)
    rows = tokens * heads // kv_here
    unroll = min(4, rows // CHUNK)
    wide_shape = sds((kv_here, rows, 2 * LANES), BF16)
    state_shape = sds((kv_here, STATE_ROWS, rows), F32)
    out_shape = sds((tokens * heads, LANES), BF16) if is_last else state_shape
    scratch = [pltpu.VMEM((blocks, tokens, LANES), BF16)]
    if is_first:
        out_shape = (wide_shape, out_shape)
        scratch.append(pltpu.VMEM((rows, LANES), F32))
    if is_last:
        out_shape = (out_shape, sds((8, LANES), F32))
        scratch.append(pltpu.VMEM((tokens * heads, LANES), BF16))
        scratch.append(pltpu.SemaphoreType.DMA((rows // CHUNK,)))
    span = blocks * tokens
    return call(
        functools.partial(attend_kernel, tokens, heads, kv_here, least, is_first, is_last, unroll),
        "attend",
        [place],
        [*first, *([] if is_first else [state]), *kv],
        out_shape,
        scratch=scratch,
        mib=24,
        estimate=cost(
            4 * tokens * heads * span * 2 * LANES, 4 * tokens * heads * LANES * 4, tokens * heads * span
        ),
        after=after,
        out_hbm=is_last,
        relay=relay,
    )


def body(
    blocks,
    lin_query,
    lin_key,
    lin_value,
    lin_gate,
    log_decay,
    norm_gain,
    doc_ids,
    soft_query,
    soft_key,
    soft_value,
):
    tokens, heads, _ = lin_query.shape
    tensor = HEADS // heads
    kv_here = max(1, heads // GROUP)
    parts = 2 if heads % 16 == 0 else 1
    longest = blocks * tokens * 5 // 8
    window = min(blocks - 1, (longest - 1 + tokens - 1) // tokens)
    flat = lambda x: x.reshape(-1, LANES)
    block = lax.axis_index("seq")
    place = block.astype(jnp.int32).reshape(1)
    start = (lax.axis_index("tp") * heads // GROUP).astype(jnp.int32).reshape(1)

    def send(x, pairs):
        return lax.ppermute(x, "seq", [(a, b % blocks) for a, b in pairs])

    everyone = range(blocks)
    swap = [(b, b ^ 1) for b in everyone]

    own_kv, docs, cumul, key, value = fetch(
        start,
        [
            doc_ids.reshape(tokens // LANES, LANES),
            jnp.transpose(log_decay),
            flat(soft_key),
            flat(soft_value),
            flat(lin_key),
            flat(lin_value),
        ],
        tokens,
        heads,
        kv_here,
    )

    forward = [(b, b + 2) for b in everyone]
    pairs = [(b, b + 1) for b in everyone if b % 2 == 0]
    longest_hop = [b for b in everyone if b % 2 and b + window < blocks] if window % 2 else []
    pairs += [(b, b + window) for b in longest_hop]
    taken = [b + window for b in longest_hop]
    pairs += [(b, b - 1) for b in everyone if b % 2 and b not in longest_hop and b - 1 not in taken]
    beside = (send(own_kv, pairs), (window if window % 2 else blocks, 1))
    ahead = send(own_kv, forward)

    size = quarter_rows(heads)
    others = range(1, GROUP_BLOCKS)
    sent = block_state(place, cumul, docs, key, value, tokens, heads)
    quarters = [sent[0]] + [send(sent[j], [(b, b ^ j) for b in everyone]) for j in others]

    state = {}

    def first_attention(after, relay):
        state["wide"], *out = attend(
            place, (docs, flat(soft_query)), None, [(own_kv, (0, 0))], False, tokens, heads, kv_here, after, relay
        )
        state["sum"] = out[0]
        return out

    def more_attention(kv, is_last, after, relay=()):
        out = attend(
            place, (state["wide"],), state["sum"], kv, is_last, tokens, heads, kv_here, after, relay
        )
        state["sum"] = out[0] if relay else out
        return out

    inner, qh = [], []

    def inner_of(part, after):
        n = heads // parts
        got = inner_part(
            cumul, docs, flat(lin_query), key, value, tokens, heads, part * n, n, after
        )
        inner.append(got[0])
        qh.append(got[1])
        return got[0]

    done, lane = first_attention([sent[0], beside[0]], [ahead])
    second = send(lane, [(b, b + 2) for b in range(2, blocks - 2)])
    if parts > 1:
        done = inner_of(0, [done])
    run, lane = group_map(place, quarters, size, [done], [lane])
    first_cross = send(lane, swap)
    stages = (blocks // GROUP_BLOCKS).bit_length() - 1
    before, done = None, run
    for stage in range(stages):
        came = send(run, [(b, b ^ (GROUP_BLOCKS << stage)) for b in everyone])
        if stage == stages - 1:
            done = more_attention([beside, (lane, (2, 2))], False, [done])
            done = inner_of(parts - 1, [done])
        else:
            run, before = scan_step(place, stage + 2, run, came, before, size, [done])
            done = run
    *priors, prior_doc, lane = prior_states(
        place, stages + 1, quarters, came, before, size, [done], [second]
    )
    priors = [priors[0]] + [send(priors[j], [(b, b ^ j) for b in everyone]) for j in others]
    done = more_attention([(first_cross, (2, 3)), (lane, (4, 4))], False, [prior_doc])
    rest = [(send(lane, swap), (4, 5))]
    for back in range(3, window // 2 + 1):
        lane = send(lane, forward)
        rest.append((lane, (2 * back, 2 * back)))
        rest.append((send(lane, swap), (2 * back, 2 * back + 1)))
    mixed, squares = mix(place, docs, prior_doc, cumul, inner, qh, priors, tokens, heads, [done])
    sums = [squares]
    for other in range(1, tensor):
        sums.append(lax.ppermute(squares, "tp", [(t, t ^ other) for t in range(tensor)]))
    done = squares
    while rest:
        got = more_attention(rest[:2], len(rest) <= 2, [done])
        rest, done = rest[2:], got
    soft_out, done = got
    lin_out = finish(norm_gain, flat(lin_gate), mixed, sums, tokens, heads, [done])
    shape = (tokens, heads, HEAD_DIM)
    return lin_out.reshape(shape), soft_out.reshape(shape)


def solution(mesh):
    in_specs = (
        P("seq", "tp", None),
        P("seq", "tp", None),
        P("seq", "tp", None),
        P("seq", "tp", None),
        P("seq", "tp"),
        P("tp", None),
        P("seq"),
        P("seq", "tp", None),
        P("seq", None, None),
        P("seq", None, None),
    )
    out_specs = (P("seq", "tp", None), P("seq", "tp", None))
    return jax.shard_map(
        functools.partial(body, mesh.shape["seq"]),
        mesh=mesh,
        in_specs=in_specs,
        out_specs=out_specs,
        check_vma=False,
    )
```

```python
import functools

import jax
import jax.numpy as jnp
import numpy as np
from jax import lax
from jax.experimental import pallas as pl
from jax.experimental.pallas import tpu as pltpu
from jax.sharding import PartitionSpec as P

HEADS = 64
HEAD_DIM = 128
KV_HEADS = 8
LANES = 128
GROUP = HEADS // KV_HEADS
F32 = jnp.float32
BF16 = jnp.bfloat16
BIG = float(2**20)
SCORE_TO_EXP2 = HEAD_DIM**-0.5 * float(np.log2(np.e))
INFO = 16
HIGHEST = lax.Precision.HIGHEST

VMEM = pl.BlockSpec(memory_space=pltpu.VMEM)
SMEM = pl.BlockSpec(memory_space=pltpu.SMEM)
HBM = pl.BlockSpec(memory_space=pltpu.HBM)
ANYWHERE = pl.BlockSpec(memory_space=pl.ANY)
STATE_ROWS = HEAD_DIM + 16
CHUNK = 256
GROUP_BLOCKS = 4


def sds(shape, dtype):
    return jax.ShapeDtypeStruct(shape, dtype)


def cost(flops, bytes_accessed, transcendentals=0):
    return pl.CostEstimate(
        flops=int(flops), bytes_accessed=int(bytes_accessed), transcendentals=int(transcendentals)
    )


def call(kernel, name, scalars, operands, out_shape, scratch=(), mib=16, estimate=None, after=(), hbm=0, out_hbm=False, relay=()):
    begin = len(scalars) + len(operands)
    skip = len(after)
    operands = [
        pltpu.with_memory_space_constraint(x, pltpu.HBM) if i < hbm else x for i, x in enumerate(operands)
    ]
    outs = out_shape if isinstance(out_shape, tuple) else (out_shape,)
    out_specs = (VMEM,) * len(outs)
    outs = tuple(
        (pltpu.HBM if out_hbm and i == 0 else pltpu.VMEM)(x.shape, x.dtype) for i, x in enumerate(outs)
    )
    if out_hbm:
        out_specs = (HBM, *out_specs[1:])

    moved = len(relay)
    many = len(outs)
    single = not isinstance(out_shape, tuple) and not relay
    out_specs += (VMEM,) * moved
    outs += tuple(pltpu.VMEM(x.shape, x.dtype) for x in relay)

    def run(*refs):
        rest = refs[begin + skip + moved :]
        for source, target in zip(refs[begin + skip : begin + skip + moved], rest[many : many + moved]):
            target[...] = source[...]
        kernel(*refs[:begin], *rest[:many], *rest[many + moved :])

    out = pl.pallas_call(
        run,
        out_shape=outs,
        in_specs=[SMEM] * len(scalars) + [HBM] * hbm + [VMEM] * (len(operands) - hbm) + [ANYWHERE] * skip + [VMEM] * moved,
        out_specs=out_specs,
        scratch_shapes=list(scratch),
        compiler_params=pltpu.CompilerParams(vmem_limit_bytes=mib * 1024 * 1024),
        cost_estimate=estimate,
        name=name,
    )(*scalars, *operands, *after, *relay)
    return out[0] if single else out


def doc_columns(doc_rows, tokens):
    parts = []
    for i in range(tokens // LANES):
        row = jnp.broadcast_to(doc_rows[i : i + 1, :], (LANES, LANES))
        parts.append(jnp.transpose(row))
    return jnp.concatenate(parts, axis=0)


def doc_line(doc_rows, tokens):
    return jnp.concatenate([doc_rows[i : i + 1, :] for i in range(tokens // LANES)], axis=1)


def lower_triangle(tokens):
    rows = lax.broadcasted_iota(jnp.int32, (tokens, tokens), 0)
    cols = lax.broadcasted_iota(jnp.int32, (tokens, tokens), 1)
    return rows >= cols


def fetch_kernel(tokens, heads, kv_here, start_ref, *refs):
    refs = list(refs)
    take = lambda n: [refs.pop(0) for _ in range(n)]
    sources = take(6)
    kv_ref, doc_out, cumul_ref, key_out, value_out = take(5)
    held = take(4)
    sems, wide, ldp = refs
    docs_in, decays, soft_key, soft_value = held
    targets = [*held, key_out, value_out]
    copies = [
        pltpu.make_async_copy(source, target, sems.at[i])
        for i, (source, target) in enumerate(zip(sources, targets))
    ]
    for copy in copies:
        copy.start()

    copies[0].wait()
    docs = docs_in[...].astype(F32) + 1.0
    line = lax.broadcasted_iota(jnp.int32, (INFO, LANES), 0)
    info = jnp.zeros((INFO, LANES), F32)
    for i in range(tokens // LANES):
        info = jnp.where(line == i, docs[i : i + 1, :], info)
    doc_out[...] = info
    end = 2 * kv_here * tokens
    kv_ref[end : end + INFO, :] = info.astype(BF16)

    copies[1].wait()
    ldp[...] = jnp.zeros_like(ldp)
    ldp[0:heads, :] = decays[...]
    cumul_ref[...] = lax.dot_general(
        lower_triangle(tokens).astype(F32),
        ldp[...],
        (((1,), (1,)), ((), ())),
        precision=HIGHEST,
        preferred_element_type=F32,
    )

    start = start_ref[0]
    for which, ref in enumerate((soft_key, soft_value)):
        copies[2 + which].wait()
        wide[...] = ref[...].astype(F32)
        for g in range(kv_here):
            rows = wide[pl.ds(start + g, tokens, stride=KV_HEADS), :]
            at = (which * kv_here + g) * tokens
            if which:
                halves = [jnp.transpose(rows[i : i + LANES, :]) for i in range(0, tokens, LANES)]
                rows = jnp.concatenate(halves, axis=0)
            kv_ref[at : at + tokens, :] = rows.astype(BF16)
    for copy in copies[4:]:
        copy.wait()


def fetch(start, operands, tokens, heads, kv_here):
    return call(
        functools.partial(fetch_kernel, tokens, heads, kv_here),
        "fetch",
        [start],
        operands,
        (
            sds((2 * kv_here * tokens + INFO, LANES), BF16),
            sds((INFO, LANES), F32),
            sds((tokens, LANES), F32),
            sds(operands[4].shape, BF16),
            sds(operands[5].shape, BF16),
        ),
        scratch=[pltpu.VMEM(x.shape, x.dtype) for x in operands[:4]]
        + [
            pltpu.SemaphoreType.DMA((len(operands),)),
            pltpu.VMEM((tokens * KV_HEADS, LANES), F32),
            pltpu.VMEM((LANES, tokens), F32),
        ],
        estimate=cost(0, 3 * tokens * heads * LANES * 2),
        hbm=len(operands),
    )


def quarter_rows(heads):
    return heads * HEAD_DIM // GROUP_BLOCKS


def state_kernel(tokens, heads, place_ref, *refs):
    refs = list(refs)
    take = lambda n: [refs.pop(0) for _ in range(n)]
    cumul_ref, doc_ref, key_ref, value_ref = take(4)
    out_refs = take(GROUP_BLOCKS)
    kf, vf, states = refs
    cumul, docs = cumul_ref[...], doc_ref[...]
    total = cumul[tokens - 1 : tokens, :]
    last_row = tokens // LANES - 1
    first_doc = docs[0:1, 0:1]
    last_doc = docs[last_row : last_row + 1, LANES - 1 : LANES]
    tail = (doc_columns(docs, tokens) == last_doc).astype(F32)
    scale = jnp.exp(total - cumul) * tail
    kf[...] = key_ref[...].astype(F32)
    vf[...] = value_ref[...].astype(F32)
    for h in range(heads):
        keys = (kf[pl.ds(h, tokens, stride=heads), :] * scale[:, h : h + 1]).astype(BF16)
        values = vf[pl.ds(h, tokens, stride=heads), :].astype(BF16)
        states[h * HEAD_DIM : (h + 1) * HEAD_DIM, :] = lax.dot_general(
            keys, values, (((0,), (0,)), ((), ())), preferred_element_type=F32
        )
    size = quarter_rows(heads)
    mine = place_ref[0] % GROUP_BLOCKS
    for j, ref in enumerate(out_refs):
        taker = mine ^ j
        ref[0:size, :] = states[pl.ds(pl.multiple_of(taker * size, size), size), :].astype(BF16)
        totals = jnp.zeros_like(total)
        for c in range(GROUP_BLOCKS):
            skip = c * heads // GROUP_BLOCKS
            moved = pltpu.roll(total, LANES - skip, 1) if skip else total
            totals = jnp.where(taker == c, moved, totals)
        ref[size : size + INFO, :] = info_rows((*in_parts(totals), first_doc, last_doc))


def block_state(place, cumul, docs, key, value, tokens, heads):
    return call(
        functools.partial(state_kernel, tokens, heads),
        "block_state",
        [place],
        [cumul, docs, key, value],
        (sds((quarter_rows(heads) + INFO, LANES), BF16),) * GROUP_BLOCKS,
        scratch=[
            pltpu.VMEM((tokens * heads, LANES), F32),
            pltpu.VMEM((tokens * heads, LANES), F32),
            pltpu.VMEM((heads * HEAD_DIM, LANES), F32),
        ],
        estimate=cost(2 * heads * tokens * HEAD_DIM**2, 5 * tokens * heads * LANES * 2),
    )


def in_parts(x):
    hi = x.astype(BF16).astype(F32)
    mid = (x - hi).astype(BF16).astype(F32)
    return hi, mid, x - hi - mid


def info_rows(parts):
    line = lax.broadcasted_iota(jnp.int32, (INFO, LANES), 0)
    info = jnp.zeros((INFO, LANES), F32)
    for i, part in enumerate(parts):
        info = jnp.where(line == i, part, info)
    return info.astype(BF16)


def read_map(ref, size):
    info = ref[size : size + INFO, :].astype(F32)
    return info[0:1] + info[1:2] + info[2:3], info[3:4], info[4:5]


def row_chunks(size):
    unit = min(HEAD_DIM, size)
    return [(slice(i * unit, (i + 1) * unit), slice(i, i + 1)) for i in range(size // unit)]


def in_block_order(place_ref, refs, blocks):
    mine = place_ref[0] % GROUP_BLOCKS
    for j, ref in enumerate(refs):
        blocks[mine ^ j] = ref[...]


def block_maps(blocks, size):
    maps = []
    for c in range(GROUP_BLOCKS):
        info = blocks[c, size : size + INFO, :].astype(F32)
        first, last = info[3:4], info[4:5]
        gain = jnp.exp(info[0:1] + info[1:2] + info[2:3]) * (first == last).astype(F32)
        maps.append((gain, first, last))
    return maps


def group_kernel(size, place_ref, *refs):
    sources = refs[:GROUP_BLOCKS]
    out_ref, blocks = refs[GROUP_BLOCKS:]
    in_block_order(place_ref, sources, blocks)
    maps = block_maps(blocks, size)
    gains = [None]
    for (gain, first, _), (_, _, last_before) in zip(maps[1:], maps[:-1]):
        gains.append(gain * (last_before == first).astype(F32))
    for rows, lane in row_chunks(size):
        total = blocks[0, rows, :].astype(F32)
        for c in range(1, GROUP_BLOCKS):
            total = gains[c][:, lane] * total + blocks[c, rows, :].astype(F32)
        out_ref[rows, :] = total.astype(BF16)
    gain = maps[0][0] * gains[1] * gains[2] * gains[3]
    out_ref[size : size + INFO, :] = info_rows((*in_parts(gain), maps[0][1], maps[-1][2]))


def group_map(place, quarters, size, after, relay):
    return call(
        functools.partial(group_kernel, size),
        "group_map",
        [place],
        quarters,
        (sds((size + INFO, LANES), BF16),),
        scratch=[pltpu.VMEM((GROUP_BLOCKS, size + INFO, LANES), BF16)],
        estimate=cost(8 * size * LANES, 10 * size * LANES * 2),
        after=after,
        relay=relay,
    )


def scan_kernel(size, has_before, bit, place_ref, *refs):
    mine_ref, came_ref = refs[:2]
    before_ref = refs[2] if has_before else None
    run_ref, out_ref = refs[-2:]
    upper = (place_ref[0] >> bit) & 1 == 1
    gain_m, first_m, last_m = read_map(mine_ref, size)
    gain_c, first_c, last_c = read_map(came_ref, size)
    link = jnp.where(upper, (last_c == first_m).astype(F32), (last_m == first_c).astype(F32))
    gain = jnp.where(upper, gain_m, gain_c) * link
    for rows, lane in row_chunks(size):
        mine, came = mine_ref[rows, :].astype(F32), came_ref[rows, :].astype(F32)
        lower_sum, upper_sum = jnp.where(upper, came, mine), jnp.where(upper, mine, came)
        run_ref[rows, :] = (gain[:, lane] * lower_sum + upper_sum).astype(BF16)
    run_ref[size : size + INFO, :] = info_rows(
        (
            *in_parts(gain * jnp.where(upper, gain_c, gain_m)),
            jnp.where(upper, first_c, first_m),
            jnp.where(upper, last_m, last_c),
        )
    )
    if not has_before:
        out_ref[...] = jnp.where(upper, came_ref[...], jnp.zeros_like(came_ref))
        return
    gain_b, first_b, last_b = read_map(before_ref, size)
    empty = first_b == 0.0
    factor = jnp.where(empty, 1.0, gain_b * (last_c == first_b).astype(F32))
    for rows, lane in row_chunks(size):
        before = before_ref[rows, :].astype(F32)
        joined = factor[:, lane] * came_ref[rows, :].astype(F32) + before
        out_ref[rows, :] = jnp.where(upper, joined, before).astype(BF16)
    out_ref[size : size + INFO, :] = info_rows(
        (
            *in_parts(jnp.where(upper, factor * gain_c, gain_b)),
            jnp.where(upper, first_c, first_b),
            jnp.where(upper, jnp.where(empty, last_c, last_b), last_b),
        )
    )


def scan_step(place, bit, mine, came, before, size, after):
    shape = sds((size + INFO, LANES), BF16)
    before = [] if before is None else [before]
    return call(
        functools.partial(scan_kernel, size, len(before), bit),
        "scan_step",
        [place],
        [mine, came, *before],
        (shape, shape),
        estimate=cost(6 * size * LANES, 6 * size * LANES * 2),
        after=after,
    )


def prior_kernel(size, has_before, bit, place_ref, *refs):
    sources, came_ref = refs[:GROUP_BLOCKS], refs[GROUP_BLOCKS]
    before_ref = refs[GROUP_BLOCKS + 1] if has_before else None
    *out_refs, doc_ref, blocks, priors = refs[GROUP_BLOCKS + 1 + has_before :]
    mine = place_ref[0] % GROUP_BLOCKS
    in_block_order(place_ref, sources, blocks)
    maps = block_maps(blocks, size)
    upper = ((place_ref[0] >> bit) & 1).astype(F32)
    _, _, last_c = read_map(came_ref, size)
    factor, doc = jnp.broadcast_to(upper, (1, LANES)), upper * last_c
    if has_before:
        gain_b, first_b, last_b = read_map(before_ref, size)
        empty = first_b == 0.0
        factor = upper * jnp.where(empty, 1.0, gain_b * (last_c == first_b).astype(F32))
        doc = jnp.where(empty, doc, last_b)
    docs = [doc] + [last for _, _, last in maps[:-1]]
    gains = [gain * (doc == first).astype(F32) for (gain, first, _), doc in zip(maps, docs)]
    for rows, lane in row_chunks(size):
        state = factor[:, lane] * came_ref[rows, :].astype(F32)
        if has_before:
            state = state + before_ref[rows, :].astype(F32)
        for c in range(GROUP_BLOCKS):
            priors[c, rows, :] = state.astype(BF16)
            if c < GROUP_BLOCKS - 1:
                state = gains[c][:, lane] * state + blocks[c, rows, :].astype(F32)
    for j, ref in enumerate(out_refs):
        ref[...] = priors[mine ^ j]
    own_doc = docs[0]
    for c in range(1, GROUP_BLOCKS):
        own_doc = jnp.where(mine == c, docs[c], own_doc)
    doc_ref[...] = jnp.broadcast_to(own_doc, (8, LANES))


def prior_states(place, bit, quarters, came, before, size, after, relay=()):
    before = [] if before is None else [before]
    return call(
        functools.partial(prior_kernel, size, len(before), bit),
        "prior_states",
        [place],
        [*quarters, came, *before],
        (*[sds((size, LANES), BF16)] * GROUP_BLOCKS, sds((8, LANES), F32)),
        scratch=[
            pltpu.VMEM((GROUP_BLOCKS, size + INFO, LANES), BF16),
            pltpu.VMEM((GROUP_BLOCKS, size, LANES), BF16),
        ],
        estimate=cost(8 * size * LANES, 10 * size * LANES * 2),
        after=after,
        relay=relay,
    )


def some_heads(ref, tokens, heads, first, count):
    x = ref[...].astype(F32)
    if count == heads:
        return x
    return x.reshape(tokens, heads, LANES)[:, first : first + count, :].reshape(tokens * count, LANES)


def inner_kernel(tokens, heads, first, count, cumul_ref, doc_ref, query_ref, key_ref, value_ref, inner_ref, qh_ref, qf, kf, vf, mask):
    cumul = cumul_ref[...]
    cumul_t = jnp.transpose(cumul)
    docs = doc_ref[...]
    column = doc_columns(docs, tokens)
    same = jnp.concatenate([column] * (tokens // LANES), axis=1) == doc_line(docs, tokens)
    mask[...] = jnp.where(lower_triangle(tokens) & same, 0.0, -1e9)
    qf[...] = some_heads(query_ref, tokens, heads, first, count)
    kf[...] = some_heads(key_ref, tokens, heads, first, count)
    vf[...] = some_heads(value_ref, tokens, heads, first, count)
    for n in range(count):
        h = first + n
        picked = pl.ds(n, tokens, stride=count)
        query = qf[picked, :].astype(BF16)
        keys = kf[picked, :].astype(BF16)
        values = vf[picked, :].astype(BF16)
        qh_ref[n * tokens : (n + 1) * tokens, :] = query
        for i in range(tokens // LANES):
            seen = (i + 1) * LANES
            rows = slice(i * LANES, seen)
            scores = lax.dot_general(
                query[rows, :], keys[0:seen, :], (((1,), (1,)), ((), ())), preferred_element_type=F32
            )
            gap = cumul[rows, h : h + 1] - cumul_t[h : h + 1, 0:seen]
            weights = (scores * jnp.exp(gap + mask[rows, 0:seen])).astype(BF16)
            inner_ref[n * tokens + i * LANES : n * tokens + seen, :] = jnp.dot(
                weights, values[0:seen, :], preferred_element_type=F32
            )


def inner_part(cumul, docs, query, key, value, tokens, heads, first, count, after):
    return call(
        functools.partial(inner_kernel, tokens, heads, first, count),
        "inner_part",
        [],
        [cumul, docs, query, key, value],
        (sds((count * tokens, LANES), F32), sds((count * tokens, LANES), BF16)),
        scratch=[pltpu.VMEM((tokens * count, LANES), F32)] * 3 + [pltpu.VMEM((tokens, tokens), F32)],
        mib=24,
        estimate=cost(
            4 * count * tokens * tokens * HEAD_DIM, tokens * heads * LANES * 12, count * tokens * tokens
        ),
        after=after,
    )


def mix_kernel(tokens, heads, parts, place_ref, doc_ref, prior_doc_ref, cumul_ref, *refs):
    refs = list(refs)
    take = lambda n: [refs.pop(0) for _ in range(n)]
    inner, qh, quarters = take(parts), take(parts), take(GROUP_BLOCKS)
    mixed_ref, square_ref, states = refs
    size = quarter_rows(heads)
    mine = place_ref[0] % GROUP_BLOCKS
    for j, ref in enumerate(quarters):
        states[pl.ds(pl.multiple_of((mine ^ j) * size, size), size), :] = ref[...]
    is_open = (doc_columns(doc_ref[...], tokens) == prior_doc_ref[0:1, :]).astype(F32)
    gain = jnp.exp(cumul_ref[...]) * is_open
    squares = jnp.zeros((tokens, LANES), F32)
    for h in range(heads):
        part, n = divmod(h, heads // parts)
        held = slice(n * tokens, (n + 1) * tokens)
        state = states[h * HEAD_DIM : (h + 1) * HEAD_DIM, :]
        carried = jnp.dot(qh[part][held, :], state, preferred_element_type=F32)
        mixed = inner[part][held, :] + carried * gain[:, h : h + 1]
        squares = squares + mixed * mixed
        mixed_ref[pl.ds(h, tokens, stride=heads), :] = mixed
    square_ref[...] = lax.dot_general(
        jnp.ones((8, LANES), F32),
        squares,
        (((1,), (1,)), ((), ())),
        precision=HIGHEST,
        preferred_element_type=F32,
    )


def mix(place, docs, prior_doc, cumul, inner, qh, quarters, tokens, heads, after):
    return call(
        functools.partial(mix_kernel, tokens, heads, len(inner)),
        "mix",
        [place],
        [docs, prior_doc, cumul, *inner, *qh, *quarters],
        (sds((tokens * heads, LANES), F32), sds((8, tokens), F32)),
        scratch=[pltpu.VMEM((heads * HEAD_DIM, LANES), BF16)],
        mib=24,
        estimate=cost(2 * heads * tokens * HEAD_DIM**2, tokens * heads * LANES * 10),
        after=after,
    )


def finish_kernel(tokens, heads, sums, step, gain_ref, gate_ref, mixed_ref, *refs):
    squares, (out_ref, done, sems) = refs[:sums], refs[sums:]
    total = squares[0][0:1, :]
    for ref in squares[1:]:
        total = total + ref[0:1, :]
    scale = lax.rsqrt(total / (HEADS * HEAD_DIM) + 1e-06)
    rows = jnp.concatenate([scale[:, i * LANES : (i + 1) * LANES] for i in range(tokens // LANES)], axis=0)
    column = doc_columns(rows, tokens)
    copies = []
    for i in range(0, tokens, step):
        at = pl.ds(i * heads, step * heads)
        gate = jax.nn.sigmoid(gate_ref[at, :].astype(F32)).reshape(step, heads, LANES)
        mixed = mixed_ref[at, :].reshape(step, heads, LANES)
        inv = column[i : i + step, :][:, None, :]
        out = mixed * inv * gain_ref[...][None] * gate
        done[at, :] = out.reshape(step * heads, LANES).astype(BF16)
        copies.append(pltpu.make_async_copy(done.at[at, :], out_ref.at[at, :], sems.at[i // step]))
        copies[-1].start()
    for copy in copies:
        copy.wait()


def finish(gain, gate, mixed, squares, tokens, heads, after):
    step = 64
    return call(
        functools.partial(finish_kernel, tokens, heads, len(squares), step),
        "finish",
        [],
        [gain, gate, mixed, *squares],
        sds((tokens * heads, LANES), BF16),
        scratch=[pltpu.VMEM((tokens * heads, LANES), BF16), pltpu.SemaphoreType.DMA((tokens // step,))],
        estimate=cost(0, tokens * heads * LANES * 8, tokens * heads * LANES),
        after=after,
        out_hbm=True,
    )


def attend_kernel(tokens, heads, kv_here, least, is_first, is_last, unroll, place_ref, *refs):
    refs = list(refs)
    take = lambda n: [refs.pop(0) for _ in range(n)]
    per_group = heads // kv_here
    rows = tokens * per_group
    step = CHUNK // per_group
    if is_first:
        doc_ref, query_ref = take(2)
    else:
        wide_ref, state_ref = take(2)
    kv = take(len(least))
    if is_first:
        wide_ref = take(1)[0]
    out_ref = take(1)[0]
    if is_last:
        take(1)[0][...] = jnp.zeros((8, LANES), F32)
    bias = take(1)[0]
    if is_first:
        doc_rep = take(1)[0]
    if is_last:
        done, sems = take(2)
    block = place_ref[0]

    lane = lax.broadcasted_iota(jnp.int32, (tokens, LANES), 1).astype(F32)
    end = 2 * kv_here * tokens
    for j, ref in enumerate(kv):
        valid = (block >= jnp.where(block % 2 == 0, *least[j])).astype(F32)
        docs = doc_columns(ref[end : end + INFO, :].astype(F32) * valid, tokens)
        bias[j] = jnp.where(docs == lane, 0.0, -BIG).astype(BF16)
    if is_first:
        column = doc_columns(doc_ref[...], tokens)
        for h in range(per_group):
            doc_rep[pl.ds(h, tokens, stride=per_group), :] = (column == lane).astype(F32)
    ones = jnp.ones((STATE_ROWS - HEAD_DIM, tokens), BF16)

    def some_chunks(i, carry):
        chains = [(u, g) for u in range(unroll) for g in range(kv_here)]
        chunk = [i * unroll + u for u in range(unroll)]
        at = [pl.ds(pl.multiple_of(c * CHUNK, CHUNK), CHUNK) for c in chunk]
        picked = [pl.ds(pl.multiple_of(c * (step * heads), step * heads), step * heads) for c in chunk]
        scores, results = {}, {}

        def begin(u, g):
            if is_first:
                query = query_ref[picked[u], :].astype(F32).reshape(step, heads, LANES)
                query = query[:, g * per_group : (g + 1) * per_group, :].reshape(CHUNK, LANES)
                wide = jnp.concatenate([query.astype(BF16), doc_rep[at[u], :].astype(BF16)], axis=1)
                wide_ref[g, at[u], :] = wide
            else:
                wide = wide_ref[g, at[u], :]
            out = []
            for j, ref in enumerate(kv):
                keys = jnp.concatenate([ref[g * tokens : (g + 1) * tokens, :], bias[j]], axis=1)
                out.append(
                    lax.dot_general(keys, wide, (((1,), (1,)), ((), ())), preferred_element_type=F32)
                )
            if is_first:
                token = chunk[u] * step + lax.broadcasted_iota(jnp.int32, (tokens, CHUNK), 1) // per_group
                key_at = lax.broadcasted_iota(jnp.int32, (tokens, CHUNK), 0)
                out[0] = jnp.where(key_at <= token, out[0], -BIG)
            scores[u, g] = out

        def end_chain(u, g):
            here = scores.pop((u, g))
            top = jnp.max(here[0], axis=0, keepdims=True)
            for score in here[1:]:
                top = jnp.maximum(top, jnp.max(score, axis=0, keepdims=True))
            total = None
            if not is_first:
                before = state_ref[g, :, at[u]]
                top_before = before[STATE_ROWS - 1 : STATE_ROWS, :]
                top = jnp.maximum(top, top_before)
                total = before * jnp.exp2((top_before - top) * SCORE_TO_EXP2)
            for ref, score in zip(kv, here):
                weights = jnp.exp2((score - top) * SCORE_TO_EXP2).astype(BF16)
                first = (kv_here + g) * tokens
                parts = [ref[first + p : first + p + LANES, :] for p in range(0, tokens, LANES)]
                values = jnp.concatenate([jnp.concatenate(parts, axis=1), ones], axis=0)
                more = jnp.dot(values, weights, preferred_element_type=F32)
                total = more if total is None else total + more
            if is_last:
                results[u, g] = jnp.transpose(total[0:HEAD_DIM] / total[HEAD_DIM : HEAD_DIM + 1])
            else:
                out_ref[g, 0 : STATE_ROWS - 8, at[u]] = total[0 : STATE_ROWS - 8]
                out_ref[g, STATE_ROWS - 8 : STATE_ROWS, at[u]] = jnp.broadcast_to(top, (8, CHUNK))

        ahead = 2
        for n in range(len(chains) + ahead):
            if n < len(chains):
                begin(*chains[n])
            if n >= ahead:
                end_chain(*chains[n - ahead])
        if is_last:
            for u in range(unroll):
                result = [results[u, g] for g in range(kv_here)]
                if kv_here > 1:
                    result = [r.reshape(step, per_group, LANES) for r in result]
                    result = [jnp.concatenate(result, axis=1).reshape(step * heads, LANES)]
                done[picked[u], :] = result[0].astype(BF16)
                pltpu.make_async_copy(
                    done.at[picked[u], :], out_ref.at[picked[u], :], sems.at[chunk[u]]
                ).start()
        return carry

    lax.fori_loop(0, rows // (CHUNK * unroll), some_chunks, 0)
    if is_last:
        for c in range(rows // CHUNK):
            at = pl.ds(c * step * heads, step * heads)
            pltpu.make_async_copy(done.at[at, :], out_ref.at[at, :], sems.at[c]).wait()


def attend(place, first, state, kv, is_last, tokens, heads, kv_here, after, relay=()):
    is_first = state is None
    least = tuple(pair for _, pair in kv)
    kv = [block for block, _ in kv]
    blocks = len(kv)
    rows = tokens * heads // kv_here
    unroll = min(4, rows // CHUNK)
    wide_shape = sds((kv_here, rows, 2 * LANES), BF16)
    state_shape = sds((kv_here, STATE_ROWS, rows), F32)
    out_shape = sds((tokens * heads, LANES), BF16) if is_last else state_shape
    scratch = [pltpu.VMEM((blocks, tokens, LANES), BF16)]
    if is_first:
        out_shape = (wide_shape, out_shape)
        scratch.append(pltpu.VMEM((rows, LANES), F32))
    if is_last:
        out_shape = (out_shape, sds((8, LANES), F32))
        scratch.append(pltpu.VMEM((tokens * heads, LANES), BF16))
        scratch.append(pltpu.SemaphoreType.DMA((rows // CHUNK,)))
    span = blocks * tokens
    return call(
        functools.partial(attend_kernel, tokens, heads, kv_here, least, is_first, is_last, unroll),
        "attend",
        [place],
        [*first, *([] if is_first else [state]), *kv],
        out_shape,
        scratch=scratch,
        mib=24,
        estimate=cost(
            4 * tokens * heads * span * 2 * LANES, 4 * tokens * heads * LANES * 4, tokens * heads * span
        ),
        after=after,
        out_hbm=is_last,
        relay=relay,
    )


def body(
    blocks,
    lin_query,
    lin_key,
    lin_value,
    lin_gate,
    log_decay,
    norm_gain,
    doc_ids,
    soft_query,
    soft_key,
    soft_value,
):
    tokens, heads, _ = lin_query.shape
    tensor = HEADS // heads
    kv_here = max(1, heads // GROUP)
    parts = 2 if heads % 16 == 0 else 1
    longest = blocks * tokens * 5 // 8
    window = min(blocks - 1, (longest - 1 + tokens - 1) // tokens)
    flat = lambda x: x.reshape(-1, LANES)
    block = lax.axis_index("seq")
    place = block.astype(jnp.int32).reshape(1)
    start = (lax.axis_index("tp") * heads // GROUP).astype(jnp.int32).reshape(1)

    def send(x, pairs):
        return lax.ppermute(x, "seq", [(a, b % blocks) for a, b in pairs])

    everyone = range(blocks)
    swap = [(b, b ^ 1) for b in everyone]

    own_kv, docs, cumul, key, value = fetch(
        start,
        [
            doc_ids.reshape(tokens // LANES, LANES),
            jnp.transpose(log_decay),
            flat(soft_key),
            flat(soft_value),
            flat(lin_key),
            flat(lin_value),
        ],
        tokens,
        heads,
        kv_here,
    )

    forward = [(b, b + 2) for b in everyone]
    pairs = [(b, b + 1) for b in everyone if b % 2 == 0]
    longest_hop = [b for b in everyone if b % 2 and b + window < blocks] if window % 2 else []
    pairs += [(b, b + window) for b in longest_hop]
    taken = [b + window for b in longest_hop]
    pairs += [(b, b - 1) for b in everyone if b % 2 and b not in longest_hop and b - 1 not in taken]
    beside = (send(own_kv, pairs), (window if window % 2 else blocks, 1))
    ahead = send(own_kv, forward)

    size = quarter_rows(heads)
    others = range(1, GROUP_BLOCKS)
    sent = block_state(place, cumul, docs, key, value, tokens, heads)
    quarters = [sent[0]] + [send(sent[j], [(b, b ^ j) for b in everyone]) for j in others]

    state = {}

    def first_attention(after, relay):
        state["wide"], *out = attend(
            place, (docs, flat(soft_query)), None, [(own_kv, (0, 0))], False, tokens, heads, kv_here, after, relay
        )
        state["sum"] = out[0]
        return out

    def more_attention(kv, is_last, after, relay=()):
        out = attend(
            place, (state["wide"],), state["sum"], kv, is_last, tokens, heads, kv_here, after, relay
        )
        state["sum"] = out[0] if relay else out
        return out

    inner, qh = [], []

    def inner_of(part, after):
        n = heads // parts
        got = inner_part(
            cumul, docs, flat(lin_query), key, value, tokens, heads, part * n, n, after
        )
        inner.append(got[0])
        qh.append(got[1])
        return got[0]

    done, lane = first_attention([sent[0]], [ahead])
    second = send(lane, [(b, b + 2) for b in range(2, blocks - 2)])
    if parts > 1:
        done = inner_of(0, [done])
    run, lane = group_map(place, quarters, size, [done, beside[0]], [lane])
    first_cross = send(lane, swap)
    stages = (blocks // GROUP_BLOCKS).bit_length() - 1
    before, done = None, run
    for stage in range(stages):
        came = send(run, [(b, b ^ (GROUP_BLOCKS << stage)) for b in everyone])
        if stage == stages - 1:
            done = more_attention([beside, (lane, (2, 2))], False, [done])
            done = inner_of(parts - 1, [done])
        else:
            run, before = scan_step(place, stage + 2, run, came, before, size, [done])
            done = run
    *priors, prior_doc, lane = prior_states(
        place, stages + 1, quarters, came, before, size, [done], [second]
    )
    priors = [priors[0]] + [send(priors[j], [(b, b ^ j) for b in everyone]) for j in others]
    done = more_attention([(first_cross, (2, 3)), (lane, (4, 4))], False, [prior_doc])
    rest = [(send(lane, swap), (4, 5))]
    for back in range(3, window // 2 + 1):
        lane = send(lane, forward)
        rest.append((lane, (2 * back, 2 * back)))
        rest.append((send(lane, swap), (2 * back, 2 * back + 1)))
    mixed, squares = mix(place, docs, prior_doc, cumul, inner, qh, priors, tokens, heads, [done])
    sums = [squares]
    for other in range(1, tensor):
        sums.append(lax.ppermute(squares, "tp", [(t, t ^ other) for t in range(tensor)]))
    done = squares
    while rest:
        got = more_attention(rest[:2], len(rest) <= 2, [done])
        rest, done = rest[2:], got
    soft_out, done = got
    lin_out = finish(norm_gain, flat(lin_gate), mixed, sums, tokens, heads, [done])
    shape = (tokens, heads, HEAD_DIM)
    return lin_out.reshape(shape), soft_out.reshape(shape)


def solution(mesh):
    in_specs = (
        P("seq", "tp", None),
        P("seq", "tp", None),
        P("seq", "tp", None),
        P("seq", "tp", None),
        P("seq", "tp"),
        P("tp", None),
        P("seq"),
        P("seq", "tp", None),
        P("seq", None, None),
        P("seq", None, None),
    )
    out_specs = (P("seq", "tp", None), P("seq", "tp", None))
    return jax.shard_map(
        functools.partial(body, mesh.shape["seq"]),
        mesh=mesh,
        in_specs=in_specs,
        out_specs=out_specs,
        check_vma=False,
    )
```

```python
import functools

import jax
import jax.numpy as jnp
import numpy as np
from jax import lax
from jax.experimental import pallas as pl
from jax.experimental.pallas import tpu as pltpu
from jax.sharding import PartitionSpec as P

HEADS = 64
HEAD_DIM = 128
KV_HEADS = 8
LANES = 128
GROUP = HEADS // KV_HEADS
F32 = jnp.float32
BF16 = jnp.bfloat16
BIG = float(2**20)
SCORE_TO_EXP2 = HEAD_DIM**-0.5 * float(np.log2(np.e))
INFO = 16
HIGHEST = lax.Precision.HIGHEST

VMEM = pl.BlockSpec(memory_space=pltpu.VMEM)
SMEM = pl.BlockSpec(memory_space=pltpu.SMEM)
HBM = pl.BlockSpec(memory_space=pltpu.HBM)
ANYWHERE = pl.BlockSpec(memory_space=pl.ANY)
STATE_ROWS = HEAD_DIM + 16
CHUNK = 256
GROUP_BLOCKS = 4


def sds(shape, dtype):
    return jax.ShapeDtypeStruct(shape, dtype)


def cost(flops, bytes_accessed, transcendentals=0):
    return pl.CostEstimate(
        flops=int(flops), bytes_accessed=int(bytes_accessed), transcendentals=int(transcendentals)
    )


def call(kernel, name, scalars, operands, out_shape, scratch=(), mib=16, estimate=None, after=(), hbm=0, out_hbm=False, relay=()):
    begin = len(scalars) + len(operands)
    skip = len(after)
    operands = [
        pltpu.with_memory_space_constraint(x, pltpu.HBM) if i < hbm else x for i, x in enumerate(operands)
    ]
    outs = out_shape if isinstance(out_shape, tuple) else (out_shape,)
    out_specs = (VMEM,) * len(outs)
    outs = tuple(
        (pltpu.HBM if out_hbm and i == 0 else pltpu.VMEM)(x.shape, x.dtype) for i, x in enumerate(outs)
    )
    if out_hbm:
        out_specs = (HBM, *out_specs[1:])

    moved = len(relay)
    many = len(outs)
    single = not isinstance(out_shape, tuple) and not relay
    out_specs += (VMEM,) * moved
    outs += tuple(pltpu.VMEM(x.shape, x.dtype) for x in relay)

    def run(*refs):
        rest = refs[begin + skip + moved :]
        for source, target in zip(refs[begin + skip : begin + skip + moved], rest[many : many + moved]):
            target[...] = source[...]
        kernel(*refs[:begin], *rest[:many], *rest[many + moved :])

    out = pl.pallas_call(
        run,
        out_shape=outs,
        in_specs=[SMEM] * len(scalars) + [HBM] * hbm + [VMEM] * (len(operands) - hbm) + [ANYWHERE] * skip + [VMEM] * moved,
        out_specs=out_specs,
        scratch_shapes=list(scratch),
        compiler_params=pltpu.CompilerParams(vmem_limit_bytes=mib * 1024 * 1024),
        cost_estimate=estimate,
        name=name,
    )(*scalars, *operands, *after, *relay)
    return out[0] if single else out


def doc_columns(doc_rows, tokens):
    parts = []
    for i in range(tokens // LANES):
        row = jnp.broadcast_to(doc_rows[i : i + 1, :], (LANES, LANES))
        parts.append(jnp.transpose(row))
    return jnp.concatenate(parts, axis=0)


def doc_line(doc_rows, tokens):
    return jnp.concatenate([doc_rows[i : i + 1, :] for i in range(tokens // LANES)], axis=1)


def lower_triangle(tokens):
    rows = lax.broadcasted_iota(jnp.int32, (tokens, tokens), 0)
    cols = lax.broadcasted_iota(jnp.int32, (tokens, tokens), 1)
    return rows >= cols


def fetch_kernel(tokens, heads, kv_here, start_ref, *refs):
    refs = list(refs)
    take = lambda n: [refs.pop(0) for _ in range(n)]
    sources = take(6)
    kv_ref, doc_out, cumul_ref, key_out, value_out = take(5)
    held = take(4)
    sems, wide, ldp = refs
    docs_in, decays, soft_key, soft_value = held
    targets = [*held, key_out, value_out]
    copies = [
        pltpu.make_async_copy(source, target, sems.at[i])
        for i, (source, target) in enumerate(zip(sources, targets))
    ]
    for copy in copies:
        copy.start()

    copies[0].wait()
    docs = docs_in[...].astype(F32) + 1.0
    line = lax.broadcasted_iota(jnp.int32, (INFO, LANES), 0)
    info = jnp.zeros((INFO, LANES), F32)
    for i in range(tokens // LANES):
        info = jnp.where(line == i, docs[i : i + 1, :], info)
    doc_out[...] = info
    end = 2 * kv_here * tokens
    kv_ref[end : end + INFO, :] = info.astype(BF16)

    copies[1].wait()
    ldp[...] = jnp.zeros_like(ldp)
    ldp[0:heads, :] = decays[...]
    cumul_ref[...] = lax.dot_general(
        lower_triangle(tokens).astype(F32),
        ldp[...],
        (((1,), (1,)), ((), ())),
        precision=HIGHEST,
        preferred_element_type=F32,
    )

    start = start_ref[0]
    for which, ref in enumerate((soft_key, soft_value)):
        copies[2 + which].wait()
        wide[...] = ref[...].astype(F32)
        for g in range(kv_here):
            rows = wide[pl.ds(start + g, tokens, stride=KV_HEADS), :]
            at = (which * kv_here + g) * tokens
            if which:
                halves = [jnp.transpose(rows[i : i + LANES, :]) for i in range(0, tokens, LANES)]
                rows = jnp.concatenate(halves, axis=0)
            kv_ref[at : at + tokens, :] = rows.astype(BF16)
    for copy in copies[4:]:
        copy.wait()


def fetch(start, operands, tokens, heads, kv_here):
    return call(
        functools.partial(fetch_kernel, tokens, heads, kv_here),
        "fetch",
        [start],
        operands,
        (
            sds((2 * kv_here * tokens + INFO, LANES), BF16),
            sds((INFO, LANES), F32),
            sds((tokens, LANES), F32),
            sds(operands[4].shape, BF16),
            sds(operands[5].shape, BF16),
        ),
        scratch=[pltpu.VMEM(x.shape, x.dtype) for x in operands[:4]]
        + [
            pltpu.SemaphoreType.DMA((len(operands),)),
            pltpu.VMEM((tokens * KV_HEADS, LANES), F32),
            pltpu.VMEM((LANES, tokens), F32),
        ],
        estimate=cost(0, 3 * tokens * heads * LANES * 2),
        hbm=len(operands),
    )


def quarter_rows(heads):
    return heads * HEAD_DIM // GROUP_BLOCKS


def state_kernel(tokens, heads, place_ref, *refs):
    refs = list(refs)
    take = lambda n: [refs.pop(0) for _ in range(n)]
    cumul_ref, doc_ref, key_ref, value_ref = take(4)
    out_refs = take(GROUP_BLOCKS)
    kf, vf, states = refs
    cumul, docs = cumul_ref[...], doc_ref[...]
    total = cumul[tokens - 1 : tokens, :]
    last_row = tokens // LANES - 1
    first_doc = docs[0:1, 0:1]
    last_doc = docs[last_row : last_row + 1, LANES - 1 : LANES]
    tail = (doc_columns(docs, tokens) == last_doc).astype(F32)
    scale = jnp.exp(total - cumul) * tail
    kf[...] = key_ref[...].astype(F32)
    vf[...] = value_ref[...].astype(F32)
    for h in range(heads):
        keys = (kf[pl.ds(h, tokens, stride=heads), :] * scale[:, h : h + 1]).astype(BF16)
        values = vf[pl.ds(h, tokens, stride=heads), :].astype(BF16)
        states[h * HEAD_DIM : (h + 1) * HEAD_DIM, :] = lax.dot_general(
            keys, values, (((0,), (0,)), ((), ())), preferred_element_type=F32
        )
    size = quarter_rows(heads)
    mine = place_ref[0] % GROUP_BLOCKS
    for j, ref in enumerate(out_refs):
        taker = mine ^ j
        ref[0:size, :] = states[pl.ds(pl.multiple_of(taker * size, size), size), :].astype(BF16)
        totals = jnp.zeros_like(total)
        for c in range(GROUP_BLOCKS):
            skip = c * heads // GROUP_BLOCKS
            moved = pltpu.roll(total, LANES - skip, 1) if skip else total
            totals = jnp.where(taker == c, moved, totals)
        ref[size : size + INFO, :] = info_rows((*in_parts(totals), first_doc, last_doc))


def block_state(place, cumul, docs, key, value, tokens, heads):
    return call(
        functools.partial(state_kernel, tokens, heads),
        "block_state",
        [place],
        [cumul, docs, key, value],
        (sds((quarter_rows(heads) + INFO, LANES), BF16),) * GROUP_BLOCKS,
        scratch=[
            pltpu.VMEM((tokens * heads, LANES), F32),
            pltpu.VMEM((tokens * heads, LANES), F32),
            pltpu.VMEM((heads * HEAD_DIM, LANES), F32),
        ],
        estimate=cost(2 * heads * tokens * HEAD_DIM**2, 5 * tokens * heads * LANES * 2),
    )


def in_parts(x):
    hi = x.astype(BF16).astype(F32)
    mid = (x - hi).astype(BF16).astype(F32)
    return hi, mid, x - hi - mid


def info_rows(parts):
    line = lax.broadcasted_iota(jnp.int32, (INFO, LANES), 0)
    info = jnp.zeros((INFO, LANES), F32)
    for i, part in enumerate(parts):
        info = jnp.where(line == i, part, info)
    return info.astype(BF16)


def read_map(ref, size):
    info = ref[size : size + INFO, :].astype(F32)
    return info[0:1] + info[1:2] + info[2:3], info[3:4], info[4:5]


def row_chunks(size):
    unit = min(HEAD_DIM, size)
    return [(slice(i * unit, (i + 1) * unit), slice(i, i + 1)) for i in range(size // unit)]


def in_block_order(place_ref, refs, blocks):
    mine = place_ref[0] % GROUP_BLOCKS
    for j, ref in enumerate(refs):
        blocks[mine ^ j] = ref[...]


def block_maps(blocks, size):
    maps = []
    for c in range(GROUP_BLOCKS):
        info = blocks[c, size : size + INFO, :].astype(F32)
        first, last = info[3:4], info[4:5]
        gain = jnp.exp(info[0:1] + info[1:2] + info[2:3]) * (first == last).astype(F32)
        maps.append((gain, first, last))
    return maps


def group_kernel(size, place_ref, *refs):
    sources = refs[:GROUP_BLOCKS]
    out_ref, blocks = refs[GROUP_BLOCKS:]
    in_block_order(place_ref, sources, blocks)
    maps = block_maps(blocks, size)
    gains = [None]
    for (gain, first, _), (_, _, last_before) in zip(maps[1:], maps[:-1]):
        gains.append(gain * (last_before == first).astype(F32))
    for rows, lane in row_chunks(size):
        total = blocks[0, rows, :].astype(F32)
        for c in range(1, GROUP_BLOCKS):
            total = gains[c][:, lane] * total + blocks[c, rows, :].astype(F32)
        out_ref[rows, :] = total.astype(BF16)
    gain = maps[0][0] * gains[1] * gains[2] * gains[3]
    out_ref[size : size + INFO, :] = info_rows((*in_parts(gain), maps[0][1], maps[-1][2]))


def group_map(place, quarters, size, after, relay):
    return call(
        functools.partial(group_kernel, size),
        "group_map",
        [place],
        quarters,
        (sds((size + INFO, LANES), BF16),),
        scratch=[pltpu.VMEM((GROUP_BLOCKS, size + INFO, LANES), BF16)],
        estimate=cost(8 * size * LANES, 10 * size * LANES * 2),
        after=after,
        relay=relay,
    )


def scan_kernel(size, has_before, bit, place_ref, *refs):
    mine_ref, came_ref = refs[:2]
    before_ref = refs[2] if has_before else None
    run_ref, out_ref = refs[-2:]
    upper = (place_ref[0] >> bit) & 1 == 1
    gain_m, first_m, last_m = read_map(mine_ref, size)
    gain_c, first_c, last_c = read_map(came_ref, size)
    link = jnp.where(upper, (last_c == first_m).astype(F32), (last_m == first_c).astype(F32))
    gain = jnp.where(upper, gain_m, gain_c) * link
    for rows, lane in row_chunks(size):
        mine, came = mine_ref[rows, :].astype(F32), came_ref[rows, :].astype(F32)
        lower_sum, upper_sum = jnp.where(upper, came, mine), jnp.where(upper, mine, came)
        run_ref[rows, :] = (gain[:, lane] * lower_sum + upper_sum).astype(BF16)
    run_ref[size : size + INFO, :] = info_rows(
        (
            *in_parts(gain * jnp.where(upper, gain_c, gain_m)),
            jnp.where(upper, first_c, first_m),
            jnp.where(upper, last_m, last_c),
        )
    )
    if not has_before:
        out_ref[...] = jnp.where(upper, came_ref[...], jnp.zeros_like(came_ref))
        return
    gain_b, first_b, last_b = read_map(before_ref, size)
    empty = first_b == 0.0
    factor = jnp.where(empty, 1.0, gain_b * (last_c == first_b).astype(F32))
    for rows, lane in row_chunks(size):
        before = before_ref[rows, :].astype(F32)
        joined = factor[:, lane] * came_ref[rows, :].astype(F32) + before
        out_ref[rows, :] = jnp.where(upper, joined, before).astype(BF16)
    out_ref[size : size + INFO, :] = info_rows(
        (
            *in_parts(jnp.where(upper, factor * gain_c, gain_b)),
            jnp.where(upper, first_c, first_b),
            jnp.where(upper, jnp.where(empty, last_c, last_b), last_b),
        )
    )


def scan_step(place, bit, mine, came, before, size, after):
    shape = sds((size + INFO, LANES), BF16)
    before = [] if before is None else [before]
    return call(
        functools.partial(scan_kernel, size, len(before), bit),
        "scan_step",
        [place],
        [mine, came, *before],
        (shape, shape),
        estimate=cost(6 * size * LANES, 6 * size * LANES * 2),
        after=after,
    )


def prior_kernel(size, has_before, bit, place_ref, *refs):
    sources, came_ref = refs[:GROUP_BLOCKS], refs[GROUP_BLOCKS]
    before_ref = refs[GROUP_BLOCKS + 1] if has_before else None
    *out_refs, doc_ref, blocks, priors = refs[GROUP_BLOCKS + 1 + has_before :]
    mine = place_ref[0] % GROUP_BLOCKS
    in_block_order(place_ref, sources, blocks)
    maps = block_maps(blocks, size)
    upper = ((place_ref[0] >> bit) & 1).astype(F32)
    _, _, last_c = read_map(came_ref, size)
    factor, doc = jnp.broadcast_to(upper, (1, LANES)), upper * last_c
    if has_before:
        gain_b, first_b, last_b = read_map(before_ref, size)
        empty = first_b == 0.0
        factor = upper * jnp.where(empty, 1.0, gain_b * (last_c == first_b).astype(F32))
        doc = jnp.where(empty, doc, last_b)
    docs = [doc] + [last for _, _, last in maps[:-1]]
    gains = [gain * (doc == first).astype(F32) for (gain, first, _), doc in zip(maps, docs)]
    for rows, lane in row_chunks(size):
        state = factor[:, lane] * came_ref[rows, :].astype(F32)
        if has_before:
            state = state + before_ref[rows, :].astype(F32)
        for c in range(GROUP_BLOCKS):
            priors[c, rows, :] = state.astype(BF16)
            if c < GROUP_BLOCKS - 1:
                state = gains[c][:, lane] * state + blocks[c, rows, :].astype(F32)
    for j, ref in enumerate(out_refs):
        ref[...] = priors[mine ^ j]
    own_doc = docs[0]
    for c in range(1, GROUP_BLOCKS):
        own_doc = jnp.where(mine == c, docs[c], own_doc)
    doc_ref[...] = jnp.broadcast_to(own_doc, (8, LANES))


def prior_states(place, bit, quarters, came, before, size, after, relay=()):
    before = [] if before is None else [before]
    return call(
        functools.partial(prior_kernel, size, len(before), bit),
        "prior_states",
        [place],
        [*quarters, came, *before],
        (*[sds((size, LANES), BF16)] * GROUP_BLOCKS, sds((8, LANES), F32)),
        scratch=[
            pltpu.VMEM((GROUP_BLOCKS, size + INFO, LANES), BF16),
            pltpu.VMEM((GROUP_BLOCKS, size, LANES), BF16),
        ],
        estimate=cost(8 * size * LANES, 10 * size * LANES * 2),
        after=after,
        relay=relay,
    )


def some_heads(ref, tokens, heads, first, count):
    x = ref[...].astype(F32)
    if count == heads:
        return x
    return x.reshape(tokens, heads, LANES)[:, first : first + count, :].reshape(tokens * count, LANES)


def inner_kernel(tokens, heads, first, count, cumul_ref, doc_ref, query_ref, key_ref, value_ref, inner_ref, qh_ref, qf, kf, vf, mask):
    cumul = cumul_ref[...]
    cumul_t = jnp.transpose(cumul)
    docs = doc_ref[...]
    column = doc_columns(docs, tokens)
    same = jnp.concatenate([column] * (tokens // LANES), axis=1) == doc_line(docs, tokens)
    mask[...] = jnp.where(lower_triangle(tokens) & same, 0.0, -1e9)
    qf[...] = some_heads(query_ref, tokens, heads, first, count)
    kf[...] = some_heads(key_ref, tokens, heads, first, count)
    vf[...] = some_heads(value_ref, tokens, heads, first, count)
    for n in range(count):
        h = first + n
        picked = pl.ds(n, tokens, stride=count)
        query = qf[picked, :].astype(BF16)
        keys = kf[picked, :].astype(BF16)
        values = vf[picked, :].astype(BF16)
        qh_ref[n * tokens : (n + 1) * tokens, :] = query
        for i in range(tokens // LANES):
            seen = (i + 1) * LANES
            rows = slice(i * LANES, seen)
            scores = lax.dot_general(
                query[rows, :], keys[0:seen, :], (((1,), (1,)), ((), ())), preferred_element_type=F32
            )
            gap = cumul[rows, h : h + 1] - cumul_t[h : h + 1, 0:seen]
            weights = (scores * jnp.exp(gap + mask[rows, 0:seen])).astype(BF16)
            inner_ref[n * tokens + i * LANES : n * tokens + seen, :] = jnp.dot(
                weights, values[0:seen, :], preferred_element_type=F32
            )


def inner_part(cumul, docs, query, key, value, tokens, heads, first, count, after, relay):
    return call(
        functools.partial(inner_kernel, tokens, heads, first, count),
        "inner_part",
        [],
        [cumul, docs, query, key, value],
        (sds((count * tokens, LANES), F32), sds((count * tokens, LANES), BF16)),
        scratch=[pltpu.VMEM((tokens * count, LANES), F32)] * 3 + [pltpu.VMEM((tokens, tokens), F32)],
        mib=24,
        estimate=cost(
            4 * count * tokens * tokens * HEAD_DIM, tokens * heads * LANES * 12, count * tokens * tokens
        ),
        after=after,
        relay=relay,
    )


def mix_kernel(tokens, heads, parts, place_ref, doc_ref, prior_doc_ref, cumul_ref, *refs):
    refs = list(refs)
    take = lambda n: [refs.pop(0) for _ in range(n)]
    inner, qh, quarters = take(parts), take(parts), take(GROUP_BLOCKS)
    mixed_ref, square_ref, states = refs
    size = quarter_rows(heads)
    mine = place_ref[0] % GROUP_BLOCKS
    for j, ref in enumerate(quarters):
        states[pl.ds(pl.multiple_of((mine ^ j) * size, size), size), :] = ref[...]
    is_open = (doc_columns(doc_ref[...], tokens) == prior_doc_ref[0:1, :]).astype(F32)
    gain = jnp.exp(cumul_ref[...]) * is_open
    squares = jnp.zeros((tokens, LANES), F32)
    for h in range(heads):
        part, n = divmod(h, heads // parts)
        held = slice(n * tokens, (n + 1) * tokens)
        state = states[h * HEAD_DIM : (h + 1) * HEAD_DIM, :]
        carried = jnp.dot(qh[part][held, :], state, preferred_element_type=F32)
        mixed = inner[part][held, :] + carried * gain[:, h : h + 1]
        squares = squares + mixed * mixed
        mixed_ref[pl.ds(h, tokens, stride=heads), :] = mixed
    square_ref[...] = lax.dot_general(
        jnp.ones((8, LANES), F32),
        squares,
        (((1,), (1,)), ((), ())),
        precision=HIGHEST,
        preferred_element_type=F32,
    )


def mix(place, docs, prior_doc, cumul, inner, qh, quarters, tokens, heads, after):
    return call(
        functools.partial(mix_kernel, tokens, heads, len(inner)),
        "mix",
        [place],
        [docs, prior_doc, cumul, *inner, *qh, *quarters],
        (sds((tokens * heads, LANES), F32), sds((8, tokens), F32)),
        scratch=[pltpu.VMEM((heads * HEAD_DIM, LANES), BF16)],
        mib=24,
        estimate=cost(2 * heads * tokens * HEAD_DIM**2, tokens * heads * LANES * 10),
        after=after,
    )


def finish_kernel(tokens, heads, sums, step, gain_ref, gate_ref, mixed_ref, *refs):
    squares, (out_ref, done, sems) = refs[:sums], refs[sums:]
    total = squares[0][0:1, :]
    for ref in squares[1:]:
        total = total + ref[0:1, :]
    scale = lax.rsqrt(total / (HEADS * HEAD_DIM) + 1e-06)
    rows = jnp.concatenate([scale[:, i * LANES : (i + 1) * LANES] for i in range(tokens // LANES)], axis=0)
    column = doc_columns(rows, tokens)
    copies = []
    for i in range(0, tokens, step):
        at = pl.ds(i * heads, step * heads)
        gate = jax.nn.sigmoid(gate_ref[at, :].astype(F32)).reshape(step, heads, LANES)
        mixed = mixed_ref[at, :].reshape(step, heads, LANES)
        inv = column[i : i + step, :][:, None, :]
        out = mixed * inv * gain_ref[...][None] * gate
        done[at, :] = out.reshape(step * heads, LANES).astype(BF16)
        copies.append(pltpu.make_async_copy(done.at[at, :], out_ref.at[at, :], sems.at[i // step]))
        copies[-1].start()
    for copy in copies:
        copy.wait()


def finish(gain, gate, mixed, squares, tokens, heads, after):
    step = 64
    return call(
        functools.partial(finish_kernel, tokens, heads, len(squares), step),
        "finish",
        [],
        [gain, gate, mixed, *squares],
        sds((tokens * heads, LANES), BF16),
        scratch=[pltpu.VMEM((tokens * heads, LANES), BF16), pltpu.SemaphoreType.DMA((tokens // step,))],
        estimate=cost(0, tokens * heads * LANES * 8, tokens * heads * LANES),
        after=after,
        out_hbm=True,
    )


def attend_kernel(tokens, heads, kv_here, least, is_first, is_last, unroll, place_ref, *refs):
    refs = list(refs)
    take = lambda n: [refs.pop(0) for _ in range(n)]
    per_group = heads // kv_here
    rows = tokens * per_group
    step = CHUNK // per_group
    if is_first:
        doc_ref, query_ref = take(2)
    else:
        wide_ref, state_ref = take(2)
    kv = take(len(least))
    if is_first:
        wide_ref = take(1)[0]
    out_ref = take(1)[0]
    if is_last:
        take(1)[0][...] = jnp.zeros((8, LANES), F32)
    bias = take(1)[0]
    if is_first:
        doc_rep = take(1)[0]
    if is_last:
        done, sems = take(2)
    block = place_ref[0]

    lane = lax.broadcasted_iota(jnp.int32, (tokens, LANES), 1).astype(F32)
    end = 2 * kv_here * tokens
    for j, ref in enumerate(kv):
        valid = (block >= jnp.where(block % 2 == 0, *least[j])).astype(F32)
        docs = doc_columns(ref[end : end + INFO, :].astype(F32) * valid, tokens)
        bias[j] = jnp.where(docs == lane, 0.0, -BIG).astype(BF16)
    if is_first:
        column = doc_columns(doc_ref[...], tokens)
        for h in range(per_group):
            doc_rep[pl.ds(h, tokens, stride=per_group), :] = (column == lane).astype(F32)
    ones = jnp.ones((STATE_ROWS - HEAD_DIM, tokens), BF16)

    def some_chunks(i, carry):
        chains = [(u, g) for u in range(unroll) for g in range(kv_here)]
        chunk = [i * unroll + u for u in range(unroll)]
        at = [pl.ds(pl.multiple_of(c * CHUNK, CHUNK), CHUNK) for c in chunk]
        picked = [pl.ds(pl.multiple_of(c * (step * heads), step * heads), step * heads) for c in chunk]
        scores, results = {}, {}

        def begin(u, g):
            if is_first:
                query = query_ref[picked[u], :].astype(F32).reshape(step, heads, LANES)
                query = query[:, g * per_group : (g + 1) * per_group, :].reshape(CHUNK, LANES)
                wide = jnp.concatenate([query.astype(BF16), doc_rep[at[u], :].astype(BF16)], axis=1)
                wide_ref[g, at[u], :] = wide
            else:
                wide = wide_ref[g, at[u], :]
            out = []
            for j, ref in enumerate(kv):
                keys = jnp.concatenate([ref[g * tokens : (g + 1) * tokens, :], bias[j]], axis=1)
                out.append(
                    lax.dot_general(keys, wide, (((1,), (1,)), ((), ())), preferred_element_type=F32)
                )
            if is_first:
                token = chunk[u] * step + lax.broadcasted_iota(jnp.int32, (tokens, CHUNK), 1) // per_group
                key_at = lax.broadcasted_iota(jnp.int32, (tokens, CHUNK), 0)
                out[0] = jnp.where(key_at <= token, out[0], -BIG)
            scores[u, g] = out

        def end_chain(u, g):
            here = scores.pop((u, g))
            top = jnp.max(here[0], axis=0, keepdims=True)
            for score in here[1:]:
                top = jnp.maximum(top, jnp.max(score, axis=0, keepdims=True))
            total = None
            if not is_first:
                before = state_ref[g, :, at[u]]
                top_before = before[STATE_ROWS - 1 : STATE_ROWS, :]
                top = jnp.maximum(top, top_before)
                total = before * jnp.exp2((top_before - top) * SCORE_TO_EXP2)
            for ref, score in zip(kv, here):
                weights = jnp.exp2((score - top) * SCORE_TO_EXP2).astype(BF16)
                first = (kv_here + g) * tokens
                parts = [ref[first + p : first + p + LANES, :] for p in range(0, tokens, LANES)]
                values = jnp.concatenate([jnp.concatenate(parts, axis=1), ones], axis=0)
                more = jnp.dot(values, weights, preferred_element_type=F32)
                total = more if total is None else total + more
            if is_last:
                results[u, g] = jnp.transpose(total[0:HEAD_DIM] / total[HEAD_DIM : HEAD_DIM + 1])
            else:
                out_ref[g, 0 : STATE_ROWS - 8, at[u]] = total[0 : STATE_ROWS - 8]
                out_ref[g, STATE_ROWS - 8 : STATE_ROWS, at[u]] = jnp.broadcast_to(top, (8, CHUNK))

        ahead = 2
        for n in range(len(chains) + ahead):
            if n < len(chains):
                begin(*chains[n])
            if n >= ahead:
                end_chain(*chains[n - ahead])
        if is_last:
            for u in range(unroll):
                result = [results[u, g] for g in range(kv_here)]
                if kv_here > 1:
                    result = [r.reshape(step, per_group, LANES) for r in result]
                    result = [jnp.concatenate(result, axis=1).reshape(step * heads, LANES)]
                done[picked[u], :] = result[0].astype(BF16)
                pltpu.make_async_copy(
                    done.at[picked[u], :], out_ref.at[picked[u], :], sems.at[chunk[u]]
                ).start()
        return carry

    lax.fori_loop(0, rows // (CHUNK * unroll), some_chunks, 0)
    if is_last:
        for c in range(rows // CHUNK):
            at = pl.ds(c * step * heads, step * heads)
            pltpu.make_async_copy(done.at[at, :], out_ref.at[at, :], sems.at[c]).wait()


def attend(place, first, state, kv, is_last, tokens, heads, kv_here, after, relay=()):
    is_first = state is None
    least = tuple(pair for _, pair in kv)
    kv = [block for block, _ in kv]
    blocks = len(kv)
    rows = tokens * heads // kv_here
    unroll = min(4, rows // CHUNK)
    wide_shape = sds((kv_here, rows, 2 * LANES), BF16)
    state_shape = sds((kv_here, STATE_ROWS, rows), F32)
    out_shape = sds((tokens * heads, LANES), BF16) if is_last else state_shape
    scratch = [pltpu.VMEM((blocks, tokens, LANES), BF16)]
    if is_first:
        out_shape = (wide_shape, out_shape)
        scratch.append(pltpu.VMEM((rows, LANES), F32))
    if is_last:
        out_shape = (out_shape, sds((8, LANES), F32))
        scratch.append(pltpu.VMEM((tokens * heads, LANES), BF16))
        scratch.append(pltpu.SemaphoreType.DMA((rows // CHUNK,)))
    span = blocks * tokens
    return call(
        functools.partial(attend_kernel, tokens, heads, kv_here, least, is_first, is_last, unroll),
        "attend",
        [place],
        [*first, *([] if is_first else [state]), *kv],
        out_shape,
        scratch=scratch,
        mib=24,
        estimate=cost(
            4 * tokens * heads * span * 2 * LANES, 4 * tokens * heads * LANES * 4, tokens * heads * span
        ),
        after=after,
        out_hbm=is_last,
        relay=relay,
    )


def body(
    blocks,
    lin_query,
    lin_key,
    lin_value,
    lin_gate,
    log_decay,
    norm_gain,
    doc_ids,
    soft_query,
    soft_key,
    soft_value,
):
    tokens, heads, _ = lin_query.shape
    tensor = HEADS // heads
    kv_here = max(1, heads // GROUP)
    parts = 2 if heads % 16 == 0 else 1
    longest = blocks * tokens * 5 // 8
    window = min(blocks - 1, (longest - 1 + tokens - 1) // tokens)
    flat = lambda x: x.reshape(-1, LANES)
    block = lax.axis_index("seq")
    place = block.astype(jnp.int32).reshape(1)
    start = (lax.axis_index("tp") * heads // GROUP).astype(jnp.int32).reshape(1)

    def send(x, pairs):
        return lax.ppermute(x, "seq", [(a, b % blocks) for a, b in pairs])

    everyone = range(blocks)
    swap = [(b, b ^ 1) for b in everyone]

    own_kv, docs, cumul, key, value = fetch(
        start,
        [
            doc_ids.reshape(tokens // LANES, LANES),
            jnp.transpose(log_decay),
            flat(soft_key),
            flat(soft_value),
            flat(lin_key),
            flat(lin_value),
        ],
        tokens,
        heads,
        kv_here,
    )

    forward = [(b, b + 2) for b in everyone]
    hop = {b: b ^ 1 for b in everyone}
    if window % 2:
        for b in range(1, blocks - window, 2):
            last = next(a for a in everyone if hop[a] == b + window)
            hop[b], hop[last] = b + window, hop[b]
    beside = (send(own_kv, list(hop.items())), (window if window % 2 else blocks, 1))
    ahead = send(own_kv, forward)

    size = quarter_rows(heads)
    others = range(1, GROUP_BLOCKS)
    sent = block_state(place, cumul, docs, key, value, tokens, heads)
    quarters = [sent[0]] + [send(sent[j], [(b, b ^ j) for b in everyone]) for j in others]

    state = {}

    def first_attention(after):
        state["wide"], state["sum"] = attend(
            place, (docs, flat(soft_query)), None, [(own_kv, (0, 0))], False, tokens, heads, kv_here, after
        )
        return state["sum"]

    def more_attention(kv, is_last, after, relay=()):
        out = attend(
            place, (state["wide"],), state["sum"], kv, is_last, tokens, heads, kv_here, after, relay
        )
        state["sum"] = out[0] if relay else out
        return out

    inner, qh = [], []

    def inner_of(part, after, relay=()):
        n = heads // parts
        got = inner_part(
            cumul, docs, flat(lin_query), key, value, tokens, heads, part * n, n, after, relay
        )
        inner.append(got[0])
        qh.append(got[1])
        return (got[0], *got[2:]) if relay else got[0]

    done = first_attention([sent[0]])
    lane = ahead
    if parts > 1:
        done, lane = inner_of(0, [done], [ahead])
    second = send(lane, [(b, b + 2) for b in range(2, blocks - 2)])
    run, lane = group_map(place, quarters, size, [done, beside[0]], [lane])
    first_cross = send(lane, swap)
    stages = (blocks // GROUP_BLOCKS).bit_length() - 1
    before, done = None, run
    for stage in range(stages):
        came = send(run, [(b, b ^ (GROUP_BLOCKS << stage)) for b in everyone])
        if stage == stages - 1:
            done = more_attention([beside, (lane, (2, 2))], False, [done])
            done = inner_of(parts - 1, [done])
        else:
            run, before = scan_step(place, stage + 2, run, came, before, size, [done])
            done = run
    *priors, prior_doc, lane = prior_states(
        place, stages + 1, quarters, came, before, size, [done], [second]
    )
    priors = [priors[0]] + [send(priors[j], [(b, b ^ j) for b in everyone]) for j in others]
    done = more_attention([(first_cross, (2, 3)), (lane, (4, 4))], False, [prior_doc])
    rest = [(send(lane, swap), (4, 5))]
    for back in range(3, window // 2 + 1):
        lane = send(lane, forward)
        rest.append((lane, (2 * back, 2 * back)))
        rest.append((send(lane, swap), (2 * back, 2 * back + 1)))
    mixed, squares = mix(place, docs, prior_doc, cumul, inner, qh, priors, tokens, heads, [done])
    sums = [squares]
    for other in range(1, tensor):
        sums.append(lax.ppermute(squares, "tp", [(t, t ^ other) for t in range(tensor)]))
    done = squares
    while rest:
        got = more_attention(rest[:2], len(rest) <= 2, [done])
        rest, done = rest[2:], got
    soft_out, done = got
    lin_out = finish(norm_gain, flat(lin_gate), mixed, sums, tokens, heads, [done])
    shape = (tokens, heads, HEAD_DIM)
    return lin_out.reshape(shape), soft_out.reshape(shape)


def solution(mesh):
    in_specs = (
        P("seq", "tp", None),
        P("seq", "tp", None),
        P("seq", "tp", None),
        P("seq", "tp", None),
        P("seq", "tp"),
        P("tp", None),
        P("seq"),
        P("seq", "tp", None),
        P("seq", None, None),
        P("seq", None, None),
    )
    out_specs = (P("seq", "tp", None), P("seq", "tp", None))
    return jax.shard_map(
        functools.partial(body, mesh.shape["seq"]),
        mesh=mesh,
        in_specs=in_specs,
        out_specs=out_specs,
        check_vma=False,
    )
```

```python
import functools

import jax
import jax.numpy as jnp
import numpy as np
from jax import lax
from jax.experimental import pallas as pl
from jax.experimental.pallas import tpu as pltpu
from jax.sharding import PartitionSpec as P

HEADS = 64
HEAD_DIM = 128
KV_HEADS = 8
LANES = 128
GROUP = HEADS // KV_HEADS
F32 = jnp.float32
BF16 = jnp.bfloat16
BIG = float(2**20)
SCORE_TO_EXP2 = HEAD_DIM**-0.5 * float(np.log2(np.e))
INFO = 16
HIGHEST = lax.Precision.HIGHEST

VMEM = pl.BlockSpec(memory_space=pltpu.VMEM)
SMEM = pl.BlockSpec(memory_space=pltpu.SMEM)
HBM = pl.BlockSpec(memory_space=pltpu.HBM)
ANYWHERE = pl.BlockSpec(memory_space=pl.ANY)
STATE_ROWS = HEAD_DIM + 16
CHUNK = 256
GROUP_BLOCKS = 4


def sds(shape, dtype):
    return jax.ShapeDtypeStruct(shape, dtype)


def cost(flops, bytes_accessed, transcendentals=0):
    return pl.CostEstimate(
        flops=int(flops), bytes_accessed=int(bytes_accessed), transcendentals=int(transcendentals)
    )


def call(kernel, name, scalars, operands, out_shape, scratch=(), mib=16, estimate=None, after=(), hbm=0, out_hbm=False, relay=()):
    begin = len(scalars) + len(operands)
    skip = len(after)
    operands = [
        pltpu.with_memory_space_constraint(x, pltpu.HBM) if i < hbm else x for i, x in enumerate(operands)
    ]
    outs = out_shape if isinstance(out_shape, tuple) else (out_shape,)
    out_specs = (VMEM,) * len(outs)
    outs = tuple(
        (pltpu.HBM if out_hbm and i == 0 else pltpu.VMEM)(x.shape, x.dtype) for i, x in enumerate(outs)
    )
    if out_hbm:
        out_specs = (HBM, *out_specs[1:])

    moved = len(relay)
    many = len(outs)
    single = not isinstance(out_shape, tuple) and not relay
    out_specs += (VMEM,) * moved
    outs += tuple(pltpu.VMEM(x.shape, x.dtype) for x in relay)

    def run(*refs):
        rest = refs[begin + skip + moved :]
        for source, target in zip(refs[begin + skip : begin + skip + moved], rest[many : many + moved]):
            target[...] = source[...]
        kernel(*refs[:begin], *rest[:many], *rest[many + moved :])

    out = pl.pallas_call(
        run,
        out_shape=outs,
        in_specs=[SMEM] * len(scalars) + [HBM] * hbm + [VMEM] * (len(operands) - hbm) + [ANYWHERE] * skip + [VMEM] * moved,
        out_specs=out_specs,
        scratch_shapes=list(scratch),
        compiler_params=pltpu.CompilerParams(vmem_limit_bytes=mib * 1024 * 1024),
        cost_estimate=estimate,
        name=name,
    )(*scalars, *operands, *after, *relay)
    return out[0] if single else out


def doc_columns(doc_rows, tokens):
    parts = []
    for i in range(tokens // LANES):
        row = jnp.broadcast_to(doc_rows[i : i + 1, :], (LANES, LANES))
        parts.append(jnp.transpose(row))
    return jnp.concatenate(parts, axis=0)


def doc_line(doc_rows, tokens):
    return jnp.concatenate([doc_rows[i : i + 1, :] for i in range(tokens // LANES)], axis=1)


def lower_triangle(tokens):
    rows = lax.broadcasted_iota(jnp.int32, (tokens, tokens), 0)
    cols = lax.broadcasted_iota(jnp.int32, (tokens, tokens), 1)
    return rows >= cols


def pass_on(x, after):
    return call(lambda: None, "pass_on", [], [], (), after=after, relay=[x])[0]


def fetch_kernel(tokens, heads, kv_here, start_ref, *refs):
    refs = list(refs)
    take = lambda n: [refs.pop(0) for _ in range(n)]
    sources = take(6)
    kv_ref, doc_out, cumul_ref, key_out, value_out = take(5)
    held = take(4)
    sems, wide, ldp = refs
    docs_in, decays, soft_key, soft_value = held
    targets = [*held, key_out, value_out]
    copies = [
        pltpu.make_async_copy(source, target, sems.at[i])
        for i, (source, target) in enumerate(zip(sources, targets))
    ]
    for copy in copies:
        copy.start()

    copies[0].wait()
    docs = docs_in[...].astype(F32) + 1.0
    line = lax.broadcasted_iota(jnp.int32, (INFO, LANES), 0)
    info = jnp.zeros((INFO, LANES), F32)
    for i in range(tokens // LANES):
        info = jnp.where(line == i, docs[i : i + 1, :], info)
    doc_out[...] = info
    end = 2 * kv_here * tokens
    kv_ref[end : end + INFO, :] = info.astype(BF16)

    copies[1].wait()
    ldp[...] = jnp.zeros_like(ldp)
    ldp[0:heads, :] = decays[...]
    cumul_ref[...] = lax.dot_general(
        lower_triangle(tokens).astype(F32),
        ldp[...],
        (((1,), (1,)), ((), ())),
        precision=HIGHEST,
        preferred_element_type=F32,
    )

    start = start_ref[0]
    for which, ref in enumerate((soft_key, soft_value)):
        copies[2 + which].wait()
        wide[...] = ref[...].astype(F32)
        for g in range(kv_here):
            rows = wide[pl.ds(start + g, tokens, stride=KV_HEADS), :]
            at = (which * kv_here + g) * tokens
            if which:
                halves = [jnp.transpose(rows[i : i + LANES, :]) for i in range(0, tokens, LANES)]
                rows = jnp.concatenate(halves, axis=0)
            kv_ref[at : at + tokens, :] = rows.astype(BF16)
    for copy in copies[4:]:
        copy.wait()


def fetch(start, operands, tokens, heads, kv_here):
    return call(
        functools.partial(fetch_kernel, tokens, heads, kv_here),
        "fetch",
        [start],
        operands,
        (
            sds((2 * kv_here * tokens + INFO, LANES), BF16),
            sds((INFO, LANES), F32),
            sds((tokens, LANES), F32),
            sds(operands[4].shape, BF16),
            sds(operands[5].shape, BF16),
        ),
        scratch=[pltpu.VMEM(x.shape, x.dtype) for x in operands[:4]]
        + [
            pltpu.SemaphoreType.DMA((len(operands),)),
            pltpu.VMEM((tokens * KV_HEADS, LANES), F32),
            pltpu.VMEM((LANES, tokens), F32),
        ],
        estimate=cost(0, 3 * tokens * heads * LANES * 2),
        hbm=len(operands),
    )


def quarter_rows(heads):
    return heads * HEAD_DIM // GROUP_BLOCKS


def state_kernel(tokens, heads, place_ref, *refs):
    refs = list(refs)
    take = lambda n: [refs.pop(0) for _ in range(n)]
    query_in, cumul_ref, doc_ref, key_ref, value_ref = take(5)
    out_refs, query_out = take(GROUP_BLOCKS), take(1)[0]
    kf, vf, states, sem = refs
    copy = pltpu.make_async_copy(query_in, query_out, sem)
    copy.start()
    cumul, docs = cumul_ref[...], doc_ref[...]
    total = cumul[tokens - 1 : tokens, :]
    last_row = tokens // LANES - 1
    first_doc = docs[0:1, 0:1]
    last_doc = docs[last_row : last_row + 1, LANES - 1 : LANES]
    tail = (doc_columns(docs, tokens) == last_doc).astype(F32)
    scale = jnp.exp(total - cumul) * tail
    kf[...] = key_ref[...].astype(F32)
    vf[...] = value_ref[...].astype(F32)
    for h in range(heads):
        keys = (kf[pl.ds(h, tokens, stride=heads), :] * scale[:, h : h + 1]).astype(BF16)
        values = vf[pl.ds(h, tokens, stride=heads), :].astype(BF16)
        states[h * HEAD_DIM : (h + 1) * HEAD_DIM, :] = lax.dot_general(
            keys, values, (((0,), (0,)), ((), ())), preferred_element_type=F32
        )
    size = quarter_rows(heads)
    mine = place_ref[0] % GROUP_BLOCKS
    for j, ref in enumerate(out_refs):
        taker = mine ^ j
        ref[0:size, :] = states[pl.ds(pl.multiple_of(taker * size, size), size), :].astype(BF16)
        totals = jnp.zeros_like(total)
        for c in range(GROUP_BLOCKS):
            skip = c * heads // GROUP_BLOCKS
            moved = pltpu.roll(total, LANES - skip, 1) if skip else total
            totals = jnp.where(taker == c, moved, totals)
        ref[size : size + INFO, :] = info_rows((*in_parts(totals), first_doc, last_doc))
    copy.wait()


def block_state(place, soft_query, cumul, docs, key, value, tokens, heads):
    return call(
        functools.partial(state_kernel, tokens, heads),
        "block_state",
        [place],
        [soft_query, cumul, docs, key, value],
        (
            *[sds((quarter_rows(heads) + INFO, LANES), BF16)] * GROUP_BLOCKS,
            sds(soft_query.shape, BF16),
        ),
        scratch=[
            pltpu.VMEM((tokens * heads, LANES), F32),
            pltpu.VMEM((tokens * heads, LANES), F32),
            pltpu.VMEM((heads * HEAD_DIM, LANES), F32),
            pltpu.SemaphoreType.DMA,
        ],
        estimate=cost(2 * heads * tokens * HEAD_DIM**2, 5 * tokens * heads * LANES * 2),
        hbm=1,
    )


def in_parts(x):
    hi = x.astype(BF16).astype(F32)
    mid = (x - hi).astype(BF16).astype(F32)
    return hi, mid, x - hi - mid


def info_rows(parts):
    line = lax.broadcasted_iota(jnp.int32, (INFO, LANES), 0)
    info = jnp.zeros((INFO, LANES), F32)
    for i, part in enumerate(parts):
        info = jnp.where(line == i, part, info)
    return info.astype(BF16)


def read_map(ref, size):
    info = ref[size : size + INFO, :].astype(F32)
    return info[0:1] + info[1:2] + info[2:3], info[3:4], info[4:5]


def row_chunks(size):
    unit = min(HEAD_DIM, size)
    return [(slice(i * unit, (i + 1) * unit), slice(i, i + 1)) for i in range(size // unit)]


def in_block_order(place_ref, refs, blocks):
    mine = place_ref[0] % GROUP_BLOCKS
    for j, ref in enumerate(refs):
        blocks[mine ^ j] = ref[...]


def block_maps(blocks, size):
    maps = []
    for c in range(GROUP_BLOCKS):
        info = blocks[c, size : size + INFO, :].astype(F32)
        first, last = info[3:4], info[4:5]
        gain = jnp.exp(info[0:1] + info[1:2] + info[2:3]) * (first == last).astype(F32)
        maps.append((gain, first, last))
    return maps


def group_kernel(size, place_ref, *refs):
    sources = refs[:GROUP_BLOCKS]
    out_ref, blocks = refs[GROUP_BLOCKS:]
    in_block_order(place_ref, sources, blocks)
    maps = block_maps(blocks, size)
    gains = [None]
    for (gain, first, _), (_, _, last_before) in zip(maps[1:], maps[:-1]):
        gains.append(gain * (last_before == first).astype(F32))
    for rows, lane in row_chunks(size):
        total = blocks[0, rows, :].astype(F32)
        for c in range(1, GROUP_BLOCKS):
            total = gains[c][:, lane] * total + blocks[c, rows, :].astype(F32)
        out_ref[rows, :] = total.astype(BF16)
    gain = maps[0][0] * gains[1] * gains[2] * gains[3]
    out_ref[size : size + INFO, :] = info_rows((*in_parts(gain), maps[0][1], maps[-1][2]))


def group_map(place, quarters, size, after, relay):
    return call(
        functools.partial(group_kernel, size),
        "group_map",
        [place],
        quarters,
        (sds((size + INFO, LANES), BF16),),
        scratch=[pltpu.VMEM((GROUP_BLOCKS, size + INFO, LANES), BF16)],
        estimate=cost(8 * size * LANES, 10 * size * LANES * 2),
        after=after,
        relay=relay,
    )


def scan_kernel(size, has_before, bit, place_ref, *refs):
    mine_ref, came_ref = refs[:2]
    before_ref = refs[2] if has_before else None
    run_ref, out_ref = refs[-2:]
    upper = (place_ref[0] >> bit) & 1 == 1
    gain_m, first_m, last_m = read_map(mine_ref, size)
    gain_c, first_c, last_c = read_map(came_ref, size)
    link = jnp.where(upper, (last_c == first_m).astype(F32), (last_m == first_c).astype(F32))
    gain = jnp.where(upper, gain_m, gain_c) * link
    for rows, lane in row_chunks(size):
        mine, came = mine_ref[rows, :].astype(F32), came_ref[rows, :].astype(F32)
        lower_sum, upper_sum = jnp.where(upper, came, mine), jnp.where(upper, mine, came)
        run_ref[rows, :] = (gain[:, lane] * lower_sum + upper_sum).astype(BF16)
    run_ref[size : size + INFO, :] = info_rows(
        (
            *in_parts(gain * jnp.where(upper, gain_c, gain_m)),
            jnp.where(upper, first_c, first_m),
            jnp.where(upper, last_m, last_c),
        )
    )
    if not has_before:
        out_ref[...] = jnp.where(upper, came_ref[...], jnp.zeros_like(came_ref))
        return
    gain_b, first_b, last_b = read_map(before_ref, size)
    empty = first_b == 0.0
    factor = jnp.where(empty, 1.0, gain_b * (last_c == first_b).astype(F32))
    for rows, lane in row_chunks(size):
        before = before_ref[rows, :].astype(F32)
        joined = factor[:, lane] * came_ref[rows, :].astype(F32) + before
        out_ref[rows, :] = jnp.where(upper, joined, before).astype(BF16)
    out_ref[size : size + INFO, :] = info_rows(
        (
            *in_parts(jnp.where(upper, factor * gain_c, gain_b)),
            jnp.where(upper, first_c, first_b),
            jnp.where(upper, jnp.where(empty, last_c, last_b), last_b),
        )
    )


def scan_step(place, bit, mine, came, before, size, after):
    shape = sds((size + INFO, LANES), BF16)
    before = [] if before is None else [before]
    return call(
        functools.partial(scan_kernel, size, len(before), bit),
        "scan_step",
        [place],
        [mine, came, *before],
        (shape, shape),
        estimate=cost(6 * size * LANES, 6 * size * LANES * 2),
        after=after,
    )


def prior_kernel(size, has_before, bit, place_ref, *refs):
    sources, came_ref = refs[:GROUP_BLOCKS], refs[GROUP_BLOCKS]
    before_ref = refs[GROUP_BLOCKS + 1] if has_before else None
    *out_refs, doc_ref, blocks, priors = refs[GROUP_BLOCKS + 1 + has_before :]
    mine = place_ref[0] % GROUP_BLOCKS
    in_block_order(place_ref, sources, blocks)
    maps = block_maps(blocks, size)
    upper = ((place_ref[0] >> bit) & 1).astype(F32)
    _, _, last_c = read_map(came_ref, size)
    factor, doc = jnp.broadcast_to(upper, (1, LANES)), upper * last_c
    if has_before:
        gain_b, first_b, last_b = read_map(before_ref, size)
        empty = first_b == 0.0
        factor = upper * jnp.where(empty, 1.0, gain_b * (last_c == first_b).astype(F32))
        doc = jnp.where(empty, doc, last_b)
    docs = [doc] + [last for _, _, last in maps[:-1]]
    gains = [gain * (doc == first).astype(F32) for (gain, first, _), doc in zip(maps, docs)]
    for rows, lane in row_chunks(size):
        state = factor[:, lane] * came_ref[rows, :].astype(F32)
        if has_before:
            state = state + before_ref[rows, :].astype(F32)
        for c in range(GROUP_BLOCKS):
            priors[c, rows, :] = state.astype(BF16)
            if c < GROUP_BLOCKS - 1:
                state = gains[c][:, lane] * state + blocks[c, rows, :].astype(F32)
    for j, ref in enumerate(out_refs):
        ref[...] = priors[mine ^ j]
    own_doc = docs[0]
    for c in range(1, GROUP_BLOCKS):
        own_doc = jnp.where(mine == c, docs[c], own_doc)
    doc_ref[...] = jnp.broadcast_to(own_doc, (8, LANES))


def prior_states(place, bit, quarters, came, before, size, after, relay=()):
    before = [] if before is None else [before]
    return call(
        functools.partial(prior_kernel, size, len(before), bit),
        "prior_states",
        [place],
        [*quarters, came, *before],
        (*[sds((size, LANES), BF16)] * GROUP_BLOCKS, sds((8, LANES), F32)),
        scratch=[
            pltpu.VMEM((GROUP_BLOCKS, size + INFO, LANES), BF16),
            pltpu.VMEM((GROUP_BLOCKS, size, LANES), BF16),
        ],
        estimate=cost(8 * size * LANES, 10 * size * LANES * 2),
        after=after,
        relay=relay,
    )


def some_heads(ref, tokens, heads, first, count):
    x = ref[...].astype(F32)
    if count == heads:
        return x
    return x.reshape(tokens, heads, LANES)[:, first : first + count, :].reshape(tokens * count, LANES)


def inner_kernel(tokens, heads, first, count, cumul_ref, doc_ref, query_ref, key_ref, value_ref, inner_ref, qh_ref, qf, kf, vf, mask):
    cumul = cumul_ref[...]
    cumul_t = jnp.transpose(cumul)
    docs = doc_ref[...]
    column = doc_columns(docs, tokens)
    same = jnp.concatenate([column] * (tokens // LANES), axis=1) == doc_line(docs, tokens)
    mask[...] = jnp.where(lower_triangle(tokens) & same, 0.0, -1e9)
    qf[...] = some_heads(query_ref, tokens, heads, first, count)
    kf[...] = some_heads(key_ref, tokens, heads, first, count)
    vf[...] = some_heads(value_ref, tokens, heads, first, count)
    for n in range(count):
        h = first + n
        picked = pl.ds(n, tokens, stride=count)
        query = qf[picked, :].astype(BF16)
        keys = kf[picked, :].astype(BF16)
        values = vf[picked, :].astype(BF16)
        qh_ref[n * tokens : (n + 1) * tokens, :] = query
        for i in range(tokens // LANES):
            seen = (i + 1) * LANES
            rows = slice(i * LANES, seen)
            scores = lax.dot_general(
                query[rows, :], keys[0:seen, :], (((1,), (1,)), ((), ())), preferred_element_type=F32
            )
            gap = cumul[rows, h : h + 1] - cumul_t[h : h + 1, 0:seen]
            weights = (scores * jnp.exp(gap + mask[rows, 0:seen])).astype(BF16)
            inner_ref[n * tokens + i * LANES : n * tokens + seen, :] = jnp.dot(
                weights, values[0:seen, :], preferred_element_type=F32
            )


def inner_part(cumul, docs, query, key, value, tokens, heads, first, count, after, relay):
    return call(
        functools.partial(inner_kernel, tokens, heads, first, count),
        "inner_part",
        [],
        [cumul, docs, query, key, value],
        (sds((count * tokens, LANES), F32), sds((count * tokens, LANES), BF16)),
        scratch=[pltpu.VMEM((tokens * count, LANES), F32)] * 3 + [pltpu.VMEM((tokens, tokens), F32)],
        mib=24,
        estimate=cost(
            4 * count * tokens * tokens * HEAD_DIM, tokens * heads * LANES * 12, count * tokens * tokens
        ),
        after=after,
        relay=relay,
    )


def mix_kernel(tokens, heads, parts, place_ref, doc_ref, prior_doc_ref, cumul_ref, *refs):
    refs = list(refs)
    take = lambda n: [refs.pop(0) for _ in range(n)]
    inner, qh, quarters = take(parts), take(parts), take(GROUP_BLOCKS)
    mixed_ref, square_ref, states = refs
    size = quarter_rows(heads)
    mine = place_ref[0] % GROUP_BLOCKS
    for j, ref in enumerate(quarters):
        states[pl.ds(pl.multiple_of((mine ^ j) * size, size), size), :] = ref[...]
    is_open = (doc_columns(doc_ref[...], tokens) == prior_doc_ref[0:1, :]).astype(F32)
    gain = jnp.exp(cumul_ref[...]) * is_open
    squares = jnp.zeros((tokens, LANES), F32)
    for h in range(heads):
        part, n = divmod(h, heads // parts)
        held = slice(n * tokens, (n + 1) * tokens)
        state = states[h * HEAD_DIM : (h + 1) * HEAD_DIM, :]
        carried = jnp.dot(qh[part][held, :], state, preferred_element_type=F32)
        mixed = inner[part][held, :] + carried * gain[:, h : h + 1]
        squares = squares + mixed * mixed
        mixed_ref[pl.ds(h, tokens, stride=heads), :] = mixed
    square_ref[...] = lax.dot_general(
        jnp.ones((8, LANES), F32),
        squares,
        (((1,), (1,)), ((), ())),
        precision=HIGHEST,
        preferred_element_type=F32,
    )


def mix(place, docs, prior_doc, cumul, inner, qh, quarters, tokens, heads, after):
    return call(
        functools.partial(mix_kernel, tokens, heads, len(inner)),
        "mix",
        [place],
        [docs, prior_doc, cumul, *inner, *qh, *quarters],
        (sds((tokens * heads, LANES), F32), sds((8, tokens), F32)),
        scratch=[pltpu.VMEM((heads * HEAD_DIM, LANES), BF16)],
        mib=24,
        estimate=cost(2 * heads * tokens * HEAD_DIM**2, tokens * heads * LANES * 10),
        after=after,
    )


def finish_kernel(tokens, heads, sums, step, gain_ref, gate_ref, mixed_ref, *refs):
    squares, (out_ref, done, sems) = refs[:sums], refs[sums:]
    total = squares[0][0:1, :]
    for ref in squares[1:]:
        total = total + ref[0:1, :]
    scale = lax.rsqrt(total / (HEADS * HEAD_DIM) + 1e-06)
    rows = jnp.concatenate([scale[:, i * LANES : (i + 1) * LANES] for i in range(tokens // LANES)], axis=0)
    column = doc_columns(rows, tokens)
    copies = []
    for i in range(0, tokens, step):
        at = pl.ds(i * heads, step * heads)
        gate = jax.nn.sigmoid(gate_ref[at, :].astype(F32)).reshape(step, heads, LANES)
        mixed = mixed_ref[at, :].reshape(step, heads, LANES)
        inv = column[i : i + step, :][:, None, :]
        out = mixed * inv * gain_ref[...][None] * gate
        done[at, :] = out.reshape(step * heads, LANES).astype(BF16)
        copies.append(pltpu.make_async_copy(done.at[at, :], out_ref.at[at, :], sems.at[i // step]))
        copies[-1].start()
    for copy in copies:
        copy.wait()


def finish(gain, gate, mixed, squares, tokens, heads, after):
    step = 64
    return call(
        functools.partial(finish_kernel, tokens, heads, len(squares), step),
        "finish",
        [],
        [gain, gate, mixed, *squares],
        sds((tokens * heads, LANES), BF16),
        scratch=[pltpu.VMEM((tokens * heads, LANES), BF16), pltpu.SemaphoreType.DMA((tokens // step,))],
        estimate=cost(0, tokens * heads * LANES * 8, tokens * heads * LANES),
        after=after,
        out_hbm=True,
    )


def attend_kernel(tokens, heads, kv_here, least, is_first, is_last, unroll, place_ref, *refs):
    refs = list(refs)
    take = lambda n: [refs.pop(0) for _ in range(n)]
    per_group = heads // kv_here
    rows = tokens * per_group
    step = CHUNK // per_group
    if is_first:
        doc_ref, query_ref = take(2)
    else:
        wide_ref, state_ref = take(2)
    kv = take(len(least))
    if is_first:
        wide_ref = take(1)[0]
    out_ref = take(1)[0]
    if is_last:
        take(1)[0][...] = jnp.zeros((8, LANES), F32)
    bias = take(1)[0]
    if is_first:
        doc_rep = take(1)[0]
    if is_last:
        done, sems = take(2)
    block = place_ref[0]

    lane = lax.broadcasted_iota(jnp.int32, (tokens, LANES), 1).astype(F32)
    end = 2 * kv_here * tokens
    for j, ref in enumerate(kv):
        valid = (block >= jnp.where(block % 2 == 0, *least[j])).astype(F32)
        docs = doc_columns(ref[end : end + INFO, :].astype(F32) * valid, tokens)
        bias[j] = jnp.where(docs == lane, 0.0, -BIG).astype(BF16)
    if is_first:
        column = doc_columns(doc_ref[...], tokens)
        for h in range(per_group):
            doc_rep[pl.ds(h, tokens, stride=per_group), :] = (column == lane).astype(F32)
    ones = jnp.ones((STATE_ROWS - HEAD_DIM, tokens), BF16)

    def some_chunks(i, carry):
        chains = [(u, g) for u in range(unroll) for g in range(kv_here)]
        chunk = [i * unroll + u for u in range(unroll)]
        at = [pl.ds(pl.multiple_of(c * CHUNK, CHUNK), CHUNK) for c in chunk]
        picked = [pl.ds(pl.multiple_of(c * (step * heads), step * heads), step * heads) for c in chunk]
        scores, results = {}, {}

        def begin(u, g):
            if is_first:
                query = query_ref[picked[u], :].astype(F32).reshape(step, heads, LANES)
                query = query[:, g * per_group : (g + 1) * per_group, :].reshape(CHUNK, LANES)
                wide = jnp.concatenate([query.astype(BF16), doc_rep[at[u], :].astype(BF16)], axis=1)
                wide_ref[g, at[u], :] = wide
            else:
                wide = wide_ref[g, at[u], :]
            out = []
            for j, ref in enumerate(kv):
                keys = jnp.concatenate([ref[g * tokens : (g + 1) * tokens, :], bias[j]], axis=1)
                out.append(
                    lax.dot_general(keys, wide, (((1,), (1,)), ((), ())), preferred_element_type=F32)
                )
            if is_first:
                token = chunk[u] * step + lax.broadcasted_iota(jnp.int32, (tokens, CHUNK), 1) // per_group
                key_at = lax.broadcasted_iota(jnp.int32, (tokens, CHUNK), 0)
                out[0] = jnp.where(key_at <= token, out[0], -BIG)
            scores[u, g] = out

        def end_chain(u, g):
            here = scores.pop((u, g))
            top = jnp.max(here[0], axis=0, keepdims=True)
            for score in here[1:]:
                top = jnp.maximum(top, jnp.max(score, axis=0, keepdims=True))
            total = None
            if not is_first:
                before = state_ref[g, :, at[u]]
                top_before = before[STATE_ROWS - 1 : STATE_ROWS, :]
                top = jnp.maximum(top, top_before)
                total = before * jnp.exp2((top_before - top) * SCORE_TO_EXP2)
            for ref, score in zip(kv, here):
                weights = jnp.exp2((score - top) * SCORE_TO_EXP2).astype(BF16)
                first = (kv_here + g) * tokens
                parts = [ref[first + p : first + p + LANES, :] for p in range(0, tokens, LANES)]
                values = jnp.concatenate([jnp.concatenate(parts, axis=1), ones], axis=0)
                more = jnp.dot(values, weights, preferred_element_type=F32)
                total = more if total is None else total + more
            if is_last:
                results[u, g] = jnp.transpose(total[0:HEAD_DIM] / total[HEAD_DIM : HEAD_DIM + 1])
            else:
                out_ref[g, 0 : STATE_ROWS - 8, at[u]] = total[0 : STATE_ROWS - 8]
                out_ref[g, STATE_ROWS - 8 : STATE_ROWS, at[u]] = jnp.broadcast_to(top, (8, CHUNK))

        ahead = 2
        for n in range(len(chains) + ahead):
            if n < len(chains):
                begin(*chains[n])
            if n >= ahead:
                end_chain(*chains[n - ahead])
        if is_last:
            for u in range(unroll):
                result = [results[u, g] for g in range(kv_here)]
                if kv_here > 1:
                    result = [r.reshape(step, per_group, LANES) for r in result]
                    result = [jnp.concatenate(result, axis=1).reshape(step * heads, LANES)]
                done[picked[u], :] = result[0].astype(BF16)
                pltpu.make_async_copy(
                    done.at[picked[u], :], out_ref.at[picked[u], :], sems.at[chunk[u]]
                ).start()
        return carry

    lax.fori_loop(0, rows // (CHUNK * unroll), some_chunks, 0)
    if is_last:
        for c in range(rows // CHUNK):
            at = pl.ds(c * step * heads, step * heads)
            pltpu.make_async_copy(done.at[at, :], out_ref.at[at, :], sems.at[c]).wait()


def attend(place, first, state, kv, is_last, tokens, heads, kv_here, after, relay=()):
    is_first = state is None
    least = tuple(pair for _, pair in kv)
    kv = [block for block, _ in kv]
    blocks = len(kv)
    rows = tokens * heads // kv_here
    unroll = min(4, rows // CHUNK)
    wide_shape = sds((kv_here, rows, 2 * LANES), BF16)
    state_shape = sds((kv_here, STATE_ROWS, rows), F32)
    out_shape = sds((tokens * heads, LANES), BF16) if is_last else state_shape
    scratch = [pltpu.VMEM((blocks, tokens, LANES), BF16)]
    if is_first:
        out_shape = (wide_shape, out_shape)
        scratch.append(pltpu.VMEM((rows, LANES), F32))
    if is_last:
        out_shape = (out_shape, sds((8, LANES), F32))
        scratch.append(pltpu.VMEM((tokens * heads, LANES), BF16))
        scratch.append(pltpu.SemaphoreType.DMA((rows // CHUNK,)))
    span = blocks * tokens
    return call(
        functools.partial(attend_kernel, tokens, heads, kv_here, least, is_first, is_last, unroll),
        "attend",
        [place],
        [*first, *([] if is_first else [state]), *kv],
        out_shape,
        scratch=scratch,
        mib=24,
        estimate=cost(
            4 * tokens * heads * span * 2 * LANES, 4 * tokens * heads * LANES * 4, tokens * heads * span
        ),
        after=after,
        out_hbm=is_last,
        relay=relay,
    )


def body(
    blocks,
    lin_query,
    lin_key,
    lin_value,
    lin_gate,
    log_decay,
    norm_gain,
    doc_ids,
    soft_query,
    soft_key,
    soft_value,
):
    tokens, heads, _ = lin_query.shape
    tensor = HEADS // heads
    kv_here = max(1, heads // GROUP)
    parts = 2 if heads % 16 == 0 else 1
    longest = blocks * tokens * 5 // 8
    window = min(blocks - 1, (longest - 1 + tokens - 1) // tokens)
    flat = lambda x: x.reshape(-1, LANES)
    block = lax.axis_index("seq")
    place = block.astype(jnp.int32).reshape(1)
    start = (lax.axis_index("tp") * heads // GROUP).astype(jnp.int32).reshape(1)

    def send(x, pairs):
        return lax.ppermute(x, "seq", [(a, b % blocks) for a, b in pairs])

    everyone = range(blocks)
    swap = [(b, b ^ 1) for b in everyone]

    own_kv, docs, cumul, key, value = fetch(
        start,
        [
            doc_ids.reshape(tokens // LANES, LANES),
            jnp.transpose(log_decay),
            flat(soft_key),
            flat(soft_value),
            flat(lin_key),
            flat(lin_value),
        ],
        tokens,
        heads,
        kv_here,
    )

    forward = [(b, b + 2) for b in everyone]
    hop = {b: b ^ 1 for b in everyone}
    if window % 2:
        for b in range(1, blocks - window, 2):
            last = next(a for a in everyone if hop[a] == b + window)
            hop[b], hop[last] = b + window, hop[b]
    ahead = send(own_kv, forward)

    size = quarter_rows(heads)
    others = range(1, GROUP_BLOCKS)
    *sent, query = block_state(
        place, flat(soft_query), cumul, docs, key, value, tokens, heads
    )
    quarters = [sent[0]] + [send(sent[j], [(b, b ^ j) for b in everyone]) for j in others]

    state = {}

    def first_attention(after):
        state["wide"], state["sum"] = attend(
            place, (docs, query), None, [(own_kv, (0, 0))], False, tokens, heads, kv_here, after
        )
        return state["sum"]

    def more_attention(kv, is_last, after, relay=()):
        out = attend(
            place, (state["wide"],), state["sum"], kv, is_last, tokens, heads, kv_here, after, relay
        )
        state["sum"] = out[0] if relay else out
        return out

    inner, qh = [], []

    def inner_of(part, after, relay=()):
        n = heads // parts
        got = inner_part(
            cumul, docs, flat(lin_query), key, value, tokens, heads, part * n, n, after, relay
        )
        inner.append(got[0])
        qh.append(got[1])
        return (got[0], *got[2:]) if relay else got[0]

    done = first_attention([sent[0]])
    lane = ahead
    if parts > 1:
        done, lane = inner_of(0, [done], [ahead])
    second = send(lane, [(b, b + 2) for b in range(2, blocks - 2)])
    run, lane, own_copy = group_map(place, quarters, size, [done], [lane, own_kv])
    first_cross = send(lane, swap)
    beside = (send(own_copy, list(hop.items())), (window if window % 2 else blocks, 1))
    stages = (blocks // GROUP_BLOCKS).bit_length() - 1
    before, done = None, run
    for stage in range(stages):
        came = send(run, [(b, b ^ (GROUP_BLOCKS << stage)) for b in everyone])
        if stage == stages - 1:
            done = more_attention([(lane, (2, 2))], False, [done])
            done = inner_of(parts - 1, [done])
        else:
            run, before = scan_step(place, stage + 2, run, came, before, size, [done])
            done = run
    *priors, prior_doc = prior_states(place, stages + 1, quarters, came, before, size, [done])
    priors = [priors[0]] + [send(priors[j], [(b, b ^ j) for b in everyone]) for j in others]
    done = more_attention([(first_cross, (2, 3)), (second, (4, 4))], False, [prior_doc])
    lane = pass_on(second, [done, *priors])
    rest = [beside, (send(lane, swap), (4, 5))]
    for back in range(3, window // 2 + 1):
        lane = send(lane, forward)
        rest.append((lane, (2 * back, 2 * back)))
        rest.append((send(lane, swap), (2 * back, 2 * back + 1)))
    mixed, squares = mix(place, docs, prior_doc, cumul, inner, qh, priors, tokens, heads, [done])
    sums = [squares]
    for other in range(1, tensor):
        sums.append(lax.ppermute(squares, "tp", [(t, t ^ other) for t in range(tensor)]))
    done = squares
    while rest:
        got = more_attention(rest[:2], len(rest) <= 2, [done])
        rest, done = rest[2:], got
    soft_out, done = got
    lin_out = finish(norm_gain, flat(lin_gate), mixed, sums, tokens, heads, [done])
    shape = (tokens, heads, HEAD_DIM)
    return lin_out.reshape(shape), soft_out.reshape(shape)


def solution(mesh):
    in_specs = (
        P("seq", "tp", None),
        P("seq", "tp", None),
        P("seq", "tp", None),
        P("seq", "tp", None),
        P("seq", "tp"),
        P("tp", None),
        P("seq"),
        P("seq", "tp", None),
        P("seq", None, None),
        P("seq", None, None),
    )
    out_specs = (P("seq", "tp", None), P("seq", "tp", None))
    return jax.shard_map(
        functools.partial(body, mesh.shape["seq"]),
        mesh=mesh,
        in_specs=in_specs,
        out_specs=out_specs,
        check_vma=False,
    )
```

```python
import functools

import jax
import jax.numpy as jnp
import numpy as np
from jax import lax
from jax.experimental import pallas as pl
from jax.experimental.pallas import tpu as pltpu
from jax.sharding import PartitionSpec as P

HEADS = 64
HEAD_DIM = 128
KV_HEADS = 8
LANES = 128
GROUP = HEADS // KV_HEADS
F32 = jnp.float32
BF16 = jnp.bfloat16
BIG = float(2**20)
SCORE_TO_EXP2 = HEAD_DIM**-0.5 * float(np.log2(np.e))
INFO = 16
HIGHEST = lax.Precision.HIGHEST

VMEM = pl.BlockSpec(memory_space=pltpu.VMEM)
SMEM = pl.BlockSpec(memory_space=pltpu.SMEM)
HBM = pl.BlockSpec(memory_space=pltpu.HBM)
ANYWHERE = pl.BlockSpec(memory_space=pl.ANY)
STATE_ROWS = HEAD_DIM + 16
CHUNK = 256
GROUP_BLOCKS = 4


def sds(shape, dtype):
    return jax.ShapeDtypeStruct(shape, dtype)


def cost(flops, bytes_accessed, transcendentals=0):
    return pl.CostEstimate(
        flops=int(flops), bytes_accessed=int(bytes_accessed), transcendentals=int(transcendentals)
    )


def call(kernel, name, scalars, operands, out_shape, scratch=(), mib=16, estimate=None, after=(), hbm=0, out_hbm=False, relay=()):
    begin = len(scalars) + len(operands)
    skip = len(after)
    operands = [
        pltpu.with_memory_space_constraint(x, pltpu.HBM) if i < hbm else x for i, x in enumerate(operands)
    ]
    outs = out_shape if isinstance(out_shape, tuple) else (out_shape,)
    out_specs = (VMEM,) * len(outs)
    outs = tuple(
        (pltpu.HBM if out_hbm and i == 0 else pltpu.VMEM)(x.shape, x.dtype) for i, x in enumerate(outs)
    )
    if out_hbm:
        out_specs = (HBM, *out_specs[1:])

    moved = len(relay)
    many = len(outs)
    single = not isinstance(out_shape, tuple) and not relay
    out_specs += (VMEM,) * moved
    outs += tuple(pltpu.VMEM(x.shape, x.dtype) for x in relay)

    def run(*refs):
        rest = refs[begin + skip + moved :]
        for source, target in zip(refs[begin + skip : begin + skip + moved], rest[many : many + moved]):
            target[...] = source[...]
        kernel(*refs[:begin], *rest[:many], *rest[many + moved :])

    out = pl.pallas_call(
        run,
        out_shape=outs,
        in_specs=[SMEM] * len(scalars) + [HBM] * hbm + [VMEM] * (len(operands) - hbm) + [ANYWHERE] * skip + [VMEM] * moved,
        out_specs=out_specs,
        scratch_shapes=list(scratch),
        compiler_params=pltpu.CompilerParams(vmem_limit_bytes=mib * 1024 * 1024),
        cost_estimate=estimate,
        name=name,
    )(*scalars, *operands, *after, *relay)
    return out[0] if single else out


def doc_columns(doc_rows, tokens):
    parts = []
    for i in range(tokens // LANES):
        row = jnp.broadcast_to(doc_rows[i : i + 1, :], (LANES, LANES))
        parts.append(jnp.transpose(row))
    return jnp.concatenate(parts, axis=0)


def doc_line(doc_rows, tokens):
    return jnp.concatenate([doc_rows[i : i + 1, :] for i in range(tokens // LANES)], axis=1)


def lower_triangle(tokens):
    rows = lax.broadcasted_iota(jnp.int32, (tokens, tokens), 0)
    cols = lax.broadcasted_iota(jnp.int32, (tokens, tokens), 1)
    return rows >= cols


def pick_kernel(place_ref, even_ref, odd_ref, out_ref):
    out_ref[...] = jnp.where(place_ref[0] % 2 == 0, even_ref[...], odd_ref[...])


def pass_on(place, even, odd, x, after):
    return call(
        pick_kernel, "pass_on", [place], [even, odd], (sds(even.shape, BF16),), after=after, relay=[x]
    )


def fetch_kernel(tokens, heads, kv_here, start_ref, *refs):
    refs = list(refs)
    take = lambda n: [refs.pop(0) for _ in range(n)]
    sources = take(6)
    kv_ref, doc_out, cumul_ref, key_out, value_out = take(5)
    held = take(4)
    sems, wide, ldp = refs
    docs_in, decays, soft_key, soft_value = held
    targets = [*held, key_out, value_out]
    copies = [
        pltpu.make_async_copy(source, target, sems.at[i])
        for i, (source, target) in enumerate(zip(sources, targets))
    ]
    for copy in copies:
        copy.start()

    copies[0].wait()
    docs = docs_in[...].astype(F32) + 1.0
    line = lax.broadcasted_iota(jnp.int32, (INFO, LANES), 0)
    info = jnp.zeros((INFO, LANES), F32)
    for i in range(tokens // LANES):
        info = jnp.where(line == i, docs[i : i + 1, :], info)
    doc_out[...] = info
    end = 2 * kv_here * tokens
    kv_ref[end : end + INFO, :] = info.astype(BF16)

    copies[1].wait()
    ldp[...] = jnp.zeros_like(ldp)
    ldp[0:heads, :] = decays[...]
    cumul_ref[...] = lax.dot_general(
        lower_triangle(tokens).astype(F32),
        ldp[...],
        (((1,), (1,)), ((), ())),
        precision=HIGHEST,
        preferred_element_type=F32,
    )

    start = start_ref[0]
    for which, ref in enumerate((soft_key, soft_value)):
        copies[2 + which].wait()
        wide[...] = ref[...].astype(F32)
        for g in range(kv_here):
            rows = wide[pl.ds(start + g, tokens, stride=KV_HEADS), :]
            at = (which * kv_here + g) * tokens
            if which:
                halves = [jnp.transpose(rows[i : i + LANES, :]) for i in range(0, tokens, LANES)]
                rows = jnp.concatenate(halves, axis=0)
            kv_ref[at : at + tokens, :] = rows.astype(BF16)
    for copy in copies[4:]:
        copy.wait()


def fetch(start, operands, tokens, heads, kv_here):
    return call(
        functools.partial(fetch_kernel, tokens, heads, kv_here),
        "fetch",
        [start],
        operands,
        (
            sds((2 * kv_here * tokens + INFO, LANES), BF16),
            sds((INFO, LANES), F32),
            sds((tokens, LANES), F32),
            sds(operands[4].shape, BF16),
            sds(operands[5].shape, BF16),
        ),
        scratch=[pltpu.VMEM(x.shape, x.dtype) for x in operands[:4]]
        + [
            pltpu.SemaphoreType.DMA((len(operands),)),
            pltpu.VMEM((tokens * KV_HEADS, LANES), F32),
            pltpu.VMEM((LANES, tokens), F32),
        ],
        estimate=cost(0, 3 * tokens * heads * LANES * 2),
        hbm=len(operands),
    )


def quarter_rows(heads):
    return heads * HEAD_DIM // GROUP_BLOCKS


def state_kernel(tokens, heads, place_ref, *refs):
    refs = list(refs)
    take = lambda n: [refs.pop(0) for _ in range(n)]
    query_in, cumul_ref, doc_ref, key_ref, value_ref = take(5)
    out_refs, query_out = take(GROUP_BLOCKS), take(1)[0]
    kf, vf, states, sem = refs
    copy = pltpu.make_async_copy(query_in, query_out, sem)
    copy.start()
    cumul, docs = cumul_ref[...], doc_ref[...]
    total = cumul[tokens - 1 : tokens, :]
    last_row = tokens // LANES - 1
    first_doc = docs[0:1, 0:1]
    last_doc = docs[last_row : last_row + 1, LANES - 1 : LANES]
    tail = (doc_columns(docs, tokens) == last_doc).astype(F32)
    scale = jnp.exp(total - cumul) * tail
    kf[...] = key_ref[...].astype(F32)
    vf[...] = value_ref[...].astype(F32)
    for h in range(heads):
        keys = (kf[pl.ds(h, tokens, stride=heads), :] * scale[:, h : h + 1]).astype(BF16)
        values = vf[pl.ds(h, tokens, stride=heads), :].astype(BF16)
        states[h * HEAD_DIM : (h + 1) * HEAD_DIM, :] = lax.dot_general(
            keys, values, (((0,), (0,)), ((), ())), preferred_element_type=F32
        )
    size = quarter_rows(heads)
    mine = place_ref[0] % GROUP_BLOCKS
    for j, ref in enumerate(out_refs):
        taker = mine ^ j
        ref[0:size, :] = states[pl.ds(pl.multiple_of(taker * size, size), size), :].astype(BF16)
        totals = jnp.zeros_like(total)
        for c in range(GROUP_BLOCKS):
            skip = c * heads // GROUP_BLOCKS
            moved = pltpu.roll(total, LANES - skip, 1) if skip else total
            totals = jnp.where(taker == c, moved, totals)
        ref[size : size + INFO, :] = info_rows((*in_parts(totals), first_doc, last_doc))
    copy.wait()


def block_state(place, soft_query, cumul, docs, key, value, tokens, heads):
    return call(
        functools.partial(state_kernel, tokens, heads),
        "block_state",
        [place],
        [soft_query, cumul, docs, key, value],
        (
            *[sds((quarter_rows(heads) + INFO, LANES), BF16)] * GROUP_BLOCKS,
            sds(soft_query.shape, BF16),
        ),
        scratch=[
            pltpu.VMEM((tokens * heads, LANES), F32),
            pltpu.VMEM((tokens * heads, LANES), F32),
            pltpu.VMEM((heads * HEAD_DIM, LANES), F32),
            pltpu.SemaphoreType.DMA,
        ],
        estimate=cost(2 * heads * tokens * HEAD_DIM**2, 5 * tokens * heads * LANES * 2),
        hbm=1,
    )


def in_parts(x):
    hi = x.astype(BF16).astype(F32)
    mid = (x - hi).astype(BF16).astype(F32)
    return hi, mid, x - hi - mid


def info_rows(parts):
    line = lax.broadcasted_iota(jnp.int32, (INFO, LANES), 0)
    info = jnp.zeros((INFO, LANES), F32)
    for i, part in enumerate(parts):
        info = jnp.where(line == i, part, info)
    return info.astype(BF16)


def read_map(ref, size):
    info = ref[size : size + INFO, :].astype(F32)
    return info[0:1] + info[1:2] + info[2:3], info[3:4], info[4:5]


def row_chunks(size):
    unit = min(HEAD_DIM, size)
    return [(slice(i * unit, (i + 1) * unit), slice(i, i + 1)) for i in range(size // unit)]


def in_block_order(place_ref, refs, blocks):
    mine = place_ref[0] % GROUP_BLOCKS
    for j, ref in enumerate(refs):
        blocks[mine ^ j] = ref[...]


def block_maps(blocks, size):
    maps = []
    for c in range(GROUP_BLOCKS):
        info = blocks[c, size : size + INFO, :].astype(F32)
        first, last = info[3:4], info[4:5]
        gain = jnp.exp(info[0:1] + info[1:2] + info[2:3]) * (first == last).astype(F32)
        maps.append((gain, first, last))
    return maps


def group_kernel(size, place_ref, *refs):
    sources = refs[:GROUP_BLOCKS]
    out_ref, blocks = refs[GROUP_BLOCKS:]
    in_block_order(place_ref, sources, blocks)
    maps = block_maps(blocks, size)
    gains = [None]
    for (gain, first, _), (_, _, last_before) in zip(maps[1:], maps[:-1]):
        gains.append(gain * (last_before == first).astype(F32))
    for rows, lane in row_chunks(size):
        total = blocks[0, rows, :].astype(F32)
        for c in range(1, GROUP_BLOCKS):
            total = gains[c][:, lane] * total + blocks[c, rows, :].astype(F32)
        out_ref[rows, :] = total.astype(BF16)
    gain = maps[0][0] * gains[1] * gains[2] * gains[3]
    out_ref[size : size + INFO, :] = info_rows((*in_parts(gain), maps[0][1], maps[-1][2]))


def group_map(place, quarters, size, after, relay):
    return call(
        functools.partial(group_kernel, size),
        "group_map",
        [place],
        quarters,
        (sds((size + INFO, LANES), BF16),),
        scratch=[pltpu.VMEM((GROUP_BLOCKS, size + INFO, LANES), BF16)],
        estimate=cost(8 * size * LANES, 10 * size * LANES * 2),
        after=after,
        relay=relay,
    )


def scan_kernel(size, has_before, bit, place_ref, *refs):
    mine_ref, came_ref = refs[:2]
    before_ref = refs[2] if has_before else None
    run_ref, out_ref = refs[-2:]
    upper = (place_ref[0] >> bit) & 1 == 1
    gain_m, first_m, last_m = read_map(mine_ref, size)
    gain_c, first_c, last_c = read_map(came_ref, size)
    link = jnp.where(upper, (last_c == first_m).astype(F32), (last_m == first_c).astype(F32))
    gain = jnp.where(upper, gain_m, gain_c) * link
    for rows, lane in row_chunks(size):
        mine, came = mine_ref[rows, :].astype(F32), came_ref[rows, :].astype(F32)
        lower_sum, upper_sum = jnp.where(upper, came, mine), jnp.where(upper, mine, came)
        run_ref[rows, :] = (gain[:, lane] * lower_sum + upper_sum).astype(BF16)
    run_ref[size : size + INFO, :] = info_rows(
        (
            *in_parts(gain * jnp.where(upper, gain_c, gain_m)),
            jnp.where(upper, first_c, first_m),
            jnp.where(upper, last_m, last_c),
        )
    )
    if not has_before:
        out_ref[...] = jnp.where(upper, came_ref[...], jnp.zeros_like(came_ref))
        return
    gain_b, first_b, last_b = read_map(before_ref, size)
    empty = first_b == 0.0
    factor = jnp.where(empty, 1.0, gain_b * (last_c == first_b).astype(F32))
    for rows, lane in row_chunks(size):
        before = before_ref[rows, :].astype(F32)
        joined = factor[:, lane] * came_ref[rows, :].astype(F32) + before
        out_ref[rows, :] = jnp.where(upper, joined, before).astype(BF16)
    out_ref[size : size + INFO, :] = info_rows(
        (
            *in_parts(jnp.where(upper, factor * gain_c, gain_b)),
            jnp.where(upper, first_c, first_b),
            jnp.where(upper, jnp.where(empty, last_c, last_b), last_b),
        )
    )


def scan_step(place, bit, mine, came, before, size, after):
    shape = sds((size + INFO, LANES), BF16)
    before = [] if before is None else [before]
    return call(
        functools.partial(scan_kernel, size, len(before), bit),
        "scan_step",
        [place],
        [mine, came, *before],
        (shape, shape),
        estimate=cost(6 * size * LANES, 6 * size * LANES * 2),
        after=after,
    )


def prior_kernel(size, has_before, bit, place_ref, *refs):
    sources, came_ref = refs[:GROUP_BLOCKS], refs[GROUP_BLOCKS]
    before_ref = refs[GROUP_BLOCKS + 1] if has_before else None
    *out_refs, doc_ref, blocks, priors = refs[GROUP_BLOCKS + 1 + has_before :]
    mine = place_ref[0] % GROUP_BLOCKS
    in_block_order(place_ref, sources, blocks)
    maps = block_maps(blocks, size)
    upper = ((place_ref[0] >> bit) & 1).astype(F32)
    _, _, last_c = read_map(came_ref, size)
    factor, doc = jnp.broadcast_to(upper, (1, LANES)), upper * last_c
    if has_before:
        gain_b, first_b, last_b = read_map(before_ref, size)
        empty = first_b == 0.0
        factor = upper * jnp.where(empty, 1.0, gain_b * (last_c == first_b).astype(F32))
        doc = jnp.where(empty, doc, last_b)
    docs = [doc] + [last for _, _, last in maps[:-1]]
    gains = [gain * (doc == first).astype(F32) for (gain, first, _), doc in zip(maps, docs)]
    for rows, lane in row_chunks(size):
        state = factor[:, lane] * came_ref[rows, :].astype(F32)
        if has_before:
            state = state + before_ref[rows, :].astype(F32)
        for c in range(GROUP_BLOCKS):
            priors[c, rows, :] = state.astype(BF16)
            if c < GROUP_BLOCKS - 1:
                state = gains[c][:, lane] * state + blocks[c, rows, :].astype(F32)
    for j, ref in enumerate(out_refs):
        ref[...] = priors[mine ^ j]
    own_doc = docs[0]
    for c in range(1, GROUP_BLOCKS):
        own_doc = jnp.where(mine == c, docs[c], own_doc)
    doc_ref[...] = jnp.broadcast_to(own_doc, (8, LANES))


def prior_states(place, bit, quarters, came, before, size, after, relay=()):
    before = [] if before is None else [before]
    return call(
        functools.partial(prior_kernel, size, len(before), bit),
        "prior_states",
        [place],
        [*quarters, came, *before],
        (*[sds((size, LANES), BF16)] * GROUP_BLOCKS, sds((8, LANES), F32)),
        scratch=[
            pltpu.VMEM((GROUP_BLOCKS, size + INFO, LANES), BF16),
            pltpu.VMEM((GROUP_BLOCKS, size, LANES), BF16),
        ],
        estimate=cost(8 * size * LANES, 10 * size * LANES * 2),
        after=after,
        relay=relay,
    )


def some_heads(ref, tokens, heads, first, count):
    x = ref[...].astype(F32)
    if count == heads:
        return x
    return x.reshape(tokens, heads, LANES)[:, first : first + count, :].reshape(tokens * count, LANES)


def inner_kernel(tokens, heads, first, count, cumul_ref, doc_ref, query_ref, key_ref, value_ref, inner_ref, qh_ref, qf, kf, vf, mask):
    cumul = cumul_ref[...]
    cumul_t = jnp.transpose(cumul)
    docs = doc_ref[...]
    column = doc_columns(docs, tokens)
    same = jnp.concatenate([column] * (tokens // LANES), axis=1) == doc_line(docs, tokens)
    mask[...] = jnp.where(lower_triangle(tokens) & same, 0.0, -1e9)
    qf[...] = some_heads(query_ref, tokens, heads, first, count)
    kf[...] = some_heads(key_ref, tokens, heads, first, count)
    vf[...] = some_heads(value_ref, tokens, heads, first, count)
    for n in range(count):
        h = first + n
        picked = pl.ds(n, tokens, stride=count)
        query = qf[picked, :].astype(BF16)
        keys = kf[picked, :].astype(BF16)
        values = vf[picked, :].astype(BF16)
        qh_ref[n * tokens : (n + 1) * tokens, :] = query
        for i in range(tokens // LANES):
            seen = (i + 1) * LANES
            rows = slice(i * LANES, seen)
            scores = lax.dot_general(
                query[rows, :], keys[0:seen, :], (((1,), (1,)), ((), ())), preferred_element_type=F32
            )
            gap = cumul[rows, h : h + 1] - cumul_t[h : h + 1, 0:seen]
            weights = (scores * jnp.exp(gap + mask[rows, 0:seen])).astype(BF16)
            inner_ref[n * tokens + i * LANES : n * tokens + seen, :] = jnp.dot(
                weights, values[0:seen, :], preferred_element_type=F32
            )


def inner_part(cumul, docs, query, key, value, tokens, heads, first, count, after, relay):
    return call(
        functools.partial(inner_kernel, tokens, heads, first, count),
        "inner_part",
        [],
        [cumul, docs, query, key, value],
        (sds((count * tokens, LANES), F32), sds((count * tokens, LANES), BF16)),
        scratch=[pltpu.VMEM((tokens * count, LANES), F32)] * 3 + [pltpu.VMEM((tokens, tokens), F32)],
        mib=24,
        estimate=cost(
            4 * count * tokens * tokens * HEAD_DIM, tokens * heads * LANES * 12, count * tokens * tokens
        ),
        after=after,
        relay=relay,
    )


def mix_kernel(tokens, heads, parts, place_ref, doc_ref, prior_doc_ref, cumul_ref, *refs):
    refs = list(refs)
    take = lambda n: [refs.pop(0) for _ in range(n)]
    inner, qh, quarters = take(parts), take(parts), take(GROUP_BLOCKS)
    mixed_ref, square_ref, states = refs
    size = quarter_rows(heads)
    mine = place_ref[0] % GROUP_BLOCKS
    for j, ref in enumerate(quarters):
        states[pl.ds(pl.multiple_of((mine ^ j) * size, size), size), :] = ref[...]
    is_open = (doc_columns(doc_ref[...], tokens) == prior_doc_ref[0:1, :]).astype(F32)
    gain = jnp.exp(cumul_ref[...]) * is_open
    squares = jnp.zeros((tokens, LANES), F32)
    for h in range(heads):
        part, n = divmod(h, heads // parts)
        held = slice(n * tokens, (n + 1) * tokens)
        state = states[h * HEAD_DIM : (h + 1) * HEAD_DIM, :]
        carried = jnp.dot(qh[part][held, :], state, preferred_element_type=F32)
        mixed = inner[part][held, :] + carried * gain[:, h : h + 1]
        squares = squares + mixed * mixed
        mixed_ref[pl.ds(h, tokens, stride=heads), :] = mixed
    square_ref[...] = lax.dot_general(
        jnp.ones((8, LANES), F32),
        squares,
        (((1,), (1,)), ((), ())),
        precision=HIGHEST,
        preferred_element_type=F32,
    )


def mix(place, docs, prior_doc, cumul, inner, qh, quarters, tokens, heads, after):
    return call(
        functools.partial(mix_kernel, tokens, heads, len(inner)),
        "mix",
        [place],
        [docs, prior_doc, cumul, *inner, *qh, *quarters],
        (sds((tokens * heads, LANES), F32), sds((8, tokens), F32)),
        scratch=[pltpu.VMEM((heads * HEAD_DIM, LANES), BF16)],
        mib=24,
        estimate=cost(2 * heads * tokens * HEAD_DIM**2, tokens * heads * LANES * 10),
        after=after,
    )


def finish_kernel(tokens, heads, sums, step, gain_ref, gate_ref, mixed_ref, *refs):
    squares, (out_ref, done, sems) = refs[:sums], refs[sums:]
    total = squares[0][0:1, :]
    for ref in squares[1:]:
        total = total + ref[0:1, :]
    scale = lax.rsqrt(total / (HEADS * HEAD_DIM) + 1e-06)
    rows = jnp.concatenate([scale[:, i * LANES : (i + 1) * LANES] for i in range(tokens // LANES)], axis=0)
    column = doc_columns(rows, tokens)
    copies = []
    for i in range(0, tokens, step):
        at = pl.ds(i * heads, step * heads)
        gate = jax.nn.sigmoid(gate_ref[at, :].astype(F32)).reshape(step, heads, LANES)
        mixed = mixed_ref[at, :].reshape(step, heads, LANES)
        inv = column[i : i + step, :][:, None, :]
        out = mixed * inv * gain_ref[...][None] * gate
        done[at, :] = out.reshape(step * heads, LANES).astype(BF16)
        copies.append(pltpu.make_async_copy(done.at[at, :], out_ref.at[at, :], sems.at[i // step]))
        copies[-1].start()
    for copy in copies:
        copy.wait()


def finish(gain, gate, mixed, squares, tokens, heads, after):
    step = 64
    return call(
        functools.partial(finish_kernel, tokens, heads, len(squares), step),
        "finish",
        [],
        [gain, gate, mixed, *squares],
        sds((tokens * heads, LANES), BF16),
        scratch=[pltpu.VMEM((tokens * heads, LANES), BF16), pltpu.SemaphoreType.DMA((tokens // step,))],
        estimate=cost(0, tokens * heads * LANES * 8, tokens * heads * LANES),
        after=after,
        out_hbm=True,
    )


def attend_kernel(tokens, heads, kv_here, least, is_first, is_last, unroll, place_ref, *refs):
    refs = list(refs)
    take = lambda n: [refs.pop(0) for _ in range(n)]
    per_group = heads // kv_here
    rows = tokens * per_group
    step = CHUNK // per_group
    if is_first:
        doc_ref, query_ref = take(2)
    else:
        wide_ref, state_ref = take(2)
    kv = take(len(least))
    if is_first:
        wide_ref = take(1)[0]
    out_ref = take(1)[0]
    if is_last:
        take(1)[0][...] = jnp.zeros((8, LANES), F32)
    bias = take(1)[0]
    if is_first:
        doc_rep = take(1)[0]
    if is_last:
        done, sems = take(2)
    block = place_ref[0]

    lane = lax.broadcasted_iota(jnp.int32, (tokens, LANES), 1).astype(F32)
    end = 2 * kv_here * tokens
    for j, ref in enumerate(kv):
        valid = (block >= jnp.where(block % 2 == 0, *least[j])).astype(F32)
        docs = doc_columns(ref[end : end + INFO, :].astype(F32) * valid, tokens)
        bias[j] = jnp.where(docs == lane, 0.0, -BIG).astype(BF16)
    if is_first:
        column = doc_columns(doc_ref[...], tokens)
        for h in range(per_group):
            doc_rep[pl.ds(h, tokens, stride=per_group), :] = (column == lane).astype(F32)
    ones = jnp.ones((STATE_ROWS - HEAD_DIM, tokens), BF16)

    def some_chunks(i, carry):
        chains = [(u, g) for u in range(unroll) for g in range(kv_here)]
        chunk = [i * unroll + u for u in range(unroll)]
        at = [pl.ds(pl.multiple_of(c * CHUNK, CHUNK), CHUNK) for c in chunk]
        picked = [pl.ds(pl.multiple_of(c * (step * heads), step * heads), step * heads) for c in chunk]
        scores, results = {}, {}

        def begin(u, g):
            if is_first:
                query = query_ref[picked[u], :].astype(F32).reshape(step, heads, LANES)
                query = query[:, g * per_group : (g + 1) * per_group, :].reshape(CHUNK, LANES)
                wide = jnp.concatenate([query.astype(BF16), doc_rep[at[u], :].astype(BF16)], axis=1)
                wide_ref[g, at[u], :] = wide
            else:
                wide = wide_ref[g, at[u], :]
            out = []
            for j, ref in enumerate(kv):
                keys = jnp.concatenate([ref[g * tokens : (g + 1) * tokens, :], bias[j]], axis=1)
                out.append(
                    lax.dot_general(keys, wide, (((1,), (1,)), ((), ())), preferred_element_type=F32)
                )
            if is_first:
                token = chunk[u] * step + lax.broadcasted_iota(jnp.int32, (tokens, CHUNK), 1) // per_group
                key_at = lax.broadcasted_iota(jnp.int32, (tokens, CHUNK), 0)
                out[0] = jnp.where(key_at <= token, out[0], -BIG)
            scores[u, g] = out

        def end_chain(u, g):
            here = scores.pop((u, g))
            top = jnp.max(here[0], axis=0, keepdims=True)
            for score in here[1:]:
                top = jnp.maximum(top, jnp.max(score, axis=0, keepdims=True))
            total = None
            if not is_first:
                before = state_ref[g, :, at[u]]
                top_before = before[STATE_ROWS - 1 : STATE_ROWS, :]
                top = jnp.maximum(top, top_before)
                total = before * jnp.exp2((top_before - top) * SCORE_TO_EXP2)
            for ref, score in zip(kv, here):
                weights = jnp.exp2((score - top) * SCORE_TO_EXP2).astype(BF16)
                first = (kv_here + g) * tokens
                parts = [ref[first + p : first + p + LANES, :] for p in range(0, tokens, LANES)]
                values = jnp.concatenate([jnp.concatenate(parts, axis=1), ones], axis=0)
                more = jnp.dot(values, weights, preferred_element_type=F32)
                total = more if total is None else total + more
            if is_last:
                results[u, g] = jnp.transpose(total[0:HEAD_DIM] / total[HEAD_DIM : HEAD_DIM + 1])
            else:
                out_ref[g, 0 : STATE_ROWS - 8, at[u]] = total[0 : STATE_ROWS - 8]
                out_ref[g, STATE_ROWS - 8 : STATE_ROWS, at[u]] = jnp.broadcast_to(top, (8, CHUNK))

        ahead = 2
        for n in range(len(chains) + ahead):
            if n < len(chains):
                begin(*chains[n])
            if n >= ahead:
                end_chain(*chains[n - ahead])
        if is_last:
            for u in range(unroll):
                result = [results[u, g] for g in range(kv_here)]
                if kv_here > 1:
                    result = [r.reshape(step, per_group, LANES) for r in result]
                    result = [jnp.concatenate(result, axis=1).reshape(step * heads, LANES)]
                done[picked[u], :] = result[0].astype(BF16)
                pltpu.make_async_copy(
                    done.at[picked[u], :], out_ref.at[picked[u], :], sems.at[chunk[u]]
                ).start()
        return carry

    lax.fori_loop(0, rows // (CHUNK * unroll), some_chunks, 0)
    if is_last:
        for c in range(rows // CHUNK):
            at = pl.ds(c * step * heads, step * heads)
            pltpu.make_async_copy(done.at[at, :], out_ref.at[at, :], sems.at[c]).wait()


def attend(place, first, state, kv, is_last, tokens, heads, kv_here, after, relay=()):
    is_first = state is None
    least = tuple(pair for _, pair in kv)
    kv = [block for block, _ in kv]
    blocks = len(kv)
    rows = tokens * heads // kv_here
    unroll = min(4, rows // CHUNK)
    wide_shape = sds((kv_here, rows, 2 * LANES), BF16)
    state_shape = sds((kv_here, STATE_ROWS, rows), F32)
    out_shape = sds((tokens * heads, LANES), BF16) if is_last else state_shape
    scratch = [pltpu.VMEM((blocks, tokens, LANES), BF16)]
    if is_first:
        out_shape = (wide_shape, out_shape)
        scratch.append(pltpu.VMEM((rows, LANES), F32))
    if is_last:
        out_shape = (out_shape, sds((8, LANES), F32))
        scratch.append(pltpu.VMEM((tokens * heads, LANES), BF16))
        scratch.append(pltpu.SemaphoreType.DMA((rows // CHUNK,)))
    span = blocks * tokens
    return call(
        functools.partial(attend_kernel, tokens, heads, kv_here, least, is_first, is_last, unroll),
        "attend",
        [place],
        [*first, *([] if is_first else [state]), *kv],
        out_shape,
        scratch=scratch,
        mib=24,
        estimate=cost(
            4 * tokens * heads * span * 2 * LANES, 4 * tokens * heads * LANES * 4, tokens * heads * span
        ),
        after=after,
        out_hbm=is_last,
        relay=relay,
    )


def body(
    blocks,
    lin_query,
    lin_key,
    lin_value,
    lin_gate,
    log_decay,
    norm_gain,
    doc_ids,
    soft_query,
    soft_key,
    soft_value,
):
    tokens, heads, _ = lin_query.shape
    tensor = HEADS // heads
    kv_here = max(1, heads // GROUP)
    parts = 2 if heads % 16 == 0 else 1
    longest = blocks * tokens * 5 // 8
    window = min(blocks - 1, (longest - 1 + tokens - 1) // tokens)
    flat = lambda x: x.reshape(-1, LANES)
    block = lax.axis_index("seq")
    place = block.astype(jnp.int32).reshape(1)
    start = (lax.axis_index("tp") * heads // GROUP).astype(jnp.int32).reshape(1)

    def send(x, pairs):
        return lax.ppermute(x, "seq", [(a, b % blocks) for a, b in pairs])

    everyone = range(blocks)
    swap = [(b, b ^ 1) for b in everyone]

    own_kv, docs, cumul, key, value = fetch(
        start,
        [
            doc_ids.reshape(tokens // LANES, LANES),
            jnp.transpose(log_decay),
            flat(soft_key),
            flat(soft_value),
            flat(lin_key),
            flat(lin_value),
        ],
        tokens,
        heads,
        kv_here,
    )

    forward = [(b, b + 2) for b in everyone]
    ahead = send(own_kv, forward)
    far = None
    if window % 2:
        far = send(own_kv, [(b, b + window) for b in range(1, blocks - window, 2)])

    size = quarter_rows(heads)
    others = range(1, GROUP_BLOCKS)
    *sent, query = block_state(
        place, flat(soft_query), cumul, docs, key, value, tokens, heads
    )
    quarters = [sent[0]] + [send(sent[j], [(b, b ^ j) for b in everyone]) for j in others]

    state = {}

    def first_attention(after):
        state["wide"], state["sum"] = attend(
            place, (docs, query), None, [(own_kv, (0, 0))], False, tokens, heads, kv_here, after
        )
        return state["sum"]

    def more_attention(kv, is_last, after, relay=()):
        out = attend(
            place, (state["wide"],), state["sum"], kv, is_last, tokens, heads, kv_here, after, relay
        )
        state["sum"] = out[0] if relay else out
        return out

    inner, qh = [], []

    def inner_of(part, after, relay=()):
        n = heads // parts
        got = inner_part(
            cumul, docs, flat(lin_query), key, value, tokens, heads, part * n, n, after, relay
        )
        inner.append(got[0])
        qh.append(got[1])
        return (got[0], *got[2:]) if relay else got[0]

    done = first_attention([sent[0]])
    lane = ahead
    if parts > 1:
        done, lane = inner_of(0, [done], [ahead])
    second = send(lane, [(b, b + 2) for b in range(2, blocks - 2)])
    run, lane, own_copy = group_map(
        place, quarters, size, [done] if far is None else [done, far], [lane, own_kv]
    )
    first_cross = send(lane, swap)
    beside = send(own_copy, swap)
    stages = (blocks // GROUP_BLOCKS).bit_length() - 1
    before, done = None, run
    for stage in range(stages):
        came = send(run, [(b, b ^ (GROUP_BLOCKS << stage)) for b in everyone])
        if stage == stages - 1:
            done = more_attention([(lane, (2, 2))], False, [done])
            done = inner_of(parts - 1, [done])
        else:
            run, before = scan_step(place, stage + 2, run, came, before, size, [done])
            done = run
    *priors, prior_doc = prior_states(place, stages + 1, quarters, came, before, size, [done])
    priors = [priors[0]] + [send(priors[j], [(b, b ^ j) for b in everyone]) for j in others]
    done = more_attention([(first_cross, (2, 3)), (second, (4, 4))], False, [prior_doc])
    slot, lane = pass_on(place, beside if far is None else far, beside, second, [done, *priors])
    rest = [(slot, (blocks if far is None else window, 1)), (send(lane, swap), (4, 5))]
    for back in range(3, window // 2 + 1):
        lane = send(lane, forward)
        rest.append((lane, (2 * back, 2 * back)))
        rest.append((send(lane, swap), (2 * back, 2 * back + 1)))
    mixed, squares = mix(place, docs, prior_doc, cumul, inner, qh, priors, tokens, heads, [done])
    sums = [squares]
    for other in range(1, tensor):
        sums.append(lax.ppermute(squares, "tp", [(t, t ^ other) for t in range(tensor)]))
    done = squares
    while rest:
        got = more_attention(rest[:2], len(rest) <= 2, [done])
        rest, done = rest[2:], got
    soft_out, done = got
    lin_out = finish(norm_gain, flat(lin_gate), mixed, sums, tokens, heads, [done])
    shape = (tokens, heads, HEAD_DIM)
    return lin_out.reshape(shape), soft_out.reshape(shape)


def solution(mesh):
    in_specs = (
        P("seq", "tp", None),
        P("seq", "tp", None),
        P("seq", "tp", None),
        P("seq", "tp", None),
        P("seq", "tp"),
        P("tp", None),
        P("seq"),
        P("seq", "tp", None),
        P("seq", None, None),
        P("seq", None, None),
    )
    out_specs = (P("seq", "tp", None), P("seq", "tp", None))
    return jax.shard_map(
        functools.partial(body, mesh.shape["seq"]),
        mesh=mesh,
        in_specs=in_specs,
        out_specs=out_specs,
        check_vma=False,
    )
```

```python
import functools

import jax
import jax.numpy as jnp
import numpy as np
from jax import lax
from jax.experimental import pallas as pl
from jax.experimental.pallas import tpu as pltpu
from jax.sharding import PartitionSpec as P

HEADS = 64
HEAD_DIM = 128
KV_HEADS = 8
LANES = 128
GROUP = HEADS // KV_HEADS
F32 = jnp.float32
BF16 = jnp.bfloat16
BIG = float(2**20)
SCORE_TO_EXP2 = HEAD_DIM**-0.5 * float(np.log2(np.e))
INFO = 16
HIGHEST = lax.Precision.HIGHEST

VMEM = pl.BlockSpec(memory_space=pltpu.VMEM)
SMEM = pl.BlockSpec(memory_space=pltpu.SMEM)
HBM = pl.BlockSpec(memory_space=pltpu.HBM)
ANYWHERE = pl.BlockSpec(memory_space=pl.ANY)
STATE_ROWS = HEAD_DIM + 16
CHUNK = 256
GROUP_BLOCKS = 4


def sds(shape, dtype):
    return jax.ShapeDtypeStruct(shape, dtype)


def cost(flops, bytes_accessed, transcendentals=0):
    return pl.CostEstimate(
        flops=int(flops), bytes_accessed=int(bytes_accessed), transcendentals=int(transcendentals)
    )


def call(kernel, name, scalars, operands, out_shape, scratch=(), mib=16, estimate=None, after=(), hbm=0, out_hbm=False, relay=()):
    begin = len(scalars) + len(operands)
    skip = len(after)
    operands = [
        pltpu.with_memory_space_constraint(x, pltpu.HBM) if i < hbm else x for i, x in enumerate(operands)
    ]
    outs = out_shape if isinstance(out_shape, tuple) else (out_shape,)
    out_specs = (VMEM,) * len(outs)
    outs = tuple(
        (pltpu.HBM if out_hbm and i == 0 else pltpu.VMEM)(x.shape, x.dtype) for i, x in enumerate(outs)
    )
    if out_hbm:
        out_specs = (HBM, *out_specs[1:])

    moved = len(relay)
    many = len(outs)
    single = not isinstance(out_shape, tuple) and not relay
    out_specs += (VMEM,) * moved
    outs += tuple(pltpu.VMEM(x.shape, x.dtype) for x in relay)

    def run(*refs):
        rest = refs[begin + skip + moved :]
        for source, target in zip(refs[begin + skip : begin + skip + moved], rest[many : many + moved]):
            target[...] = source[...]
        kernel(*refs[:begin], *rest[:many], *rest[many + moved :])

    out = pl.pallas_call(
        run,
        out_shape=outs,
        in_specs=[SMEM] * len(scalars) + [HBM] * hbm + [VMEM] * (len(operands) - hbm) + [ANYWHERE] * skip + [VMEM] * moved,
        out_specs=out_specs,
        scratch_shapes=list(scratch),
        compiler_params=pltpu.CompilerParams(vmem_limit_bytes=mib * 1024 * 1024),
        cost_estimate=estimate,
        name=name,
    )(*scalars, *operands, *after, *relay)
    return out[0] if single else out


def doc_columns(doc_rows, tokens):
    parts = []
    for i in range(tokens // LANES):
        row = jnp.broadcast_to(doc_rows[i : i + 1, :], (LANES, LANES))
        parts.append(jnp.transpose(row))
    return jnp.concatenate(parts, axis=0)


def doc_line(doc_rows, tokens):
    return jnp.concatenate([doc_rows[i : i + 1, :] for i in range(tokens // LANES)], axis=1)


def lower_triangle(tokens):
    rows = lax.broadcasted_iota(jnp.int32, (tokens, tokens), 0)
    cols = lax.broadcasted_iota(jnp.int32, (tokens, tokens), 1)
    return rows >= cols


def pick_kernel(place_ref, even_ref, odd_ref, out_ref):
    out_ref[...] = jnp.where(place_ref[0] % 2 == 0, even_ref[...], odd_ref[...])


def pick(place, even, odd, x, after):
    return call(
        pick_kernel, "pick", [place], [even, odd], (sds(even.shape, BF16),), after=after, relay=[x]
    )


def pass_on(x, after):
    return call(lambda: None, "pass_on", [], [], (), after=after, relay=[x])[0]


def fetch_kernel(tokens, heads, kv_here, start_ref, *refs):
    refs = list(refs)
    take = lambda n: [refs.pop(0) for _ in range(n)]
    sources = take(6)
    kv_ref, doc_out, cumul_ref, key_out, value_out = take(5)
    held = take(4)
    sems, wide, ldp = refs
    docs_in, decays, soft_key, soft_value = held
    targets = [*held, key_out, value_out]
    copies = [
        pltpu.make_async_copy(source, target, sems.at[i])
        for i, (source, target) in enumerate(zip(sources, targets))
    ]
    for copy in copies:
        copy.start()

    copies[0].wait()
    docs = docs_in[...].astype(F32) + 1.0
    line = lax.broadcasted_iota(jnp.int32, (INFO, LANES), 0)
    info = jnp.zeros((INFO, LANES), F32)
    for i in range(tokens // LANES):
        info = jnp.where(line == i, docs[i : i + 1, :], info)
    doc_out[...] = info
    end = 2 * kv_here * tokens
    kv_ref[end : end + INFO, :] = info.astype(BF16)

    copies[1].wait()
    ldp[...] = jnp.zeros_like(ldp)
    ldp[0:heads, :] = decays[...]
    cumul_ref[...] = lax.dot_general(
        lower_triangle(tokens).astype(F32),
        ldp[...],
        (((1,), (1,)), ((), ())),
        precision=HIGHEST,
        preferred_element_type=F32,
    )

    start = start_ref[0]
    for which, ref in enumerate((soft_key, soft_value)):
        copies[2 + which].wait()
        wide[...] = ref[...].astype(F32)
        for g in range(kv_here):
            rows = wide[pl.ds(start + g, tokens, stride=KV_HEADS), :]
            at = (which * kv_here + g) * tokens
            if which:
                halves = [jnp.transpose(rows[i : i + LANES, :]) for i in range(0, tokens, LANES)]
                rows = jnp.concatenate(halves, axis=0)
            kv_ref[at : at + tokens, :] = rows.astype(BF16)
    for copy in copies[4:]:
        copy.wait()


def fetch(start, operands, tokens, heads, kv_here):
    return call(
        functools.partial(fetch_kernel, tokens, heads, kv_here),
        "fetch",
        [start],
        operands,
        (
            sds((2 * kv_here * tokens + INFO, LANES), BF16),
            sds((INFO, LANES), F32),
            sds((tokens, LANES), F32),
            sds(operands[4].shape, BF16),
            sds(operands[5].shape, BF16),
        ),
        scratch=[pltpu.VMEM(x.shape, x.dtype) for x in operands[:4]]
        + [
            pltpu.SemaphoreType.DMA((len(operands),)),
            pltpu.VMEM((tokens * KV_HEADS, LANES), F32),
            pltpu.VMEM((LANES, tokens), F32),
        ],
        estimate=cost(0, 3 * tokens * heads * LANES * 2),
        hbm=len(operands),
    )


def quarter_rows(heads):
    return heads * HEAD_DIM // GROUP_BLOCKS


def state_kernel(tokens, heads, place_ref, *refs):
    refs = list(refs)
    take = lambda n: [refs.pop(0) for _ in range(n)]
    query_in, cumul_ref, doc_ref, key_ref, value_ref = take(5)
    out_refs, query_out = take(GROUP_BLOCKS), take(1)[0]
    kf, vf, states, sem = refs
    copy = pltpu.make_async_copy(query_in, query_out, sem)
    copy.start()
    cumul, docs = cumul_ref[...], doc_ref[...]
    total = cumul[tokens - 1 : tokens, :]
    last_row = tokens // LANES - 1
    first_doc = docs[0:1, 0:1]
    last_doc = docs[last_row : last_row + 1, LANES - 1 : LANES]
    tail = (doc_columns(docs, tokens) == last_doc).astype(F32)
    scale = jnp.exp(total - cumul) * tail
    kf[...] = key_ref[...].astype(F32)
    vf[...] = value_ref[...].astype(F32)
    for h in range(heads):
        keys = (kf[pl.ds(h, tokens, stride=heads), :] * scale[:, h : h + 1]).astype(BF16)
        values = vf[pl.ds(h, tokens, stride=heads), :].astype(BF16)
        states[h * HEAD_DIM : (h + 1) * HEAD_DIM, :] = lax.dot_general(
            keys, values, (((0,), (0,)), ((), ())), preferred_element_type=F32
        )
    size = quarter_rows(heads)
    mine = place_ref[0] % GROUP_BLOCKS
    for j, ref in enumerate(out_refs):
        taker = mine ^ j
        ref[0:size, :] = states[pl.ds(pl.multiple_of(taker * size, size), size), :].astype(BF16)
        totals = jnp.zeros_like(total)
        for c in range(GROUP_BLOCKS):
            skip = c * heads // GROUP_BLOCKS
            moved = pltpu.roll(total, LANES - skip, 1) if skip else total
            totals = jnp.where(taker == c, moved, totals)
        ref[size : size + INFO, :] = info_rows((*in_parts(totals), first_doc, last_doc))
    copy.wait()


def block_state(place, soft_query, cumul, docs, key, value, tokens, heads):
    return call(
        functools.partial(state_kernel, tokens, heads),
        "block_state",
        [place],
        [soft_query, cumul, docs, key, value],
        (
            *[sds((quarter_rows(heads) + INFO, LANES), BF16)] * GROUP_BLOCKS,
            sds(soft_query.shape, BF16),
        ),
        scratch=[
            pltpu.VMEM((tokens * heads, LANES), F32),
            pltpu.VMEM((tokens * heads, LANES), F32),
            pltpu.VMEM((heads * HEAD_DIM, LANES), F32),
            pltpu.SemaphoreType.DMA,
        ],
        estimate=cost(2 * heads * tokens * HEAD_DIM**2, 5 * tokens * heads * LANES * 2),
        hbm=1,
    )


def in_parts(x):
    hi = x.astype(BF16).astype(F32)
    mid = (x - hi).astype(BF16).astype(F32)
    return hi, mid, x - hi - mid


def info_rows(parts):
    line = lax.broadcasted_iota(jnp.int32, (INFO, LANES), 0)
    info = jnp.zeros((INFO, LANES), F32)
    for i, part in enumerate(parts):
        info = jnp.where(line == i, part, info)
    return info.astype(BF16)


def read_map(ref, size):
    info = ref[size : size + INFO, :].astype(F32)
    return info[0:1] + info[1:2] + info[2:3], info[3:4], info[4:5]


def row_chunks(size):
    unit = min(HEAD_DIM, size)
    return [(slice(i * unit, (i + 1) * unit), slice(i, i + 1)) for i in range(size // unit)]


def in_block_order(place_ref, refs, blocks):
    mine = place_ref[0] % GROUP_BLOCKS
    for j, ref in enumerate(refs):
        blocks[mine ^ j] = ref[...]


def block_maps(blocks, size):
    maps = []
    for c in range(GROUP_BLOCKS):
        info = blocks[c, size : size + INFO, :].astype(F32)
        first, last = info[3:4], info[4:5]
        gain = jnp.exp(info[0:1] + info[1:2] + info[2:3]) * (first == last).astype(F32)
        maps.append((gain, first, last))
    return maps


def group_kernel(size, place_ref, *refs):
    sources = refs[:GROUP_BLOCKS]
    out_ref, blocks = refs[GROUP_BLOCKS:]
    in_block_order(place_ref, sources, blocks)
    maps = block_maps(blocks, size)
    gains = [None]
    for (gain, first, _), (_, _, last_before) in zip(maps[1:], maps[:-1]):
        gains.append(gain * (last_before == first).astype(F32))
    for rows, lane in row_chunks(size):
        total = blocks[0, rows, :].astype(F32)
        for c in range(1, GROUP_BLOCKS):
            total = gains[c][:, lane] * total + blocks[c, rows, :].astype(F32)
        out_ref[rows, :] = total.astype(BF16)
    gain = maps[0][0] * gains[1] * gains[2] * gains[3]
    out_ref[size : size + INFO, :] = info_rows((*in_parts(gain), maps[0][1], maps[-1][2]))


def group_map(place, quarters, size, after):
    return call(
        functools.partial(group_kernel, size),
        "group_map",
        [place],
        quarters,
        sds((size + INFO, LANES), BF16),
        scratch=[pltpu.VMEM((GROUP_BLOCKS, size + INFO, LANES), BF16)],
        estimate=cost(8 * size * LANES, 10 * size * LANES * 2),
        after=after,
    )


def scan_kernel(size, has_before, bit, place_ref, *refs):
    mine_ref, came_ref = refs[:2]
    before_ref = refs[2] if has_before else None
    run_ref, out_ref = refs[-2:]
    upper = (place_ref[0] >> bit) & 1 == 1
    gain_m, first_m, last_m = read_map(mine_ref, size)
    gain_c, first_c, last_c = read_map(came_ref, size)
    link = jnp.where(upper, (last_c == first_m).astype(F32), (last_m == first_c).astype(F32))
    gain = jnp.where(upper, gain_m, gain_c) * link
    for rows, lane in row_chunks(size):
        mine, came = mine_ref[rows, :].astype(F32), came_ref[rows, :].astype(F32)
        lower_sum, upper_sum = jnp.where(upper, came, mine), jnp.where(upper, mine, came)
        run_ref[rows, :] = (gain[:, lane] * lower_sum + upper_sum).astype(BF16)
    run_ref[size : size + INFO, :] = info_rows(
        (
            *in_parts(gain * jnp.where(upper, gain_c, gain_m)),
            jnp.where(upper, first_c, first_m),
            jnp.where(upper, last_m, last_c),
        )
    )
    if not has_before:
        out_ref[...] = jnp.where(upper, came_ref[...], jnp.zeros_like(came_ref))
        return
    gain_b, first_b, last_b = read_map(before_ref, size)
    empty = first_b == 0.0
    factor = jnp.where(empty, 1.0, gain_b * (last_c == first_b).astype(F32))
    for rows, lane in row_chunks(size):
        before = before_ref[rows, :].astype(F32)
        joined = factor[:, lane] * came_ref[rows, :].astype(F32) + before
        out_ref[rows, :] = jnp.where(upper, joined, before).astype(BF16)
    out_ref[size : size + INFO, :] = info_rows(
        (
            *in_parts(jnp.where(upper, factor * gain_c, gain_b)),
            jnp.where(upper, first_c, first_b),
            jnp.where(upper, jnp.where(empty, last_c, last_b), last_b),
        )
    )


def scan_step(place, bit, mine, came, before, size, after):
    shape = sds((size + INFO, LANES), BF16)
    before = [] if before is None else [before]
    return call(
        functools.partial(scan_kernel, size, len(before), bit),
        "scan_step",
        [place],
        [mine, came, *before],
        (shape, shape),
        estimate=cost(6 * size * LANES, 6 * size * LANES * 2),
        after=after,
    )


def prior_kernel(size, has_before, bit, place_ref, *refs):
    sources, came_ref = refs[:GROUP_BLOCKS], refs[GROUP_BLOCKS]
    before_ref = refs[GROUP_BLOCKS + 1] if has_before else None
    *out_refs, doc_ref, blocks, priors = refs[GROUP_BLOCKS + 1 + has_before :]
    mine = place_ref[0] % GROUP_BLOCKS
    in_block_order(place_ref, sources, blocks)
    maps = block_maps(blocks, size)
    upper = ((place_ref[0] >> bit) & 1).astype(F32)
    _, _, last_c = read_map(came_ref, size)
    factor, doc = jnp.broadcast_to(upper, (1, LANES)), upper * last_c
    if has_before:
        gain_b, first_b, last_b = read_map(before_ref, size)
        empty = first_b == 0.0
        factor = upper * jnp.where(empty, 1.0, gain_b * (last_c == first_b).astype(F32))
        doc = jnp.where(empty, doc, last_b)
    docs = [doc] + [last for _, _, last in maps[:-1]]
    gains = [gain * (doc == first).astype(F32) for (gain, first, _), doc in zip(maps, docs)]
    for rows, lane in row_chunks(size):
        state = factor[:, lane] * came_ref[rows, :].astype(F32)
        if has_before:
            state = state + before_ref[rows, :].astype(F32)
        for c in range(GROUP_BLOCKS):
            priors[c, rows, :] = state.astype(BF16)
            if c < GROUP_BLOCKS - 1:
                state = gains[c][:, lane] * state + blocks[c, rows, :].astype(F32)
    for j, ref in enumerate(out_refs):
        ref[...] = priors[mine ^ j]
    own_doc = docs[0]
    for c in range(1, GROUP_BLOCKS):
        own_doc = jnp.where(mine == c, docs[c], own_doc)
    doc_ref[...] = jnp.broadcast_to(own_doc, (8, LANES))


def prior_states(place, bit, quarters, came, before, size, after, relay=()):
    before = [] if before is None else [before]
    return call(
        functools.partial(prior_kernel, size, len(before), bit),
        "prior_states",
        [place],
        [*quarters, came, *before],
        (*[sds((size, LANES), BF16)] * GROUP_BLOCKS, sds((8, LANES), F32)),
        scratch=[
            pltpu.VMEM((GROUP_BLOCKS, size + INFO, LANES), BF16),
            pltpu.VMEM((GROUP_BLOCKS, size, LANES), BF16),
        ],
        estimate=cost(8 * size * LANES, 10 * size * LANES * 2),
        after=after,
        relay=relay,
    )


def some_heads(ref, tokens, heads, first, count):
    x = ref[...].astype(F32)
    if count == heads:
        return x
    return x.reshape(tokens, heads, LANES)[:, first : first + count, :].reshape(tokens * count, LANES)


def inner_kernel(tokens, heads, first, count, cumul_ref, doc_ref, query_ref, key_ref, value_ref, inner_ref, qh_ref, qf, kf, vf, mask):
    cumul = cumul_ref[...]
    cumul_t = jnp.transpose(cumul)
    docs = doc_ref[...]
    column = doc_columns(docs, tokens)
    same = jnp.concatenate([column] * (tokens // LANES), axis=1) == doc_line(docs, tokens)
    mask[...] = jnp.where(lower_triangle(tokens) & same, 0.0, -1e9)
    qf[...] = some_heads(query_ref, tokens, heads, first, count)
    kf[...] = some_heads(key_ref, tokens, heads, first, count)
    vf[...] = some_heads(value_ref, tokens, heads, first, count)
    for n in range(count):
        h = first + n
        picked = pl.ds(n, tokens, stride=count)
        query = qf[picked, :].astype(BF16)
        keys = kf[picked, :].astype(BF16)
        values = vf[picked, :].astype(BF16)
        qh_ref[n * tokens : (n + 1) * tokens, :] = query
        for i in range(tokens // LANES):
            seen = (i + 1) * LANES
            rows = slice(i * LANES, seen)
            scores = lax.dot_general(
                query[rows, :], keys[0:seen, :], (((1,), (1,)), ((), ())), preferred_element_type=F32
            )
            gap = cumul[rows, h : h + 1] - cumul_t[h : h + 1, 0:seen]
            weights = (scores * jnp.exp(gap + mask[rows, 0:seen])).astype(BF16)
            inner_ref[n * tokens + i * LANES : n * tokens + seen, :] = jnp.dot(
                weights, values[0:seen, :], preferred_element_type=F32
            )


def inner_part(cumul, docs, query, key, value, tokens, heads, first, count, after, relay):
    return call(
        functools.partial(inner_kernel, tokens, heads, first, count),
        "inner_part",
        [],
        [cumul, docs, query, key, value],
        (sds((count * tokens, LANES), F32), sds((count * tokens, LANES), BF16)),
        scratch=[pltpu.VMEM((tokens * count, LANES), F32)] * 3 + [pltpu.VMEM((tokens, tokens), F32)],
        mib=24,
        estimate=cost(
            4 * count * tokens * tokens * HEAD_DIM, tokens * heads * LANES * 12, count * tokens * tokens
        ),
        after=after,
        relay=relay,
    )


def mix_kernel(tokens, heads, parts, place_ref, doc_ref, prior_doc_ref, cumul_ref, *refs):
    refs = list(refs)
    take = lambda n: [refs.pop(0) for _ in range(n)]
    inner, qh, quarters = take(parts), take(parts), take(GROUP_BLOCKS)
    mixed_ref, square_ref, states = refs
    size = quarter_rows(heads)
    mine = place_ref[0] % GROUP_BLOCKS
    for j, ref in enumerate(quarters):
        states[pl.ds(pl.multiple_of((mine ^ j) * size, size), size), :] = ref[...]
    is_open = (doc_columns(doc_ref[...], tokens) == prior_doc_ref[0:1, :]).astype(F32)
    gain = jnp.exp(cumul_ref[...]) * is_open
    squares = jnp.zeros((tokens, LANES), F32)
    for h in range(heads):
        part, n = divmod(h, heads // parts)
        held = slice(n * tokens, (n + 1) * tokens)
        state = states[h * HEAD_DIM : (h + 1) * HEAD_DIM, :]
        carried = jnp.dot(qh[part][held, :], state, preferred_element_type=F32)
        mixed = inner[part][held, :] + carried * gain[:, h : h + 1]
        squares = squares + mixed * mixed
        mixed_ref[pl.ds(h, tokens, stride=heads), :] = mixed
    square_ref[...] = lax.dot_general(
        jnp.ones((8, LANES), F32),
        squares,
        (((1,), (1,)), ((), ())),
        precision=HIGHEST,
        preferred_element_type=F32,
    )


def mix(place, docs, prior_doc, cumul, inner, qh, quarters, tokens, heads, after):
    return call(
        functools.partial(mix_kernel, tokens, heads, len(inner)),
        "mix",
        [place],
        [docs, prior_doc, cumul, *inner, *qh, *quarters],
        (sds((tokens * heads, LANES), F32), sds((8, tokens), F32)),
        scratch=[pltpu.VMEM((heads * HEAD_DIM, LANES), BF16)],
        mib=24,
        estimate=cost(2 * heads * tokens * HEAD_DIM**2, tokens * heads * LANES * 10),
        after=after,
    )


def finish_kernel(tokens, heads, sums, step, gain_ref, gate_ref, mixed_ref, *refs):
    squares, (out_ref, token_ref, done, sems) = refs[:sums], refs[sums:]
    token_ref[...] = jnp.zeros((8, LANES), F32)
    total = squares[0][0:1, :]
    for ref in squares[1:]:
        total = total + ref[0:1, :]
    scale = lax.rsqrt(total / (HEADS * HEAD_DIM) + 1e-06)
    rows = jnp.concatenate([scale[:, i * LANES : (i + 1) * LANES] for i in range(tokens // LANES)], axis=0)
    column = doc_columns(rows, tokens)
    copies = []
    for i in range(0, tokens, step):
        at = pl.ds(i * heads, step * heads)
        gate = jax.nn.sigmoid(gate_ref[at, :].astype(F32)).reshape(step, heads, LANES)
        mixed = mixed_ref[at, :].reshape(step, heads, LANES)
        inv = column[i : i + step, :][:, None, :]
        out = mixed * inv * gain_ref[...][None] * gate
        done[at, :] = out.reshape(step * heads, LANES).astype(BF16)
        copies.append(pltpu.make_async_copy(done.at[at, :], out_ref.at[at, :], sems.at[i // step]))
        copies[-1].start()
    for copy in copies:
        copy.wait()


def finish(gain, gate, mixed, squares, tokens, heads, after):
    step = 64
    return call(
        functools.partial(finish_kernel, tokens, heads, len(squares), step),
        "finish",
        [],
        [gain, gate, mixed, *squares],
        (sds((tokens * heads, LANES), BF16), sds((8, LANES), F32)),
        scratch=[pltpu.VMEM((tokens * heads, LANES), BF16), pltpu.SemaphoreType.DMA((tokens // step,))],
        estimate=cost(0, tokens * heads * LANES * 8, tokens * heads * LANES),
        after=after,
        out_hbm=True,
    )


def attend_kernel(tokens, heads, kv_here, least, is_first, is_last, unroll, place_ref, *refs):
    refs = list(refs)
    take = lambda n: [refs.pop(0) for _ in range(n)]
    per_group = heads // kv_here
    rows = tokens * per_group
    step = CHUNK // per_group
    if is_first:
        doc_ref, query_ref = take(2)
    else:
        wide_ref, state_ref = take(2)
    kv = take(len(least))
    if is_first:
        wide_ref = take(1)[0]
    out_ref = take(1)[0]
    if is_last:
        take(1)[0][...] = jnp.zeros((8, LANES), F32)
    bias = take(1)[0]
    if is_first:
        doc_rep = take(1)[0]
    if is_last:
        done, sems = take(2)
    block = place_ref[0]

    lane = lax.broadcasted_iota(jnp.int32, (tokens, LANES), 1).astype(F32)
    end = 2 * kv_here * tokens
    for j, ref in enumerate(kv):
        valid = (block >= jnp.where(block % 2 == 0, *least[j])).astype(F32)
        docs = doc_columns(ref[end : end + INFO, :].astype(F32) * valid, tokens)
        bias[j] = jnp.where(docs == lane, 0.0, -BIG).astype(BF16)
    if is_first:
        column = doc_columns(doc_ref[...], tokens)
        for h in range(per_group):
            doc_rep[pl.ds(h, tokens, stride=per_group), :] = (column == lane).astype(F32)
    ones = jnp.ones((STATE_ROWS - HEAD_DIM, tokens), BF16)

    def some_chunks(i, carry):
        chains = [(u, g) for u in range(unroll) for g in range(kv_here)]
        chunk = [i * unroll + u for u in range(unroll)]
        at = [pl.ds(pl.multiple_of(c * CHUNK, CHUNK), CHUNK) for c in chunk]
        picked = [pl.ds(pl.multiple_of(c * (step * heads), step * heads), step * heads) for c in chunk]
        scores, results = {}, {}

        def begin(u, g):
            if is_first:
                query = query_ref[picked[u], :].astype(F32).reshape(step, heads, LANES)
                query = query[:, g * per_group : (g + 1) * per_group, :].reshape(CHUNK, LANES)
                wide = jnp.concatenate([query.astype(BF16), doc_rep[at[u], :].astype(BF16)], axis=1)
                wide_ref[g, at[u], :] = wide
            else:
                wide = wide_ref[g, at[u], :]
            out = []
            for j, ref in enumerate(kv):
                keys = jnp.concatenate([ref[g * tokens : (g + 1) * tokens, :], bias[j]], axis=1)
                out.append(
                    lax.dot_general(keys, wide, (((1,), (1,)), ((), ())), preferred_element_type=F32)
                )
            if is_first:
                token = chunk[u] * step + lax.broadcasted_iota(jnp.int32, (tokens, CHUNK), 1) // per_group
                key_at = lax.broadcasted_iota(jnp.int32, (tokens, CHUNK), 0)
                out[0] = jnp.where(key_at <= token, out[0], -BIG)
            scores[u, g] = out

        def end_chain(u, g):
            here = scores.pop((u, g))
            top = jnp.max(here[0], axis=0, keepdims=True)
            for score in here[1:]:
                top = jnp.maximum(top, jnp.max(score, axis=0, keepdims=True))
            total = None
            if not is_first:
                before = state_ref[g, :, at[u]]
                top_before = before[STATE_ROWS - 1 : STATE_ROWS, :]
                top = jnp.maximum(top, top_before)
                total = before * jnp.exp2((top_before - top) * SCORE_TO_EXP2)
            for ref, score in zip(kv, here):
                weights = jnp.exp2((score - top) * SCORE_TO_EXP2).astype(BF16)
                first = (kv_here + g) * tokens
                parts = [ref[first + p : first + p + LANES, :] for p in range(0, tokens, LANES)]
                values = jnp.concatenate([jnp.concatenate(parts, axis=1), ones], axis=0)
                more = jnp.dot(values, weights, preferred_element_type=F32)
                total = more if total is None else total + more
            if is_last:
                results[u, g] = jnp.transpose(total[0:HEAD_DIM] / total[HEAD_DIM : HEAD_DIM + 1])
            else:
                out_ref[g, 0 : STATE_ROWS - 8, at[u]] = total[0 : STATE_ROWS - 8]
                out_ref[g, STATE_ROWS - 8 : STATE_ROWS, at[u]] = jnp.broadcast_to(top, (8, CHUNK))

        ahead = 2
        for n in range(len(chains) + ahead):
            if n < len(chains):
                begin(*chains[n])
            if n >= ahead:
                end_chain(*chains[n - ahead])
        if is_last:
            for u in range(unroll):
                result = [results[u, g] for g in range(kv_here)]
                if kv_here > 1:
                    result = [r.reshape(step, per_group, LANES) for r in result]
                    result = [jnp.concatenate(result, axis=1).reshape(step * heads, LANES)]
                done[picked[u], :] = result[0].astype(BF16)
                pltpu.make_async_copy(
                    done.at[picked[u], :], out_ref.at[picked[u], :], sems.at[chunk[u]]
                ).start()
        return carry

    lax.fori_loop(0, rows // (CHUNK * unroll), some_chunks, 0)
    if is_last:
        for c in range(rows // CHUNK):
            at = pl.ds(c * step * heads, step * heads)
            pltpu.make_async_copy(done.at[at, :], out_ref.at[at, :], sems.at[c]).wait()


def attend(place, first, state, kv, is_last, tokens, heads, kv_here, after, relay=()):
    is_first = state is None
    least = tuple(pair for _, pair in kv)
    kv = [block for block, _ in kv]
    blocks = len(kv)
    rows = tokens * heads // kv_here
    unroll = min(4, rows // CHUNK)
    wide_shape = sds((kv_here, rows, 2 * LANES), BF16)
    state_shape = sds((kv_here, STATE_ROWS, rows), F32)
    out_shape = sds((tokens * heads, LANES), BF16) if is_last else state_shape
    scratch = [pltpu.VMEM((blocks, tokens, LANES), BF16)]
    if is_first:
        out_shape = (wide_shape, out_shape)
        scratch.append(pltpu.VMEM((rows, LANES), F32))
    if is_last:
        out_shape = (out_shape, sds((8, LANES), F32))
        scratch.append(pltpu.VMEM((tokens * heads, LANES), BF16))
        scratch.append(pltpu.SemaphoreType.DMA((rows // CHUNK,)))
    span = blocks * tokens
    return call(
        functools.partial(attend_kernel, tokens, heads, kv_here, least, is_first, is_last, unroll),
        "attend",
        [place],
        [*first, *([] if is_first else [state]), *kv],
        out_shape,
        scratch=scratch,
        mib=24,
        estimate=cost(
            4 * tokens * heads * span * 2 * LANES, 4 * tokens * heads * LANES * 4, tokens * heads * span
        ),
        after=after,
        out_hbm=is_last,
        relay=relay,
    )


def body(
    blocks,
    lin_query,
    lin_key,
    lin_value,
    lin_gate,
    log_decay,
    norm_gain,
    doc_ids,
    soft_query,
    soft_key,
    soft_value,
):
    tokens, heads, _ = lin_query.shape
    tensor = HEADS // heads
    kv_here = max(1, heads // GROUP)
    parts = 2 if heads % 16 == 0 else 1
    longest = blocks * tokens * 5 // 8
    window = min(blocks - 1, (longest - 1 + tokens - 1) // tokens)
    flat = lambda x: x.reshape(-1, LANES)
    block = lax.axis_index("seq")
    place = block.astype(jnp.int32).reshape(1)
    start = (lax.axis_index("tp") * heads // GROUP).astype(jnp.int32).reshape(1)

    def send(x, pairs):
        return lax.ppermute(x, "seq", [(a, b % blocks) for a, b in pairs])

    everyone = range(blocks)
    swap = [(b, b ^ 1) for b in everyone]

    own_kv, docs, cumul, key, value = fetch(
        start,
        [
            doc_ids.reshape(tokens // LANES, LANES),
            jnp.transpose(log_decay),
            flat(soft_key),
            flat(soft_value),
            flat(lin_key),
            flat(lin_value),
        ],
        tokens,
        heads,
        kv_here,
    )

    forward = [(b, b + 2) for b in everyone]
    ahead = send(own_kv, forward)
    beside = send(own_kv, swap)
    far = None
    if window % 2:
        far = send(own_kv, [(b, b + window) for b in range(1, blocks - window, 2)])

    size = quarter_rows(heads)
    others = range(1, GROUP_BLOCKS)
    *sent, query = block_state(
        place, flat(soft_query), cumul, docs, key, value, tokens, heads
    )
    quarters = [sent[0]] + [send(sent[j], [(b, b ^ j) for b in everyone]) for j in others]

    state = {}

    def first_attention(after):
        state["wide"], state["sum"] = attend(
            place, (docs, query), None, [(own_kv, (0, 0))], False, tokens, heads, kv_here, after
        )
        return state["sum"]

    def more_attention(kv, is_last, after, relay=()):
        out = attend(
            place, (state["wide"],), state["sum"], kv, is_last, tokens, heads, kv_here, after, relay
        )
        state["sum"] = out[0] if relay else out
        return out

    inner, qh = [], []

    def inner_of(part, after, relay=()):
        n = heads // parts
        got = inner_part(
            cumul, docs, flat(lin_query), key, value, tokens, heads, part * n, n, after, relay
        )
        inner.append(got[0])
        qh.append(got[1])
        return (got[0], *got[2:]) if relay else got[0]

    done = first_attention([sent[0], beside])
    if parts > 1:
        done = inner_of(0, [done])
    run = group_map(place, quarters, size, [done])
    slot, lane = pick(place, beside if far is None else far, beside, ahead, [run])
    slot = (slot, (blocks if far is None else window, 1))
    first_cross = send(lane, swap)
    second = send(lane, [(b, b + 2) for b in range(2, blocks - 2)])
    stages = (blocks // GROUP_BLOCKS).bit_length() - 1
    before, done = None, run
    for stage in range(stages):
        came = send(run, [(b, b ^ (GROUP_BLOCKS << stage)) for b in everyone])
        if stage == stages - 1:
            done = more_attention([slot, (lane, (2, 2))], False, [done])
            done = inner_of(parts - 1, [done])
        else:
            run, before = scan_step(place, stage + 2, run, came, before, size, [done])
            done = run
    *priors, prior_doc = prior_states(place, stages + 1, quarters, came, before, size, [done])
    priors = [priors[0]] + [send(priors[j], [(b, b ^ j) for b in everyone]) for j in others]
    done = more_attention([(first_cross, (2, 3)), (second, (4, 4))], False, [prior_doc])
    lane = pass_on(second, [done, *priors])
    rest = [(send(lane, swap), (4, 5))]
    for back in range(3, window // 2 + 1):
        lane = send(lane, forward)
        rest.append((lane, (2 * back, 2 * back)))
        rest.append((send(lane, swap), (2 * back, 2 * back + 1)))
    mixed, squares = mix(place, docs, prior_doc, cumul, inner, qh, priors, tokens, heads, [done])
    sums = [squares]
    for other in range(1, tensor):
        sums.append(lax.ppermute(squares, "tp", [(t, t ^ other) for t in range(tensor)]))
    lin_out, done = finish(norm_gain, flat(lin_gate), mixed, sums, tokens, heads, [squares])
    while rest:
        got = more_attention(rest[:2], len(rest) <= 2, [done])
        rest, done = rest[2:], got
    soft_out = got[0]
    shape = (tokens, heads, HEAD_DIM)
    return lin_out.reshape(shape), soft_out.reshape(shape)


def solution(mesh):
    in_specs = (
        P("seq", "tp", None),
        P("seq", "tp", None),
        P("seq", "tp", None),
        P("seq", "tp", None),
        P("seq", "tp"),
        P("tp", None),
        P("seq"),
        P("seq", "tp", None),
        P("seq", None, None),
        P("seq", None, None),
    )
    out_specs = (P("seq", "tp", None), P("seq", "tp", None))
    return jax.shard_map(
        functools.partial(body, mesh.shape["seq"]),
        mesh=mesh,
        in_specs=in_specs,
        out_specs=out_specs,
        check_vma=False,
    )
```

```python
import functools

import jax
import jax.numpy as jnp
import numpy as np
from jax import lax
from jax.experimental import pallas as pl
from jax.experimental.pallas import tpu as pltpu
from jax.sharding import PartitionSpec as P

HEADS = 64
HEAD_DIM = 128
KV_HEADS = 8
LANES = 128
GROUP = HEADS // KV_HEADS
F32 = jnp.float32
BF16 = jnp.bfloat16
BIG = float(2**20)
SCORE_TO_EXP2 = HEAD_DIM**-0.5 * float(np.log2(np.e))
INFO = 16
HIGHEST = lax.Precision.HIGHEST

VMEM = pl.BlockSpec(memory_space=pltpu.VMEM)
SMEM = pl.BlockSpec(memory_space=pltpu.SMEM)
HBM = pl.BlockSpec(memory_space=pltpu.HBM)
ANYWHERE = pl.BlockSpec(memory_space=pl.ANY)
STATE_ROWS = HEAD_DIM + 16
CHUNK = 256
GROUP_BLOCKS = 4


def sds(shape, dtype):
    return jax.ShapeDtypeStruct(shape, dtype)


def cost(flops, bytes_accessed, transcendentals=0):
    return pl.CostEstimate(
        flops=int(flops), bytes_accessed=int(bytes_accessed), transcendentals=int(transcendentals)
    )


def call(kernel, name, scalars, operands, out_shape, scratch=(), mib=16, estimate=None, after=(), hbm=0, out_hbm=False, relay=()):
    begin = len(scalars) + len(operands)
    skip = len(after)
    operands = [
        pltpu.with_memory_space_constraint(x, pltpu.HBM) if i < hbm else x for i, x in enumerate(operands)
    ]
    outs = out_shape if isinstance(out_shape, tuple) else (out_shape,)
    out_specs = (VMEM,) * len(outs)
    outs = tuple(
        (pltpu.HBM if out_hbm and i == 0 else pltpu.VMEM)(x.shape, x.dtype) for i, x in enumerate(outs)
    )
    if out_hbm:
        out_specs = (HBM, *out_specs[1:])

    moved = len(relay)
    many = len(outs)
    single = not isinstance(out_shape, tuple) and not relay
    out_specs += (VMEM,) * moved
    outs += tuple(pltpu.VMEM(x.shape, x.dtype) for x in relay)

    def run(*refs):
        rest = refs[begin + skip + moved :]
        for source, target in zip(refs[begin + skip : begin + skip + moved], rest[many : many + moved]):
            target[...] = source[...]
        kernel(*refs[:begin], *rest[:many], *rest[many + moved :])

    out = pl.pallas_call(
        run,
        out_shape=outs,
        in_specs=[SMEM] * len(scalars) + [HBM] * hbm + [VMEM] * (len(operands) - hbm) + [ANYWHERE] * skip + [VMEM] * moved,
        out_specs=out_specs,
        scratch_shapes=list(scratch),
        compiler_params=pltpu.CompilerParams(vmem_limit_bytes=mib * 1024 * 1024),
        cost_estimate=estimate,
        name=name,
    )(*scalars, *operands, *after, *relay)
    return out[0] if single else out


def doc_columns(doc_rows, tokens):
    parts = []
    for i in range(tokens // LANES):
        row = jnp.broadcast_to(doc_rows[i : i + 1, :], (LANES, LANES))
        parts.append(jnp.transpose(row))
    return jnp.concatenate(parts, axis=0)


def doc_line(doc_rows, tokens):
    return jnp.concatenate([doc_rows[i : i + 1, :] for i in range(tokens // LANES)], axis=1)


def lower_triangle(tokens):
    rows = lax.broadcasted_iota(jnp.int32, (tokens, tokens), 0)
    cols = lax.broadcasted_iota(jnp.int32, (tokens, tokens), 1)
    return rows >= cols


def pass_on(x, after):
    return call(lambda: None, "pass_on", [], [], (), after=after, relay=[x])[0]


def fetch_kernel(tokens, heads, kv_here, start_ref, *refs):
    refs = list(refs)
    take = lambda n: [refs.pop(0) for _ in range(n)]
    sources = take(6)
    kv_ref, doc_out, cumul_ref, key_out, value_out = take(5)
    held = take(4)
    sems, wide, ldp = refs
    docs_in, decays, soft_key, soft_value = held
    targets = [*held, key_out, value_out]
    copies = [
        pltpu.make_async_copy(source, target, sems.at[i])
        for i, (source, target) in enumerate(zip(sources, targets))
    ]
    for copy in copies:
        copy.start()

    copies[0].wait()
    docs = docs_in[...].astype(F32) + 1.0
    line = lax.broadcasted_iota(jnp.int32, (INFO, LANES), 0)
    info = jnp.zeros((INFO, LANES), F32)
    for i in range(tokens // LANES):
        info = jnp.where(line == i, docs[i : i + 1, :], info)
    doc_out[...] = info
    end = 2 * kv_here * tokens
    kv_ref[end : end + INFO, :] = info.astype(BF16)

    copies[1].wait()
    ldp[...] = jnp.zeros_like(ldp)
    ldp[0:heads, :] = decays[...]
    cumul_ref[...] = lax.dot_general(
        lower_triangle(tokens).astype(F32),
        ldp[...],
        (((1,), (1,)), ((), ())),
        precision=HIGHEST,
        preferred_element_type=F32,
    )

    start = start_ref[0]
    for which, ref in enumerate((soft_key, soft_value)):
        copies[2 + which].wait()
        wide[...] = ref[...].astype(F32)
        for g in range(kv_here):
            rows = wide[pl.ds(start + g, tokens, stride=KV_HEADS), :]
            at = (which * kv_here + g) * tokens
            if which:
                halves = [jnp.transpose(rows[i : i + LANES, :]) for i in range(0, tokens, LANES)]
                rows = jnp.concatenate(halves, axis=0)
            kv_ref[at : at + tokens, :] = rows.astype(BF16)
    for copy in copies[4:]:
        copy.wait()


def fetch(start, operands, tokens, heads, kv_here):
    return call(
        functools.partial(fetch_kernel, tokens, heads, kv_here),
        "fetch",
        [start],
        operands,
        (
            sds((2 * kv_here * tokens + INFO, LANES), BF16),
            sds((INFO, LANES), F32),
            sds((tokens, LANES), F32),
            sds(operands[4].shape, BF16),
            sds(operands[5].shape, BF16),
        ),
        scratch=[pltpu.VMEM(x.shape, x.dtype) for x in operands[:4]]
        + [
            pltpu.SemaphoreType.DMA((len(operands),)),
            pltpu.VMEM((tokens * KV_HEADS, LANES), F32),
            pltpu.VMEM((LANES, tokens), F32),
        ],
        estimate=cost(0, 3 * tokens * heads * LANES * 2),
        hbm=len(operands),
    )


def quarter_rows(heads):
    return heads * HEAD_DIM // GROUP_BLOCKS


def state_kernel(tokens, heads, place_ref, *refs):
    refs = list(refs)
    take = lambda n: [refs.pop(0) for _ in range(n)]
    query_in, cumul_ref, doc_ref, key_ref, value_ref = take(5)
    out_refs, query_out = take(GROUP_BLOCKS), take(1)[0]
    kf, vf, states, sem = refs
    copy = pltpu.make_async_copy(query_in, query_out, sem)
    copy.start()
    cumul, docs = cumul_ref[...], doc_ref[...]
    total = cumul[tokens - 1 : tokens, :]
    last_row = tokens // LANES - 1
    first_doc = docs[0:1, 0:1]
    last_doc = docs[last_row : last_row + 1, LANES - 1 : LANES]
    tail = (doc_columns(docs, tokens) == last_doc).astype(F32)
    scale = jnp.exp(total - cumul) * tail
    kf[...] = key_ref[...].astype(F32)
    vf[...] = value_ref[...].astype(F32)
    for h in range(heads):
        keys = (kf[pl.ds(h, tokens, stride=heads), :] * scale[:, h : h + 1]).astype(BF16)
        values = vf[pl.ds(h, tokens, stride=heads), :].astype(BF16)
        states[h * HEAD_DIM : (h + 1) * HEAD_DIM, :] = lax.dot_general(
            keys, values, (((0,), (0,)), ((), ())), preferred_element_type=F32
        )
    size = quarter_rows(heads)
    mine = place_ref[0] % GROUP_BLOCKS
    for j, ref in enumerate(out_refs):
        taker = mine ^ j
        ref[0:size, :] = states[pl.ds(pl.multiple_of(taker * size, size), size), :].astype(BF16)
        totals = jnp.zeros_like(total)
        for c in range(GROUP_BLOCKS):
            skip = c * heads // GROUP_BLOCKS
            moved = pltpu.roll(total, LANES - skip, 1) if skip else total
            totals = jnp.where(taker == c, moved, totals)
        ref[size : size + INFO, :] = info_rows((*in_parts(totals), first_doc, last_doc))
    copy.wait()


def block_state(place, soft_query, cumul, docs, key, value, tokens, heads):
    return call(
        functools.partial(state_kernel, tokens, heads),
        "block_state",
        [place],
        [soft_query, cumul, docs, key, value],
        (
            *[sds((quarter_rows(heads) + INFO, LANES), BF16)] * GROUP_BLOCKS,
            sds(soft_query.shape, BF16),
        ),
        scratch=[
            pltpu.VMEM((tokens * heads, LANES), F32),
            pltpu.VMEM((tokens * heads, LANES), F32),
            pltpu.VMEM((heads * HEAD_DIM, LANES), F32),
            pltpu.SemaphoreType.DMA,
        ],
        estimate=cost(2 * heads * tokens * HEAD_DIM**2, 5 * tokens * heads * LANES * 2),
        hbm=1,
    )


def in_parts(x):
    hi = x.astype(BF16).astype(F32)
    mid = (x - hi).astype(BF16).astype(F32)
    return hi, mid, x - hi - mid


def info_rows(parts):
    line = lax.broadcasted_iota(jnp.int32, (INFO, LANES), 0)
    info = jnp.zeros((INFO, LANES), F32)
    for i, part in enumerate(parts):
        info = jnp.where(line == i, part, info)
    return info.astype(BF16)


def read_map(ref, size):
    info = ref[size : size + INFO, :].astype(F32)
    return info[0:1] + info[1:2] + info[2:3], info[3:4], info[4:5]


def row_chunks(size):
    unit = min(HEAD_DIM, size)
    return [(slice(i * unit, (i + 1) * unit), slice(i, i + 1)) for i in range(size // unit)]


def in_block_order(place_ref, refs, blocks):
    mine = place_ref[0] % GROUP_BLOCKS
    for j, ref in enumerate(refs):
        blocks[mine ^ j] = ref[...]


def block_maps(blocks, size):
    maps = []
    for c in range(GROUP_BLOCKS):
        info = blocks[c, size : size + INFO, :].astype(F32)
        first, last = info[3:4], info[4:5]
        gain = jnp.exp(info[0:1] + info[1:2] + info[2:3]) * (first == last).astype(F32)
        maps.append((gain, first, last))
    return maps


def group_kernel(size, place_ref, *refs):
    sources = refs[:GROUP_BLOCKS]
    out_ref, blocks = refs[GROUP_BLOCKS:]
    in_block_order(place_ref, sources, blocks)
    maps = block_maps(blocks, size)
    gains = [None]
    for (gain, first, _), (_, _, last_before) in zip(maps[1:], maps[:-1]):
        gains.append(gain * (last_before == first).astype(F32))
    for rows, lane in row_chunks(size):
        total = blocks[0, rows, :].astype(F32)
        for c in range(1, GROUP_BLOCKS):
            total = gains[c][:, lane] * total + blocks[c, rows, :].astype(F32)
        out_ref[rows, :] = total.astype(BF16)
    gain = maps[0][0] * gains[1] * gains[2] * gains[3]
    out_ref[size : size + INFO, :] = info_rows((*in_parts(gain), maps[0][1], maps[-1][2]))


def group_map(place, quarters, size, after, relay):
    return call(
        functools.partial(group_kernel, size),
        "group_map",
        [place],
        quarters,
        (sds((size + INFO, LANES), BF16),),
        scratch=[pltpu.VMEM((GROUP_BLOCKS, size + INFO, LANES), BF16)],
        estimate=cost(8 * size * LANES, 10 * size * LANES * 2),
        after=after,
        relay=relay,
    )


def scan_kernel(size, has_before, bit, place_ref, *refs):
    mine_ref, came_ref = refs[:2]
    before_ref = refs[2] if has_before else None
    run_ref, out_ref = refs[-2:]
    upper = (place_ref[0] >> bit) & 1 == 1
    gain_m, first_m, last_m = read_map(mine_ref, size)
    gain_c, first_c, last_c = read_map(came_ref, size)
    link = jnp.where(upper, (last_c == first_m).astype(F32), (last_m == first_c).astype(F32))
    gain = jnp.where(upper, gain_m, gain_c) * link
    for rows, lane in row_chunks(size):
        mine, came = mine_ref[rows, :].astype(F32), came_ref[rows, :].astype(F32)
        lower_sum, upper_sum = jnp.where(upper, came, mine), jnp.where(upper, mine, came)
        run_ref[rows, :] = (gain[:, lane] * lower_sum + upper_sum).astype(BF16)
    run_ref[size : size + INFO, :] = info_rows(
        (
            *in_parts(gain * jnp.where(upper, gain_c, gain_m)),
            jnp.where(upper, first_c, first_m),
            jnp.where(upper, last_m, last_c),
        )
    )
    if not has_before:
        out_ref[...] = jnp.where(upper, came_ref[...], jnp.zeros_like(came_ref))
        return
    gain_b, first_b, last_b = read_map(before_ref, size)
    empty = first_b == 0.0
    factor = jnp.where(empty, 1.0, gain_b * (last_c == first_b).astype(F32))
    for rows, lane in row_chunks(size):
        before = before_ref[rows, :].astype(F32)
        joined = factor[:, lane] * came_ref[rows, :].astype(F32) + before
        out_ref[rows, :] = jnp.where(upper, joined, before).astype(BF16)
    out_ref[size : size + INFO, :] = info_rows(
        (
            *in_parts(jnp.where(upper, factor * gain_c, gain_b)),
            jnp.where(upper, first_c, first_b),
            jnp.where(upper, jnp.where(empty, last_c, last_b), last_b),
        )
    )


def scan_step(place, bit, mine, came, before, size, after):
    shape = sds((size + INFO, LANES), BF16)
    before = [] if before is None else [before]
    return call(
        functools.partial(scan_kernel, size, len(before), bit),
        "scan_step",
        [place],
        [mine, came, *before],
        (shape, shape),
        estimate=cost(6 * size * LANES, 6 * size * LANES * 2),
        after=after,
    )


def prior_kernel(size, has_before, bit, place_ref, *refs):
    sources, came_ref = refs[:GROUP_BLOCKS], refs[GROUP_BLOCKS]
    before_ref = refs[GROUP_BLOCKS + 1] if has_before else None
    *out_refs, doc_ref, blocks, priors = refs[GROUP_BLOCKS + 1 + has_before :]
    mine = place_ref[0] % GROUP_BLOCKS
    in_block_order(place_ref, sources, blocks)
    maps = block_maps(blocks, size)
    upper = ((place_ref[0] >> bit) & 1).astype(F32)
    _, _, last_c = read_map(came_ref, size)
    factor, doc = jnp.broadcast_to(upper, (1, LANES)), upper * last_c
    if has_before:
        gain_b, first_b, last_b = read_map(before_ref, size)
        empty = first_b == 0.0
        factor = upper * jnp.where(empty, 1.0, gain_b * (last_c == first_b).astype(F32))
        doc = jnp.where(empty, doc, last_b)
    docs = [doc] + [last for _, _, last in maps[:-1]]
    gains = [gain * (doc == first).astype(F32) for (gain, first, _), doc in zip(maps, docs)]
    for rows, lane in row_chunks(size):
        state = factor[:, lane] * came_ref[rows, :].astype(F32)
        if has_before:
            state = state + before_ref[rows, :].astype(F32)
        for c in range(GROUP_BLOCKS):
            priors[c, rows, :] = state.astype(BF16)
            if c < GROUP_BLOCKS - 1:
                state = gains[c][:, lane] * state + blocks[c, rows, :].astype(F32)
    for j, ref in enumerate(out_refs):
        ref[...] = priors[mine ^ j]
    own_doc = docs[0]
    for c in range(1, GROUP_BLOCKS):
        own_doc = jnp.where(mine == c, docs[c], own_doc)
    doc_ref[...] = jnp.broadcast_to(own_doc, (8, LANES))


def prior_states(place, bit, quarters, came, before, size, after, relay=()):
    before = [] if before is None else [before]
    return call(
        functools.partial(prior_kernel, size, len(before), bit),
        "prior_states",
        [place],
        [*quarters, came, *before],
        (*[sds((size, LANES), BF16)] * GROUP_BLOCKS, sds((8, LANES), F32)),
        scratch=[
            pltpu.VMEM((GROUP_BLOCKS, size + INFO, LANES), BF16),
            pltpu.VMEM((GROUP_BLOCKS, size, LANES), BF16),
        ],
        estimate=cost(8 * size * LANES, 10 * size * LANES * 2),
        after=after,
        relay=relay,
    )


def some_heads(ref, tokens, heads, first, count):
    x = ref[...].astype(F32)
    if count == heads:
        return x
    return x.reshape(tokens, heads, LANES)[:, first : first + count, :].reshape(tokens * count, LANES)


def inner_kernel(tokens, heads, first, count, cumul_ref, doc_ref, query_ref, key_ref, value_ref, inner_ref, qh_ref, qf, kf, vf, mask):
    cumul = cumul_ref[...]
    cumul_t = jnp.transpose(cumul)
    docs = doc_ref[...]
    column = doc_columns(docs, tokens)
    same = jnp.concatenate([column] * (tokens // LANES), axis=1) == doc_line(docs, tokens)
    mask[...] = jnp.where(lower_triangle(tokens) & same, 0.0, -1e9)
    qf[...] = some_heads(query_ref, tokens, heads, first, count)
    kf[...] = some_heads(key_ref, tokens, heads, first, count)
    vf[...] = some_heads(value_ref, tokens, heads, first, count)
    for n in range(count):
        h = first + n
        picked = pl.ds(n, tokens, stride=count)
        query = qf[picked, :].astype(BF16)
        keys = kf[picked, :].astype(BF16)
        values = vf[picked, :].astype(BF16)
        qh_ref[n * tokens : (n + 1) * tokens, :] = query
        for i in range(tokens // LANES):
            seen = (i + 1) * LANES
            rows = slice(i * LANES, seen)
            scores = lax.dot_general(
                query[rows, :], keys[0:seen, :], (((1,), (1,)), ((), ())), preferred_element_type=F32
            )
            gap = cumul[rows, h : h + 1] - cumul_t[h : h + 1, 0:seen]
            weights = (scores * jnp.exp(gap + mask[rows, 0:seen])).astype(BF16)
            inner_ref[n * tokens + i * LANES : n * tokens + seen, :] = jnp.dot(
                weights, values[0:seen, :], preferred_element_type=F32
            )


def inner_part(cumul, docs, query, key, value, tokens, heads, first, count, after, relay):
    return call(
        functools.partial(inner_kernel, tokens, heads, first, count),
        "inner_part",
        [],
        [cumul, docs, query, key, value],
        (sds((count * tokens, LANES), F32), sds((count * tokens, LANES), BF16)),
        scratch=[pltpu.VMEM((tokens * count, LANES), F32)] * 3 + [pltpu.VMEM((tokens, tokens), F32)],
        mib=24,
        estimate=cost(
            4 * count * tokens * tokens * HEAD_DIM, tokens * heads * LANES * 12, count * tokens * tokens
        ),
        after=after,
        relay=relay,
    )


def mix_kernel(tokens, heads, parts, place_ref, doc_ref, prior_doc_ref, cumul_ref, *refs):
    refs = list(refs)
    take = lambda n: [refs.pop(0) for _ in range(n)]
    inner, qh, quarters = take(parts), take(parts), take(GROUP_BLOCKS)
    mixed_ref, square_ref, states = refs
    size = quarter_rows(heads)
    mine = place_ref[0] % GROUP_BLOCKS
    for j, ref in enumerate(quarters):
        states[pl.ds(pl.multiple_of((mine ^ j) * size, size), size), :] = ref[...]
    is_open = (doc_columns(doc_ref[...], tokens) == prior_doc_ref[0:1, :]).astype(F32)
    gain = jnp.exp(cumul_ref[...]) * is_open
    squares = jnp.zeros((tokens, LANES), F32)
    for h in range(heads):
        part, n = divmod(h, heads // parts)
        held = slice(n * tokens, (n + 1) * tokens)
        state = states[h * HEAD_DIM : (h + 1) * HEAD_DIM, :]
        carried = jnp.dot(qh[part][held, :], state, preferred_element_type=F32)
        mixed = inner[part][held, :] + carried * gain[:, h : h + 1]
        squares = squares + mixed * mixed
        mixed_ref[pl.ds(h, tokens, stride=heads), :] = mixed
    square_ref[...] = lax.dot_general(
        jnp.ones((8, LANES), F32),
        squares,
        (((1,), (1,)), ((), ())),
        precision=HIGHEST,
        preferred_element_type=F32,
    )


def mix(place, docs, prior_doc, cumul, inner, qh, quarters, tokens, heads, after):
    return call(
        functools.partial(mix_kernel, tokens, heads, len(inner)),
        "mix",
        [place],
        [docs, prior_doc, cumul, *inner, *qh, *quarters],
        (sds((tokens * heads, LANES), F32), sds((8, tokens), F32)),
        scratch=[pltpu.VMEM((heads * HEAD_DIM, LANES), BF16)],
        mib=24,
        estimate=cost(2 * heads * tokens * HEAD_DIM**2, tokens * heads * LANES * 10),
        after=after,
    )


def finish_kernel(tokens, heads, sums, step, gain_ref, gate_ref, mixed_ref, *refs):
    squares, (out_ref, done, sems) = refs[:sums], refs[sums:]
    total = squares[0][0:1, :]
    for ref in squares[1:]:
        total = total + ref[0:1, :]
    scale = lax.rsqrt(total / (HEADS * HEAD_DIM) + 1e-06)
    rows = jnp.concatenate([scale[:, i * LANES : (i + 1) * LANES] for i in range(tokens // LANES)], axis=0)
    column = doc_columns(rows, tokens)
    copies = []
    for i in range(0, tokens, step):
        at = pl.ds(i * heads, step * heads)
        gate = jax.nn.sigmoid(gate_ref[at, :].astype(F32)).reshape(step, heads, LANES)
        mixed = mixed_ref[at, :].reshape(step, heads, LANES)
        inv = column[i : i + step, :][:, None, :]
        out = mixed * inv * gain_ref[...][None] * gate
        done[at, :] = out.reshape(step * heads, LANES).astype(BF16)
        copies.append(pltpu.make_async_copy(done.at[at, :], out_ref.at[at, :], sems.at[i // step]))
        copies[-1].start()
    for copy in copies:
        copy.wait()


def finish(gain, gate, mixed, squares, tokens, heads, after):
    step = 64
    return call(
        functools.partial(finish_kernel, tokens, heads, len(squares), step),
        "finish",
        [],
        [gain, gate, mixed, *squares],
        sds((tokens * heads, LANES), BF16),
        scratch=[pltpu.VMEM((tokens * heads, LANES), BF16), pltpu.SemaphoreType.DMA((tokens // step,))],
        estimate=cost(0, tokens * heads * LANES * 8, tokens * heads * LANES),
        after=after,
        out_hbm=True,
    )


def attend_kernel(tokens, heads, kv_here, least, is_first, is_last, unroll, place_ref, *refs):
    refs = list(refs)
    take = lambda n: [refs.pop(0) for _ in range(n)]
    per_group = heads // kv_here
    rows = tokens * per_group
    step = CHUNK // per_group
    if is_first:
        doc_ref, query_ref = take(2)
    else:
        wide_ref, state_ref = take(2)
    kv = take(len(least))
    if is_first:
        wide_ref = take(1)[0]
    out_ref = take(1)[0]
    if is_last:
        take(1)[0][...] = jnp.zeros((8, LANES), F32)
    bias = take(1)[0]
    if is_first:
        doc_rep = take(1)[0]
    if is_last:
        done, sems = take(2)
    block = place_ref[0]

    lane = lax.broadcasted_iota(jnp.int32, (tokens, LANES), 1).astype(F32)
    end = 2 * kv_here * tokens
    for j, ref in enumerate(kv):
        valid = (block >= jnp.where(block % 2 == 0, *least[j])).astype(F32)
        docs = doc_columns(ref[end : end + INFO, :].astype(F32) * valid, tokens)
        bias[j] = jnp.where(docs == lane, 0.0, -BIG).astype(BF16)
    if is_first:
        column = doc_columns(doc_ref[...], tokens)
        for h in range(per_group):
            doc_rep[pl.ds(h, tokens, stride=per_group), :] = (column == lane).astype(F32)
    ones = jnp.ones((STATE_ROWS - HEAD_DIM, tokens), BF16)

    def some_chunks(i, carry):
        chains = [(u, g) for u in range(unroll) for g in range(kv_here)]
        chunk = [i * unroll + u for u in range(unroll)]
        at = [pl.ds(pl.multiple_of(c * CHUNK, CHUNK), CHUNK) for c in chunk]
        picked = [pl.ds(pl.multiple_of(c * (step * heads), step * heads), step * heads) for c in chunk]
        scores, results = {}, {}

        def begin(u, g):
            if is_first:
                query = query_ref[picked[u], :].astype(F32).reshape(step, heads, LANES)
                query = query[:, g * per_group : (g + 1) * per_group, :].reshape(CHUNK, LANES)
                wide = jnp.concatenate([query.astype(BF16), doc_rep[at[u], :].astype(BF16)], axis=1)
                wide_ref[g, at[u], :] = wide
            else:
                wide = wide_ref[g, at[u], :]
            out = []
            for j, ref in enumerate(kv):
                keys = jnp.concatenate([ref[g * tokens : (g + 1) * tokens, :], bias[j]], axis=1)
                out.append(
                    lax.dot_general(keys, wide, (((1,), (1,)), ((), ())), preferred_element_type=F32)
                )
            if is_first:
                token = chunk[u] * step + lax.broadcasted_iota(jnp.int32, (tokens, CHUNK), 1) // per_group
                key_at = lax.broadcasted_iota(jnp.int32, (tokens, CHUNK), 0)
                out[0] = jnp.where(key_at <= token, out[0], -BIG)
            scores[u, g] = out

        def end_chain(u, g):
            here = scores.pop((u, g))
            top = jnp.max(here[0], axis=0, keepdims=True)
            for score in here[1:]:
                top = jnp.maximum(top, jnp.max(score, axis=0, keepdims=True))
            total = None
            if not is_first:
                before = state_ref[g, :, at[u]]
                top_before = before[STATE_ROWS - 1 : STATE_ROWS, :]
                top = jnp.maximum(top, top_before)
                total = before * jnp.exp2((top_before - top) * SCORE_TO_EXP2)
            for ref, score in zip(kv, here):
                weights = jnp.exp2((score - top) * SCORE_TO_EXP2).astype(BF16)
                first = (kv_here + g) * tokens
                parts = [ref[first + p : first + p + LANES, :] for p in range(0, tokens, LANES)]
                values = jnp.concatenate([jnp.concatenate(parts, axis=1), ones], axis=0)
                more = jnp.dot(values, weights, preferred_element_type=F32)
                total = more if total is None else total + more
            if is_last:
                results[u, g] = jnp.transpose(total[0:HEAD_DIM] / total[HEAD_DIM : HEAD_DIM + 1])
            else:
                out_ref[g, 0 : STATE_ROWS - 8, at[u]] = total[0 : STATE_ROWS - 8]
                out_ref[g, STATE_ROWS - 8 : STATE_ROWS, at[u]] = jnp.broadcast_to(top, (8, CHUNK))

        ahead = 3
        for n in range(len(chains) + ahead):
            if n < len(chains):
                begin(*chains[n])
            if n >= ahead:
                end_chain(*chains[n - ahead])
        if is_last:
            for u in range(unroll):
                result = [results[u, g] for g in range(kv_here)]
                if kv_here > 1:
                    result = [r.reshape(step, per_group, LANES) for r in result]
                    result = [jnp.concatenate(result, axis=1).reshape(step * heads, LANES)]
                done[picked[u], :] = result[0].astype(BF16)
                pltpu.make_async_copy(
                    done.at[picked[u], :], out_ref.at[picked[u], :], sems.at[chunk[u]]
                ).start()
        return carry

    lax.fori_loop(0, rows // (CHUNK * unroll), some_chunks, 0)
    if is_last:
        for c in range(rows // CHUNK):
            at = pl.ds(c * step * heads, step * heads)
            pltpu.make_async_copy(done.at[at, :], out_ref.at[at, :], sems.at[c]).wait()


def attend(place, first, state, kv, is_last, tokens, heads, kv_here, after, relay=()):
    is_first = state is None
    least = tuple(pair for _, pair in kv)
    kv = [block for block, _ in kv]
    blocks = len(kv)
    rows = tokens * heads // kv_here
    unroll = min(8, rows // CHUNK)
    wide_shape = sds((kv_here, rows, 2 * LANES), BF16)
    state_shape = sds((kv_here, STATE_ROWS, rows), F32)
    out_shape = sds((tokens * heads, LANES), BF16) if is_last else state_shape
    scratch = [pltpu.VMEM((blocks, tokens, LANES), BF16)]
    if is_first:
        out_shape = (wide_shape, out_shape)
        scratch.append(pltpu.VMEM((rows, LANES), F32))
    if is_last:
        out_shape = (out_shape, sds((8, LANES), F32))
        scratch.append(pltpu.VMEM((tokens * heads, LANES), BF16))
        scratch.append(pltpu.SemaphoreType.DMA((rows // CHUNK,)))
    span = blocks * tokens
    return call(
        functools.partial(attend_kernel, tokens, heads, kv_here, least, is_first, is_last, unroll),
        "attend",
        [place],
        [*first, *([] if is_first else [state]), *kv],
        out_shape,
        scratch=scratch,
        mib=24,
        estimate=cost(
            4 * tokens * heads * span * 2 * LANES, 4 * tokens * heads * LANES * 4, tokens * heads * span
        ),
        after=after,
        out_hbm=is_last,
        relay=relay,
    )


def body(
    blocks,
    lin_query,
    lin_key,
    lin_value,
    lin_gate,
    log_decay,
    norm_gain,
    doc_ids,
    soft_query,
    soft_key,
    soft_value,
):
    tokens, heads, _ = lin_query.shape
    tensor = HEADS // heads
    kv_here = max(1, heads // GROUP)
    parts = 2 if heads % 16 == 0 else 1
    longest = blocks * tokens * 5 // 8
    window = min(blocks - 1, (longest - 1 + tokens - 1) // tokens)
    flat = lambda x: x.reshape(-1, LANES)
    block = lax.axis_index("seq")
    place = block.astype(jnp.int32).reshape(1)
    start = (lax.axis_index("tp") * heads // GROUP).astype(jnp.int32).reshape(1)

    def send(x, pairs):
        return lax.ppermute(x, "seq", [(a, b % blocks) for a, b in pairs])

    everyone = range(blocks)
    swap = [(b, b ^ 1) for b in everyone]

    own_kv, docs, cumul, key, value = fetch(
        start,
        [
            doc_ids.reshape(tokens // LANES, LANES),
            jnp.transpose(log_decay),
            flat(soft_key),
            flat(soft_value),
            flat(lin_key),
            flat(lin_value),
        ],
        tokens,
        heads,
        kv_here,
    )

    forward = [(b, b + 2) for b in everyone]
    hop = {b: b ^ 1 for b in everyone}
    if window % 2:
        for b in range(1, blocks - window, 2):
            last = next(a for a in everyone if hop[a] == b + window)
            hop[b], hop[last] = b + window, hop[b]
    ahead = send(own_kv, forward)
    beside = (send(own_kv, list(hop.items())), (window if window % 2 else blocks, 1))

    size = quarter_rows(heads)
    others = range(1, GROUP_BLOCKS)
    *sent, query = block_state(
        place, flat(soft_query), cumul, docs, key, value, tokens, heads
    )
    quarters = [sent[0]] + [send(sent[j], [(b, b ^ j) for b in everyone]) for j in others]

    state = {}

    def first_attention(after):
        state["wide"], state["sum"] = attend(
            place, (docs, query), None, [(own_kv, (0, 0))], False, tokens, heads, kv_here, after
        )
        return state["sum"]

    def more_attention(kv, is_last, after, relay=()):
        out = attend(
            place, (state["wide"],), state["sum"], kv, is_last, tokens, heads, kv_here, after, relay
        )
        state["sum"] = out[0] if relay else out
        return out

    inner, qh = [], []

    def inner_of(part, after, relay=()):
        n = heads // parts
        got = inner_part(
            cumul, docs, flat(lin_query), key, value, tokens, heads, part * n, n, after, relay
        )
        inner.append(got[0])
        qh.append(got[1])
        return (got[0], *got[2:]) if relay else got[0]

    done, lane = first_attention([sent[0]]), ahead
    if parts > 1:
        done, lane = inner_of(0, [done], [ahead])
    second = send(lane, forward)
    run, lane = group_map(place, quarters, size, [done, beside[0]], [lane])
    first_cross = send(lane, swap)
    stages = (blocks // GROUP_BLOCKS).bit_length() - 1
    before, done = None, run
    for stage in range(stages):
        came = send(run, [(b, b ^ (GROUP_BLOCKS << stage)) for b in everyone])
        if stage == stages - 1:
            done = more_attention([beside, (lane, (2, 2))], False, [done])
            done = inner_of(parts - 1, [done])
        else:
            run, before = scan_step(place, stage + 2, run, came, before, size, [done])
            done = run
    *priors, prior_doc = prior_states(place, stages + 1, quarters, came, before, size, [done])
    priors = [priors[0]] + [send(priors[j], [(b, b ^ j) for b in everyone]) for j in others]
    done = more_attention([(first_cross, (2, 3)), (second, (4, 4))], False, [prior_doc])
    lane = pass_on(second, [done, *priors])
    rest = [(send(lane, swap), (4, 5))]
    for back in range(3, window // 2 + 1):
        lane = send(lane, forward)
        rest.append((lane, (2 * back, 2 * back)))
        rest.append((send(lane, swap), (2 * back, 2 * back + 1)))
    mixed, squares = mix(place, docs, prior_doc, cumul, inner, qh, priors, tokens, heads, [done])
    sums = [squares]
    for other in range(1, tensor):
        sums.append(lax.ppermute(squares, "tp", [(t, t ^ other) for t in range(tensor)]))
    done = squares
    while rest:
        got = more_attention(rest[:2], len(rest) <= 2, [done])
        rest, done = rest[2:], got
    soft_out, done = got
    lin_out = finish(norm_gain, flat(lin_gate), mixed, sums, tokens, heads, [done])
    shape = (tokens, heads, HEAD_DIM)
    return lin_out.reshape(shape), soft_out.reshape(shape)


def solution(mesh):
    in_specs = (
        P("seq", "tp", None),
        P("seq", "tp", None),
        P("seq", "tp", None),
        P("seq", "tp", None),
        P("seq", "tp"),
        P("tp", None),
        P("seq"),
        P("seq", "tp", None),
        P("seq", None, None),
        P("seq", None, None),
    )
    out_specs = (P("seq", "tp", None), P("seq", "tp", None))
    return jax.shard_map(
        functools.partial(body, mesh.shape["seq"]),
        mesh=mesh,
        in_specs=in_specs,
        out_specs=out_specs,
        check_vma=False,
    )
```

```python
import functools

import jax
import jax.numpy as jnp
import numpy as np
from jax import lax
from jax.experimental import pallas as pl
from jax.experimental.pallas import tpu as pltpu
from jax.sharding import PartitionSpec as P

HEADS = 64
HEAD_DIM = 128
KV_HEADS = 8
LANES = 128
GROUP = HEADS // KV_HEADS
F32 = jnp.float32
BF16 = jnp.bfloat16
BIG = float(2**20)
SCORE_TO_EXP2 = HEAD_DIM**-0.5 * float(np.log2(np.e))
INFO = 16
HIGHEST = lax.Precision.HIGHEST

VMEM = pl.BlockSpec(memory_space=pltpu.VMEM)
SMEM = pl.BlockSpec(memory_space=pltpu.SMEM)
HBM = pl.BlockSpec(memory_space=pltpu.HBM)
ANYWHERE = pl.BlockSpec(memory_space=pl.ANY)
STATE_ROWS = HEAD_DIM + 16
CHUNK = 256
GROUP_BLOCKS = 4


def sds(shape, dtype):
    return jax.ShapeDtypeStruct(shape, dtype)


def cost(flops, bytes_accessed, transcendentals=0):
    return pl.CostEstimate(
        flops=int(flops), bytes_accessed=int(bytes_accessed), transcendentals=int(transcendentals)
    )


def call(kernel, name, scalars, operands, out_shape, scratch=(), mib=16, estimate=None, after=(), hbm=0, out_hbm=False, relay=()):
    begin = len(scalars) + len(operands)
    skip = len(after)
    operands = [
        pltpu.with_memory_space_constraint(x, pltpu.HBM) if i < hbm else x for i, x in enumerate(operands)
    ]
    outs = out_shape if isinstance(out_shape, tuple) else (out_shape,)
    out_specs = (VMEM,) * len(outs)
    outs = tuple(
        (pltpu.HBM if out_hbm and i == 0 else pltpu.VMEM)(x.shape, x.dtype) for i, x in enumerate(outs)
    )
    if out_hbm:
        out_specs = (HBM, *out_specs[1:])

    moved = len(relay)
    many = len(outs)
    single = not isinstance(out_shape, tuple) and not relay
    out_specs += (VMEM,) * moved
    outs += tuple(pltpu.VMEM(x.shape, x.dtype) for x in relay)

    def run(*refs):
        rest = refs[begin + skip + moved :]
        for source, target in zip(refs[begin + skip : begin + skip + moved], rest[many : many + moved]):
            target[...] = source[...]
        kernel(*refs[:begin], *rest[:many], *rest[many + moved :])

    out = pl.pallas_call(
        run,
        out_shape=outs,
        in_specs=[SMEM] * len(scalars) + [HBM] * hbm + [VMEM] * (len(operands) - hbm) + [ANYWHERE] * skip + [VMEM] * moved,
        out_specs=out_specs,
        scratch_shapes=list(scratch),
        compiler_params=pltpu.CompilerParams(vmem_limit_bytes=mib * 1024 * 1024),
        cost_estimate=estimate,
        name=name,
    )(*scalars, *operands, *after, *relay)
    return out[0] if single else out


def doc_columns(doc_rows, tokens):
    parts = []
    for i in range(tokens // LANES):
        row = jnp.broadcast_to(doc_rows[i : i + 1, :], (LANES, LANES))
        parts.append(jnp.transpose(row))
    return jnp.concatenate(parts, axis=0)


def doc_line(doc_rows, tokens):
    return jnp.concatenate([doc_rows[i : i + 1, :] for i in range(tokens // LANES)], axis=1)


def lower_triangle(tokens):
    rows = lax.broadcasted_iota(jnp.int32, (tokens, tokens), 0)
    cols = lax.broadcasted_iota(jnp.int32, (tokens, tokens), 1)
    return rows >= cols


def pick_kernel(place_ref, even_ref, odd_ref, out_ref):
    out_ref[...] = jnp.where(place_ref[0] % 2 == 0, even_ref[...], odd_ref[...])


def pick(place, even, odd, after):
    return call(pick_kernel, "pick", [place], [even, odd], sds(even.shape, BF16), after=after)


def pass_on(arrays, after):
    return call(lambda: None, "pass_on", [], [], (), after=after, relay=arrays)


def fetch_kernel(tokens, heads, kv_here, start_ref, *refs):
    refs = list(refs)
    take = lambda n: [refs.pop(0) for _ in range(n)]
    sources = take(6)
    kv_ref, doc_out, cumul_ref, key_out, value_out = take(5)
    held = take(4)
    sems, wide, ldp = refs
    docs_in, decays, soft_key, soft_value = held
    targets = [*held, key_out, value_out]
    copies = [
        pltpu.make_async_copy(source, target, sems.at[i])
        for i, (source, target) in enumerate(zip(sources, targets))
    ]
    for copy in copies:
        copy.start()

    copies[0].wait()
    docs = docs_in[...].astype(F32) + 1.0
    line = lax.broadcasted_iota(jnp.int32, (INFO, LANES), 0)
    info = jnp.zeros((INFO, LANES), F32)
    for i in range(tokens // LANES):
        info = jnp.where(line == i, docs[i : i + 1, :], info)
    doc_out[...] = info
    end = 2 * kv_here * tokens
    kv_ref[end : end + INFO, :] = info.astype(BF16)

    copies[1].wait()
    ldp[...] = jnp.zeros_like(ldp)
    ldp[0:heads, :] = decays[...]
    cumul_ref[...] = lax.dot_general(
        lower_triangle(tokens).astype(F32),
        ldp[...],
        (((1,), (1,)), ((), ())),
        precision=HIGHEST,
        preferred_element_type=F32,
    )

    start = start_ref[0]
    for which, ref in enumerate((soft_key, soft_value)):
        copies[2 + which].wait()
        wide[...] = ref[...].astype(F32)
        for g in range(kv_here):
            rows = wide[pl.ds(start + g, tokens, stride=KV_HEADS), :]
            at = (which * kv_here + g) * tokens
            if which:
                halves = [jnp.transpose(rows[i : i + LANES, :]) for i in range(0, tokens, LANES)]
                rows = jnp.concatenate(halves, axis=0)
            kv_ref[at : at + tokens, :] = rows.astype(BF16)
    for copy in copies[4:]:
        copy.wait()


def fetch(start, operands, tokens, heads, kv_here):
    return call(
        functools.partial(fetch_kernel, tokens, heads, kv_here),
        "fetch",
        [start],
        operands,
        (
            sds((2 * kv_here * tokens + INFO, LANES), BF16),
            sds((INFO, LANES), F32),
            sds((tokens, LANES), F32),
            sds(operands[4].shape, BF16),
            sds(operands[5].shape, BF16),
        ),
        scratch=[pltpu.VMEM(x.shape, x.dtype) for x in operands[:4]]
        + [
            pltpu.SemaphoreType.DMA((len(operands),)),
            pltpu.VMEM((tokens * KV_HEADS, LANES), F32),
            pltpu.VMEM((LANES, tokens), F32),
        ],
        estimate=cost(0, 3 * tokens * heads * LANES * 2),
        hbm=len(operands),
    )


def quarter_rows(heads):
    return heads * HEAD_DIM // GROUP_BLOCKS


def state_kernel(tokens, heads, place_ref, *refs):
    refs = list(refs)
    take = lambda n: [refs.pop(0) for _ in range(n)]
    query_in, cumul_ref, doc_ref, key_ref, value_ref = take(5)
    out_refs, query_out = take(GROUP_BLOCKS), take(1)[0]
    kf, vf, states, sem = refs
    copy = pltpu.make_async_copy(query_in, query_out, sem)
    copy.start()
    cumul, docs = cumul_ref[...], doc_ref[...]
    total = cumul[tokens - 1 : tokens, :]
    last_row = tokens // LANES - 1
    first_doc = docs[0:1, 0:1]
    last_doc = docs[last_row : last_row + 1, LANES - 1 : LANES]
    tail = (doc_columns(docs, tokens) == last_doc).astype(F32)
    scale = jnp.exp(total - cumul) * tail
    kf[...] = key_ref[...].astype(F32)
    vf[...] = value_ref[...].astype(F32)
    for h in range(heads):
        keys = (kf[pl.ds(h, tokens, stride=heads), :] * scale[:, h : h + 1]).astype(BF16)
        values = vf[pl.ds(h, tokens, stride=heads), :].astype(BF16)
        states[h * HEAD_DIM : (h + 1) * HEAD_DIM, :] = lax.dot_general(
            keys, values, (((0,), (0,)), ((), ())), preferred_element_type=F32
        )
    size = quarter_rows(heads)
    mine = place_ref[0] % GROUP_BLOCKS
    for j, ref in enumerate(out_refs):
        taker = mine ^ j
        ref[0:size, :] = states[pl.ds(pl.multiple_of(taker * size, size), size), :].astype(BF16)
        totals = jnp.zeros_like(total)
        for c in range(GROUP_BLOCKS):
            skip = c * heads // GROUP_BLOCKS
            moved = pltpu.roll(total, LANES - skip, 1) if skip else total
            totals = jnp.where(taker == c, moved, totals)
        ref[size : size + INFO, :] = info_rows((*in_parts(totals), first_doc, last_doc))
    copy.wait()


def block_state(place, soft_query, cumul, docs, key, value, tokens, heads):
    return call(
        functools.partial(state_kernel, tokens, heads),
        "block_state",
        [place],
        [soft_query, cumul, docs, key, value],
        (
            *[sds((quarter_rows(heads) + INFO, LANES), BF16)] * GROUP_BLOCKS,
            sds(soft_query.shape, BF16),
        ),
        scratch=[
            pltpu.VMEM((tokens * heads, LANES), F32),
            pltpu.VMEM((tokens * heads, LANES), F32),
            pltpu.VMEM((heads * HEAD_DIM, LANES), F32),
            pltpu.SemaphoreType.DMA,
        ],
        estimate=cost(2 * heads * tokens * HEAD_DIM**2, 5 * tokens * heads * LANES * 2),
        hbm=1,
    )


def in_parts(x):
    hi = x.astype(BF16).astype(F32)
    mid = (x - hi).astype(BF16).astype(F32)
    return hi, mid, x - hi - mid


def info_rows(parts):
    line = lax.broadcasted_iota(jnp.int32, (INFO, LANES), 0)
    info = jnp.zeros((INFO, LANES), F32)
    for i, part in enumerate(parts):
        info = jnp.where(line == i, part, info)
    return info.astype(BF16)


def read_map(ref, size):
    info = ref[size : size + INFO, :].astype(F32)
    return info[0:1] + info[1:2] + info[2:3], info[3:4], info[4:5]


def row_chunks(size):
    unit = min(HEAD_DIM, size)
    return [(slice(i * unit, (i + 1) * unit), slice(i, i + 1)) for i in range(size // unit)]


def in_block_order(place_ref, refs, blocks):
    mine = place_ref[0] % GROUP_BLOCKS
    for j, ref in enumerate(refs):
        blocks[mine ^ j] = ref[...]


def block_maps(blocks, size):
    maps = []
    for c in range(GROUP_BLOCKS):
        info = blocks[c, size : size + INFO, :].astype(F32)
        first, last = info[3:4], info[4:5]
        gain = jnp.exp(info[0:1] + info[1:2] + info[2:3]) * (first == last).astype(F32)
        maps.append((gain, first, last))
    return maps


def group_kernel(size, place_ref, *refs):
    sources = refs[:GROUP_BLOCKS]
    out_ref, blocks = refs[GROUP_BLOCKS:]
    in_block_order(place_ref, sources, blocks)
    maps = block_maps(blocks, size)
    gains = [None]
    for (gain, first, _), (_, _, last_before) in zip(maps[1:], maps[:-1]):
        gains.append(gain * (last_before == first).astype(F32))
    for rows, lane in row_chunks(size):
        total = blocks[0, rows, :].astype(F32)
        for c in range(1, GROUP_BLOCKS):
            total = gains[c][:, lane] * total + blocks[c, rows, :].astype(F32)
        out_ref[rows, :] = total.astype(BF16)
    gain = maps[0][0] * gains[1] * gains[2] * gains[3]
    out_ref[size : size + INFO, :] = info_rows((*in_parts(gain), maps[0][1], maps[-1][2]))


def group_map(place, quarters, size, after, relay):
    return call(
        functools.partial(group_kernel, size),
        "group_map",
        [place],
        quarters,
        (sds((size + INFO, LANES), BF16),),
        scratch=[pltpu.VMEM((GROUP_BLOCKS, size + INFO, LANES), BF16)],
        estimate=cost(8 * size * LANES, 10 * size * LANES * 2),
        after=after,
        relay=relay,
    )


def scan_kernel(size, has_before, bit, place_ref, *refs):
    mine_ref, came_ref = refs[:2]
    before_ref = refs[2] if has_before else None
    run_ref, out_ref = refs[-2:]
    upper = (place_ref[0] >> bit) & 1 == 1
    gain_m, first_m, last_m = read_map(mine_ref, size)
    gain_c, first_c, last_c = read_map(came_ref, size)
    link = jnp.where(upper, (last_c == first_m).astype(F32), (last_m == first_c).astype(F32))
    gain = jnp.where(upper, gain_m, gain_c) * link
    for rows, lane in row_chunks(size):
        mine, came = mine_ref[rows, :].astype(F32), came_ref[rows, :].astype(F32)
        lower_sum, upper_sum = jnp.where(upper, came, mine), jnp.where(upper, mine, came)
        run_ref[rows, :] = (gain[:, lane] * lower_sum + upper_sum).astype(BF16)
    run_ref[size : size + INFO, :] = info_rows(
        (
            *in_parts(gain * jnp.where(upper, gain_c, gain_m)),
            jnp.where(upper, first_c, first_m),
            jnp.where(upper, last_m, last_c),
        )
    )
    if not has_before:
        out_ref[...] = jnp.where(upper, came_ref[...], jnp.zeros_like(came_ref))
        return
    gain_b, first_b, last_b = read_map(before_ref, size)
    empty = first_b == 0.0
    factor = jnp.where(empty, 1.0, gain_b * (last_c == first_b).astype(F32))
    for rows, lane in row_chunks(size):
        before = before_ref[rows, :].astype(F32)
        joined = factor[:, lane] * came_ref[rows, :].astype(F32) + before
        out_ref[rows, :] = jnp.where(upper, joined, before).astype(BF16)
    out_ref[size : size + INFO, :] = info_rows(
        (
            *in_parts(jnp.where(upper, factor * gain_c, gain_b)),
            jnp.where(upper, first_c, first_b),
            jnp.where(upper, jnp.where(empty, last_c, last_b), last_b),
        )
    )


def scan_step(place, bit, mine, came, before, size, after):
    shape = sds((size + INFO, LANES), BF16)
    before = [] if before is None else [before]
    return call(
        functools.partial(scan_kernel, size, len(before), bit),
        "scan_step",
        [place],
        [mine, came, *before],
        (shape, shape),
        estimate=cost(6 * size * LANES, 6 * size * LANES * 2),
        after=after,
    )


def prior_kernel(size, has_before, bit, place_ref, *refs):
    sources, came_ref = refs[:GROUP_BLOCKS], refs[GROUP_BLOCKS]
    before_ref = refs[GROUP_BLOCKS + 1] if has_before else None
    *out_refs, doc_ref, blocks, priors = refs[GROUP_BLOCKS + 1 + has_before :]
    mine = place_ref[0] % GROUP_BLOCKS
    in_block_order(place_ref, sources, blocks)
    maps = block_maps(blocks, size)
    upper = ((place_ref[0] >> bit) & 1).astype(F32)
    _, _, last_c = read_map(came_ref, size)
    factor, doc = jnp.broadcast_to(upper, (1, LANES)), upper * last_c
    if has_before:
        gain_b, first_b, last_b = read_map(before_ref, size)
        empty = first_b == 0.0
        factor = upper * jnp.where(empty, 1.0, gain_b * (last_c == first_b).astype(F32))
        doc = jnp.where(empty, doc, last_b)
    docs = [doc] + [last for _, _, last in maps[:-1]]
    gains = [gain * (doc == first).astype(F32) for (gain, first, _), doc in zip(maps, docs)]
    for rows, lane in row_chunks(size):
        state = factor[:, lane] * came_ref[rows, :].astype(F32)
        if has_before:
            state = state + before_ref[rows, :].astype(F32)
        for c in range(GROUP_BLOCKS):
            priors[c, rows, :] = state.astype(BF16)
            if c < GROUP_BLOCKS - 1:
                state = gains[c][:, lane] * state + blocks[c, rows, :].astype(F32)
    for j, ref in enumerate(out_refs):
        ref[...] = priors[mine ^ j]
    own_doc = docs[0]
    for c in range(1, GROUP_BLOCKS):
        own_doc = jnp.where(mine == c, docs[c], own_doc)
    doc_ref[...] = jnp.broadcast_to(own_doc, (8, LANES))


def prior_states(place, bit, quarters, came, before, size, after, relay=()):
    before = [] if before is None else [before]
    return call(
        functools.partial(prior_kernel, size, len(before), bit),
        "prior_states",
        [place],
        [*quarters, came, *before],
        (*[sds((size, LANES), BF16)] * GROUP_BLOCKS, sds((8, LANES), F32)),
        scratch=[
            pltpu.VMEM((GROUP_BLOCKS, size + INFO, LANES), BF16),
            pltpu.VMEM((GROUP_BLOCKS, size, LANES), BF16),
        ],
        estimate=cost(8 * size * LANES, 10 * size * LANES * 2),
        after=after,
        relay=relay,
    )


def some_heads(ref, tokens, heads, first, count):
    x = ref[...].astype(F32)
    if count == heads:
        return x
    return x.reshape(tokens, heads, LANES)[:, first : first + count, :].reshape(tokens * count, LANES)


def inner_kernel(tokens, heads, first, count, cumul_ref, doc_ref, query_ref, key_ref, value_ref, inner_ref, qh_ref, qf, kf, vf, mask):
    cumul = cumul_ref[...]
    cumul_t = jnp.transpose(cumul)
    docs = doc_ref[...]
    column = doc_columns(docs, tokens)
    same = jnp.concatenate([column] * (tokens // LANES), axis=1) == doc_line(docs, tokens)
    mask[...] = jnp.where(lower_triangle(tokens) & same, 0.0, -1e9)
    qf[...] = some_heads(query_ref, tokens, heads, first, count)
    kf[...] = some_heads(key_ref, tokens, heads, first, count)
    vf[...] = some_heads(value_ref, tokens, heads, first, count)
    for n in range(count):
        h = first + n
        picked = pl.ds(n, tokens, stride=count)
        query = qf[picked, :].astype(BF16)
        keys = kf[picked, :].astype(BF16)
        values = vf[picked, :].astype(BF16)
        qh_ref[n * tokens : (n + 1) * tokens, :] = query
        for i in range(tokens // LANES):
            seen = (i + 1) * LANES
            rows = slice(i * LANES, seen)
            scores = lax.dot_general(
                query[rows, :], keys[0:seen, :], (((1,), (1,)), ((), ())), preferred_element_type=F32
            )
            gap = cumul[rows, h : h + 1] - cumul_t[h : h + 1, 0:seen]
            weights = (scores * jnp.exp(gap + mask[rows, 0:seen])).astype(BF16)
            inner_ref[n * tokens + i * LANES : n * tokens + seen, :] = jnp.dot(
                weights, values[0:seen, :], preferred_element_type=F32
            )


def inner_part(cumul, docs, query, key, value, tokens, heads, first, count, after, relay):
    return call(
        functools.partial(inner_kernel, tokens, heads, first, count),
        "inner_part",
        [],
        [cumul, docs, query, key, value],
        (sds((count * tokens, LANES), F32), sds((count * tokens, LANES), BF16)),
        scratch=[pltpu.VMEM((tokens * count, LANES), F32)] * 3 + [pltpu.VMEM((tokens, tokens), F32)],
        mib=24,
        estimate=cost(
            4 * count * tokens * tokens * HEAD_DIM, tokens * heads * LANES * 12, count * tokens * tokens
        ),
        after=after,
        relay=relay,
    )


def mix_kernel(tokens, heads, parts, place_ref, doc_ref, prior_doc_ref, cumul_ref, *refs):
    refs = list(refs)
    take = lambda n: [refs.pop(0) for _ in range(n)]
    inner, qh, quarters = take(parts), take(parts), take(GROUP_BLOCKS)
    mixed_ref, square_ref, states = refs
    size = quarter_rows(heads)
    mine = place_ref[0] % GROUP_BLOCKS
    for j, ref in enumerate(quarters):
        states[pl.ds(pl.multiple_of((mine ^ j) * size, size), size), :] = ref[...]
    is_open = (doc_columns(doc_ref[...], tokens) == prior_doc_ref[0:1, :]).astype(F32)
    gain = jnp.exp(cumul_ref[...]) * is_open
    squares = jnp.zeros((tokens, LANES), F32)
    for h in range(heads):
        part, n = divmod(h, heads // parts)
        held = slice(n * tokens, (n + 1) * tokens)
        state = states[h * HEAD_DIM : (h + 1) * HEAD_DIM, :]
        carried = jnp.dot(qh[part][held, :], state, preferred_element_type=F32)
        mixed = inner[part][held, :] + carried * gain[:, h : h + 1]
        squares = squares + mixed * mixed
        mixed_ref[pl.ds(h, tokens, stride=heads), :] = mixed
    square_ref[...] = lax.dot_general(
        jnp.ones((8, LANES), F32),
        squares,
        (((1,), (1,)), ((), ())),
        precision=HIGHEST,
        preferred_element_type=F32,
    )


def mix(place, docs, prior_doc, cumul, inner, qh, quarters, tokens, heads, after):
    return call(
        functools.partial(mix_kernel, tokens, heads, len(inner)),
        "mix",
        [place],
        [docs, prior_doc, cumul, *inner, *qh, *quarters],
        (sds((tokens * heads, LANES), F32), sds((8, tokens), F32)),
        scratch=[pltpu.VMEM((heads * HEAD_DIM, LANES), BF16)],
        mib=24,
        estimate=cost(2 * heads * tokens * HEAD_DIM**2, tokens * heads * LANES * 10),
        after=after,
    )


def finish_kernel(tokens, heads, sums, step, gain_ref, gate_ref, mixed_ref, *refs):
    squares, (out_ref, done, sems) = refs[:sums], refs[sums:]
    total = squares[0][0:1, :]
    for ref in squares[1:]:
        total = total + ref[0:1, :]
    scale = lax.rsqrt(total / (HEADS * HEAD_DIM) + 1e-06)
    rows = jnp.concatenate([scale[:, i * LANES : (i + 1) * LANES] for i in range(tokens // LANES)], axis=0)
    column = doc_columns(rows, tokens)
    copies = []
    for i in range(0, tokens, step):
        at = pl.ds(i * heads, step * heads)
        gate = jax.nn.sigmoid(gate_ref[at, :].astype(F32)).reshape(step, heads, LANES)
        mixed = mixed_ref[at, :].reshape(step, heads, LANES)
        inv = column[i : i + step, :][:, None, :]
        out = mixed * inv * gain_ref[...][None] * gate
        done[at, :] = out.reshape(step * heads, LANES).astype(BF16)
        copies.append(pltpu.make_async_copy(done.at[at, :], out_ref.at[at, :], sems.at[i // step]))
        copies[-1].start()
    for copy in copies:
        copy.wait()


def finish(gain, gate, mixed, squares, tokens, heads, after):
    step = 64
    return call(
        functools.partial(finish_kernel, tokens, heads, len(squares), step),
        "finish",
        [],
        [gain, gate, mixed, *squares],
        sds((tokens * heads, LANES), BF16),
        scratch=[pltpu.VMEM((tokens * heads, LANES), BF16), pltpu.SemaphoreType.DMA((tokens // step,))],
        estimate=cost(0, tokens * heads * LANES * 8, tokens * heads * LANES),
        after=after,
        out_hbm=True,
    )


def attend_kernel(tokens, heads, kv_here, least, is_first, is_last, unroll, place_ref, *refs):
    refs = list(refs)
    take = lambda n: [refs.pop(0) for _ in range(n)]
    per_group = heads // kv_here
    rows = tokens * per_group
    step = CHUNK // per_group
    if is_first:
        doc_ref, query_ref = take(2)
    else:
        wide_ref, state_ref = take(2)
    kv = take(len(least))
    if is_first:
        wide_ref = take(1)[0]
    out_ref = take(1)[0]
    if is_last:
        take(1)[0][...] = jnp.zeros((8, LANES), F32)
    bias = take(1)[0]
    if is_first:
        doc_rep = take(1)[0]
    if is_last:
        done, sems = take(2)
    block = place_ref[0]

    lane = lax.broadcasted_iota(jnp.int32, (tokens, LANES), 1).astype(F32)
    end = 2 * kv_here * tokens
    for j, ref in enumerate(kv):
        valid = (block >= jnp.where(block % 2 == 0, *least[j])).astype(F32)
        docs = doc_columns(ref[end : end + INFO, :].astype(F32) * valid, tokens)
        bias[j] = jnp.where(docs == lane, 0.0, -BIG).astype(BF16)
    if is_first:
        column = doc_columns(doc_ref[...], tokens)
        for h in range(per_group):
            doc_rep[pl.ds(h, tokens, stride=per_group), :] = (column == lane).astype(F32)
    ones = jnp.ones((STATE_ROWS - HEAD_DIM, tokens), BF16)

    def some_chunks(i, carry):
        chains = [(u, g) for u in range(unroll) for g in range(kv_here)]
        chunk = [i * unroll + u for u in range(unroll)]
        at = [pl.ds(pl.multiple_of(c * CHUNK, CHUNK), CHUNK) for c in chunk]
        picked = [pl.ds(pl.multiple_of(c * (step * heads), step * heads), step * heads) for c in chunk]
        scores, results = {}, {}

        def begin(u, g):
            if is_first:
                query = query_ref[picked[u], :].astype(F32).reshape(step, heads, LANES)
                query = query[:, g * per_group : (g + 1) * per_group, :].reshape(CHUNK, LANES)
                wide = jnp.concatenate([query.astype(BF16), doc_rep[at[u], :].astype(BF16)], axis=1)
                wide_ref[g, at[u], :] = wide
            else:
                wide = wide_ref[g, at[u], :]
            out = []
            for j, ref in enumerate(kv):
                keys = jnp.concatenate([ref[g * tokens : (g + 1) * tokens, :], bias[j]], axis=1)
                out.append(
                    lax.dot_general(keys, wide, (((1,), (1,)), ((), ())), preferred_element_type=F32)
                )
            if is_first:
                token = chunk[u] * step + lax.broadcasted_iota(jnp.int32, (tokens, CHUNK), 1) // per_group
                key_at = lax.broadcasted_iota(jnp.int32, (tokens, CHUNK), 0)
                out[0] = jnp.where(key_at <= token, out[0], -BIG)
            scores[u, g] = out

        def end_chain(u, g):
            here = scores.pop((u, g))
            top = jnp.max(here[0], axis=0, keepdims=True)
            for score in here[1:]:
                top = jnp.maximum(top, jnp.max(score, axis=0, keepdims=True))
            total = None
            if not is_first:
                before = state_ref[g, :, at[u]]
                top_before = before[STATE_ROWS - 1 : STATE_ROWS, :]
                top = jnp.maximum(top, top_before)
                total = before * jnp.exp2((top_before - top) * SCORE_TO_EXP2)
            for ref, score in zip(kv, here):
                weights = jnp.exp2((score - top) * SCORE_TO_EXP2).astype(BF16)
                first = (kv_here + g) * tokens
                parts = [ref[first + p : first + p + LANES, :] for p in range(0, tokens, LANES)]
                values = jnp.concatenate([jnp.concatenate(parts, axis=1), ones], axis=0)
                more = jnp.dot(values, weights, preferred_element_type=F32)
                total = more if total is None else total + more
            if is_last:
                results[u, g] = jnp.transpose(total[0:HEAD_DIM] / total[HEAD_DIM : HEAD_DIM + 1])
            else:
                out_ref[g, 0 : STATE_ROWS - 8, at[u]] = total[0 : STATE_ROWS - 8]
                out_ref[g, STATE_ROWS - 8 : STATE_ROWS, at[u]] = jnp.broadcast_to(top, (8, CHUNK))

        ahead = 3
        for n in range(len(chains) + ahead):
            if n < len(chains):
                begin(*chains[n])
            if n >= ahead:
                end_chain(*chains[n - ahead])
        if is_last:
            for u in range(unroll):
                result = [results[u, g] for g in range(kv_here)]
                if kv_here > 1:
                    result = [r.reshape(step, per_group, LANES) for r in result]
                    result = [jnp.concatenate(result, axis=1).reshape(step * heads, LANES)]
                done[picked[u], :] = result[0].astype(BF16)
                pltpu.make_async_copy(
                    done.at[picked[u], :], out_ref.at[picked[u], :], sems.at[chunk[u]]
                ).start()
        return carry

    lax.fori_loop(0, rows // (CHUNK * unroll), some_chunks, 0)
    if is_last:
        for c in range(rows // CHUNK):
            at = pl.ds(c * step * heads, step * heads)
            pltpu.make_async_copy(done.at[at, :], out_ref.at[at, :], sems.at[c]).wait()


def attend(place, first, state, kv, is_last, tokens, heads, kv_here, after, relay=()):
    is_first = state is None
    least = tuple(pair for _, pair in kv)
    kv = [block for block, _ in kv]
    blocks = len(kv)
    rows = tokens * heads // kv_here
    unroll = min(8, rows // CHUNK)
    wide_shape = sds((kv_here, rows, 2 * LANES), BF16)
    state_shape = sds((kv_here, STATE_ROWS, rows), F32)
    out_shape = sds((tokens * heads, LANES), BF16) if is_last else state_shape
    scratch = [pltpu.VMEM((blocks, tokens, LANES), BF16)]
    if is_first:
        out_shape = (wide_shape, out_shape)
        scratch.append(pltpu.VMEM((rows, LANES), F32))
    if is_last:
        out_shape = (out_shape, sds((8, LANES), F32))
        scratch.append(pltpu.VMEM((tokens * heads, LANES), BF16))
        scratch.append(pltpu.SemaphoreType.DMA((rows // CHUNK,)))
    span = blocks * tokens
    return call(
        functools.partial(attend_kernel, tokens, heads, kv_here, least, is_first, is_last, unroll),
        "attend",
        [place],
        [*first, *([] if is_first else [state]), *kv],
        out_shape,
        scratch=scratch,
        mib=24,
        estimate=cost(
            4 * tokens * heads * span * 2 * LANES, 4 * tokens * heads * LANES * 4, tokens * heads * span
        ),
        after=after,
        out_hbm=is_last,
        relay=relay,
    )


def body(
    blocks,
    lin_query,
    lin_key,
    lin_value,
    lin_gate,
    log_decay,
    norm_gain,
    doc_ids,
    soft_query,
    soft_key,
    soft_value,
):
    tokens, heads, _ = lin_query.shape
    tensor = HEADS // heads
    kv_here = max(1, heads // GROUP)
    parts = 2 if heads % 16 == 0 else 1
    longest = blocks * tokens * 5 // 8
    window = min(blocks - 1, (longest - 1 + tokens - 1) // tokens)
    flat = lambda x: x.reshape(-1, LANES)
    block = lax.axis_index("seq")
    place = block.astype(jnp.int32).reshape(1)
    start = (lax.axis_index("tp") * heads // GROUP).astype(jnp.int32).reshape(1)

    def send(x, pairs):
        return lax.ppermute(x, "seq", [(a, b % blocks) for a, b in pairs])

    everyone = range(blocks)
    swap = [(b, b ^ 1) for b in everyone]

    own_kv, docs, cumul, key, value = fetch(
        start,
        [
            doc_ids.reshape(tokens // LANES, LANES),
            jnp.transpose(log_decay),
            flat(soft_key),
            flat(soft_value),
            flat(lin_key),
            flat(lin_value),
        ],
        tokens,
        heads,
        kv_here,
    )

    forward = [(b, b + 2) for b in everyone]
    ahead = send(own_kv, forward)

    size = quarter_rows(heads)
    others = range(1, GROUP_BLOCKS)
    *sent, query = block_state(
        place, flat(soft_query), cumul, docs, key, value, tokens, heads
    )
    quarters = [sent[0]] + [send(sent[j], [(b, b ^ j) for b in everyone]) for j in others]

    state = {}

    def first_attention(after):
        state["wide"], state["sum"] = attend(
            place, (docs, query), None, [(own_kv, (0, 0))], False, tokens, heads, kv_here, after
        )
        return state["sum"]

    def more_attention(kv, is_last, after, relay=()):
        out = attend(
            place, (state["wide"],), state["sum"], kv, is_last, tokens, heads, kv_here, after, relay
        )
        state["sum"] = out[0] if relay else out
        return out

    inner, qh = [], []

    def inner_of(part, after, relay=()):
        n = heads // parts
        got = inner_part(
            cumul, docs, flat(lin_query), key, value, tokens, heads, part * n, n, after, relay
        )
        inner.append(got[0])
        qh.append(got[1])
        return (got[0], *got[2:]) if relay else got[0]

    done, lane = first_attention([sent[0]]), ahead
    if parts > 1:
        done, lane = inner_of(0, [done], [ahead])
    second = send(lane, [(b, b + 2) for b in range(2, blocks - 2)])
    run, lane, own_copy = group_map(place, quarters, size, [done], [lane, own_kv])
    first_cross = send(lane, swap)
    beside = send(own_copy, swap)
    stages = (blocks // GROUP_BLOCKS).bit_length() - 1
    before, done = None, run
    for stage in range(stages):
        came = send(run, [(b, b ^ (GROUP_BLOCKS << stage)) for b in everyone])
        if stage == stages - 1:
            done = more_attention([(lane, (2, 2))], False, [done])
            done = inner_of(parts - 1, [done])
        else:
            run, before = scan_step(place, stage + 2, run, came, before, size, [done])
            done = run
    *priors, prior_doc = prior_states(place, stages + 1, quarters, came, before, size, [done])
    priors = [priors[0]] + [send(priors[j], [(b, b ^ j) for b in everyone]) for j in others]
    done = more_attention([(first_cross, (2, 3)), (second, (4, 4))], False, [prior_doc])
    lane, own_copy = pass_on([second, own_kv], [done, *priors])
    rest = [(send(lane, [(b, b ^ 1) for b in range(4, blocks)]), (4, 5))]
    far = None
    if window % 2:
        far = send(own_copy, [(b, b + window) for b in range(1, blocks - window, 2)])
    for back in range(3, window // 2 + 1):
        lane = send(lane, forward)
        rest.append((lane, (2 * back, 2 * back)))
        rest.append((send(lane, swap), (2 * back, 2 * back + 1)))
    mixed, squares = mix(place, docs, prior_doc, cumul, inner, qh, priors, tokens, heads, [done])
    sums = [squares]
    for other in range(1, tensor):
        sums.append(lax.ppermute(squares, "tp", [(t, t ^ other) for t in range(tensor)]))
    slot = beside if far is None else pick(place, far, beside, [squares])
    rest.insert(0, (slot, (blocks if far is None else window, 1)))
    done = squares
    while rest:
        got = more_attention(rest[:2], len(rest) <= 2, [done])
        rest, done = rest[2:], got
    soft_out, done = got
    lin_out = finish(norm_gain, flat(lin_gate), mixed, sums, tokens, heads, [done])
    shape = (tokens, heads, HEAD_DIM)
    return lin_out.reshape(shape), soft_out.reshape(shape)


def solution(mesh):
    in_specs = (
        P("seq", "tp", None),
        P("seq", "tp", None),
        P("seq", "tp", None),
        P("seq", "tp", None),
        P("seq", "tp"),
        P("tp", None),
        P("seq"),
        P("seq", "tp", None),
        P("seq", None, None),
        P("seq", None, None),
    )
    out_specs = (P("seq", "tp", None), P("seq", "tp", None))
    return jax.shard_map(
        functools.partial(body, mesh.shape["seq"]),
        mesh=mesh,
        in_specs=in_specs,
        out_specs=out_specs,
        check_vma=False,
    )
```

```python
import functools

import jax
import jax.numpy as jnp
import numpy as np
from jax import lax
from jax.experimental import pallas as pl
from jax.experimental.pallas import tpu as pltpu
from jax.sharding import PartitionSpec as P

HEADS = 64
HEAD_DIM = 128
KV_HEADS = 8
LANES = 128
GROUP = HEADS // KV_HEADS
F32 = jnp.float32
BF16 = jnp.bfloat16
BIG = float(2**20)
SCORE_TO_EXP2 = HEAD_DIM**-0.5 * float(np.log2(np.e))
INFO = 16
HIGHEST = lax.Precision.HIGHEST

VMEM = pl.BlockSpec(memory_space=pltpu.VMEM)
SMEM = pl.BlockSpec(memory_space=pltpu.SMEM)
HBM = pl.BlockSpec(memory_space=pltpu.HBM)
ANYWHERE = pl.BlockSpec(memory_space=pl.ANY)
STATE_ROWS = HEAD_DIM + 16
CHUNK = 256
GROUP_BLOCKS = 4


def sds(shape, dtype):
    return jax.ShapeDtypeStruct(shape, dtype)


def cost(flops, bytes_accessed, transcendentals=0):
    return pl.CostEstimate(
        flops=int(flops), bytes_accessed=int(bytes_accessed), transcendentals=int(transcendentals)
    )


def call(kernel, name, scalars, operands, out_shape, scratch=(), mib=16, estimate=None, after=(), hbm=0, out_hbm=False, relay=()):
    begin = len(scalars) + len(operands)
    skip = len(after)
    operands = [
        pltpu.with_memory_space_constraint(x, pltpu.HBM) if i < hbm else x for i, x in enumerate(operands)
    ]
    outs = out_shape if isinstance(out_shape, tuple) else (out_shape,)
    out_specs = (VMEM,) * len(outs)
    outs = tuple(
        (pltpu.HBM if out_hbm and i == 0 else pltpu.VMEM)(x.shape, x.dtype) for i, x in enumerate(outs)
    )
    if out_hbm:
        out_specs = (HBM, *out_specs[1:])

    moved = len(relay)
    many = len(outs)
    single = not isinstance(out_shape, tuple) and not relay
    out_specs += (VMEM,) * moved
    outs += tuple(pltpu.VMEM(x.shape, x.dtype) for x in relay)

    def run(*refs):
        rest = refs[begin + skip + moved :]
        for source, target in zip(refs[begin + skip : begin + skip + moved], rest[many : many + moved]):
            target[...] = source[...]
        kernel(*refs[:begin], *rest[:many], *rest[many + moved :])

    out = pl.pallas_call(
        run,
        out_shape=outs,
        in_specs=[SMEM] * len(scalars) + [HBM] * hbm + [VMEM] * (len(operands) - hbm) + [ANYWHERE] * skip + [VMEM] * moved,
        out_specs=out_specs,
        scratch_shapes=list(scratch),
        compiler_params=pltpu.CompilerParams(vmem_limit_bytes=mib * 1024 * 1024),
        cost_estimate=estimate,
        name=name,
    )(*scalars, *operands, *after, *relay)
    return out[0] if single else out


def doc_columns(doc_rows, tokens):
    parts = []
    for i in range(tokens // LANES):
        row = jnp.broadcast_to(doc_rows[i : i + 1, :], (LANES, LANES))
        parts.append(jnp.transpose(row))
    return jnp.concatenate(parts, axis=0)


def doc_line(doc_rows, tokens):
    return jnp.concatenate([doc_rows[i : i + 1, :] for i in range(tokens // LANES)], axis=1)


def lower_triangle(tokens):
    rows = lax.broadcasted_iota(jnp.int32, (tokens, tokens), 0)
    cols = lax.broadcasted_iota(jnp.int32, (tokens, tokens), 1)
    return rows >= cols


def pick_kernel(place_ref, even_ref, odd_ref, out_ref):
    out_ref[...] = jnp.where(place_ref[0] % 2 == 0, even_ref[...], odd_ref[...])


def pick(place, even, odd, after):
    return call(pick_kernel, "pick", [place], [even, odd], sds(even.shape, BF16), after=after)


def pass_on(arrays, after):
    return call(lambda: None, "pass_on", [], [], (), after=after, relay=arrays)


def fetch_kernel(tokens, heads, kv_here, start_ref, *refs):
    refs = list(refs)
    take = lambda n: [refs.pop(0) for _ in range(n)]
    sources = take(6)
    kv_ref, doc_out, cumul_ref, key_out, value_out = take(5)
    held = take(4)
    sems, wide, ldp = refs
    docs_in, decays, soft_key, soft_value = held
    targets = [*held, key_out, value_out]
    copies = [
        pltpu.make_async_copy(source, target, sems.at[i])
        for i, (source, target) in enumerate(zip(sources, targets))
    ]
    for copy in copies:
        copy.start()

    copies[0].wait()
    docs = docs_in[...].astype(F32) + 1.0
    line = lax.broadcasted_iota(jnp.int32, (INFO, LANES), 0)
    info = jnp.zeros((INFO, LANES), F32)
    for i in range(tokens // LANES):
        info = jnp.where(line == i, docs[i : i + 1, :], info)
    doc_out[...] = info
    end = 2 * kv_here * tokens
    kv_ref[end : end + INFO, :] = info.astype(BF16)

    copies[1].wait()
    ldp[...] = jnp.zeros_like(ldp)
    ldp[0:heads, :] = decays[...]
    cumul_ref[...] = lax.dot_general(
        lower_triangle(tokens).astype(F32),
        ldp[...],
        (((1,), (1,)), ((), ())),
        precision=HIGHEST,
        preferred_element_type=F32,
    )

    start = start_ref[0]
    for which, ref in enumerate((soft_key, soft_value)):
        copies[2 + which].wait()
        wide[...] = ref[...].astype(F32)
        for g in range(kv_here):
            rows = wide[pl.ds(start + g, tokens, stride=KV_HEADS), :]
            at = (which * kv_here + g) * tokens
            if which:
                halves = [jnp.transpose(rows[i : i + LANES, :]) for i in range(0, tokens, LANES)]
                rows = jnp.concatenate(halves, axis=0)
            kv_ref[at : at + tokens, :] = rows.astype(BF16)
    for copy in copies[4:]:
        copy.wait()


def fetch(start, operands, tokens, heads, kv_here):
    return call(
        functools.partial(fetch_kernel, tokens, heads, kv_here),
        "fetch",
        [start],
        operands,
        (
            sds((2 * kv_here * tokens + INFO, LANES), BF16),
            sds((INFO, LANES), F32),
            sds((tokens, LANES), F32),
            sds(operands[4].shape, BF16),
            sds(operands[5].shape, BF16),
        ),
        scratch=[pltpu.VMEM(x.shape, x.dtype) for x in operands[:4]]
        + [
            pltpu.SemaphoreType.DMA((len(operands),)),
            pltpu.VMEM((tokens * KV_HEADS, LANES), F32),
            pltpu.VMEM((LANES, tokens), F32),
        ],
        estimate=cost(0, 3 * tokens * heads * LANES * 2),
        hbm=len(operands),
    )


def quarter_rows(heads):
    return heads * HEAD_DIM // GROUP_BLOCKS


def state_kernel(tokens, heads, place_ref, *refs):
    refs = list(refs)
    take = lambda n: [refs.pop(0) for _ in range(n)]
    query_in, cumul_ref, doc_ref, key_ref, value_ref = take(5)
    out_refs, query_out = take(GROUP_BLOCKS), take(1)[0]
    kf, vf, states, sem = refs
    copy = pltpu.make_async_copy(query_in, query_out, sem)
    copy.start()
    cumul, docs = cumul_ref[...], doc_ref[...]
    total = cumul[tokens - 1 : tokens, :]
    last_row = tokens // LANES - 1
    first_doc = docs[0:1, 0:1]
    last_doc = docs[last_row : last_row + 1, LANES - 1 : LANES]
    tail = (doc_columns(docs, tokens) == last_doc).astype(F32)
    scale = jnp.exp(total - cumul) * tail
    kf[...] = key_ref[...].astype(F32)
    vf[...] = value_ref[...].astype(F32)
    for h in range(heads):
        keys = (kf[pl.ds(h, tokens, stride=heads), :] * scale[:, h : h + 1]).astype(BF16)
        values = vf[pl.ds(h, tokens, stride=heads), :].astype(BF16)
        states[h * HEAD_DIM : (h + 1) * HEAD_DIM, :] = lax.dot_general(
            keys, values, (((0,), (0,)), ((), ())), preferred_element_type=F32
        )
    size = quarter_rows(heads)
    mine = place_ref[0] % GROUP_BLOCKS
    for j, ref in enumerate(out_refs):
        taker = mine ^ j
        ref[0:size, :] = states[pl.ds(pl.multiple_of(taker * size, size), size), :].astype(BF16)
        totals = jnp.zeros_like(total)
        for c in range(GROUP_BLOCKS):
            skip = c * heads // GROUP_BLOCKS
            moved = pltpu.roll(total, LANES - skip, 1) if skip else total
            totals = jnp.where(taker == c, moved, totals)
        ref[size : size + INFO, :] = info_rows((*in_parts(totals), first_doc, last_doc))
    copy.wait()


def block_state(place, soft_query, cumul, docs, key, value, tokens, heads):
    return call(
        functools.partial(state_kernel, tokens, heads),
        "block_state",
        [place],
        [soft_query, cumul, docs, key, value],
        (
            *[sds((quarter_rows(heads) + INFO, LANES), BF16)] * GROUP_BLOCKS,
            sds(soft_query.shape, BF16),
        ),
        scratch=[
            pltpu.VMEM((tokens * heads, LANES), F32),
            pltpu.VMEM((tokens * heads, LANES), F32),
            pltpu.VMEM((heads * HEAD_DIM, LANES), F32),
            pltpu.SemaphoreType.DMA,
        ],
        estimate=cost(2 * heads * tokens * HEAD_DIM**2, 5 * tokens * heads * LANES * 2),
        hbm=1,
    )


def in_parts(x):
    hi = x.astype(BF16).astype(F32)
    mid = (x - hi).astype(BF16).astype(F32)
    return hi, mid, x - hi - mid


def info_rows(parts):
    line = lax.broadcasted_iota(jnp.int32, (INFO, LANES), 0)
    info = jnp.zeros((INFO, LANES), F32)
    for i, part in enumerate(parts):
        info = jnp.where(line == i, part, info)
    return info.astype(BF16)


def read_map(ref, size):
    info = ref[size : size + INFO, :].astype(F32)
    return info[0:1] + info[1:2] + info[2:3], info[3:4], info[4:5]


def row_chunks(size):
    unit = min(HEAD_DIM, size)
    return [(slice(i * unit, (i + 1) * unit), slice(i, i + 1)) for i in range(size // unit)]


def in_block_order(place_ref, refs, blocks):
    mine = place_ref[0] % GROUP_BLOCKS
    for j, ref in enumerate(refs):
        blocks[mine ^ j] = ref[...]


def block_maps(blocks, size):
    maps = []
    for c in range(GROUP_BLOCKS):
        info = blocks[c, size : size + INFO, :].astype(F32)
        first, last = info[3:4], info[4:5]
        gain = jnp.exp(info[0:1] + info[1:2] + info[2:3]) * (first == last).astype(F32)
        maps.append((gain, first, last))
    return maps


def group_kernel(size, place_ref, *refs):
    sources = refs[:GROUP_BLOCKS]
    out_ref, blocks = refs[GROUP_BLOCKS:]
    in_block_order(place_ref, sources, blocks)
    maps = block_maps(blocks, size)
    gains = [None]
    for (gain, first, _), (_, _, last_before) in zip(maps[1:], maps[:-1]):
        gains.append(gain * (last_before == first).astype(F32))
    for rows, lane in row_chunks(size):
        total = blocks[0, rows, :].astype(F32)
        for c in range(1, GROUP_BLOCKS):
            total = gains[c][:, lane] * total + blocks[c, rows, :].astype(F32)
        out_ref[rows, :] = total.astype(BF16)
    gain = maps[0][0] * gains[1] * gains[2] * gains[3]
    out_ref[size : size + INFO, :] = info_rows((*in_parts(gain), maps[0][1], maps[-1][2]))


def group_map(place, quarters, size, after, relay):
    return call(
        functools.partial(group_kernel, size),
        "group_map",
        [place],
        quarters,
        (sds((size + INFO, LANES), BF16),),
        scratch=[pltpu.VMEM((GROUP_BLOCKS, size + INFO, LANES), BF16)],
        estimate=cost(8 * size * LANES, 10 * size * LANES * 2),
        after=after,
        relay=relay,
    )


def scan_kernel(size, has_before, bit, place_ref, *refs):
    mine_ref, came_ref = refs[:2]
    before_ref = refs[2] if has_before else None
    run_ref, out_ref = refs[-2:]
    upper = (place_ref[0] >> bit) & 1 == 1
    gain_m, first_m, last_m = read_map(mine_ref, size)
    gain_c, first_c, last_c = read_map(came_ref, size)
    link = jnp.where(upper, (last_c == first_m).astype(F32), (last_m == first_c).astype(F32))
    gain = jnp.where(upper, gain_m, gain_c) * link
    for rows, lane in row_chunks(size):
        mine, came = mine_ref[rows, :].astype(F32), came_ref[rows, :].astype(F32)
        lower_sum, upper_sum = jnp.where(upper, came, mine), jnp.where(upper, mine, came)
        run_ref[rows, :] = (gain[:, lane] * lower_sum + upper_sum).astype(BF16)
    run_ref[size : size + INFO, :] = info_rows(
        (
            *in_parts(gain * jnp.where(upper, gain_c, gain_m)),
            jnp.where(upper, first_c, first_m),
            jnp.where(upper, last_m, last_c),
        )
    )
    if not has_before:
        out_ref[...] = jnp.where(upper, came_ref[...], jnp.zeros_like(came_ref))
        return
    gain_b, first_b, last_b = read_map(before_ref, size)
    empty = first_b == 0.0
    factor = jnp.where(empty, 1.0, gain_b * (last_c == first_b).astype(F32))
    for rows, lane in row_chunks(size):
        before = before_ref[rows, :].astype(F32)
        joined = factor[:, lane] * came_ref[rows, :].astype(F32) + before
        out_ref[rows, :] = jnp.where(upper, joined, before).astype(BF16)
    out_ref[size : size + INFO, :] = info_rows(
        (
            *in_parts(jnp.where(upper, factor * gain_c, gain_b)),
            jnp.where(upper, first_c, first_b),
            jnp.where(upper, jnp.where(empty, last_c, last_b), last_b),
        )
    )


def scan_step(place, bit, mine, came, before, size, after):
    shape = sds((size + INFO, LANES), BF16)
    before = [] if before is None else [before]
    return call(
        functools.partial(scan_kernel, size, len(before), bit),
        "scan_step",
        [place],
        [mine, came, *before],
        (shape, shape),
        estimate=cost(6 * size * LANES, 6 * size * LANES * 2),
        after=after,
    )


def prior_kernel(size, has_before, bit, place_ref, *refs):
    sources, came_ref = refs[:GROUP_BLOCKS], refs[GROUP_BLOCKS]
    before_ref = refs[GROUP_BLOCKS + 1] if has_before else None
    *out_refs, doc_ref, blocks, priors = refs[GROUP_BLOCKS + 1 + has_before :]
    mine = place_ref[0] % GROUP_BLOCKS
    in_block_order(place_ref, sources, blocks)
    maps = block_maps(blocks, size)
    upper = ((place_ref[0] >> bit) & 1).astype(F32)
    _, _, last_c = read_map(came_ref, size)
    factor, doc = jnp.broadcast_to(upper, (1, LANES)), upper * last_c
    if has_before:
        gain_b, first_b, last_b = read_map(before_ref, size)
        empty = first_b == 0.0
        factor = upper * jnp.where(empty, 1.0, gain_b * (last_c == first_b).astype(F32))
        doc = jnp.where(empty, doc, last_b)
    docs = [doc] + [last for _, _, last in maps[:-1]]
    gains = [gain * (doc == first).astype(F32) for (gain, first, _), doc in zip(maps, docs)]
    for rows, lane in row_chunks(size):
        state = factor[:, lane] * came_ref[rows, :].astype(F32)
        if has_before:
            state = state + before_ref[rows, :].astype(F32)
        for c in range(GROUP_BLOCKS):
            priors[c, rows, :] = state.astype(BF16)
            if c < GROUP_BLOCKS - 1:
                state = gains[c][:, lane] * state + blocks[c, rows, :].astype(F32)
    for j, ref in enumerate(out_refs):
        ref[...] = priors[mine ^ j]
    own_doc = docs[0]
    for c in range(1, GROUP_BLOCKS):
        own_doc = jnp.where(mine == c, docs[c], own_doc)
    doc_ref[...] = jnp.broadcast_to(own_doc, (8, LANES))


def prior_states(place, bit, quarters, came, before, size, after, relay=()):
    before = [] if before is None else [before]
    return call(
        functools.partial(prior_kernel, size, len(before), bit),
        "prior_states",
        [place],
        [*quarters, came, *before],
        (*[sds((size, LANES), BF16)] * GROUP_BLOCKS, sds((8, LANES), F32)),
        scratch=[
            pltpu.VMEM((GROUP_BLOCKS, size + INFO, LANES), BF16),
            pltpu.VMEM((GROUP_BLOCKS, size, LANES), BF16),
        ],
        estimate=cost(8 * size * LANES, 10 * size * LANES * 2),
        after=after,
        relay=relay,
    )


def some_heads(ref, tokens, heads, first, count):
    x = ref[...].astype(F32)
    if count == heads:
        return x
    return x.reshape(tokens, heads, LANES)[:, first : first + count, :].reshape(tokens * count, LANES)


def inner_kernel(tokens, heads, first, count, cumul_ref, doc_ref, query_ref, key_ref, value_ref, inner_ref, qh_ref, qf, kf, vf, mask):
    cumul = cumul_ref[...]
    cumul_t = jnp.transpose(cumul)
    docs = doc_ref[...]
    column = doc_columns(docs, tokens)
    same = jnp.concatenate([column] * (tokens // LANES), axis=1) == doc_line(docs, tokens)
    mask[...] = jnp.where(lower_triangle(tokens) & same, 0.0, -1e9)
    qf[...] = some_heads(query_ref, tokens, heads, first, count)
    kf[...] = some_heads(key_ref, tokens, heads, first, count)
    vf[...] = some_heads(value_ref, tokens, heads, first, count)
    for n in range(count):
        h = first + n
        picked = pl.ds(n, tokens, stride=count)
        query = qf[picked, :].astype(BF16)
        keys = kf[picked, :].astype(BF16)
        values = vf[picked, :].astype(BF16)
        qh_ref[n * tokens : (n + 1) * tokens, :] = query
        for i in range(tokens // LANES):
            seen = (i + 1) * LANES
            rows = slice(i * LANES, seen)
            scores = lax.dot_general(
                query[rows, :], keys[0:seen, :], (((1,), (1,)), ((), ())), preferred_element_type=F32
            )
            gap = cumul[rows, h : h + 1] - cumul_t[h : h + 1, 0:seen]
            weights = (scores * jnp.exp(gap + mask[rows, 0:seen])).astype(BF16)
            inner_ref[n * tokens + i * LANES : n * tokens + seen, :] = jnp.dot(
                weights, values[0:seen, :], preferred_element_type=F32
            )


def inner_part(cumul, docs, query, key, value, tokens, heads, first, count, after, relay):
    return call(
        functools.partial(inner_kernel, tokens, heads, first, count),
        "inner_part",
        [],
        [cumul, docs, query, key, value],
        (sds((count * tokens, LANES), F32), sds((count * tokens, LANES), BF16)),
        scratch=[pltpu.VMEM((tokens * count, LANES), F32)] * 3 + [pltpu.VMEM((tokens, tokens), F32)],
        mib=24,
        estimate=cost(
            4 * count * tokens * tokens * HEAD_DIM, tokens * heads * LANES * 12, count * tokens * tokens
        ),
        after=after,
        relay=relay,
    )


def mix_kernel(tokens, heads, parts, place_ref, doc_ref, prior_doc_ref, cumul_ref, *refs):
    refs = list(refs)
    take = lambda n: [refs.pop(0) for _ in range(n)]
    inner, qh, quarters = take(parts), take(parts), take(GROUP_BLOCKS)
    mixed_ref, square_ref, states = refs
    size = quarter_rows(heads)
    mine = place_ref[0] % GROUP_BLOCKS
    for j, ref in enumerate(quarters):
        states[pl.ds(pl.multiple_of((mine ^ j) * size, size), size), :] = ref[...]
    is_open = (doc_columns(doc_ref[...], tokens) == prior_doc_ref[0:1, :]).astype(F32)
    gain = jnp.exp(cumul_ref[...]) * is_open
    squares = jnp.zeros((tokens, LANES), F32)
    for h in range(heads):
        part, n = divmod(h, heads // parts)
        held = slice(n * tokens, (n + 1) * tokens)
        state = states[h * HEAD_DIM : (h + 1) * HEAD_DIM, :]
        carried = jnp.dot(qh[part][held, :], state, preferred_element_type=F32)
        mixed = inner[part][held, :] + carried * gain[:, h : h + 1]
        squares = squares + mixed * mixed
        mixed_ref[pl.ds(h, tokens, stride=heads), :] = mixed
    square_ref[...] = lax.dot_general(
        jnp.ones((8, LANES), F32),
        squares,
        (((1,), (1,)), ((), ())),
        precision=HIGHEST,
        preferred_element_type=F32,
    )


def mix(place, docs, prior_doc, cumul, inner, qh, quarters, tokens, heads, after):
    return call(
        functools.partial(mix_kernel, tokens, heads, len(inner)),
        "mix",
        [place],
        [docs, prior_doc, cumul, *inner, *qh, *quarters],
        (sds((tokens * heads, LANES), F32), sds((8, tokens), F32)),
        scratch=[pltpu.VMEM((heads * HEAD_DIM, LANES), BF16)],
        mib=24,
        estimate=cost(2 * heads * tokens * HEAD_DIM**2, tokens * heads * LANES * 10),
        after=after,
    )


def finish_kernel(tokens, heads, sums, step, gain_ref, gate_ref, mixed_ref, *refs):
    squares, (out_ref, done, sems) = refs[:sums], refs[sums:]
    total = squares[0][0:1, :]
    for ref in squares[1:]:
        total = total + ref[0:1, :]
    scale = lax.rsqrt(total / (HEADS * HEAD_DIM) + 1e-06)
    rows = jnp.concatenate([scale[:, i * LANES : (i + 1) * LANES] for i in range(tokens // LANES)], axis=0)
    column = doc_columns(rows, tokens)
    copies = []
    for i in range(0, tokens, step):
        at = pl.ds(i * heads, step * heads)
        gate = jax.nn.sigmoid(gate_ref[at, :].astype(F32)).reshape(step, heads, LANES)
        mixed = mixed_ref[at, :].reshape(step, heads, LANES)
        inv = column[i : i + step, :][:, None, :]
        out = mixed * inv * gain_ref[...][None] * gate
        done[at, :] = out.reshape(step * heads, LANES).astype(BF16)
        copies.append(pltpu.make_async_copy(done.at[at, :], out_ref.at[at, :], sems.at[i // step]))
        copies[-1].start()
    for copy in copies:
        copy.wait()


def finish(gain, gate, mixed, squares, tokens, heads, after):
    step = 64
    return call(
        functools.partial(finish_kernel, tokens, heads, len(squares), step),
        "finish",
        [],
        [gain, gate, mixed, *squares],
        sds((tokens * heads, LANES), BF16),
        scratch=[pltpu.VMEM((tokens * heads, LANES), BF16), pltpu.SemaphoreType.DMA((tokens // step,))],
        estimate=cost(0, tokens * heads * LANES * 8, tokens * heads * LANES),
        after=after,
        out_hbm=True,
    )


def attend_kernel(tokens, heads, kv_here, least, is_first, is_last, unroll, place_ref, *refs):
    refs = list(refs)
    take = lambda n: [refs.pop(0) for _ in range(n)]
    per_group = heads // kv_here
    rows = tokens * per_group
    step = CHUNK // per_group
    if is_first:
        doc_ref, query_ref = take(2)
    else:
        wide_ref, state_ref = take(2)
    kv = take(len(least))
    if is_first:
        wide_ref = take(1)[0]
    out_ref = take(1)[0]
    if is_last:
        take(1)[0][...] = jnp.zeros((8, LANES), F32)
    bias = take(1)[0]
    if is_first:
        doc_rep = take(1)[0]
    if is_last:
        done, sems = take(2)
    block = place_ref[0]

    lane = lax.broadcasted_iota(jnp.int32, (tokens, LANES), 1).astype(F32)
    end = 2 * kv_here * tokens
    for j, ref in enumerate(kv):
        valid = (block >= jnp.where(block % 2 == 0, *least[j])).astype(F32)
        docs = doc_columns(ref[end : end + INFO, :].astype(F32) * valid, tokens)
        bias[j] = jnp.where(docs == lane, 0.0, -BIG).astype(BF16)
    if is_first:
        column = doc_columns(doc_ref[...], tokens)
        for h in range(per_group):
            doc_rep[pl.ds(h, tokens, stride=per_group), :] = (column == lane).astype(F32)
    ones = jnp.ones((STATE_ROWS - HEAD_DIM, tokens), BF16)

    def some_chunks(i, carry):
        chains = [(u, g) for u in range(unroll) for g in range(kv_here)]
        chunk = [i * unroll + u for u in range(unroll)]
        at = [pl.ds(pl.multiple_of(c * CHUNK, CHUNK), CHUNK) for c in chunk]
        picked = [pl.ds(pl.multiple_of(c * (step * heads), step * heads), step * heads) for c in chunk]
        scores, results = {}, {}

        def begin(u, g):
            if is_first:
                query = query_ref[picked[u], :].astype(F32).reshape(step, heads, LANES)
                query = query[:, g * per_group : (g + 1) * per_group, :].reshape(CHUNK, LANES)
                wide = jnp.concatenate([query.astype(BF16), doc_rep[at[u], :].astype(BF16)], axis=1)
                wide_ref[g, at[u], :] = wide
            else:
                wide = wide_ref[g, at[u], :]
            out = []
            for j, ref in enumerate(kv):
                keys = jnp.concatenate([ref[g * tokens : (g + 1) * tokens, :], bias[j]], axis=1)
                out.append(
                    lax.dot_general(keys, wide, (((1,), (1,)), ((), ())), preferred_element_type=F32)
                )
            if is_first:
                token = chunk[u] * step + lax.broadcasted_iota(jnp.int32, (tokens, CHUNK), 1) // per_group
                key_at = lax.broadcasted_iota(jnp.int32, (tokens, CHUNK), 0)
                out[0] = jnp.where(key_at <= token, out[0], -BIG)
            scores[u, g] = out

        def end_chain(u, g):
            here = scores.pop((u, g))
            top = jnp.max(here[0], axis=0, keepdims=True)
            for score in here[1:]:
                top = jnp.maximum(top, jnp.max(score, axis=0, keepdims=True))
            total = None
            if not is_first:
                before = state_ref[g, :, at[u]]
                top_before = before[STATE_ROWS - 1 : STATE_ROWS, :]
                top = jnp.maximum(top, top_before)
                total = before * jnp.exp2((top_before - top) * SCORE_TO_EXP2)
            for ref, score in zip(kv, here):
                weights = jnp.exp2((score - top) * SCORE_TO_EXP2).astype(BF16)
                first = (kv_here + g) * tokens
                parts = [ref[first + p : first + p + LANES, :] for p in range(0, tokens, LANES)]
                values = jnp.concatenate([jnp.concatenate(parts, axis=1), ones], axis=0)
                more = jnp.dot(values, weights, preferred_element_type=F32)
                total = more if total is None else total + more
            if is_last:
                results[u, g] = jnp.transpose(total[0:HEAD_DIM] / total[HEAD_DIM : HEAD_DIM + 1])
            else:
                out_ref[g, 0 : STATE_ROWS - 8, at[u]] = total[0 : STATE_ROWS - 8]
                out_ref[g, STATE_ROWS - 8 : STATE_ROWS, at[u]] = jnp.broadcast_to(top, (8, CHUNK))

        ahead = 3
        for n in range(len(chains) + ahead):
            if n < len(chains):
                begin(*chains[n])
            if n >= ahead:
                end_chain(*chains[n - ahead])
        if is_last:
            for u in range(unroll):
                result = [results[u, g] for g in range(kv_here)]
                if kv_here > 1:
                    result = [r.reshape(step, per_group, LANES) for r in result]
                    result = [jnp.concatenate(result, axis=1).reshape(step * heads, LANES)]
                done[picked[u], :] = result[0].astype(BF16)
                pltpu.make_async_copy(
                    done.at[picked[u], :], out_ref.at[picked[u], :], sems.at[chunk[u]]
                ).start()
        return carry

    lax.fori_loop(0, rows // (CHUNK * unroll), some_chunks, 0)
    if is_last:
        for c in range(rows // CHUNK):
            at = pl.ds(c * step * heads, step * heads)
            pltpu.make_async_copy(done.at[at, :], out_ref.at[at, :], sems.at[c]).wait()


def attend(place, first, state, kv, is_last, tokens, heads, kv_here, after, relay=()):
    is_first = state is None
    least = tuple(pair for _, pair in kv)
    kv = [block for block, _ in kv]
    blocks = len(kv)
    rows = tokens * heads // kv_here
    unroll = min(8, rows // CHUNK)
    wide_shape = sds((kv_here, rows, 2 * LANES), BF16)
    state_shape = sds((kv_here, STATE_ROWS, rows), F32)
    out_shape = sds((tokens * heads, LANES), BF16) if is_last else state_shape
    scratch = [pltpu.VMEM((blocks, tokens, LANES), BF16)]
    if is_first:
        out_shape = (wide_shape, out_shape)
        scratch.append(pltpu.VMEM((rows, LANES), F32))
    if is_last:
        out_shape = (out_shape, sds((8, LANES), F32))
        scratch.append(pltpu.VMEM((tokens * heads, LANES), BF16))
        scratch.append(pltpu.SemaphoreType.DMA((rows // CHUNK,)))
    span = blocks * tokens
    return call(
        functools.partial(attend_kernel, tokens, heads, kv_here, least, is_first, is_last, unroll),
        "attend",
        [place],
        [*first, *([] if is_first else [state]), *kv],
        out_shape,
        scratch=scratch,
        mib=24,
        estimate=cost(
            4 * tokens * heads * span * 2 * LANES, 4 * tokens * heads * LANES * 4, tokens * heads * span
        ),
        after=after,
        out_hbm=is_last,
        relay=relay,
    )


def body(
    blocks,
    lin_query,
    lin_key,
    lin_value,
    lin_gate,
    log_decay,
    norm_gain,
    doc_ids,
    soft_query,
    soft_key,
    soft_value,
):
    tokens, heads, _ = lin_query.shape
    tensor = HEADS // heads
    kv_here = max(1, heads // GROUP)
    parts = 2 if heads % 16 == 0 else 1
    longest = blocks * tokens * 5 // 8
    window = min(blocks - 1, (longest - 1 + tokens - 1) // tokens)
    flat = lambda x: x.reshape(-1, LANES)
    block = lax.axis_index("seq")
    place = block.astype(jnp.int32).reshape(1)
    start = (lax.axis_index("tp") * heads // GROUP).astype(jnp.int32).reshape(1)

    def send(x, pairs):
        return lax.ppermute(x, "seq", [(a, b % blocks) for a, b in pairs])

    everyone = range(blocks)
    swap = [(b, b ^ 1) for b in everyone]

    own_kv, docs, cumul, key, value = fetch(
        start,
        [
            doc_ids.reshape(tokens // LANES, LANES),
            jnp.transpose(log_decay),
            flat(soft_key),
            flat(soft_value),
            flat(lin_key),
            flat(lin_value),
        ],
        tokens,
        heads,
        kv_here,
    )

    forward = [(b, b + 2) for b in everyone]
    ahead = send(own_kv, forward)

    size = quarter_rows(heads)
    others = range(1, GROUP_BLOCKS)
    *sent, query = block_state(
        place, flat(soft_query), cumul, docs, key, value, tokens, heads
    )
    quarters = [sent[0]] + [send(sent[j], [(b, b ^ j) for b in everyone]) for j in others]

    state = {}

    def first_attention(after):
        state["wide"], state["sum"] = attend(
            place, (docs, query), None, [(own_kv, (0, 0))], False, tokens, heads, kv_here, after
        )
        return state["sum"]

    def more_attention(kv, is_last, after, relay=()):
        out = attend(
            place, (state["wide"],), state["sum"], kv, is_last, tokens, heads, kv_here, after, relay
        )
        state["sum"] = out[0] if relay else out
        return out

    inner, qh = [], []

    def inner_of(part, after, relay=()):
        n = heads // parts
        got = inner_part(
            cumul, docs, flat(lin_query), key, value, tokens, heads, part * n, n, after, relay
        )
        inner.append(got[0])
        qh.append(got[1])
        return (got[0], *got[2:]) if relay else got[0]

    done, lane = first_attention([sent[0]]), ahead
    if parts > 1:
        done, lane = inner_of(0, [done], [ahead])
    second = send(lane, [(b, b + 2) for b in range(2, blocks - 2)])
    run, lane, own_copy = group_map(place, quarters, size, [done], [lane, own_kv])
    first_cross = send(lane, swap)
    beside = send(own_copy, swap)
    stages = (blocks // GROUP_BLOCKS).bit_length() - 1
    before, done = None, run
    for stage in range(stages):
        came = send(run, [(b, b ^ (GROUP_BLOCKS << stage)) for b in everyone])
        if stage == stages - 1:
            done = more_attention([(lane, (2, 2))], False, [done])
            done = inner_of(parts - 1, [done])
        else:
            run, before = scan_step(place, stage + 2, run, came, before, size, [done])
            done = run
    *priors, prior_doc = prior_states(place, stages + 1, quarters, came, before, size, [done])
    priors = [priors[0]] + [send(priors[j], [(b, b ^ j) for b in everyone]) for j in others]
    done = more_attention([(first_cross, (2, 3)), (second, (4, 4))], False, [prior_doc])
    lane, own_copy = pass_on([second, own_kv], [done, *priors, beside])
    rest = [(send(lane, [(b, b ^ 1 if b >= 4 else b) for b in everyone]), (4, 5))]
    far = None
    if window % 2:
        far = send(own_copy, [(b, b + window) for b in range(1, blocks - window, 2)])
    for back in range(3, window // 2 + 1):
        lane = send(lane, forward)
        rest.append((lane, (2 * back, 2 * back)))
        rest.append((send(lane, swap), (2 * back, 2 * back + 1)))
    mixed, squares = mix(place, docs, prior_doc, cumul, inner, qh, priors, tokens, heads, [done])
    sums = [squares]
    for other in range(1, tensor):
        sums.append(lax.ppermute(squares, "tp", [(t, t ^ other) for t in range(tensor)]))
    done = squares
    while rest:
        done = more_attention(rest[:2], False, [done])
        rest = rest[2:]
    slot = beside if far is None else pick(place, far, beside, [done])
    slot = (slot, (blocks if far is None else window, 1))
    soft_out, done = more_attention([slot], True, [done])
    lin_out = finish(norm_gain, flat(lin_gate), mixed, sums, tokens, heads, [done])
    shape = (tokens, heads, HEAD_DIM)
    return lin_out.reshape(shape), soft_out.reshape(shape)


def solution(mesh):
    in_specs = (
        P("seq", "tp", None),
        P("seq", "tp", None),
        P("seq", "tp", None),
        P("seq", "tp", None),
        P("seq", "tp"),
        P("tp", None),
        P("seq"),
        P("seq", "tp", None),
        P("seq", None, None),
        P("seq", None, None),
    )
    out_specs = (P("seq", "tp", None), P("seq", "tp", None))
    return jax.shard_map(
        functools.partial(body, mesh.shape["seq"]),
        mesh=mesh,
        in_specs=in_specs,
        out_specs=out_specs,
        check_vma=False,
    )
```

```python
import functools

import jax
import jax.numpy as jnp
import numpy as np
from jax import lax
from jax.experimental import pallas as pl
from jax.experimental.pallas import tpu as pltpu
from jax.sharding import PartitionSpec as P

HEADS = 64
HEAD_DIM = 128
KV_HEADS = 8
LANES = 128
GROUP = HEADS // KV_HEADS
F32 = jnp.float32
BF16 = jnp.bfloat16
BIG = float(2**20)
SCORE_TO_EXP2 = HEAD_DIM**-0.5 * float(np.log2(np.e))
INFO = 16
HIGHEST = lax.Precision.HIGHEST

VMEM = pl.BlockSpec(memory_space=pltpu.VMEM)
SMEM = pl.BlockSpec(memory_space=pltpu.SMEM)
HBM = pl.BlockSpec(memory_space=pltpu.HBM)
ANYWHERE = pl.BlockSpec(memory_space=pl.ANY)
STATE_ROWS = HEAD_DIM + 16
CHUNK = 256
GROUP_BLOCKS = 4


def sds(shape, dtype):
    return jax.ShapeDtypeStruct(shape, dtype)


def cost(flops, bytes_accessed, transcendentals=0):
    return pl.CostEstimate(
        flops=int(flops), bytes_accessed=int(bytes_accessed), transcendentals=int(transcendentals)
    )


def call(kernel, name, scalars, operands, out_shape, scratch=(), mib=16, estimate=None, after=(), hbm=0, out_hbm=False, relay=()):
    begin = len(scalars) + len(operands)
    skip = len(after)
    operands = [
        pltpu.with_memory_space_constraint(x, pltpu.HBM) if i < hbm else x for i, x in enumerate(operands)
    ]
    outs = out_shape if isinstance(out_shape, tuple) else (out_shape,)
    out_specs = (VMEM,) * len(outs)
    outs = tuple(
        (pltpu.HBM if out_hbm and i == 0 else pltpu.VMEM)(x.shape, x.dtype) for i, x in enumerate(outs)
    )
    if out_hbm:
        out_specs = (HBM, *out_specs[1:])

    moved = len(relay)
    many = len(outs)
    single = not isinstance(out_shape, tuple) and not relay
    out_specs += (VMEM,) * moved
    outs += tuple(pltpu.VMEM(x.shape, x.dtype) for x in relay)

    def run(*refs):
        rest = refs[begin + skip + moved :]
        for source, target in zip(refs[begin + skip : begin + skip + moved], rest[many : many + moved]):
            target[...] = source[...]
        kernel(*refs[:begin], *rest[:many], *rest[many + moved :])

    out = pl.pallas_call(
        run,
        out_shape=outs,
        in_specs=[SMEM] * len(scalars) + [HBM] * hbm + [VMEM] * (len(operands) - hbm) + [ANYWHERE] * skip + [VMEM] * moved,
        out_specs=out_specs,
        scratch_shapes=list(scratch),
        compiler_params=pltpu.CompilerParams(vmem_limit_bytes=mib * 1024 * 1024),
        cost_estimate=estimate,
        name=name,
    )(*scalars, *operands, *after, *relay)
    return out[0] if single else out


def doc_columns(doc_rows, tokens):
    parts = []
    for i in range(tokens // LANES):
        row = jnp.broadcast_to(doc_rows[i : i + 1, :], (LANES, LANES))
        parts.append(jnp.transpose(row))
    return jnp.concatenate(parts, axis=0)


def doc_line(doc_rows, tokens):
    return jnp.concatenate([doc_rows[i : i + 1, :] for i in range(tokens // LANES)], axis=1)


def lower_triangle(tokens):
    rows = lax.broadcasted_iota(jnp.int32, (tokens, tokens), 0)
    cols = lax.broadcasted_iota(jnp.int32, (tokens, tokens), 1)
    return rows >= cols


def pick_kernel(place_ref, even_ref, odd_ref, out_ref):
    out_ref[...] = jnp.where(place_ref[0] % 2 == 0, even_ref[...], odd_ref[...])


def pick(place, even, odd, after):
    return call(pick_kernel, "pick", [place], [even, odd], sds(even.shape, BF16), after=after)


def pass_on(arrays, after):
    return call(lambda: None, "pass_on", [], [], (), after=after, relay=arrays)


def fetch_kernel(tokens, heads, kv_here, start_ref, *refs):
    refs = list(refs)
    take = lambda n: [refs.pop(0) for _ in range(n)]
    sources = take(6)
    kv_ref, doc_out, cumul_ref, key_out, value_out = take(5)
    held = take(4)
    sems, wide, ldp = refs
    docs_in, decays, soft_key, soft_value = held
    targets = [*held, key_out, value_out]
    copies = [
        pltpu.make_async_copy(source, target, sems.at[i])
        for i, (source, target) in enumerate(zip(sources, targets))
    ]
    for copy in copies:
        copy.start()

    copies[0].wait()
    docs = docs_in[...].astype(F32) + 1.0
    line = lax.broadcasted_iota(jnp.int32, (INFO, LANES), 0)
    info = jnp.zeros((INFO, LANES), F32)
    for i in range(tokens // LANES):
        info = jnp.where(line == i, docs[i : i + 1, :], info)
    doc_out[...] = info
    end = 2 * kv_here * tokens
    kv_ref[end : end + INFO, :] = info.astype(BF16)

    copies[1].wait()
    ldp[...] = jnp.zeros_like(ldp)
    ldp[0:heads, :] = decays[...]
    cumul_ref[...] = lax.dot_general(
        lower_triangle(tokens).astype(F32),
        ldp[...],
        (((1,), (1,)), ((), ())),
        precision=HIGHEST,
        preferred_element_type=F32,
    )

    start = start_ref[0]
    for which, ref in enumerate((soft_key, soft_value)):
        copies[2 + which].wait()
        wide[...] = ref[...].astype(F32)
        for g in range(kv_here):
            rows = wide[pl.ds(start + g, tokens, stride=KV_HEADS), :]
            at = (which * kv_here + g) * tokens
            if which:
                halves = [jnp.transpose(rows[i : i + LANES, :]) for i in range(0, tokens, LANES)]
                rows = jnp.concatenate(halves, axis=0)
            kv_ref[at : at + tokens, :] = rows.astype(BF16)
    for copy in copies[4:]:
        copy.wait()


def fetch(start, operands, tokens, heads, kv_here):
    return call(
        functools.partial(fetch_kernel, tokens, heads, kv_here),
        "fetch",
        [start],
        operands,
        (
            sds((2 * kv_here * tokens + INFO, LANES), BF16),
            sds((INFO, LANES), F32),
            sds((tokens, LANES), F32),
            sds(operands[4].shape, BF16),
            sds(operands[5].shape, BF16),
        ),
        scratch=[pltpu.VMEM(x.shape, x.dtype) for x in operands[:4]]
        + [
            pltpu.SemaphoreType.DMA((len(operands),)),
            pltpu.VMEM((tokens * KV_HEADS, LANES), F32),
            pltpu.VMEM((LANES, tokens), F32),
        ],
        estimate=cost(0, 3 * tokens * heads * LANES * 2),
        hbm=len(operands),
    )


def quarter_rows(heads):
    return heads * HEAD_DIM // GROUP_BLOCKS


def state_kernel(tokens, heads, place_ref, *refs):
    refs = list(refs)
    take = lambda n: [refs.pop(0) for _ in range(n)]
    query_in, cumul_ref, doc_ref, key_ref, value_ref = take(5)
    out_refs, query_out = take(GROUP_BLOCKS), take(1)[0]
    kf, vf, states, sem = refs
    copy = pltpu.make_async_copy(query_in, query_out, sem)
    copy.start()
    cumul, docs = cumul_ref[...], doc_ref[...]
    total = cumul[tokens - 1 : tokens, :]
    last_row = tokens // LANES - 1
    first_doc = docs[0:1, 0:1]
    last_doc = docs[last_row : last_row + 1, LANES - 1 : LANES]
    tail = (doc_columns(docs, tokens) == last_doc).astype(F32)
    scale = jnp.exp(total - cumul) * tail
    kf[...] = key_ref[...].astype(F32)
    vf[...] = value_ref[...].astype(F32)
    for h in range(heads):
        keys = (kf[pl.ds(h, tokens, stride=heads), :] * scale[:, h : h + 1]).astype(BF16)
        values = vf[pl.ds(h, tokens, stride=heads), :].astype(BF16)
        states[h * HEAD_DIM : (h + 1) * HEAD_DIM, :] = lax.dot_general(
            keys, values, (((0,), (0,)), ((), ())), preferred_element_type=F32
        )
    size = quarter_rows(heads)
    mine = place_ref[0] % GROUP_BLOCKS
    for j, ref in enumerate(out_refs):
        taker = mine ^ j
        ref[0:size, :] = states[pl.ds(pl.multiple_of(taker * size, size), size), :].astype(BF16)
        totals = jnp.zeros_like(total)
        for c in range(GROUP_BLOCKS):
            skip = c * heads // GROUP_BLOCKS
            moved = pltpu.roll(total, LANES - skip, 1) if skip else total
            totals = jnp.where(taker == c, moved, totals)
        ref[size : size + INFO, :] = info_rows((*in_parts(totals), first_doc, last_doc))
    copy.wait()


def block_state(place, soft_query, cumul, docs, key, value, tokens, heads):
    return call(
        functools.partial(state_kernel, tokens, heads),
        "block_state",
        [place],
        [soft_query, cumul, docs, key, value],
        (
            *[sds((quarter_rows(heads) + INFO, LANES), BF16)] * GROUP_BLOCKS,
            sds(soft_query.shape, BF16),
        ),
        scratch=[
            pltpu.VMEM((tokens * heads, LANES), F32),
            pltpu.VMEM((tokens * heads, LANES), F32),
            pltpu.VMEM((heads * HEAD_DIM, LANES), F32),
            pltpu.SemaphoreType.DMA,
        ],
        estimate=cost(2 * heads * tokens * HEAD_DIM**2, 5 * tokens * heads * LANES * 2),
        hbm=1,
    )


def in_parts(x):
    hi = x.astype(BF16).astype(F32)
    mid = (x - hi).astype(BF16).astype(F32)
    return hi, mid, x - hi - mid


def info_rows(parts):
    line = lax.broadcasted_iota(jnp.int32, (INFO, LANES), 0)
    info = jnp.zeros((INFO, LANES), F32)
    for i, part in enumerate(parts):
        info = jnp.where(line == i, part, info)
    return info.astype(BF16)


def read_map(ref, size):
    info = ref[size : size + INFO, :].astype(F32)
    return info[0:1] + info[1:2] + info[2:3], info[3:4], info[4:5]


def row_chunks(size):
    unit = min(HEAD_DIM, size)
    return [(slice(i * unit, (i + 1) * unit), slice(i, i + 1)) for i in range(size // unit)]


def in_block_order(place_ref, refs, blocks):
    mine = place_ref[0] % GROUP_BLOCKS
    for j, ref in enumerate(refs):
        blocks[mine ^ j] = ref[...]


def block_maps(blocks, size):
    maps = []
    for c in range(GROUP_BLOCKS):
        info = blocks[c, size : size + INFO, :].astype(F32)
        first, last = info[3:4], info[4:5]
        gain = jnp.exp(info[0:1] + info[1:2] + info[2:3]) * (first == last).astype(F32)
        maps.append((gain, first, last))
    return maps


def group_kernel(size, place_ref, *refs):
    sources = refs[:GROUP_BLOCKS]
    out_ref, blocks = refs[GROUP_BLOCKS:]
    in_block_order(place_ref, sources, blocks)
    maps = block_maps(blocks, size)
    gains = [None]
    for (gain, first, _), (_, _, last_before) in zip(maps[1:], maps[:-1]):
        gains.append(gain * (last_before == first).astype(F32))
    for rows, lane in row_chunks(size):
        total = blocks[0, rows, :].astype(F32)
        for c in range(1, GROUP_BLOCKS):
            total = gains[c][:, lane] * total + blocks[c, rows, :].astype(F32)
        out_ref[rows, :] = total.astype(BF16)
    gain = maps[0][0] * gains[1] * gains[2] * gains[3]
    out_ref[size : size + INFO, :] = info_rows((*in_parts(gain), maps[0][1], maps[-1][2]))


def group_map(place, quarters, size, after, relay):
    return call(
        functools.partial(group_kernel, size),
        "group_map",
        [place],
        quarters,
        (sds((size + INFO, LANES), BF16),),
        scratch=[pltpu.VMEM((GROUP_BLOCKS, size + INFO, LANES), BF16)],
        estimate=cost(8 * size * LANES, 10 * size * LANES * 2),
        after=after,
        relay=relay,
    )


def scan_kernel(size, has_before, bit, place_ref, *refs):
    mine_ref, came_ref = refs[:2]
    before_ref = refs[2] if has_before else None
    run_ref, out_ref = refs[-2:]
    upper = (place_ref[0] >> bit) & 1 == 1
    gain_m, first_m, last_m = read_map(mine_ref, size)
    gain_c, first_c, last_c = read_map(came_ref, size)
    link = jnp.where(upper, (last_c == first_m).astype(F32), (last_m == first_c).astype(F32))
    gain = jnp.where(upper, gain_m, gain_c) * link
    for rows, lane in row_chunks(size):
        mine, came = mine_ref[rows, :].astype(F32), came_ref[rows, :].astype(F32)
        lower_sum, upper_sum = jnp.where(upper, came, mine), jnp.where(upper, mine, came)
        run_ref[rows, :] = (gain[:, lane] * lower_sum + upper_sum).astype(BF16)
    run_ref[size : size + INFO, :] = info_rows(
        (
            *in_parts(gain * jnp.where(upper, gain_c, gain_m)),
            jnp.where(upper, first_c, first_m),
            jnp.where(upper, last_m, last_c),
        )
    )
    if not has_before:
        out_ref[...] = jnp.where(upper, came_ref[...], jnp.zeros_like(came_ref))
        return
    gain_b, first_b, last_b = read_map(before_ref, size)
    empty = first_b == 0.0
    factor = jnp.where(empty, 1.0, gain_b * (last_c == first_b).astype(F32))
    for rows, lane in row_chunks(size):
        before = before_ref[rows, :].astype(F32)
        joined = factor[:, lane] * came_ref[rows, :].astype(F32) + before
        out_ref[rows, :] = jnp.where(upper, joined, before).astype(BF16)
    out_ref[size : size + INFO, :] = info_rows(
        (
            *in_parts(jnp.where(upper, factor * gain_c, gain_b)),
            jnp.where(upper, first_c, first_b),
            jnp.where(upper, jnp.where(empty, last_c, last_b), last_b),
        )
    )


def scan_step(place, bit, mine, came, before, size, after):
    shape = sds((size + INFO, LANES), BF16)
    before = [] if before is None else [before]
    return call(
        functools.partial(scan_kernel, size, len(before), bit),
        "scan_step",
        [place],
        [mine, came, *before],
        (shape, shape),
        estimate=cost(6 * size * LANES, 6 * size * LANES * 2),
        after=after,
    )


def prior_kernel(size, has_before, bit, place_ref, *refs):
    sources, came_ref = refs[:GROUP_BLOCKS], refs[GROUP_BLOCKS]
    before_ref = refs[GROUP_BLOCKS + 1] if has_before else None
    *out_refs, doc_ref, blocks, priors = refs[GROUP_BLOCKS + 1 + has_before :]
    mine = place_ref[0] % GROUP_BLOCKS
    in_block_order(place_ref, sources, blocks)
    maps = block_maps(blocks, size)
    upper = ((place_ref[0] >> bit) & 1).astype(F32)
    _, _, last_c = read_map(came_ref, size)
    factor, doc = jnp.broadcast_to(upper, (1, LANES)), upper * last_c
    if has_before:
        gain_b, first_b, last_b = read_map(before_ref, size)
        empty = first_b == 0.0
        factor = upper * jnp.where(empty, 1.0, gain_b * (last_c == first_b).astype(F32))
        doc = jnp.where(empty, doc, last_b)
    docs = [doc] + [last for _, _, last in maps[:-1]]
    gains = [gain * (doc == first).astype(F32) for (gain, first, _), doc in zip(maps, docs)]
    for rows, lane in row_chunks(size):
        state = factor[:, lane] * came_ref[rows, :].astype(F32)
        if has_before:
            state = state + before_ref[rows, :].astype(F32)
        for c in range(GROUP_BLOCKS):
            priors[c, rows, :] = state.astype(BF16)
            if c < GROUP_BLOCKS - 1:
                state = gains[c][:, lane] * state + blocks[c, rows, :].astype(F32)
    for j, ref in enumerate(out_refs):
        ref[...] = priors[mine ^ j]
    own_doc = docs[0]
    for c in range(1, GROUP_BLOCKS):
        own_doc = jnp.where(mine == c, docs[c], own_doc)
    doc_ref[...] = jnp.broadcast_to(own_doc, (8, LANES))


def prior_states(place, bit, quarters, came, before, size, after, relay=()):
    before = [] if before is None else [before]
    return call(
        functools.partial(prior_kernel, size, len(before), bit),
        "prior_states",
        [place],
        [*quarters, came, *before],
        (*[sds((size, LANES), BF16)] * GROUP_BLOCKS, sds((8, LANES), F32)),
        scratch=[
            pltpu.VMEM((GROUP_BLOCKS, size + INFO, LANES), BF16),
            pltpu.VMEM((GROUP_BLOCKS, size, LANES), BF16),
        ],
        estimate=cost(8 * size * LANES, 10 * size * LANES * 2),
        after=after,
        relay=relay,
    )


def some_heads(ref, tokens, heads, first, count):
    x = ref[...].astype(F32)
    if count == heads:
        return x
    return x.reshape(tokens, heads, LANES)[:, first : first + count, :].reshape(tokens * count, LANES)


def inner_kernel(tokens, heads, first, count, cumul_ref, doc_ref, query_ref, key_ref, value_ref, inner_ref, qh_ref, qf, kf, vf, mask):
    cumul = cumul_ref[...]
    cumul_t = jnp.transpose(cumul)
    docs = doc_ref[...]
    column = doc_columns(docs, tokens)
    same = jnp.concatenate([column] * (tokens // LANES), axis=1) == doc_line(docs, tokens)
    mask[...] = jnp.where(lower_triangle(tokens) & same, 0.0, -1e9)
    qf[...] = some_heads(query_ref, tokens, heads, first, count)
    kf[...] = some_heads(key_ref, tokens, heads, first, count)
    vf[...] = some_heads(value_ref, tokens, heads, first, count)
    for n in range(count):
        h = first + n
        picked = pl.ds(n, tokens, stride=count)
        query = qf[picked, :].astype(BF16)
        keys = kf[picked, :].astype(BF16)
        values = vf[picked, :].astype(BF16)
        qh_ref[n * tokens : (n + 1) * tokens, :] = query
        for i in range(tokens // LANES):
            seen = (i + 1) * LANES
            rows = slice(i * LANES, seen)
            scores = lax.dot_general(
                query[rows, :], keys[0:seen, :], (((1,), (1,)), ((), ())), preferred_element_type=F32
            )
            gap = cumul[rows, h : h + 1] - cumul_t[h : h + 1, 0:seen]
            weights = (scores * jnp.exp(gap + mask[rows, 0:seen])).astype(BF16)
            inner_ref[n * tokens + i * LANES : n * tokens + seen, :] = jnp.dot(
                weights, values[0:seen, :], preferred_element_type=F32
            )


def inner_part(cumul, docs, query, key, value, tokens, heads, first, count, after, relay):
    return call(
        functools.partial(inner_kernel, tokens, heads, first, count),
        "inner_part",
        [],
        [cumul, docs, query, key, value],
        (sds((count * tokens, LANES), F32), sds((count * tokens, LANES), BF16)),
        scratch=[pltpu.VMEM((tokens * count, LANES), F32)] * 3 + [pltpu.VMEM((tokens, tokens), F32)],
        mib=24,
        estimate=cost(
            4 * count * tokens * tokens * HEAD_DIM, tokens * heads * LANES * 12, count * tokens * tokens
        ),
        after=after,
        relay=relay,
    )


def mix_kernel(tokens, heads, parts, place_ref, doc_ref, prior_doc_ref, cumul_ref, *refs):
    refs = list(refs)
    take = lambda n: [refs.pop(0) for _ in range(n)]
    inner, qh, quarters = take(parts), take(parts), take(GROUP_BLOCKS)
    mixed_ref, square_ref, states = refs
    size = quarter_rows(heads)
    mine = place_ref[0] % GROUP_BLOCKS
    for j, ref in enumerate(quarters):
        states[pl.ds(pl.multiple_of((mine ^ j) * size, size), size), :] = ref[...]
    is_open = (doc_columns(doc_ref[...], tokens) == prior_doc_ref[0:1, :]).astype(F32)
    gain = jnp.exp(cumul_ref[...]) * is_open
    squares = jnp.zeros((tokens, LANES), F32)
    for h in range(heads):
        part, n = divmod(h, heads // parts)
        held = slice(n * tokens, (n + 1) * tokens)
        state = states[h * HEAD_DIM : (h + 1) * HEAD_DIM, :]
        carried = jnp.dot(qh[part][held, :], state, preferred_element_type=F32)
        mixed = inner[part][held, :] + carried * gain[:, h : h + 1]
        squares = squares + mixed * mixed
        mixed_ref[pl.ds(h, tokens, stride=heads), :] = mixed
    square_ref[...] = lax.dot_general(
        jnp.ones((8, LANES), F32),
        squares,
        (((1,), (1,)), ((), ())),
        precision=HIGHEST,
        preferred_element_type=F32,
    )


def mix(place, docs, prior_doc, cumul, inner, qh, quarters, tokens, heads, after):
    return call(
        functools.partial(mix_kernel, tokens, heads, len(inner)),
        "mix",
        [place],
        [docs, prior_doc, cumul, *inner, *qh, *quarters],
        (sds((tokens * heads, LANES), F32), sds((8, tokens), F32)),
        scratch=[pltpu.VMEM((heads * HEAD_DIM, LANES), BF16)],
        mib=24,
        estimate=cost(2 * heads * tokens * HEAD_DIM**2, tokens * heads * LANES * 10),
        after=after,
    )


def finish_kernel(tokens, heads, sums, step, gain_ref, gate_ref, mixed_ref, *refs):
    squares, (out_ref, done, sems) = refs[:sums], refs[sums:]
    total = squares[0][0:1, :]
    for ref in squares[1:]:
        total = total + ref[0:1, :]
    scale = lax.rsqrt(total / (HEADS * HEAD_DIM) + 1e-06)
    rows = jnp.concatenate([scale[:, i * LANES : (i + 1) * LANES] for i in range(tokens // LANES)], axis=0)
    column = doc_columns(rows, tokens)
    copies = []
    for i in range(0, tokens, step):
        at = pl.ds(i * heads, step * heads)
        gate = jax.nn.sigmoid(gate_ref[at, :].astype(F32)).reshape(step, heads, LANES)
        mixed = mixed_ref[at, :].reshape(step, heads, LANES)
        inv = column[i : i + step, :][:, None, :]
        out = mixed * inv * gain_ref[...][None] * gate
        done[at, :] = out.reshape(step * heads, LANES).astype(BF16)
        copies.append(pltpu.make_async_copy(done.at[at, :], out_ref.at[at, :], sems.at[i // step]))
        copies[-1].start()
    for copy in copies:
        copy.wait()


def finish(gain, gate, mixed, squares, tokens, heads, after):
    step = 64
    return call(
        functools.partial(finish_kernel, tokens, heads, len(squares), step),
        "finish",
        [],
        [gain, gate, mixed, *squares],
        sds((tokens * heads, LANES), BF16),
        scratch=[pltpu.VMEM((tokens * heads, LANES), BF16), pltpu.SemaphoreType.DMA((tokens // step,))],
        estimate=cost(0, tokens * heads * LANES * 8, tokens * heads * LANES),
        after=after,
        out_hbm=True,
    )


def attend_kernel(tokens, heads, kv_here, least, is_first, is_last, unroll, place_ref, *refs):
    refs = list(refs)
    take = lambda n: [refs.pop(0) for _ in range(n)]
    per_group = heads // kv_here
    rows = tokens * per_group
    step = CHUNK // per_group
    if is_first:
        doc_ref, query_ref = take(2)
    else:
        wide_ref, state_ref = take(2)
    kv = take(len(least))
    if is_first:
        wide_ref = take(1)[0]
    out_ref = take(1)[0]
    if is_last:
        take(1)[0][...] = jnp.zeros((8, LANES), F32)
    bias = take(1)[0]
    if is_first:
        doc_rep = take(1)[0]
    if is_last:
        done, sems = take(2)
    block = place_ref[0]

    lane = lax.broadcasted_iota(jnp.int32, (tokens, LANES), 1).astype(F32)
    end = 2 * kv_here * tokens
    for j, ref in enumerate(kv):
        valid = (block >= jnp.where(block % 2 == 0, *least[j])).astype(F32)
        docs = doc_columns(ref[end : end + INFO, :].astype(F32) * valid, tokens)
        bias[j] = jnp.where(docs == lane, 0.0, -BIG).astype(BF16)
    if is_first:
        column = doc_columns(doc_ref[...], tokens)
        for h in range(per_group):
            doc_rep[pl.ds(h, tokens, stride=per_group), :] = (column == lane).astype(F32)
    ones = jnp.ones((STATE_ROWS - HEAD_DIM, tokens), BF16)

    def some_chunks(i, carry):
        chains = [(u, g) for u in range(unroll) for g in range(kv_here)]
        chunk = [i * unroll + u for u in range(unroll)]
        at = [pl.ds(pl.multiple_of(c * CHUNK, CHUNK), CHUNK) for c in chunk]
        picked = [pl.ds(pl.multiple_of(c * (step * heads), step * heads), step * heads) for c in chunk]
        scores, results = {}, {}

        def begin(u, g):
            if is_first:
                query = query_ref[picked[u], :].astype(F32).reshape(step, heads, LANES)
                query = query[:, g * per_group : (g + 1) * per_group, :].reshape(CHUNK, LANES)
                wide = jnp.concatenate([query.astype(BF16), doc_rep[at[u], :].astype(BF16)], axis=1)
                wide_ref[g, at[u], :] = wide
            else:
                wide = wide_ref[g, at[u], :]
            out = []
            for j, ref in enumerate(kv):
                keys = jnp.concatenate([ref[g * tokens : (g + 1) * tokens, :], bias[j]], axis=1)
                out.append(
                    lax.dot_general(keys, wide, (((1,), (1,)), ((), ())), preferred_element_type=F32)
                )
            if is_first:
                token = chunk[u] * step + lax.broadcasted_iota(jnp.int32, (tokens, CHUNK), 1) // per_group
                key_at = lax.broadcasted_iota(jnp.int32, (tokens, CHUNK), 0)
                out[0] = jnp.where(key_at <= token, out[0], -BIG)
            scores[u, g] = out

        def end_chain(u, g):
            here = scores.pop((u, g))
            top = jnp.max(here[0], axis=0, keepdims=True)
            for score in here[1:]:
                top = jnp.maximum(top, jnp.max(score, axis=0, keepdims=True))
            total = None
            if not is_first:
                before = state_ref[g, :, at[u]]
                top_before = before[STATE_ROWS - 1 : STATE_ROWS, :]
                top = jnp.maximum(top, top_before)
                total = before * jnp.exp2((top_before - top) * SCORE_TO_EXP2)
            for ref, score in zip(kv, here):
                weights = jnp.exp2((score - top) * SCORE_TO_EXP2).astype(BF16)
                first = (kv_here + g) * tokens
                parts = [ref[first + p : first + p + LANES, :] for p in range(0, tokens, LANES)]
                values = jnp.concatenate([jnp.concatenate(parts, axis=1), ones], axis=0)
                more = jnp.dot(values, weights, preferred_element_type=F32)
                total = more if total is None else total + more
            if is_last:
                results[u, g] = jnp.transpose(total[0:HEAD_DIM] / total[HEAD_DIM : HEAD_DIM + 1])
            else:
                out_ref[g, 0 : STATE_ROWS - 8, at[u]] = total[0 : STATE_ROWS - 8]
                out_ref[g, STATE_ROWS - 8 : STATE_ROWS, at[u]] = jnp.broadcast_to(top, (8, CHUNK))

        ahead = 3
        for n in range(len(chains) + ahead):
            if n < len(chains):
                begin(*chains[n])
            if n >= ahead:
                end_chain(*chains[n - ahead])
        if is_last:
            for u in range(unroll):
                result = [results[u, g] for g in range(kv_here)]
                if kv_here > 1:
                    result = [r.reshape(step, per_group, LANES) for r in result]
                    result = [jnp.concatenate(result, axis=1).reshape(step * heads, LANES)]
                done[picked[u], :] = result[0].astype(BF16)
                pltpu.make_async_copy(
                    done.at[picked[u], :], out_ref.at[picked[u], :], sems.at[chunk[u]]
                ).start()
        return carry

    lax.fori_loop(0, rows // (CHUNK * unroll), some_chunks, 0)
    if is_last:
        for c in range(rows // CHUNK):
            at = pl.ds(c * step * heads, step * heads)
            pltpu.make_async_copy(done.at[at, :], out_ref.at[at, :], sems.at[c]).wait()


def attend(place, first, state, kv, is_last, tokens, heads, kv_here, after, relay=()):
    is_first = state is None
    least = tuple(pair for _, pair in kv)
    kv = [block for block, _ in kv]
    blocks = len(kv)
    rows = tokens * heads // kv_here
    unroll = min(8, rows // CHUNK)
    wide_shape = sds((kv_here, rows, 2 * LANES), BF16)
    state_shape = sds((kv_here, STATE_ROWS, rows), F32)
    out_shape = sds((tokens * heads, LANES), BF16) if is_last else state_shape
    scratch = [pltpu.VMEM((blocks, tokens, LANES), BF16)]
    if is_first:
        out_shape = (wide_shape, out_shape)
        scratch.append(pltpu.VMEM((rows, LANES), F32))
    if is_last:
        out_shape = (out_shape, sds((8, LANES), F32))
        scratch.append(pltpu.VMEM((tokens * heads, LANES), BF16))
        scratch.append(pltpu.SemaphoreType.DMA((rows // CHUNK,)))
    span = blocks * tokens
    return call(
        functools.partial(attend_kernel, tokens, heads, kv_here, least, is_first, is_last, unroll),
        "attend",
        [place],
        [*first, *([] if is_first else [state]), *kv],
        out_shape,
        scratch=scratch,
        mib=24,
        estimate=cost(
            4 * tokens * heads * span * 2 * LANES, 4 * tokens * heads * LANES * 4, tokens * heads * span
        ),
        after=after,
        out_hbm=is_last,
        relay=relay,
    )


def body(
    blocks,
    lin_query,
    lin_key,
    lin_value,
    lin_gate,
    log_decay,
    norm_gain,
    doc_ids,
    soft_query,
    soft_key,
    soft_value,
):
    tokens, heads, _ = lin_query.shape
    tensor = HEADS // heads
    kv_here = max(1, heads // GROUP)
    parts = 2 if heads % 16 == 0 else 1
    longest = blocks * tokens * 5 // 8
    window = min(blocks - 1, (longest - 1 + tokens - 1) // tokens)
    flat = lambda x: x.reshape(-1, LANES)
    block = lax.axis_index("seq")
    place = block.astype(jnp.int32).reshape(1)
    start = (lax.axis_index("tp") * heads // GROUP).astype(jnp.int32).reshape(1)

    def send(x, pairs):
        return lax.ppermute(x, "seq", [(a, b % blocks) for a, b in pairs])

    everyone = range(blocks)
    swap = [(b, b ^ 1) for b in everyone]

    own_kv, docs, cumul, key, value = fetch(
        start,
        [
            doc_ids.reshape(tokens // LANES, LANES),
            jnp.transpose(log_decay),
            flat(soft_key),
            flat(soft_value),
            flat(lin_key),
            flat(lin_value),
        ],
        tokens,
        heads,
        kv_here,
    )

    forward = [(b, b + 2) for b in everyone]
    ahead = send(own_kv, forward)

    size = quarter_rows(heads)
    others = range(1, GROUP_BLOCKS)
    *sent, query = block_state(
        place, flat(soft_query), cumul, docs, key, value, tokens, heads
    )
    quarters = [sent[0]] + [send(sent[j], [(b, b ^ j) for b in everyone]) for j in others]

    state = {}

    def first_attention(after):
        state["wide"], state["sum"] = attend(
            place, (docs, query), None, [(own_kv, (0, 0))], False, tokens, heads, kv_here, after
        )
        return state["sum"]

    def more_attention(kv, is_last, after, relay=()):
        out = attend(
            place, (state["wide"],), state["sum"], kv, is_last, tokens, heads, kv_here, after, relay
        )
        state["sum"] = out[0] if relay else out
        return out

    inner, qh = [], []

    def inner_of(part, after, relay=()):
        n = heads // parts
        got = inner_part(
            cumul, docs, flat(lin_query), key, value, tokens, heads, part * n, n, after, relay
        )
        inner.append(got[0])
        qh.append(got[1])
        return (got[0], *got[2:]) if relay else got[0]

    done, lane = first_attention([sent[0]]), ahead
    if parts > 1:
        done, lane = inner_of(0, [done], [ahead])
    second = send(lane, [(b, b + 2) for b in range(2, blocks - 2)])
    run, lane = group_map(place, quarters, size, [done], [lane])
    first_cross = send(lane, swap)
    stages = (blocks // GROUP_BLOCKS).bit_length() - 1
    before, done = None, run
    for stage in range(stages):
        came = send(run, [(b, b ^ (GROUP_BLOCKS << stage)) for b in everyone])
        if stage == stages - 1:
            done = more_attention([(lane, (2, 2))], False, [done])
            done = inner_of(parts - 1, [done])
        else:
            run, before = scan_step(place, stage + 2, run, came, before, size, [done])
            done = run
    assert window % 2 == 0 or window == 5
    payload = pick(place, own_kv, second, [done])
    slot = (send(payload, [(b, b + 1) for b in everyone]), (window if window % 2 else blocks, 1))
    *priors, prior_doc = prior_states(place, stages + 1, quarters, came, before, size, [done])
    priors = [priors[0]] + [send(priors[j], [(b, b ^ j) for b in everyone]) for j in others]
    done = more_attention([(first_cross, (2, 3)), (second, (4, 4))], False, [prior_doc])
    (lane,) = pass_on([second], [done, *priors])
    rest = [(send(lane, swap), (4, 5))]
    for back in range(3, window // 2 + 1):
        lane = send(lane, forward)
        rest.append((lane, (2 * back, 2 * back)))
        rest.append((send(lane, swap), (2 * back, 2 * back + 1)))
    mixed, squares = mix(place, docs, prior_doc, cumul, inner, qh, priors, tokens, heads, [done])
    sums = [squares]
    for other in range(1, tensor):
        sums.append(lax.ppermute(squares, "tp", [(t, t ^ other) for t in range(tensor)]))
    rest.insert(0, slot)
    done = squares
    while rest:
        got = more_attention(rest[:1], len(rest) == 1, [done])
        rest, done = rest[1:], got
    soft_out, done = got
    lin_out = finish(norm_gain, flat(lin_gate), mixed, sums, tokens, heads, [done])
    shape = (tokens, heads, HEAD_DIM)
    return lin_out.reshape(shape), soft_out.reshape(shape)


def solution(mesh):
    in_specs = (
        P("seq", "tp", None),
        P("seq", "tp", None),
        P("seq", "tp", None),
        P("seq", "tp", None),
        P("seq", "tp"),
        P("tp", None),
        P("seq"),
        P("seq", "tp", None),
        P("seq", None, None),
        P("seq", None, None),
    )
    out_specs = (P("seq", "tp", None), P("seq", "tp", None))
    return jax.shard_map(
        functools.partial(body, mesh.shape["seq"]),
        mesh=mesh,
        in_specs=in_specs,
        out_specs=out_specs,
        check_vma=False,
    )
```

```python
import functools

import jax
import jax.numpy as jnp
import numpy as np
from jax import lax
from jax.experimental import pallas as pl
from jax.experimental.pallas import tpu as pltpu
from jax.sharding import PartitionSpec as P

HEADS = 64
HEAD_DIM = 128
KV_HEADS = 8
LANES = 128
GROUP = HEADS // KV_HEADS
F32 = jnp.float32
BF16 = jnp.bfloat16
BIG = float(2**20)
SCORE_TO_EXP2 = HEAD_DIM**-0.5 * float(np.log2(np.e))
INFO = 16
HIGHEST = lax.Precision.HIGHEST

VMEM = pl.BlockSpec(memory_space=pltpu.VMEM)
SMEM = pl.BlockSpec(memory_space=pltpu.SMEM)
HBM = pl.BlockSpec(memory_space=pltpu.HBM)
ANYWHERE = pl.BlockSpec(memory_space=pl.ANY)
STATE_ROWS = HEAD_DIM + 16
CHUNK = 256
GROUP_BLOCKS = 4


def sds(shape, dtype):
    return jax.ShapeDtypeStruct(shape, dtype)


def cost(flops, bytes_accessed, transcendentals=0):
    return pl.CostEstimate(
        flops=int(flops), bytes_accessed=int(bytes_accessed), transcendentals=int(transcendentals)
    )


def call(kernel, name, scalars, operands, out_shape, scratch=(), mib=16, estimate=None, after=(), hbm=0, out_hbm=False, relay=()):
    begin = len(scalars) + len(operands)
    skip = len(after)
    operands = [
        pltpu.with_memory_space_constraint(x, pltpu.HBM) if i < hbm else x for i, x in enumerate(operands)
    ]
    outs = out_shape if isinstance(out_shape, tuple) else (out_shape,)
    out_specs = (VMEM,) * len(outs)
    outs = tuple(
        (pltpu.HBM if out_hbm and i == 0 else pltpu.VMEM)(x.shape, x.dtype) for i, x in enumerate(outs)
    )
    if out_hbm:
        out_specs = (HBM, *out_specs[1:])

    moved = len(relay)
    many = len(outs)
    single = not isinstance(out_shape, tuple) and not relay
    out_specs += (VMEM,) * moved
    outs += tuple(pltpu.VMEM(x.shape, x.dtype) for x in relay)

    def run(*refs):
        rest = refs[begin + skip + moved :]
        for source, target in zip(refs[begin + skip : begin + skip + moved], rest[many : many + moved]):
            target[...] = source[...]
        kernel(*refs[:begin], *rest[:many], *rest[many + moved :])

    out = pl.pallas_call(
        run,
        out_shape=outs,
        in_specs=[SMEM] * len(scalars) + [HBM] * hbm + [VMEM] * (len(operands) - hbm) + [ANYWHERE] * skip + [VMEM] * moved,
        out_specs=out_specs,
        scratch_shapes=list(scratch),
        compiler_params=pltpu.CompilerParams(vmem_limit_bytes=mib * 1024 * 1024),
        cost_estimate=estimate,
        name=name,
    )(*scalars, *operands, *after, *relay)
    return out[0] if single else out


def doc_columns(doc_rows, tokens):
    parts = []
    for i in range(tokens // LANES):
        row = jnp.broadcast_to(doc_rows[i : i + 1, :], (LANES, LANES))
        parts.append(jnp.transpose(row))
    return jnp.concatenate(parts, axis=0)


def doc_line(doc_rows, tokens):
    return jnp.concatenate([doc_rows[i : i + 1, :] for i in range(tokens // LANES)], axis=1)


def lower_triangle(tokens):
    rows = lax.broadcasted_iota(jnp.int32, (tokens, tokens), 0)
    cols = lax.broadcasted_iota(jnp.int32, (tokens, tokens), 1)
    return rows >= cols


def pick_kernel(place_ref, even_ref, odd_ref, out_ref):
    out_ref[...] = jnp.where(place_ref[0] % 2 == 0, even_ref[...], odd_ref[...])


def pick(place, even, odd, after):
    return call(pick_kernel, "pick", [place], [even, odd], sds(even.shape, BF16), after=after)


def pass_on(arrays, after):
    return call(lambda: None, "pass_on", [], [], (), after=after, relay=arrays)


def fetch_kernel(tokens, heads, kv_here, start_ref, *refs):
    refs = list(refs)
    take = lambda n: [refs.pop(0) for _ in range(n)]
    sources = take(6)
    kv_ref, doc_out, cumul_ref, key_out, value_out = take(5)
    held = take(4)
    sems, wide, ldp = refs
    docs_in, decays, soft_key, soft_value = held
    targets = [*held, key_out, value_out]
    copies = [
        pltpu.make_async_copy(source, target, sems.at[i])
        for i, (source, target) in enumerate(zip(sources, targets))
    ]
    for copy in copies:
        copy.start()

    copies[0].wait()
    docs = docs_in[...].astype(F32) + 1.0
    line = lax.broadcasted_iota(jnp.int32, (INFO, LANES), 0)
    info = jnp.zeros((INFO, LANES), F32)
    for i in range(tokens // LANES):
        info = jnp.where(line == i, docs[i : i + 1, :], info)
    doc_out[...] = info
    end = 2 * kv_here * tokens
    kv_ref[end : end + INFO, :] = info.astype(BF16)

    copies[1].wait()
    ldp[...] = jnp.zeros_like(ldp)
    ldp[0:heads, :] = decays[...]
    cumul_ref[...] = lax.dot_general(
        lower_triangle(tokens).astype(F32),
        ldp[...],
        (((1,), (1,)), ((), ())),
        precision=HIGHEST,
        preferred_element_type=F32,
    )

    start = start_ref[0]
    for which, ref in enumerate((soft_key, soft_value)):
        copies[2 + which].wait()
        wide[...] = ref[...].astype(F32)
        for g in range(kv_here):
            rows = wide[pl.ds(start + g, tokens, stride=KV_HEADS), :]
            at = (which * kv_here + g) * tokens
            if which:
                halves = [jnp.transpose(rows[i : i + LANES, :]) for i in range(0, tokens, LANES)]
                rows = jnp.concatenate(halves, axis=0)
            kv_ref[at : at + tokens, :] = rows.astype(BF16)
    for copy in copies[4:]:
        copy.wait()


def fetch(start, operands, tokens, heads, kv_here):
    return call(
        functools.partial(fetch_kernel, tokens, heads, kv_here),
        "fetch",
        [start],
        operands,
        (
            sds((2 * kv_here * tokens + INFO, LANES), BF16),
            sds((INFO, LANES), F32),
            sds((tokens, LANES), F32),
            sds(operands[4].shape, BF16),
            sds(operands[5].shape, BF16),
        ),
        scratch=[pltpu.VMEM(x.shape, x.dtype) for x in operands[:4]]
        + [
            pltpu.SemaphoreType.DMA((len(operands),)),
            pltpu.VMEM((tokens * KV_HEADS, LANES), F32),
            pltpu.VMEM((LANES, tokens), F32),
        ],
        estimate=cost(0, 3 * tokens * heads * LANES * 2),
        hbm=len(operands),
    )


def quarter_rows(heads):
    return heads * HEAD_DIM // GROUP_BLOCKS


def state_kernel(tokens, heads, place_ref, *refs):
    refs = list(refs)
    take = lambda n: [refs.pop(0) for _ in range(n)]
    query_in, cumul_ref, doc_ref, key_ref, value_ref = take(5)
    out_refs, query_out = take(GROUP_BLOCKS), take(1)[0]
    kf, vf, states, sem = refs
    copy = pltpu.make_async_copy(query_in, query_out, sem)
    copy.start()
    cumul, docs = cumul_ref[...], doc_ref[...]
    total = cumul[tokens - 1 : tokens, :]
    last_row = tokens // LANES - 1
    first_doc = docs[0:1, 0:1]
    last_doc = docs[last_row : last_row + 1, LANES - 1 : LANES]
    tail = (doc_columns(docs, tokens) == last_doc).astype(F32)
    scale = jnp.exp(total - cumul) * tail
    kf[...] = key_ref[...].astype(F32)
    vf[...] = value_ref[...].astype(F32)
    for h in range(heads):
        keys = (kf[pl.ds(h, tokens, stride=heads), :] * scale[:, h : h + 1]).astype(BF16)
        values = vf[pl.ds(h, tokens, stride=heads), :].astype(BF16)
        states[h * HEAD_DIM : (h + 1) * HEAD_DIM, :] = lax.dot_general(
            keys, values, (((0,), (0,)), ((), ())), preferred_element_type=F32
        )
    size = quarter_rows(heads)
    mine = place_ref[0] % GROUP_BLOCKS
    for j, ref in enumerate(out_refs):
        taker = mine ^ j
        ref[0:size, :] = states[pl.ds(pl.multiple_of(taker * size, size), size), :].astype(BF16)
        totals = jnp.zeros_like(total)
        for c in range(GROUP_BLOCKS):
            skip = c * heads // GROUP_BLOCKS
            moved = pltpu.roll(total, LANES - skip, 1) if skip else total
            totals = jnp.where(taker == c, moved, totals)
        ref[size : size + INFO, :] = info_rows((*in_parts(totals), first_doc, last_doc))
    copy.wait()


def block_state(place, soft_query, cumul, docs, key, value, tokens, heads):
    return call(
        functools.partial(state_kernel, tokens, heads),
        "block_state",
        [place],
        [soft_query, cumul, docs, key, value],
        (
            *[sds((quarter_rows(heads) + INFO, LANES), BF16)] * GROUP_BLOCKS,
            sds(soft_query.shape, BF16),
        ),
        scratch=[
            pltpu.VMEM((tokens * heads, LANES), F32),
            pltpu.VMEM((tokens * heads, LANES), F32),
            pltpu.VMEM((heads * HEAD_DIM, LANES), F32),
            pltpu.SemaphoreType.DMA,
        ],
        estimate=cost(2 * heads * tokens * HEAD_DIM**2, 5 * tokens * heads * LANES * 2),
        hbm=1,
    )


def in_parts(x):
    hi = x.astype(BF16).astype(F32)
    mid = (x - hi).astype(BF16).astype(F32)
    return hi, mid, x - hi - mid


def info_rows(parts):
    line = lax.broadcasted_iota(jnp.int32, (INFO, LANES), 0)
    info = jnp.zeros((INFO, LANES), F32)
    for i, part in enumerate(parts):
        info = jnp.where(line == i, part, info)
    return info.astype(BF16)


def read_map(ref, size):
    info = ref[size : size + INFO, :].astype(F32)
    return info[0:1] + info[1:2] + info[2:3], info[3:4], info[4:5]


def row_chunks(size):
    unit = min(HEAD_DIM, size)
    return [(slice(i * unit, (i + 1) * unit), slice(i, i + 1)) for i in range(size // unit)]


def in_block_order(place_ref, refs, blocks):
    mine = place_ref[0] % GROUP_BLOCKS
    for j, ref in enumerate(refs):
        blocks[mine ^ j] = ref[...]


def block_maps(blocks, size):
    maps = []
    for c in range(GROUP_BLOCKS):
        info = blocks[c, size : size + INFO, :].astype(F32)
        first, last = info[3:4], info[4:5]
        gain = jnp.exp(info[0:1] + info[1:2] + info[2:3]) * (first == last).astype(F32)
        maps.append((gain, first, last))
    return maps


def group_kernel(size, place_ref, *refs):
    sources = refs[:GROUP_BLOCKS]
    out_ref, blocks = refs[GROUP_BLOCKS:]
    in_block_order(place_ref, sources, blocks)
    maps = block_maps(blocks, size)
    gains = [None]
    for (gain, first, _), (_, _, last_before) in zip(maps[1:], maps[:-1]):
        gains.append(gain * (last_before == first).astype(F32))
    for rows, lane in row_chunks(size):
        total = blocks[0, rows, :].astype(F32)
        for c in range(1, GROUP_BLOCKS):
            total = gains[c][:, lane] * total + blocks[c, rows, :].astype(F32)
        out_ref[rows, :] = total.astype(BF16)
    gain = maps[0][0] * gains[1] * gains[2] * gains[3]
    out_ref[size : size + INFO, :] = info_rows((*in_parts(gain), maps[0][1], maps[-1][2]))


def group_map(place, quarters, size, after, relay):
    return call(
        functools.partial(group_kernel, size),
        "group_map",
        [place],
        quarters,
        (sds((size + INFO, LANES), BF16),),
        scratch=[pltpu.VMEM((GROUP_BLOCKS, size + INFO, LANES), BF16)],
        estimate=cost(8 * size * LANES, 10 * size * LANES * 2),
        after=after,
        relay=relay,
    )


def scan_kernel(size, has_before, bit, place_ref, *refs):
    mine_ref, came_ref = refs[:2]
    before_ref = refs[2] if has_before else None
    run_ref, out_ref = refs[-2:]
    upper = (place_ref[0] >> bit) & 1 == 1
    gain_m, first_m, last_m = read_map(mine_ref, size)
    gain_c, first_c, last_c = read_map(came_ref, size)
    link = jnp.where(upper, (last_c == first_m).astype(F32), (last_m == first_c).astype(F32))
    gain = jnp.where(upper, gain_m, gain_c) * link
    for rows, lane in row_chunks(size):
        mine, came = mine_ref[rows, :].astype(F32), came_ref[rows, :].astype(F32)
        lower_sum, upper_sum = jnp.where(upper, came, mine), jnp.where(upper, mine, came)
        run_ref[rows, :] = (gain[:, lane] * lower_sum + upper_sum).astype(BF16)
    run_ref[size : size + INFO, :] = info_rows(
        (
            *in_parts(gain * jnp.where(upper, gain_c, gain_m)),
            jnp.where(upper, first_c, first_m),
            jnp.where(upper, last_m, last_c),
        )
    )
    if not has_before:
        out_ref[...] = jnp.where(upper, came_ref[...], jnp.zeros_like(came_ref))
        return
    gain_b, first_b, last_b = read_map(before_ref, size)
    empty = first_b == 0.0
    factor = jnp.where(empty, 1.0, gain_b * (last_c == first_b).astype(F32))
    for rows, lane in row_chunks(size):
        before = before_ref[rows, :].astype(F32)
        joined = factor[:, lane] * came_ref[rows, :].astype(F32) + before
        out_ref[rows, :] = jnp.where(upper, joined, before).astype(BF16)
    out_ref[size : size + INFO, :] = info_rows(
        (
            *in_parts(jnp.where(upper, factor * gain_c, gain_b)),
            jnp.where(upper, first_c, first_b),
            jnp.where(upper, jnp.where(empty, last_c, last_b), last_b),
        )
    )


def scan_step(place, bit, mine, came, before, size, after):
    shape = sds((size + INFO, LANES), BF16)
    before = [] if before is None else [before]
    return call(
        functools.partial(scan_kernel, size, len(before), bit),
        "scan_step",
        [place],
        [mine, came, *before],
        (shape, shape),
        estimate=cost(6 * size * LANES, 6 * size * LANES * 2),
        after=after,
    )


def prior_kernel(size, has_before, bit, place_ref, *refs):
    sources, came_ref = refs[:GROUP_BLOCKS], refs[GROUP_BLOCKS]
    before_ref = refs[GROUP_BLOCKS + 1] if has_before else None
    *out_refs, doc_ref, blocks, priors = refs[GROUP_BLOCKS + 1 + has_before :]
    mine = place_ref[0] % GROUP_BLOCKS
    in_block_order(place_ref, sources, blocks)
    maps = block_maps(blocks, size)
    upper = ((place_ref[0] >> bit) & 1).astype(F32)
    _, _, last_c = read_map(came_ref, size)
    factor, doc = jnp.broadcast_to(upper, (1, LANES)), upper * last_c
    if has_before:
        gain_b, first_b, last_b = read_map(before_ref, size)
        empty = first_b == 0.0
        factor = upper * jnp.where(empty, 1.0, gain_b * (last_c == first_b).astype(F32))
        doc = jnp.where(empty, doc, last_b)
    docs = [doc] + [last for _, _, last in maps[:-1]]
    gains = [gain * (doc == first).astype(F32) for (gain, first, _), doc in zip(maps, docs)]
    for rows, lane in row_chunks(size):
        state = factor[:, lane] * came_ref[rows, :].astype(F32)
        if has_before:
            state = state + before_ref[rows, :].astype(F32)
        for c in range(GROUP_BLOCKS):
            priors[c, rows, :] = state.astype(BF16)
            if c < GROUP_BLOCKS - 1:
                state = gains[c][:, lane] * state + blocks[c, rows, :].astype(F32)
    for j, ref in enumerate(out_refs):
        ref[...] = priors[mine ^ j]
    own_doc = docs[0]
    for c in range(1, GROUP_BLOCKS):
        own_doc = jnp.where(mine == c, docs[c], own_doc)
    doc_ref[...] = jnp.broadcast_to(own_doc, (8, LANES))


def prior_states(place, bit, quarters, came, before, size, after, relay=()):
    before = [] if before is None else [before]
    return call(
        functools.partial(prior_kernel, size, len(before), bit),
        "prior_states",
        [place],
        [*quarters, came, *before],
        (*[sds((size, LANES), BF16)] * GROUP_BLOCKS, sds((8, LANES), F32)),
        scratch=[
            pltpu.VMEM((GROUP_BLOCKS, size + INFO, LANES), BF16),
            pltpu.VMEM((GROUP_BLOCKS, size, LANES), BF16),
        ],
        estimate=cost(8 * size * LANES, 10 * size * LANES * 2),
        after=after,
        relay=relay,
    )


def some_heads(ref, tokens, heads, first, count):
    x = ref[...].astype(F32)
    if count == heads:
        return x
    return x.reshape(tokens, heads, LANES)[:, first : first + count, :].reshape(tokens * count, LANES)


def inner_kernel(tokens, heads, first, count, cumul_ref, doc_ref, query_ref, key_ref, value_ref, inner_ref, qh_ref, qf, kf, vf, mask):
    cumul = cumul_ref[...]
    cumul_t = jnp.transpose(cumul)
    docs = doc_ref[...]
    column = doc_columns(docs, tokens)
    same = jnp.concatenate([column] * (tokens // LANES), axis=1) == doc_line(docs, tokens)
    mask[...] = jnp.where(lower_triangle(tokens) & same, 0.0, -1e9)
    qf[...] = some_heads(query_ref, tokens, heads, first, count)
    kf[...] = some_heads(key_ref, tokens, heads, first, count)
    vf[...] = some_heads(value_ref, tokens, heads, first, count)
    for n in range(count):
        h = first + n
        picked = pl.ds(n, tokens, stride=count)
        query = qf[picked, :].astype(BF16)
        keys = kf[picked, :].astype(BF16)
        values = vf[picked, :].astype(BF16)
        qh_ref[n * tokens : (n + 1) * tokens, :] = query
        for i in range(tokens // LANES):
            seen = (i + 1) * LANES
            rows = slice(i * LANES, seen)
            scores = lax.dot_general(
                query[rows, :], keys[0:seen, :], (((1,), (1,)), ((), ())), preferred_element_type=F32
            )
            gap = cumul[rows, h : h + 1] - cumul_t[h : h + 1, 0:seen]
            weights = (scores * jnp.exp(gap + mask[rows, 0:seen])).astype(BF16)
            inner_ref[n * tokens + i * LANES : n * tokens + seen, :] = jnp.dot(
                weights, values[0:seen, :], preferred_element_type=F32
            )


def inner_part(cumul, docs, query, key, value, tokens, heads, first, count, after, relay):
    return call(
        functools.partial(inner_kernel, tokens, heads, first, count),
        "inner_part",
        [],
        [cumul, docs, query, key, value],
        (sds((count * tokens, LANES), F32), sds((count * tokens, LANES), BF16)),
        scratch=[pltpu.VMEM((tokens * count, LANES), F32)] * 3 + [pltpu.VMEM((tokens, tokens), F32)],
        mib=24,
        estimate=cost(
            4 * count * tokens * tokens * HEAD_DIM, tokens * heads * LANES * 12, count * tokens * tokens
        ),
        after=after,
        relay=relay,
    )


def mix_kernel(tokens, heads, parts, place_ref, doc_ref, prior_doc_ref, cumul_ref, *refs):
    refs = list(refs)
    take = lambda n: [refs.pop(0) for _ in range(n)]
    inner, qh, quarters = take(parts), take(parts), take(GROUP_BLOCKS)
    mixed_ref, square_ref, states = refs
    size = quarter_rows(heads)
    mine = place_ref[0] % GROUP_BLOCKS
    for j, ref in enumerate(quarters):
        states[pl.ds(pl.multiple_of((mine ^ j) * size, size), size), :] = ref[...]
    is_open = (doc_columns(doc_ref[...], tokens) == prior_doc_ref[0:1, :]).astype(F32)
    gain = jnp.exp(cumul_ref[...]) * is_open
    squares = jnp.zeros((tokens, LANES), F32)
    for h in range(heads):
        part, n = divmod(h, heads // parts)
        held = slice(n * tokens, (n + 1) * tokens)
        state = states[h * HEAD_DIM : (h + 1) * HEAD_DIM, :]
        carried = jnp.dot(qh[part][held, :], state, preferred_element_type=F32)
        mixed = inner[part][held, :] + carried * gain[:, h : h + 1]
        squares = squares + mixed * mixed
        mixed_ref[pl.ds(h, tokens, stride=heads), :] = mixed
    square_ref[...] = lax.dot_general(
        jnp.ones((8, LANES), F32),
        squares,
        (((1,), (1,)), ((), ())),
        precision=HIGHEST,
        preferred_element_type=F32,
    )


def mix(place, docs, prior_doc, cumul, inner, qh, quarters, tokens, heads, after):
    return call(
        functools.partial(mix_kernel, tokens, heads, len(inner)),
        "mix",
        [place],
        [docs, prior_doc, cumul, *inner, *qh, *quarters],
        (sds((tokens * heads, LANES), F32), sds((8, tokens), F32)),
        scratch=[pltpu.VMEM((heads * HEAD_DIM, LANES), BF16)],
        mib=24,
        estimate=cost(2 * heads * tokens * HEAD_DIM**2, tokens * heads * LANES * 10),
        after=after,
    )


def finish_kernel(tokens, heads, sums, step, gain_ref, gate_ref, mixed_ref, *refs):
    squares, (out_ref, done, sems) = refs[:sums], refs[sums:]
    total = squares[0][0:1, :]
    for ref in squares[1:]:
        total = total + ref[0:1, :]
    scale = lax.rsqrt(total / (HEADS * HEAD_DIM) + 1e-06)
    rows = jnp.concatenate([scale[:, i * LANES : (i + 1) * LANES] for i in range(tokens // LANES)], axis=0)
    column = doc_columns(rows, tokens)
    copies = []
    for i in range(0, tokens, step):
        at = pl.ds(i * heads, step * heads)
        gate = jax.nn.sigmoid(gate_ref[at, :].astype(F32)).reshape(step, heads, LANES)
        mixed = mixed_ref[at, :].reshape(step, heads, LANES)
        inv = column[i : i + step, :][:, None, :]
        out = mixed * inv * gain_ref[...][None] * gate
        done[at, :] = out.reshape(step * heads, LANES).astype(BF16)
        copies.append(pltpu.make_async_copy(done.at[at, :], out_ref.at[at, :], sems.at[i // step]))
        copies[-1].start()
    for copy in copies:
        copy.wait()


def finish(gain, gate, mixed, squares, tokens, heads, after):
    step = 64
    return call(
        functools.partial(finish_kernel, tokens, heads, len(squares), step),
        "finish",
        [],
        [gain, gate, mixed, *squares],
        sds((tokens * heads, LANES), BF16),
        scratch=[pltpu.VMEM((tokens * heads, LANES), BF16), pltpu.SemaphoreType.DMA((tokens // step,))],
        estimate=cost(0, tokens * heads * LANES * 8, tokens * heads * LANES),
        after=after,
        out_hbm=True,
    )


def attend_kernel(tokens, heads, kv_here, least, is_first, is_last, unroll, place_ref, *refs):
    refs = list(refs)
    take = lambda n: [refs.pop(0) for _ in range(n)]
    per_group = heads // kv_here
    rows = tokens * per_group
    step = CHUNK // per_group
    if is_first:
        doc_ref, query_ref = take(2)
    else:
        wide_ref, state_ref = take(2)
    kv = take(len(least))
    if is_first:
        wide_ref = take(1)[0]
    out_ref = take(1)[0]
    if is_last:
        take(1)[0][...] = jnp.zeros((8, LANES), F32)
    bias = take(1)[0]
    if is_first:
        doc_rep = take(1)[0]
    if is_last:
        done, sems = take(2)
    block = place_ref[0]

    lane = lax.broadcasted_iota(jnp.int32, (tokens, LANES), 1).astype(F32)
    end = 2 * kv_here * tokens
    for j, ref in enumerate(kv):
        valid = (block >= jnp.where(block % 2 == 0, *least[j])).astype(F32)
        docs = doc_columns(ref[end : end + INFO, :].astype(F32) * valid, tokens)
        bias[j] = jnp.where(docs == lane, 0.0, -BIG).astype(BF16)
    if is_first:
        column = doc_columns(doc_ref[...], tokens)
        for h in range(per_group):
            doc_rep[pl.ds(h, tokens, stride=per_group), :] = (column == lane).astype(F32)
    ones = jnp.ones((STATE_ROWS - HEAD_DIM, tokens), BF16)

    def some_chunks(i, carry):
        chains = [(u, g) for u in range(unroll) for g in range(kv_here)]
        chunk = [i * unroll + u for u in range(unroll)]
        at = [pl.ds(pl.multiple_of(c * CHUNK, CHUNK), CHUNK) for c in chunk]
        picked = [pl.ds(pl.multiple_of(c * (step * heads), step * heads), step * heads) for c in chunk]
        scores, results = {}, {}

        def begin(u, g):
            if is_first:
                query = query_ref[picked[u], :].astype(F32).reshape(step, heads, LANES)
                query = query[:, g * per_group : (g + 1) * per_group, :].reshape(CHUNK, LANES)
                wide = jnp.concatenate([query.astype(BF16), doc_rep[at[u], :].astype(BF16)], axis=1)
                wide_ref[g, at[u], :] = wide
            else:
                wide = wide_ref[g, at[u], :]
            out = []
            for j, ref in enumerate(kv):
                keys = jnp.concatenate([ref[g * tokens : (g + 1) * tokens, :], bias[j]], axis=1)
                out.append(
                    lax.dot_general(keys, wide, (((1,), (1,)), ((), ())), preferred_element_type=F32)
                )
            if is_first:
                token = chunk[u] * step + lax.broadcasted_iota(jnp.int32, (tokens, CHUNK), 1) // per_group
                key_at = lax.broadcasted_iota(jnp.int32, (tokens, CHUNK), 0)
                out[0] = jnp.where(key_at <= token, out[0], -BIG)
            scores[u, g] = out

        def end_chain(u, g):
            here = scores.pop((u, g))
            top = jnp.max(here[0], axis=0, keepdims=True)
            for score in here[1:]:
                top = jnp.maximum(top, jnp.max(score, axis=0, keepdims=True))
            total = None
            if not is_first:
                before = state_ref[g, :, at[u]]
                top_before = before[STATE_ROWS - 1 : STATE_ROWS, :]
                top = jnp.maximum(top, top_before)
                total = before * jnp.exp2((top_before - top) * SCORE_TO_EXP2)
            for ref, score in zip(kv, here):
                weights = jnp.exp2((score - top) * SCORE_TO_EXP2).astype(BF16)
                first = (kv_here + g) * tokens
                parts = [ref[first + p : first + p + LANES, :] for p in range(0, tokens, LANES)]
                values = jnp.concatenate([jnp.concatenate(parts, axis=1), ones], axis=0)
                more = jnp.dot(values, weights, preferred_element_type=F32)
                total = more if total is None else total + more
            if is_last:
                results[u, g] = jnp.transpose(total[0:HEAD_DIM] / total[HEAD_DIM : HEAD_DIM + 1])
            else:
                out_ref[g, 0 : STATE_ROWS - 8, at[u]] = total[0 : STATE_ROWS - 8]
                out_ref[g, STATE_ROWS - 8 : STATE_ROWS, at[u]] = jnp.broadcast_to(top, (8, CHUNK))

        ahead = 3
        for n in range(len(chains) + ahead):
            if n < len(chains):
                begin(*chains[n])
            if n >= ahead:
                end_chain(*chains[n - ahead])
        if is_last:
            for u in range(unroll):
                result = [results[u, g] for g in range(kv_here)]
                if kv_here > 1:
                    result = [r.reshape(step, per_group, LANES) for r in result]
                    result = [jnp.concatenate(result, axis=1).reshape(step * heads, LANES)]
                done[picked[u], :] = result[0].astype(BF16)
                pltpu.make_async_copy(
                    done.at[picked[u], :], out_ref.at[picked[u], :], sems.at[chunk[u]]
                ).start()
        return carry

    lax.fori_loop(0, rows // (CHUNK * unroll), some_chunks, 0)
    if is_last:
        for c in range(rows // CHUNK):
            at = pl.ds(c * step * heads, step * heads)
            pltpu.make_async_copy(done.at[at, :], out_ref.at[at, :], sems.at[c]).wait()


def attend(place, first, state, kv, is_last, tokens, heads, kv_here, after, relay=()):
    is_first = state is None
    least = tuple(pair for _, pair in kv)
    kv = [block for block, _ in kv]
    blocks = len(kv)
    rows = tokens * heads // kv_here
    unroll = min(8, rows // CHUNK)
    wide_shape = sds((kv_here, rows, 2 * LANES), BF16)
    state_shape = sds((kv_here, STATE_ROWS, rows), F32)
    out_shape = sds((tokens * heads, LANES), BF16) if is_last else state_shape
    scratch = [pltpu.VMEM((blocks, tokens, LANES), BF16)]
    if is_first:
        out_shape = (wide_shape, out_shape)
        scratch.append(pltpu.VMEM((rows, LANES), F32))
    if is_last:
        out_shape = (out_shape, sds((8, LANES), F32))
        scratch.append(pltpu.VMEM((tokens * heads, LANES), BF16))
        scratch.append(pltpu.SemaphoreType.DMA((rows // CHUNK,)))
    span = blocks * tokens
    return call(
        functools.partial(attend_kernel, tokens, heads, kv_here, least, is_first, is_last, unroll),
        "attend",
        [place],
        [*first, *([] if is_first else [state]), *kv],
        out_shape,
        scratch=scratch,
        mib=24,
        estimate=cost(
            4 * tokens * heads * span * 2 * LANES, 4 * tokens * heads * LANES * 4, tokens * heads * span
        ),
        after=after,
        out_hbm=is_last,
        relay=relay,
    )


def body(
    blocks,
    lin_query,
    lin_key,
    lin_value,
    lin_gate,
    log_decay,
    norm_gain,
    doc_ids,
    soft_query,
    soft_key,
    soft_value,
):
    tokens, heads, _ = lin_query.shape
    tensor = HEADS // heads
    kv_here = max(1, heads // GROUP)
    parts = 2 if heads % 16 == 0 else 1
    longest = blocks * tokens * 5 // 8
    window = min(blocks - 1, (longest - 1 + tokens - 1) // tokens)
    flat = lambda x: x.reshape(-1, LANES)
    block = lax.axis_index("seq")
    place = block.astype(jnp.int32).reshape(1)
    start = (lax.axis_index("tp") * heads // GROUP).astype(jnp.int32).reshape(1)

    def send(x, pairs):
        return lax.ppermute(x, "seq", [(a, b % blocks) for a, b in pairs])

    everyone = range(blocks)
    swap = [(b, b ^ 1) for b in everyone]

    own_kv, docs, cumul, key, value = fetch(
        start,
        [
            doc_ids.reshape(tokens // LANES, LANES),
            jnp.transpose(log_decay),
            flat(soft_key),
            flat(soft_value),
            flat(lin_key),
            flat(lin_value),
        ],
        tokens,
        heads,
        kv_here,
    )

    forward = [(b, b + 2) for b in everyone]
    ahead = send(own_kv, forward)

    size = quarter_rows(heads)
    others = range(1, GROUP_BLOCKS)
    *sent, query = block_state(
        place, flat(soft_query), cumul, docs, key, value, tokens, heads
    )
    quarters = [sent[0]] + [send(sent[j], [(b, b ^ j) for b in everyone]) for j in others]

    state = {}

    def first_attention(after):
        state["wide"], state["sum"] = attend(
            place, (docs, query), None, [(own_kv, (0, 0))], False, tokens, heads, kv_here, after
        )
        return state["sum"]

    def more_attention(kv, is_last, after, relay=()):
        out = attend(
            place, (state["wide"],), state["sum"], kv, is_last, tokens, heads, kv_here, after, relay
        )
        state["sum"] = out[0] if relay else out
        return out

    inner, qh = [], []

    def inner_of(part, after, relay=()):
        n = heads // parts
        got = inner_part(
            cumul, docs, flat(lin_query), key, value, tokens, heads, part * n, n, after, relay
        )
        inner.append(got[0])
        qh.append(got[1])
        return (got[0], *got[2:]) if relay else got[0]

    done, lane = first_attention([sent[0]]), ahead
    if parts > 1:
        done, lane = inner_of(0, [done], [ahead])
    second = send(lane, [(b, b + 2) for b in range(2, blocks - 2)])
    run, lane = group_map(place, quarters, size, [done], [lane])
    first_cross = send(lane, swap)
    stages = (blocks // GROUP_BLOCKS).bit_length() - 1
    before, done = None, run
    for stage in range(stages):
        came = send(run, [(b, b ^ (GROUP_BLOCKS << stage)) for b in everyone])
        if stage == stages - 1:
            done = more_attention([(lane, (2, 2))], False, [done])
            done = inner_of(parts - 1, [done])
        else:
            run, before = scan_step(place, stage + 2, run, came, before, size, [done])
            done = run
    assert window % 2 == 0 or window == 5
    payload = pick(place, own_kv, second, [done])
    slot = (send(payload, [(b, b + 1) for b in everyone]), (window if window % 2 else blocks, 1))
    *priors, prior_doc = prior_states(place, stages + 1, quarters, came, before, size, [payload])
    priors = [priors[0]] + [send(priors[j], [(b, b ^ j) for b in everyone]) for j in others]
    done = more_attention([(first_cross, (2, 3)), (second, (4, 4))], False, [prior_doc])
    (lane,) = pass_on([second], [done, *priors])
    rest = [(send(lane, swap), (4, 5))]
    for back in range(3, window // 2 + 1):
        lane = send(lane, forward)
        rest.append((lane, (2 * back, 2 * back)))
        rest.append((send(lane, swap), (2 * back, 2 * back + 1)))
    mixed, squares = mix(place, docs, prior_doc, cumul, inner, qh, priors, tokens, heads, [done])
    sums = [squares]
    for other in range(1, tensor):
        sums.append(lax.ppermute(squares, "tp", [(t, t ^ other) for t in range(tensor)]))
    rest.insert(0, slot)
    done = squares
    while rest:
        got = more_attention(rest[:1], len(rest) == 1, [done])
        rest, done = rest[1:], got
    soft_out, done = got
    lin_out = finish(norm_gain, flat(lin_gate), mixed, sums, tokens, heads, [done])
    shape = (tokens, heads, HEAD_DIM)
    return lin_out.reshape(shape), soft_out.reshape(shape)


def solution(mesh):
    in_specs = (
        P("seq", "tp", None),
        P("seq", "tp", None),
        P("seq", "tp", None),
        P("seq", "tp", None),
        P("seq", "tp"),
        P("tp", None),
        P("seq"),
        P("seq", "tp", None),
        P("seq", None, None),
        P("seq", None, None),
    )
    out_specs = (P("seq", "tp", None), P("seq", "tp", None))
    return jax.shard_map(
        functools.partial(body, mesh.shape["seq"]),
        mesh=mesh,
        in_specs=in_specs,
        out_specs=out_specs,
        check_vma=False,
    )
```

```python
import functools

import jax
import jax.numpy as jnp
import numpy as np
from jax import lax
from jax.experimental import pallas as pl
from jax.experimental.pallas import tpu as pltpu
from jax.sharding import PartitionSpec as P

HEADS = 64
HEAD_DIM = 128
KV_HEADS = 8
LANES = 128
GROUP = HEADS // KV_HEADS
F32 = jnp.float32
BF16 = jnp.bfloat16
BIG = float(2**20)
SCORE_TO_EXP2 = HEAD_DIM**-0.5 * float(np.log2(np.e))
INFO = 16
HIGHEST = lax.Precision.HIGHEST

VMEM = pl.BlockSpec(memory_space=pltpu.VMEM)
SMEM = pl.BlockSpec(memory_space=pltpu.SMEM)
HBM = pl.BlockSpec(memory_space=pltpu.HBM)
ANYWHERE = pl.BlockSpec(memory_space=pl.ANY)
STATE_ROWS = HEAD_DIM + 16
CHUNK = 256
GROUP_BLOCKS = 4


def sds(shape, dtype):
    return jax.ShapeDtypeStruct(shape, dtype)


def cost(flops, bytes_accessed, transcendentals=0):
    return pl.CostEstimate(
        flops=int(flops), bytes_accessed=int(bytes_accessed), transcendentals=int(transcendentals)
    )


def call(kernel, name, scalars, operands, out_shape, scratch=(), mib=16, estimate=None, after=(), hbm=0, out_hbm=False, relay=()):
    begin = len(scalars) + len(operands)
    skip = len(after)
    operands = [
        pltpu.with_memory_space_constraint(x, pltpu.HBM) if i < hbm else x for i, x in enumerate(operands)
    ]
    outs = out_shape if isinstance(out_shape, tuple) else (out_shape,)
    out_specs = (VMEM,) * len(outs)
    outs = tuple(
        (pltpu.HBM if out_hbm and i == 0 else pltpu.VMEM)(x.shape, x.dtype) for i, x in enumerate(outs)
    )
    if out_hbm:
        out_specs = (HBM, *out_specs[1:])

    moved = len(relay)
    many = len(outs)
    single = not isinstance(out_shape, tuple) and not relay
    out_specs += (VMEM,) * moved
    outs += tuple(pltpu.VMEM(x.shape, x.dtype) for x in relay)

    def run(*refs):
        rest = refs[begin + skip + moved :]
        for source, target in zip(refs[begin + skip : begin + skip + moved], rest[many : many + moved]):
            target[...] = source[...]
        kernel(*refs[:begin], *rest[:many], *rest[many + moved :])

    out = pl.pallas_call(
        run,
        out_shape=outs,
        in_specs=[SMEM] * len(scalars) + [HBM] * hbm + [VMEM] * (len(operands) - hbm) + [ANYWHERE] * skip + [VMEM] * moved,
        out_specs=out_specs,
        scratch_shapes=list(scratch),
        compiler_params=pltpu.CompilerParams(vmem_limit_bytes=mib * 1024 * 1024),
        cost_estimate=estimate,
        name=name,
    )(*scalars, *operands, *after, *relay)
    return out[0] if single else out


def doc_columns(doc_rows, tokens):
    parts = []
    for i in range(tokens // LANES):
        row = jnp.broadcast_to(doc_rows[i : i + 1, :], (LANES, LANES))
        parts.append(jnp.transpose(row))
    return jnp.concatenate(parts, axis=0)


def doc_line(doc_rows, tokens):
    return jnp.concatenate([doc_rows[i : i + 1, :] for i in range(tokens // LANES)], axis=1)


def lower_triangle(tokens):
    rows = lax.broadcasted_iota(jnp.int32, (tokens, tokens), 0)
    cols = lax.broadcasted_iota(jnp.int32, (tokens, tokens), 1)
    return rows >= cols


def pick_kernel(place_ref, even_ref, odd_ref, out_ref):
    out_ref[...] = jnp.where(place_ref[0] % 2 == 0, even_ref[...], odd_ref[...])


def pick(place, even, odd, after):
    return call(pick_kernel, "pick", [place], [even, odd], sds(even.shape, BF16), after=after)


def pass_on(arrays, after):
    return call(lambda: None, "pass_on", [], [], (), after=after, relay=arrays)


def fetch_kernel(tokens, heads, kv_here, start_ref, *refs):
    refs = list(refs)
    take = lambda n: [refs.pop(0) for _ in range(n)]
    sources = take(6)
    kv_ref, doc_out, cumul_ref, key_out, value_out = take(5)
    held = take(4)
    sems, wide, ldp = refs
    docs_in, decays, soft_key, soft_value = held
    targets = [*held, key_out, value_out]
    copies = [
        pltpu.make_async_copy(source, target, sems.at[i])
        for i, (source, target) in enumerate(zip(sources, targets))
    ]
    for copy in copies:
        copy.start()

    copies[0].wait()
    docs = docs_in[...].astype(F32) + 1.0
    line = lax.broadcasted_iota(jnp.int32, (INFO, LANES), 0)
    info = jnp.zeros((INFO, LANES), F32)
    for i in range(tokens // LANES):
        info = jnp.where(line == i, docs[i : i + 1, :], info)
    doc_out[...] = info
    end = 2 * kv_here * tokens
    kv_ref[end : end + INFO, :] = info.astype(BF16)

    copies[1].wait()
    ldp[...] = jnp.zeros_like(ldp)
    ldp[0:heads, :] = decays[...]
    cumul_ref[...] = lax.dot_general(
        lower_triangle(tokens).astype(F32),
        ldp[...],
        (((1,), (1,)), ((), ())),
        precision=HIGHEST,
        preferred_element_type=F32,
    )

    start = start_ref[0]
    for which, ref in enumerate((soft_key, soft_value)):
        copies[2 + which].wait()
        wide[...] = ref[...].astype(F32)
        for g in range(kv_here):
            rows = wide[pl.ds(start + g, tokens, stride=KV_HEADS), :]
            at = (which * kv_here + g) * tokens
            if which:
                halves = [jnp.transpose(rows[i : i + LANES, :]) for i in range(0, tokens, LANES)]
                rows = jnp.concatenate(halves, axis=0)
            kv_ref[at : at + tokens, :] = rows.astype(BF16)
    for copy in copies[4:]:
        copy.wait()


def fetch(start, operands, tokens, heads, kv_here):
    return call(
        functools.partial(fetch_kernel, tokens, heads, kv_here),
        "fetch",
        [start],
        operands,
        (
            sds((2 * kv_here * tokens + INFO, LANES), BF16),
            sds((INFO, LANES), F32),
            sds((tokens, LANES), F32),
            sds(operands[4].shape, BF16),
            sds(operands[5].shape, BF16),
        ),
        scratch=[pltpu.VMEM(x.shape, x.dtype) for x in operands[:4]]
        + [
            pltpu.SemaphoreType.DMA((len(operands),)),
            pltpu.VMEM((tokens * KV_HEADS, LANES), F32),
            pltpu.VMEM((LANES, tokens), F32),
        ],
        estimate=cost(0, 3 * tokens * heads * LANES * 2),
        hbm=len(operands),
    )


def quarter_rows(heads):
    return heads * HEAD_DIM // GROUP_BLOCKS


def state_kernel(tokens, heads, place_ref, *refs):
    refs = list(refs)
    take = lambda n: [refs.pop(0) for _ in range(n)]
    query_in, cumul_ref, doc_ref, key_ref, value_ref = take(5)
    out_refs, query_out = take(GROUP_BLOCKS), take(1)[0]
    kf, vf, states, sem = refs
    copy = pltpu.make_async_copy(query_in, query_out, sem)
    copy.start()
    cumul, docs = cumul_ref[...], doc_ref[...]
    total = cumul[tokens - 1 : tokens, :]
    last_row = tokens // LANES - 1
    first_doc = docs[0:1, 0:1]
    last_doc = docs[last_row : last_row + 1, LANES - 1 : LANES]
    tail = (doc_columns(docs, tokens) == last_doc).astype(F32)
    scale = jnp.exp(total - cumul) * tail
    kf[...] = key_ref[...].astype(F32)
    vf[...] = value_ref[...].astype(F32)
    for h in range(heads):
        keys = (kf[pl.ds(h, tokens, stride=heads), :] * scale[:, h : h + 1]).astype(BF16)
        values = vf[pl.ds(h, tokens, stride=heads), :].astype(BF16)
        states[h * HEAD_DIM : (h + 1) * HEAD_DIM, :] = lax.dot_general(
            keys, values, (((0,), (0,)), ((), ())), preferred_element_type=F32
        )
    size = quarter_rows(heads)
    mine = place_ref[0] % GROUP_BLOCKS
    for j, ref in enumerate(out_refs):
        taker = mine ^ j
        ref[0:size, :] = states[pl.ds(pl.multiple_of(taker * size, size), size), :].astype(BF16)
        totals = jnp.zeros_like(total)
        for c in range(GROUP_BLOCKS):
            skip = c * heads // GROUP_BLOCKS
            moved = pltpu.roll(total, LANES - skip, 1) if skip else total
            totals = jnp.where(taker == c, moved, totals)
        ref[size : size + INFO, :] = info_rows((*in_parts(totals), first_doc, last_doc))
    copy.wait()


def block_state(place, soft_query, cumul, docs, key, value, tokens, heads):
    return call(
        functools.partial(state_kernel, tokens, heads),
        "block_state",
        [place],
        [soft_query, cumul, docs, key, value],
        (
            *[sds((quarter_rows(heads) + INFO, LANES), BF16)] * GROUP_BLOCKS,
            sds(soft_query.shape, BF16),
        ),
        scratch=[
            pltpu.VMEM((tokens * heads, LANES), F32),
            pltpu.VMEM((tokens * heads, LANES), F32),
            pltpu.VMEM((heads * HEAD_DIM, LANES), F32),
            pltpu.SemaphoreType.DMA,
        ],
        estimate=cost(2 * heads * tokens * HEAD_DIM**2, 5 * tokens * heads * LANES * 2),
        hbm=1,
    )


def in_parts(x):
    hi = x.astype(BF16).astype(F32)
    mid = (x - hi).astype(BF16).astype(F32)
    return hi, mid, x - hi - mid


def info_rows(parts):
    line = lax.broadcasted_iota(jnp.int32, (INFO, LANES), 0)
    info = jnp.zeros((INFO, LANES), F32)
    for i, part in enumerate(parts):
        info = jnp.where(line == i, part, info)
    return info.astype(BF16)


def read_map(ref, size):
    info = ref[size : size + INFO, :].astype(F32)
    return info[0:1] + info[1:2] + info[2:3], info[3:4], info[4:5]


def row_chunks(size):
    unit = min(HEAD_DIM, size)
    return [(slice(i * unit, (i + 1) * unit), slice(i, i + 1)) for i in range(size // unit)]


def in_block_order(place_ref, refs, blocks):
    mine = place_ref[0] % GROUP_BLOCKS
    for j, ref in enumerate(refs):
        blocks[mine ^ j] = ref[...]


def block_maps(blocks, size):
    maps = []
    for c in range(GROUP_BLOCKS):
        info = blocks[c, size : size + INFO, :].astype(F32)
        first, last = info[3:4], info[4:5]
        gain = jnp.exp(info[0:1] + info[1:2] + info[2:3]) * (first == last).astype(F32)
        maps.append((gain, first, last))
    return maps


def group_kernel(size, place_ref, *refs):
    sources = refs[:GROUP_BLOCKS]
    out_ref, blocks = refs[GROUP_BLOCKS:]
    in_block_order(place_ref, sources, blocks)
    maps = block_maps(blocks, size)
    gains = [None]
    for (gain, first, _), (_, _, last_before) in zip(maps[1:], maps[:-1]):
        gains.append(gain * (last_before == first).astype(F32))
    for rows, lane in row_chunks(size):
        total = blocks[0, rows, :].astype(F32)
        for c in range(1, GROUP_BLOCKS):
            total = gains[c][:, lane] * total + blocks[c, rows, :].astype(F32)
        out_ref[rows, :] = total.astype(BF16)
    gain = maps[0][0] * gains[1] * gains[2] * gains[3]
    out_ref[size : size + INFO, :] = info_rows((*in_parts(gain), maps[0][1], maps[-1][2]))


def group_map(place, quarters, size, after, relay):
    return call(
        functools.partial(group_kernel, size),
        "group_map",
        [place],
        quarters,
        (sds((size + INFO, LANES), BF16),),
        scratch=[pltpu.VMEM((GROUP_BLOCKS, size + INFO, LANES), BF16)],
        estimate=cost(8 * size * LANES, 10 * size * LANES * 2),
        after=after,
        relay=relay,
    )


def scan_kernel(size, has_before, bit, place_ref, *refs):
    mine_ref, came_ref = refs[:2]
    before_ref = refs[2] if has_before else None
    run_ref, out_ref = refs[-2:]
    upper = (place_ref[0] >> bit) & 1 == 1
    gain_m, first_m, last_m = read_map(mine_ref, size)
    gain_c, first_c, last_c = read_map(came_ref, size)
    link = jnp.where(upper, (last_c == first_m).astype(F32), (last_m == first_c).astype(F32))
    gain = jnp.where(upper, gain_m, gain_c) * link
    for rows, lane in row_chunks(size):
        mine, came = mine_ref[rows, :].astype(F32), came_ref[rows, :].astype(F32)
        lower_sum, upper_sum = jnp.where(upper, came, mine), jnp.where(upper, mine, came)
        run_ref[rows, :] = (gain[:, lane] * lower_sum + upper_sum).astype(BF16)
    run_ref[size : size + INFO, :] = info_rows(
        (
            *in_parts(gain * jnp.where(upper, gain_c, gain_m)),
            jnp.where(upper, first_c, first_m),
            jnp.where(upper, last_m, last_c),
        )
    )
    if not has_before:
        out_ref[...] = jnp.where(upper, came_ref[...], jnp.zeros_like(came_ref))
        return
    gain_b, first_b, last_b = read_map(before_ref, size)
    empty = first_b == 0.0
    factor = jnp.where(empty, 1.0, gain_b * (last_c == first_b).astype(F32))
    for rows, lane in row_chunks(size):
        before = before_ref[rows, :].astype(F32)
        joined = factor[:, lane] * came_ref[rows, :].astype(F32) + before
        out_ref[rows, :] = jnp.where(upper, joined, before).astype(BF16)
    out_ref[size : size + INFO, :] = info_rows(
        (
            *in_parts(jnp.where(upper, factor * gain_c, gain_b)),
            jnp.where(upper, first_c, first_b),
            jnp.where(upper, jnp.where(empty, last_c, last_b), last_b),
        )
    )


def scan_step(place, bit, mine, came, before, size, after):
    shape = sds((size + INFO, LANES), BF16)
    before = [] if before is None else [before]
    return call(
        functools.partial(scan_kernel, size, len(before), bit),
        "scan_step",
        [place],
        [mine, came, *before],
        (shape, shape),
        estimate=cost(6 * size * LANES, 6 * size * LANES * 2),
        after=after,
    )


def prior_kernel(size, has_before, bit, place_ref, *refs):
    sources, came_ref = refs[:GROUP_BLOCKS], refs[GROUP_BLOCKS]
    before_ref = refs[GROUP_BLOCKS + 1] if has_before else None
    *out_refs, doc_ref, blocks, priors = refs[GROUP_BLOCKS + 1 + has_before :]
    mine = place_ref[0] % GROUP_BLOCKS
    in_block_order(place_ref, sources, blocks)
    maps = block_maps(blocks, size)
    upper = ((place_ref[0] >> bit) & 1).astype(F32)
    _, _, last_c = read_map(came_ref, size)
    factor, doc = jnp.broadcast_to(upper, (1, LANES)), upper * last_c
    if has_before:
        gain_b, first_b, last_b = read_map(before_ref, size)
        empty = first_b == 0.0
        factor = upper * jnp.where(empty, 1.0, gain_b * (last_c == first_b).astype(F32))
        doc = jnp.where(empty, doc, last_b)
    docs = [doc] + [last for _, _, last in maps[:-1]]
    gains = [gain * (doc == first).astype(F32) for (gain, first, _), doc in zip(maps, docs)]
    for rows, lane in row_chunks(size):
        state = factor[:, lane] * came_ref[rows, :].astype(F32)
        if has_before:
            state = state + before_ref[rows, :].astype(F32)
        for c in range(GROUP_BLOCKS):
            priors[c, rows, :] = state.astype(BF16)
            if c < GROUP_BLOCKS - 1:
                state = gains[c][:, lane] * state + blocks[c, rows, :].astype(F32)
    for j, ref in enumerate(out_refs):
        ref[...] = priors[mine ^ j]
    own_doc = docs[0]
    for c in range(1, GROUP_BLOCKS):
        own_doc = jnp.where(mine == c, docs[c], own_doc)
    doc_ref[...] = jnp.broadcast_to(own_doc, (8, LANES))


def prior_states(place, bit, quarters, came, before, size, after, relay=()):
    before = [] if before is None else [before]
    return call(
        functools.partial(prior_kernel, size, len(before), bit),
        "prior_states",
        [place],
        [*quarters, came, *before],
        (*[sds((size, LANES), BF16)] * GROUP_BLOCKS, sds((8, LANES), F32)),
        scratch=[
            pltpu.VMEM((GROUP_BLOCKS, size + INFO, LANES), BF16),
            pltpu.VMEM((GROUP_BLOCKS, size, LANES), BF16),
        ],
        estimate=cost(8 * size * LANES, 10 * size * LANES * 2),
        after=after,
        relay=relay,
    )


def some_heads(ref, tokens, heads, first, count):
    x = ref[...].astype(F32)
    if count == heads:
        return x
    return x.reshape(tokens, heads, LANES)[:, first : first + count, :].reshape(tokens * count, LANES)


def inner_kernel(tokens, heads, first, count, cumul_ref, doc_ref, query_ref, key_ref, value_ref, inner_ref, qh_ref, qf, kf, vf, mask):
    cumul = cumul_ref[...]
    cumul_t = jnp.transpose(cumul)
    docs = doc_ref[...]
    column = doc_columns(docs, tokens)
    same = jnp.concatenate([column] * (tokens // LANES), axis=1) == doc_line(docs, tokens)
    mask[...] = jnp.where(lower_triangle(tokens) & same, 0.0, -1e9)
    qf[...] = some_heads(query_ref, tokens, heads, first, count)
    kf[...] = some_heads(key_ref, tokens, heads, first, count)
    vf[...] = some_heads(value_ref, tokens, heads, first, count)
    for n in range(count):
        h = first + n
        picked = pl.ds(n, tokens, stride=count)
        query = qf[picked, :].astype(BF16)
        keys = kf[picked, :].astype(BF16)
        values = vf[picked, :].astype(BF16)
        qh_ref[n * tokens : (n + 1) * tokens, :] = query
        for i in range(tokens // LANES):
            seen = (i + 1) * LANES
            rows = slice(i * LANES, seen)
            scores = lax.dot_general(
                query[rows, :], keys[0:seen, :], (((1,), (1,)), ((), ())), preferred_element_type=F32
            )
            gap = cumul[rows, h : h + 1] - cumul_t[h : h + 1, 0:seen]
            weights = (scores * jnp.exp(gap + mask[rows, 0:seen])).astype(BF16)
            inner_ref[n * tokens + i * LANES : n * tokens + seen, :] = jnp.dot(
                weights, values[0:seen, :], preferred_element_type=F32
            )


def inner_part(cumul, docs, query, key, value, tokens, heads, first, count, after, relay):
    return call(
        functools.partial(inner_kernel, tokens, heads, first, count),
        "inner_part",
        [],
        [cumul, docs, query, key, value],
        (sds((count * tokens, LANES), F32), sds((count * tokens, LANES), BF16)),
        scratch=[pltpu.VMEM((tokens * count, LANES), F32)] * 3 + [pltpu.VMEM((tokens, tokens), F32)],
        mib=24,
        estimate=cost(
            4 * count * tokens * tokens * HEAD_DIM, tokens * heads * LANES * 12, count * tokens * tokens
        ),
        after=after,
        relay=relay,
    )


def mix_kernel(tokens, heads, parts, place_ref, doc_ref, prior_doc_ref, cumul_ref, *refs):
    refs = list(refs)
    take = lambda n: [refs.pop(0) for _ in range(n)]
    inner, qh, quarters = take(parts), take(parts), take(GROUP_BLOCKS)
    mixed_ref, square_ref, states = refs
    size = quarter_rows(heads)
    mine = place_ref[0] % GROUP_BLOCKS
    for j, ref in enumerate(quarters):
        states[pl.ds(pl.multiple_of((mine ^ j) * size, size), size), :] = ref[...]
    is_open = (doc_columns(doc_ref[...], tokens) == prior_doc_ref[0:1, :]).astype(F32)
    gain = jnp.exp(cumul_ref[...]) * is_open
    squares = jnp.zeros((tokens, LANES), F32)
    for h in range(heads):
        part, n = divmod(h, heads // parts)
        held = slice(n * tokens, (n + 1) * tokens)
        state = states[h * HEAD_DIM : (h + 1) * HEAD_DIM, :]
        carried = jnp.dot(qh[part][held, :], state, preferred_element_type=F32)
        mixed = inner[part][held, :] + carried * gain[:, h : h + 1]
        squares = squares + mixed * mixed
        mixed_ref[pl.ds(h, tokens, stride=heads), :] = mixed
    square_ref[...] = lax.dot_general(
        jnp.ones((8, LANES), F32),
        squares,
        (((1,), (1,)), ((), ())),
        precision=HIGHEST,
        preferred_element_type=F32,
    )


def mix(place, docs, prior_doc, cumul, inner, qh, quarters, tokens, heads, after):
    return call(
        functools.partial(mix_kernel, tokens, heads, len(inner)),
        "mix",
        [place],
        [docs, prior_doc, cumul, *inner, *qh, *quarters],
        (sds((tokens * heads, LANES), F32), sds((8, tokens), F32)),
        scratch=[pltpu.VMEM((heads * HEAD_DIM, LANES), BF16)],
        mib=24,
        estimate=cost(2 * heads * tokens * HEAD_DIM**2, tokens * heads * LANES * 10),
        after=after,
    )


def finish_kernel(tokens, heads, sums, step, gain_ref, gate_ref, mixed_ref, *refs):
    squares, (out_ref, done, sems) = refs[:sums], refs[sums:]
    total = squares[0][0:1, :]
    for ref in squares[1:]:
        total = total + ref[0:1, :]
    scale = lax.rsqrt(total / (HEADS * HEAD_DIM) + 1e-06)
    rows = jnp.concatenate([scale[:, i * LANES : (i + 1) * LANES] for i in range(tokens // LANES)], axis=0)
    column = doc_columns(rows, tokens)
    copies = []
    for i in range(0, tokens, step):
        at = pl.ds(i * heads, step * heads)
        gate = jax.nn.sigmoid(gate_ref[at, :].astype(F32)).reshape(step, heads, LANES)
        mixed = mixed_ref[at, :].reshape(step, heads, LANES)
        inv = column[i : i + step, :][:, None, :]
        out = mixed * inv * gain_ref[...][None] * gate
        done[at, :] = out.reshape(step * heads, LANES).astype(BF16)
        copies.append(pltpu.make_async_copy(done.at[at, :], out_ref.at[at, :], sems.at[i // step]))
        copies[-1].start()
    for copy in copies:
        copy.wait()


def finish(gain, gate, mixed, squares, tokens, heads, after):
    step = 64
    return call(
        functools.partial(finish_kernel, tokens, heads, len(squares), step),
        "finish",
        [],
        [gain, gate, mixed, *squares],
        sds((tokens * heads, LANES), BF16),
        scratch=[pltpu.VMEM((tokens * heads, LANES), BF16), pltpu.SemaphoreType.DMA((tokens // step,))],
        estimate=cost(0, tokens * heads * LANES * 8, tokens * heads * LANES),
        after=after,
        out_hbm=True,
    )


def attend_kernel(tokens, heads, kv_here, least, is_first, is_last, unroll, place_ref, *refs):
    refs = list(refs)
    take = lambda n: [refs.pop(0) for _ in range(n)]
    per_group = heads // kv_here
    rows = tokens * per_group
    step = CHUNK // per_group
    if is_first:
        doc_ref, query_ref = take(2)
    else:
        wide_ref, state_ref = take(2)
    kv = take(len(least))
    if is_first:
        wide_ref = take(1)[0]
    out_ref = take(1)[0]
    if is_last:
        take(1)[0][...] = jnp.zeros((8, LANES), F32)
    bias = take(1)[0]
    if is_first:
        doc_rep = take(1)[0]
    if is_last:
        done, sems = take(2)
    block = place_ref[0]

    lane = lax.broadcasted_iota(jnp.int32, (tokens, LANES), 1).astype(F32)
    end = 2 * kv_here * tokens
    for j, ref in enumerate(kv):
        valid = (block >= jnp.where(block % 2 == 0, *least[j])).astype(F32)
        docs = doc_columns(ref[end : end + INFO, :].astype(F32) * valid, tokens)
        bias[j] = jnp.where(docs == lane, 0.0, -BIG).astype(BF16)
    if is_first:
        column = doc_columns(doc_ref[...], tokens)
        for h in range(per_group):
            doc_rep[pl.ds(h, tokens, stride=per_group), :] = (column == lane).astype(F32)
    ones = jnp.ones((STATE_ROWS - HEAD_DIM, tokens), BF16)

    def some_chunks(i, carry):
        chains = [(u, g) for u in range(unroll) for g in range(kv_here)]
        chunk = [i * unroll + u for u in range(unroll)]
        at = [pl.ds(pl.multiple_of(c * CHUNK, CHUNK), CHUNK) for c in chunk]
        picked = [pl.ds(pl.multiple_of(c * (step * heads), step * heads), step * heads) for c in chunk]
        scores, results = {}, {}

        def begin(u, g):
            if is_first:
                query = query_ref[picked[u], :].astype(F32).reshape(step, heads, LANES)
                query = query[:, g * per_group : (g + 1) * per_group, :].reshape(CHUNK, LANES)
                wide = jnp.concatenate([query.astype(BF16), doc_rep[at[u], :].astype(BF16)], axis=1)
                wide_ref[g, at[u], :] = wide
            else:
                wide = wide_ref[g, at[u], :]
            out = []
            for j, ref in enumerate(kv):
                keys = jnp.concatenate([ref[g * tokens : (g + 1) * tokens, :], bias[j]], axis=1)
                out.append(
                    lax.dot_general(keys, wide, (((1,), (1,)), ((), ())), preferred_element_type=F32)
                )
            if is_first:
                token = chunk[u] * step + lax.broadcasted_iota(jnp.int32, (tokens, CHUNK), 1) // per_group
                key_at = lax.broadcasted_iota(jnp.int32, (tokens, CHUNK), 0)
                out[0] = jnp.where(key_at <= token, out[0], -BIG)
            scores[u, g] = out

        def end_chain(u, g):
            here = scores.pop((u, g))
            top = jnp.max(here[0], axis=0, keepdims=True)
            for score in here[1:]:
                top = jnp.maximum(top, jnp.max(score, axis=0, keepdims=True))
            total = None
            if not is_first:
                before = state_ref[g, :, at[u]]
                top_before = before[STATE_ROWS - 1 : STATE_ROWS, :]
                top = jnp.maximum(top, top_before)
                total = before * jnp.exp2((top_before - top) * SCORE_TO_EXP2)
            for ref, score in zip(kv, here):
                weights = jnp.exp2((score - top) * SCORE_TO_EXP2).astype(BF16)
                first = (kv_here + g) * tokens
                parts = [ref[first + p : first + p + LANES, :] for p in range(0, tokens, LANES)]
                values = jnp.concatenate([jnp.concatenate(parts, axis=1), ones], axis=0)
                more = jnp.dot(values, weights, preferred_element_type=F32)
                total = more if total is None else total + more
            if is_last:
                results[u, g] = jnp.transpose(total[0:HEAD_DIM] / total[HEAD_DIM : HEAD_DIM + 1])
            else:
                out_ref[g, 0 : STATE_ROWS - 8, at[u]] = total[0 : STATE_ROWS - 8]
                out_ref[g, STATE_ROWS - 8 : STATE_ROWS, at[u]] = jnp.broadcast_to(top, (8, CHUNK))

        ahead = 3
        for n in range(len(chains) + ahead):
            if n < len(chains):
                begin(*chains[n])
            if n >= ahead:
                end_chain(*chains[n - ahead])
        if is_last:
            for u in range(unroll):
                result = [results[u, g] for g in range(kv_here)]
                if kv_here > 1:
                    result = [r.reshape(step, per_group, LANES) for r in result]
                    result = [jnp.concatenate(result, axis=1).reshape(step * heads, LANES)]
                done[picked[u], :] = result[0].astype(BF16)
                pltpu.make_async_copy(
                    done.at[picked[u], :], out_ref.at[picked[u], :], sems.at[chunk[u]]
                ).start()
        return carry

    lax.fori_loop(0, rows // (CHUNK * unroll), some_chunks, 0)
    if is_last:
        for c in range(rows // CHUNK):
            at = pl.ds(c * step * heads, step * heads)
            pltpu.make_async_copy(done.at[at, :], out_ref.at[at, :], sems.at[c]).wait()


def attend(place, first, state, kv, is_last, tokens, heads, kv_here, after, relay=()):
    is_first = state is None
    least = tuple(pair for _, pair in kv)
    kv = [block for block, _ in kv]
    blocks = len(kv)
    rows = tokens * heads // kv_here
    unroll = min(8, rows // CHUNK)
    wide_shape = sds((kv_here, rows, 2 * LANES), BF16)
    state_shape = sds((kv_here, STATE_ROWS, rows), F32)
    out_shape = sds((tokens * heads, LANES), BF16) if is_last else state_shape
    scratch = [pltpu.VMEM((blocks, tokens, LANES), BF16)]
    if is_first:
        out_shape = (wide_shape, out_shape)
        scratch.append(pltpu.VMEM((rows, LANES), F32))
    if is_last:
        out_shape = (out_shape, sds((8, LANES), F32))
        scratch.append(pltpu.VMEM((tokens * heads, LANES), BF16))
        scratch.append(pltpu.SemaphoreType.DMA((rows // CHUNK,)))
    span = blocks * tokens
    return call(
        functools.partial(attend_kernel, tokens, heads, kv_here, least, is_first, is_last, unroll),
        "attend",
        [place],
        [*first, *([] if is_first else [state]), *kv],
        out_shape,
        scratch=scratch,
        mib=24,
        estimate=cost(
            4 * tokens * heads * span * 2 * LANES, 4 * tokens * heads * LANES * 4, tokens * heads * span
        ),
        after=after,
        out_hbm=is_last,
        relay=relay,
    )


def body(
    blocks,
    lin_query,
    lin_key,
    lin_value,
    lin_gate,
    log_decay,
    norm_gain,
    doc_ids,
    soft_query,
    soft_key,
    soft_value,
):
    tokens, heads, _ = lin_query.shape
    tensor = HEADS // heads
    kv_here = max(1, heads // GROUP)
    parts = 2 if heads % 16 == 0 else 1
    longest = blocks * tokens * 5 // 8
    window = min(blocks - 1, (longest - 1 + tokens - 1) // tokens)
    flat = lambda x: x.reshape(-1, LANES)
    block = lax.axis_index("seq")
    place = block.astype(jnp.int32).reshape(1)
    start = (lax.axis_index("tp") * heads // GROUP).astype(jnp.int32).reshape(1)

    def send(x, pairs):
        return lax.ppermute(x, "seq", [(a, b % blocks) for a, b in pairs])

    everyone = range(blocks)
    swap = [(b, b ^ 1) for b in everyone]

    own_kv, docs, cumul, key, value = fetch(
        start,
        [
            doc_ids.reshape(tokens // LANES, LANES),
            jnp.transpose(log_decay),
            flat(soft_key),
            flat(soft_value),
            flat(lin_key),
            flat(lin_value),
        ],
        tokens,
        heads,
        kv_here,
    )

    forward = [(b, b + 2) for b in everyone]
    ahead = send(own_kv, forward)

    size = quarter_rows(heads)
    others = range(1, GROUP_BLOCKS)
    *sent, query = block_state(
        place, flat(soft_query), cumul, docs, key, value, tokens, heads
    )
    quarters = [sent[0]] + [send(sent[j], [(b, b ^ j) for b in everyone]) for j in others]

    state = {}

    def first_attention(after, relay):
        state["wide"], state["sum"], copy = attend(
            place, (docs, query), None, [(own_kv, (0, 0))], False, tokens, heads, kv_here, after, relay
        )
        return state["sum"], copy

    def more_attention(kv, is_last, after, relay=()):
        out = attend(
            place, (state["wide"],), state["sum"], kv, is_last, tokens, heads, kv_here, after, relay
        )
        state["sum"] = out[0] if relay else out
        return out

    inner, qh = [], []

    def inner_of(part, after, relay=()):
        n = heads // parts
        got = inner_part(
            cumul, docs, flat(lin_query), key, value, tokens, heads, part * n, n, after, relay
        )
        inner.append(got[0])
        qh.append(got[1])
        return (got[0], *got[2:]) if relay else got[0]

    done, lane = first_attention([sent[0]], [ahead])
    if parts > 1:
        done = inner_of(0, [done])
    second = send(lane, [(b, b + 2) for b in range(2, blocks - 2)])
    run, lane = group_map(place, quarters, size, [done], [lane])
    first_cross = send(lane, swap)
    stages = (blocks // GROUP_BLOCKS).bit_length() - 1
    before, done = None, run
    for stage in range(stages):
        came = send(run, [(b, b ^ (GROUP_BLOCKS << stage)) for b in everyone])
        if stage == stages - 1:
            done = more_attention([(lane, (2, 2))], False, [done])
            done = inner_of(parts - 1, [done])
        else:
            run, before = scan_step(place, stage + 2, run, came, before, size, [done])
            done = run
    assert window % 2 == 0 or window == 5
    payload = pick(place, own_kv, second, [done])
    slot = (send(payload, [(b, b + 1) for b in everyone]), (window if window % 2 else blocks, 1))
    *priors, prior_doc = prior_states(place, stages + 1, quarters, came, before, size, [payload])
    priors = [priors[0]] + [send(priors[j], [(b, b ^ j) for b in everyone]) for j in others]
    done = more_attention([(first_cross, (2, 3)), (second, (4, 4))], False, [prior_doc])
    (lane,) = pass_on([second], [done, *priors])
    rest = [(send(lane, swap), (4, 5))]
    for back in range(3, window // 2 + 1):
        lane = send(lane, forward)
        rest.append((lane, (2 * back, 2 * back)))
        rest.append((send(lane, swap), (2 * back, 2 * back + 1)))
    mixed, squares = mix(place, docs, prior_doc, cumul, inner, qh, priors, tokens, heads, [done])
    sums = [squares]
    for other in range(1, tensor):
        sums.append(lax.ppermute(squares, "tp", [(t, t ^ other) for t in range(tensor)]))
    rest.insert(0, slot)
    done = squares
    while rest:
        got = more_attention(rest[:1], len(rest) == 1, [done])
        rest, done = rest[1:], got
    soft_out, done = got
    lin_out = finish(norm_gain, flat(lin_gate), mixed, sums, tokens, heads, [done])
    shape = (tokens, heads, HEAD_DIM)
    return lin_out.reshape(shape), soft_out.reshape(shape)


def solution(mesh):
    in_specs = (
        P("seq", "tp", None),
        P("seq", "tp", None),
        P("seq", "tp", None),
        P("seq", "tp", None),
        P("seq", "tp"),
        P("tp", None),
        P("seq"),
        P("seq", "tp", None),
        P("seq", None, None),
        P("seq", None, None),
    )
    out_specs = (P("seq", "tp", None), P("seq", "tp", None))
    return jax.shard_map(
        functools.partial(body, mesh.shape["seq"]),
        mesh=mesh,
        in_specs=in_specs,
        out_specs=out_specs,
        check_vma=False,
    )
```
